32 devices in a mesh: rep: 2 (over y), exp: 4 (over z), unit: 4 (over x, core).
Axes of the slice: x: 2, y: 2, z: 4, core: 2. Of those that a mesh axis runs over, the one named last changes fastest.
Arguments:
- tokens: bfloat16 [1024, 4096], P(('rep', 'exp')), parts along dimension 0, may hold values from -6 to 6
- norm_gain: float32 [4096], replicated, may hold values from 0.1 to 1.9
- route_ids: int32 [1024, 2], P(('rep', 'exp')), parts along dimension 0, may hold values from 0 to 7, all different within a row; in each aligned block of 128 rows (0 to 127, 128 to 255, ...) at most 40 rows name the same one
- route_weight: float32 [1024, 2], P(('rep', 'exp')), parts along dimension 0, may hold values from 0.2 to 1
- active_blocks: int32 [4, 8, 48], P('rep'), parts along dimension 0, may hold values from 0 to 112, as said below
- gate_weight: bfloat16 [4096, 57344], P(None, ('exp', 'unit')), may hold values from -0.09375 to 0.09375
- up_weight: bfloat16 [4096, 57344], P(None, ('exp', 'unit')), may hold values from -0.09375 to 0.09375
- down_weight: bfloat16 [57344, 4096], P(('exp', 'unit')), may hold values from -0.1875 to 0.1875
Outputs:
- mixed: bfloat16 [1024, 4096], P(('rep', 'exp'), 'unit'), parts along dimension 0
The draws below stay inside these ranges and needn't reach their ends.
There are 2 independent parts, one for each index of `rep`. The reference program is written for one: setup_inputs(seed, part) draws one part's arguments, and reference() takes and returns one part's arrays. A program takes and returns all parts, laid end to end along the dimension named above; an argument that names none is the same for every part. Nothing has to cross between parts.
Inputs may be any that keep to these rules, and one draw needn't show every extreme that they name: `route_ids`: in each aligned block of 128 tokens (those of one index of exp) no expert is named by more than 40 route entries, a bound that some block reaches; the two experts of a token differ; every expert is named somewhere. `active_blocks`: each list holds 24 to 48 distinct block numbers below 112, followed by 112 as padding; some list is full and some list is padded.
All inputs are finite; a program needn't handle non-finite values.
Results may differ from the reference program's by a relative error of at most 0.0095.
Values may be sent and summed in bfloat16 or wider, within the bound.
No kernel may reach another device: no remote copies, remote signals or barrier semaphores. Data moves between devices by JAX's collectives and lax.ppermute only.
A program may use at most 192 MiB of HBM per device.

```python
import math
import jax
import jax.numpy as jnp
import numpy as np
from jax import lax

D = 4096
EXPERTS = 8
FF = 7168
BLK = 64
ACT = 48
TILE = 256
TOK_DEV = 128
TOKENS = 512
CAP = 40
NBLK = 112
TILES = 2
UNITS_DEV = 3584
N_EXP = 4


def draw_active_blocks(key, part):
    key = jax.random.fold_in(key, 7)
    perm_key, count_key = jax.random.split(key)
    list_count = TILES * EXPERTS
    list_keys = jax.random.split(perm_key, list_count)
    chosen = jax.vmap(lambda one_key: jax.random.permutation(one_key, NBLK)[:ACT])(list_keys)
    counts = jax.random.randint(count_key, (list_count,), ACT // 2, ACT + 1)
    counts = counts.at[0].set(ACT).at[1].set(ACT // 2)
    filled = jnp.arange(ACT)[None, :] < counts[:, None]
    return jnp.where(filled, chosen, NBLK).reshape(TILES, EXPERTS, ACT).astype(jnp.int32)


def block_levels(rng, dims, cuts, least, top_value):
    def one(position, blocks):
        heights = jax.random.uniform(jax.random.fold_in(jax.random.fold_in(rng, 6), position), (blocks,), jnp.float32, least / len(cuts), top_value / len(cuts))
        return jnp.repeat(jnp.exp(heights), dims[position] // blocks).reshape((-1,) + (1,) * (len(dims) - position - 1))

    factor_of = one(*cuts[0])
    for cut in cuts[1:]:
        factor_of = factor_of * one(*cut)
    return factor_of


def shared_out(key, own, number, rows, number_of, top, bound, lean):
    sequence = jax.random.permutation(key, number_of)
    crowded, usual = shares(number_of, rows * top, bound, lean, True), shares(number_of, rows * top, bound, lean, False)
    places = jnp.arange(number_of)

    def named(lengths, turn):
        used = int((lengths > 0).sum())
        fixed = max(1, used // 4)
        shifted = fixed + (places - fixed + turn * (used - fixed)) % max(1, number_of - fixed)
        return jnp.zeros((number_of,), jnp.int32).at[sequence[jnp.where(places < fixed, places, shifted)]].set(jnp.asarray(lengths, jnp.int32))

    lengths = jnp.where(number % 4 == 0, named(crowded, number // 4), named(usual, number - number // 4 - 1))
    mixed = jax.random.permutation(jax.random.fold_in(own, 3), number_of)
    donor, sink = mixed[0:number_of // 2 * 2:2], mixed[1:number_of // 2 * 2:2]
    margin = jnp.minimum(lengths[donor] - 1, bound - lengths[sink]) // 2
    margin = jnp.where((donor == sequence[0]) | (sink == sequence[0]) | (lengths[sink] == 0), 0, jnp.maximum(margin, 0))
    shifted = jax.random.randint(jax.random.fold_in(own, 4), (number_of // 2,), 0, 1 << 20) % (margin + 1)
    lengths = lengths.at[donor].add(-shifted).at[sink].add(shifted)
    labels = jnp.searchsorted(jnp.cumsum(lengths), jnp.arange(rows * top), side="right").astype(jnp.int32)
    grid = labels.reshape(top, rows).T
    grid = grid[jax.random.permutation(jax.random.fold_in(own, 1), rows)]
    turn = jax.random.randint(jax.random.fold_in(own, 2), (rows, 1), 0, top)
    return jnp.take_along_axis(grid, (jnp.arange(top)[None, :] + turn) % top, axis=1)


def shares(number_of, total, bound, slope, full):
    loads = [(1 << 20) // math.isqrt(standing ** slope) + 1 for standing in range(1, number_of + 1)]
    largest = bound if full else min(bound, max(-(-total // number_of), total * loads[0] // sum(loads)))
    least = 1 if total - largest >= number_of - 1 else 0
    given, rest = [largest] + [least] * (number_of - 1), total - largest - least * (number_of - 1)
    while rest > 0:
        candidates = [i for i in range(1, number_of) if given[i] < largest] or [i for i in range(1, number_of) if given[i] < bound]
        mass, left = sum([loads[i] for i in candidates]), rest
        for i in candidates:
            more = min(bound - given[i], max(1, left * loads[i] // mass), rest)
            given[i] = given[i] + more
            rest = rest - more
    return np.array(given)


def gaussian(key, dims, width, reach, shards=(), kind=jnp.bfloat16):
    result = jax.random.normal(key, dims, jnp.float32) * width
    if len(shards) > 0:
        result = block_levels(key, dims, shards, -0.22, 0.18) * result
    return jnp.clip(result, min=-reach, max=reach).astype(kind)


def setup_inputs(seed: int = 0, part: int = 0) -> dict:
    arg_keys = jax.random.split(jax.random.key(seed), 9)
    part_keys = jax.random.split(jax.random.fold_in(arg_keys[8], part), 9)
    tokens = gaussian(part_keys[0], (TOKENS, D), 1.0, 6.0, ((0, 4),))
    norm_gain = jnp.clip(1.0 + 0.18 * jax.random.normal(arg_keys[1], (D,), jnp.float32), 0.1, 1.9)
    route_ids_keys = jax.random.split(jax.random.fold_in(part_keys[2], 1), TOKENS // TOK_DEV)
    route_ids_turns = jax.random.permutation(jax.random.fold_in(part_keys[2], 3), TOKENS // TOK_DEV)
    route_ids = jax.vmap(lambda own, number: shared_out(jax.random.fold_in(part_keys[2], 2), own, number, TOK_DEV, EXPERTS, 2, CAP, 2))(route_ids_keys, route_ids_turns).reshape((TOKENS, 2))
    route_weight = jnp.clip(0.2 + 0.8 * jax.random.uniform(part_keys[3], (TOKENS, 2), jnp.float32) ** block_levels(part_keys[3], (TOKENS, 2), ((0, 4),), -0.2, 0.2), 0.2, 1.0)
    active_blocks = draw_active_blocks(jax.random.fold_in(jax.random.fold_in(arg_keys[8], part), 71), part)
    gate_weight = gaussian(arg_keys[5], (D, EXPERTS * FF), D ** -0.5, 0.09375, ((1, 16),))
    up_weight = gaussian(arg_keys[6], (D, EXPERTS * FF), D ** -0.5, 0.09375, ((1, 16),))
    down_weight = gaussian(arg_keys[7], (EXPERTS * FF, D), (FF // 8) ** -0.5, 0.1875, ((0, 16),))
    return dict(tokens=tokens, norm_gain=norm_gain, route_ids=route_ids, route_weight=route_weight, active_blocks=active_blocks, gate_weight=gate_weight, up_weight=up_weight, down_weight=down_weight)


EPSILON = 1e-05

def normalize(tokens, norm_gain):
    values = tokens.astype(jnp.float32)
    inv_rms = lax.rsqrt(lax.optimization_barrier(jnp.mean(values * values, axis=-1, keepdims=True)) + EPSILON)
    return (values * inv_rms * norm_gain).astype(jnp.bfloat16)

def slot_numbers(entries, expert_count):
    onehot = (entries[..., None] == jnp.arange(expert_count, dtype=jnp.int32)).astype(jnp.int32)
    before = jnp.cumsum(onehot, axis=-2, dtype=jnp.int32) - onehot
    return lax.optimization_barrier(jnp.sum(before * onehot, axis=-1)).astype(jnp.int32)

def reference(tokens, norm_gain, route_ids, route_weight, active_blocks, gate_weight, up_weight, down_weight):
    normed = normalize(tokens, norm_gain)
    slot_index = slot_numbers(route_ids.reshape(N_EXP, 2 * TOK_DEV), EXPERTS).reshape(TOKENS, 2)
    positions = jnp.arange(TOKENS, dtype=jnp.int32)
    buffer_row = ((positions // TOK_DEV)[:, None] * CAP + slot_index).astype(jnp.int32)
    capacity = N_EXP * CAP
    slot_rows = jnp.zeros((EXPERTS, capacity, D), jnp.bfloat16).at[route_ids, buffer_row].set(jnp.broadcast_to(normed[:, None, :], (TOKENS, 2, D)))
    slot_tiles = jnp.zeros((EXPERTS, capacity), jnp.int32).at[route_ids, buffer_row].set(jnp.broadcast_to((positions // TILE)[:, None], (TOKENS, 2)).astype(jnp.int32))
    block_ids = jnp.arange(NBLK, dtype=jnp.int32)
    block_on = jnp.any(active_blocks[:, :, :, None] == block_ids, axis=2).astype(jnp.float32)
    block_on = jnp.transpose(block_on, (1, 0, 2))
    group_count = FF // UNITS_DEV

    def expert_output(packed):
        expert_rows, expert_tiles, expert_blocks, expert = packed
        gate_cols = lax.dynamic_slice_in_dim(gate_weight, expert * FF, FF, 1)
        up_cols = lax.dynamic_slice_in_dim(up_weight, expert * FF, FF, 1)
        down_rows = lax.dynamic_slice_in_dim(down_weight, expert * FF, FF, 0)
        gate_acts = jnp.dot(expert_rows, gate_cols, preferred_element_type=jnp.float32)
        up_acts = jnp.dot(expert_rows, up_cols, preferred_element_type=jnp.float32)
        row_mask = expert_blocks[expert_tiles]
        hidden = jax.nn.relu(gate_acts) * jax.nn.relu(up_acts)
        hidden = (hidden.reshape(capacity, NBLK, BLK) * row_mask[:, :, None]).reshape(capacity, FF)
        hidden = hidden.astype(jnp.bfloat16)
        hidden_groups = jnp.transpose(hidden.reshape(capacity, group_count, UNITS_DEV), (1, 0, 2))
        down_groups = down_rows.reshape(group_count, UNITS_DEV, D)

        def add_group(total, pair):
            group_hidden, group_down = pair
            term = jnp.dot(group_hidden, group_down, preferred_element_type=jnp.float32)
            rounded = lax.optimization_barrier(term.astype(jnp.bfloat16))
            return (total + rounded.astype(jnp.float32), None)
        total, _ = lax.scan(add_group, jnp.zeros((capacity, D), jnp.float32), (hidden_groups, down_groups))
        return total
    expert_outs = lax.map(expert_output, (slot_rows, slot_tiles, block_on, jnp.arange(EXPERTS, dtype=jnp.int32)))
    picked = expert_outs[route_ids, buffer_row]
    mixed = lax.optimization_barrier(jnp.sum(route_weight[:, :, None] * picked, axis=1))
    return mixed.astype(jnp.bfloat16)
```

```python
import functools

import jax
import jax.numpy as jnp
import numpy as np
from jax import lax
from jax.experimental import pallas as pl
from jax.experimental.pallas import tpu as pltpu
from jax.sharding import PartitionSpec as P

EXPERTS = 8
FF = 7168
BLK = 64
TILE = 256
CAP = 40

EPSILON = 1e-05

IN_CHUNKS = 2
OUT_CHUNKS = 2
K_SLAB = 256
K_DEPTH = 6
N_SLAB = 256
N_DEPTH = 4
VMEM_LIMIT = 40 * 1024 * 1024

F32 = jnp.float32
BF16 = jnp.bfloat16


def normalize(tokens, norm_gain):
    values = tokens.astype(jnp.float32)
    inv_rms = lax.rsqrt(jnp.mean(values * values, axis=-1, keepdims=True) + EPSILON)
    return (values * inv_rms * norm_gain).astype(jnp.bfloat16)


def slot_numbers(entries, expert_count):
    onehot = (entries[..., None] == jnp.arange(expert_count, dtype=jnp.int32)).astype(jnp.int32)
    before = jnp.cumsum(onehot, axis=-2, dtype=jnp.int32) - onehot
    return jnp.sum(before * onehot, axis=-1)


def spread_experts(
    tokens, norm_gain, route_ids, route_weight, active_blocks, gate_weight, up_weight, down_weight
):
    exp_count = lax.axis_size("exp")
    unit_count = lax.axis_size("unit")
    tok_count, feature_width = tokens.shape
    unit_width = gate_weight.shape[1]
    row_units = unit_count * unit_width
    per_exp = max(1, row_units // FF)
    part_width = feature_width // unit_count
    block_count = unit_width // BLK
    tile_count = active_blocks.shape[0]
    exp_index = lax.axis_index("exp")
    unit_index = lax.axis_index("unit")
    first_unit = (exp_index * unit_count + unit_index) * unit_width
    own_expert = first_unit // FF
    first_block = first_unit % FF // BLK
    local_expert = own_expert - exp_index * row_units // FF
    normed = normalize(tokens, norm_gain)
    slot_index = slot_numbers(route_ids.reshape(1, -1), EXPERTS).reshape(tok_count, 2)
    positions = jnp.arange(tok_count, dtype=jnp.int32)
    tile_of = (exp_index * tok_count + positions) // TILE
    route_slot = (route_ids * CAP + slot_index).reshape(-1)
    token_source = (
        jnp.full((EXPERTS * CAP,), tok_count, jnp.int32)
        .at[route_slot]
        .set(jnp.repeat(positions, 2))
    )
    row_experts = np.arange(exp_count)[:, None] * row_units // FF + np.arange(per_exp)[None, :]
    slot_source = token_source.reshape(EXPERTS, CAP)[row_experts]
    padded_tiles = jnp.concatenate([tile_of, jnp.zeros((1,), jnp.int32)])
    slot_tiles = padded_tiles[slot_source]
    active_mine = lax.dynamic_index_in_dim(active_blocks, own_expert, 1, keepdims=False)
    local_blocks = first_block + jnp.arange(block_count, dtype=jnp.int32)
    block_on = jnp.any(active_mine[:, :, None] == local_blocks[None, None, :], axis=1).astype(
        jnp.float32
    )
    row_part = lax.dynamic_slice_in_dim(normed, unit_index * part_width, part_width, 1)
    padded_rows = jnp.concatenate([row_part, jnp.zeros((1, part_width), jnp.bfloat16)], 0)
    whole_rows = lax.all_gather(
        lax.all_to_all(padded_rows[slot_source], "exp", split_axis=0, concat_axis=0, tiled=True),
        "unit",
        axis=3,
        tiled=True,
    )
    slot_count = whole_rows.shape[2]
    own_rows = lax.dynamic_index_in_dim(whole_rows, local_expert, 1, keepdims=False).reshape(
        -1, feature_width
    )
    own_tiles = lax.dynamic_index_in_dim(
        lax.all_to_all(slot_tiles, "exp", split_axis=0, concat_axis=0, tiled=True),
        local_expert,
        1,
        keepdims=False,
    ).reshape(-1)
    tile_hot = (own_tiles[:, None] == jnp.arange(tile_count, dtype=jnp.int32)[None, :]).astype(
        jnp.float32
    )
    row_mask = jnp.dot(tile_hot, block_on, precision=lax.Precision.HIGHEST)
    gate_acts = jnp.dot(own_rows, gate_weight, preferred_element_type=jnp.float32)
    up_acts = jnp.dot(own_rows, up_weight, preferred_element_type=jnp.float32)
    hidden = jax.nn.relu(gate_acts) * jax.nn.relu(up_acts)
    hidden = (hidden.reshape(-1, block_count, BLK) * row_mask[:, :, None]).reshape(-1, unit_width)
    hidden = hidden.astype(jnp.bfloat16)
    partial_value = jnp.dot(hidden, down_weight, preferred_element_type=jnp.float32)
    partial_value = partial_value.reshape(exp_count, slot_count, feature_width)
    result = jnp.zeros((exp_count, per_exp, slot_count, feature_width), jnp.float32)
    partial_all = lax.dynamic_update_index_in_dim(result, partial_value, local_expert, 1)

    def by_expert(returned):
        last_width = returned.shape[-1]
        if per_exp == 1:
            grouped = returned.reshape(EXPERTS, exp_count // EXPERTS, CAP, last_width)
            return jnp.sum(grouped, axis=1, dtype=jnp.float32)
        return returned.reshape(EXPERTS, CAP, last_width).astype(jnp.float32)

    summed = lax.psum_scatter(
        partial_all.astype(jnp.bfloat16), "unit", scatter_dimension=3, tiled=True
    ).astype(jnp.float32)
    returned = lax.all_to_all(
        summed.astype(jnp.bfloat16), "exp", split_axis=0, concat_axis=0, tiled=True
    ).astype(summed.dtype)
    per_expert = by_expert(returned)
    last_width = per_expert.shape[-1]
    picked = per_expert.reshape(EXPERTS * CAP, last_width)[route_slot].reshape(
        tok_count, 2, last_width
    )
    mixed = jnp.sum(route_weight[:, :, None] * picked, axis=1)
    return mixed.astype(jnp.bfloat16)


def place(sizes):
    exp_count, groups = sizes
    return lax.axis_index("exp"), lax.axis_index("unit") // 2, lax.axis_index("unit") % 2


def route_kernel(sizes, width, tokens, gain, ids, own, *rest):
    exp_count, groups = sizes
    sends, normed = rest[:-1], rest[-1]
    rows, features = tokens.shape
    z, g, s = place(sizes)
    step = 16
    for first in range(0, rows, step):
        values = tokens[first : first + step, :].astype(F32)
        mean = jnp.sum(values * values, axis=1, keepdims=True) * (1.0 / features)
        inv_rms = lax.rsqrt(mean + EPSILON)
        normed[first : first + step, :] = (values * inv_rms * gain[...]).astype(BF16)
    earlier = (
        lax.broadcasted_iota(jnp.int32, (rows, rows), 0)
        < lax.broadcasted_iota(jnp.int32, (rows, rows), 1)
    ).astype(BF16)
    ids0, ids1 = ids[0:1, :], ids[1:2, :]
    slots = lax.broadcasted_iota(jnp.int32, (CAP, rows), 0)
    distance = lax.broadcasted_iota(jnp.int32, (max(8, exp_count), rows), 0)
    experts = lax.rem(z + distance, exp_count) * groups + g
    named = (ids0 == experts) | (ids1 == experts)
    before = jnp.dot(named.astype(BF16), earlier, preferred_element_type=F32).astype(jnp.int32)
    picks = []
    for d in range(exp_count):
        hit = named[d : d + 1, :].astype(jnp.int32)
        place_of = jnp.where(hit > 0, before[d : d + 1, :], -1)
        picks.append((place_of == slots).astype(F32))
    own[...] = jnp.dot(
        picks[0].astype(BF16), normed[...], preferred_element_type=F32
    ).astype(BF16)
    others = jnp.concatenate(picks[1:], axis=0).astype(BF16)
    half = features // 2
    for chunk in range(half // width):
        start = pl.multiple_of(s * half + chunk * width, 128)
        found = jnp.dot(others, normed[:, pl.ds(start, width)], preferred_element_type=F32)
        for d in range(1, exp_count):
            part = found[(d - 1) * CAP : d * CAP, :].astype(BF16)
            sends[chunk * (exp_count - 1) + d - 1][...] = part


def prepare_kernel(sizes, ids, weights, active, combine_high, combine_low, mask):
    exp_count, groups = sizes
    rows = ids.shape[1]
    z, g, s = place(sizes)
    earlier = (
        lax.broadcasted_iota(jnp.int32, (rows, rows), 0)
        < lax.broadcasted_iota(jnp.int32, (rows, rows), 1)
    ).astype(BF16)
    ids0, ids1 = ids[0:1, :], ids[1:2, :]
    slots = lax.broadcasted_iota(jnp.int32, (CAP, rows), 0)

    def expert_at(j):
        return lax.rem(z + j // groups, exp_count) * groups + lax.rem(
            g + groups - lax.rem(j, groups), groups
        )

    experts = expert_at(lax.broadcasted_iota(jnp.int32, (EXPERTS, rows), 0))
    named = (ids0 == experts) | (ids1 == experts)
    before = jnp.dot(named.astype(BF16), earlier, preferred_element_type=F32).astype(jnp.int32)
    zero = jnp.zeros((CAP, rows), F32)
    parts = []
    for j in range(EXPERTS):
        here = before[j : j + 1, :] == slots
        expert = expert_at(j)
        first = jnp.where(here & (ids0 == expert), weights[0:1, :], zero)
        second = jnp.where(here & (ids1 == expert), weights[1:2, :], zero)
        parts.append(first + second)
    total = EXPERTS * CAP
    padded = -(-total // 128) * 128
    if padded > total:
        parts.append(jnp.zeros((padded - total, rows), F32))
    table = jnp.concatenate(parts, axis=0).T
    high = table.astype(BF16)
    low = (table - high.astype(F32)).astype(BF16)
    combine_high[...] = high
    combine_low[...] = low
    unit_width = mask.shape[1]
    blocks = lax.broadcasted_iota(jnp.int32, mask.shape, 1) // BLK + s * (unit_width // BLK)
    source = lax.broadcasted_iota(jnp.int32, (mask.shape[0], 1), 0)
    own_expert = z * groups + g

    def add_entry(k, found):
        entry = jnp.full((mask.shape[0], 1), -1, jnp.int32)
        for d in range(exp_count):
            tile = lax.rem(z - d + exp_count, exp_count) * rows // TILE
            entry = jnp.where(source == d, active[tile, own_expert, k], entry)
        return jnp.where(blocks == entry, 1.0, found)

    mask[...] = lax.fori_loop(0, active.shape[2], add_entry, jnp.zeros(mask.shape, F32))


def hidden_kernel(sizes, chunk, width, first, last, *refs):
    exp_count, groups = sizes
    z, g, s = place(sizes)
    refs = list(refs)
    own = refs.pop(0)
    mine = [refs.pop(0) for _ in range(exp_count - 1)]
    other = [refs.pop(0) for _ in range(exp_count - 1)]
    gate, up = refs.pop(0), refs.pop(0)
    gate_in, up_in = (None, None) if first else (refs.pop(0), refs.pop(0))
    mask = refs.pop(0) if last else None
    if last:
        hidden = refs.pop(0)
        gate_sum, up_sum = refs.pop(0), refs.pop(0)
    else:
        gate_sum, up_sum = refs.pop(0), refs.pop(0)
    rows, slabs, sems = refs
    half = own.shape[1] // 2
    slab_count = width // K_SLAB
    total = 2 * slab_count
    depth = min(K_DEPTH, 2 * total)

    def copy(index, ref, which):
        side = jnp.where(index < slab_count, s, 1 - s)
        row = side * half + chunk * width + lax.rem(index, slab_count) * K_SLAB
        slot = lax.rem(index * 2 + which, depth)
        return pltpu.make_async_copy(
            ref.at[pl.ds(pl.multiple_of(row, K_SLAB), K_SLAB), :], slabs.at[slot], sems.at[slot]
        )

    for n in range(depth):
        copy(n // 2, (gate, up)[n % 2], n % 2).start()
    for side_of in range(2):
        source = (mine, other)[side_of]
        side = s if side_of == 0 else 1 - s
        start = pl.multiple_of(side * half + chunk * width, 128)
        pieces = [own[:, pl.ds(start, width)].astype(F32)] + [r[...].astype(F32) for r in source]
        whole = jnp.concatenate(pieces, axis=0).astype(BF16)
        for n in range(slab_count):
            rows[side_of * slab_count + n] = whole[:, n * K_SLAB : (n + 1) * K_SLAB]
    unit_width = gate.shape[1]
    n_tile = 512
    if first:
        gate_sum[...] = jnp.zeros_like(gate_sum)
        up_sum[...] = jnp.zeros_like(up_sum)
    else:
        gate_sum[...] = gate_in[...]
        up_sum[...] = up_in[...]

    def body(index, carry):
        left = rows[index]
        for which, (ref, acc) in enumerate(((gate, gate_sum), (up, up_sum))):
            copy(index, ref, which).wait()
            slot = lax.rem(index * 2 + which, depth)
            for col in range(0, unit_width, n_tile):
                end = min(col + n_tile, unit_width)
                acc[:, col:end] += jnp.dot(
                    left, slabs[slot, :, col:end], preferred_element_type=F32
                )

            @pl.when(index * 2 + which + depth < 2 * total)
            def _():
                copy(index + depth // 2, ref, which).start()

        return carry

    lax.fori_loop(0, total, body, 0)
    if last:
        for d in range(exp_count):
            lines = slice(d * CAP, (d + 1) * CAP)
            for col in range(0, unit_width, n_tile):
                cols = slice(col, min(col + n_tile, unit_width))
                product = jnp.maximum(gate_sum[lines, cols], 0.0) * jnp.maximum(
                    up_sum[lines, cols], 0.0
                )
                gate_sum[lines, cols] = product * mask[d : d + 1, cols]
        hidden[...] = gate_sum[...].astype(BF16)


def output_kernel(sizes, chunk, width, keep, *refs):
    exp_count, groups = sizes
    z, g, s = place(sizes)
    refs = list(refs)
    hidden, down = refs.pop(0), refs.pop(0)
    received = [refs.pop(0) for _ in range(groups)] if keep else None
    count = groups * exp_count if keep else groups
    outs = [refs.pop(0) for _ in range(count)]
    slabs, sems = refs
    side = s if keep else 1 - s
    part = down.shape[1] // (2 * groups)
    per_group = width // N_SLAB
    total = groups * per_group
    depth = min(N_DEPTH, total)

    def copy(index):
        group = lax.rem(g + index // per_group, groups)
        column = (group * 2 + side) * part + chunk * width + index % per_group * N_SLAB
        return pltpu.make_async_copy(
            down.at[:, pl.ds(pl.multiple_of(column, 128), N_SLAB)],
            slabs.at[index % depth],
            sems.at[index % depth],
        )

    for index in range(depth):
        copy(index).start()
    for index in range(total):
        copy(index).wait()
        value = jnp.dot(hidden[...], slabs[index % depth], preferred_element_type=F32)
        if index + depth < total:
            copy(index + depth).start()
        group = index // per_group
        cols = slice(index % per_group * N_SLAB, (index % per_group + 1) * N_SLAB)
        if keep:
            value = value + received[group][:, cols].astype(F32)
            for d in range(exp_count):
                lines = value[d * CAP : (d + 1) * CAP, :].astype(BF16)
                outs[group * exp_count + d][:, cols] = lines
        else:
            outs[group][:, cols] = value.astype(BF16)


def combine_kernel(sizes, high, low, *refs):
    refs = list(refs)
    out = refs.pop()
    total = EXPERTS * CAP
    per_chunk = EXPERTS
    width = refs[0].shape[1]
    for chunk in range(len(refs) // per_chunk):
        pieces = [r[...].astype(F32) for r in refs[chunk * per_chunk : (chunk + 1) * per_chunk]]
        found = jnp.concatenate(pieces, axis=0).astype(BF16)
        value = jnp.dot(high[:, :total], found, preferred_element_type=F32)
        value = value + jnp.dot(low[:, :total], found, preferred_element_type=F32)
        out[:, chunk * width : (chunk + 1) * width] = value.astype(BF16)


def call(kernel, outs, ins, scratch=(), flops=0, moved=0, aliases=None):
    vmem = pl.BlockSpec(memory_space=pltpu.VMEM)
    arrays = [a for a, _ in ins]
    specs = [vmem if space is None else pl.BlockSpec(memory_space=space) for _, space in ins]
    return pl.pallas_call(
        kernel,
        out_shape=[jax.ShapeDtypeStruct(shape, kind) for shape, kind in outs],
        in_specs=specs,
        out_specs=[vmem] * len(outs),
        scratch_shapes=list(scratch),
        compiler_params=pltpu.CompilerParams(vmem_limit_bytes=VMEM_LIMIT),
        cost_estimate=pl.CostEstimate(flops=flops, bytes_accessed=moved, transcendentals=0),
    )(*arrays)


def paired_experts(
    tokens, norm_gain, route_ids, route_weight, active_blocks, gate_weight, up_weight, down_weight
):
    exp_count, unit_count = lax.axis_size("exp"), lax.axis_size("unit")
    groups = unit_count // 2
    sizes = (exp_count, groups)
    tok_count, features = tokens.shape
    unit_width = gate_weight.shape[1]
    slots = exp_count * CAP
    half = features // 2
    width = half // IN_CHUNKS
    ids = route_ids.T
    weights = route_weight.T

    def shift(value, distance, group_shift=0):
        pairs = []
        for z in range(exp_count):
            for u in range(unit_count):
                target = (z + distance) % exp_count
                group = (u // 2 + group_shift) % groups
                pairs.append((z * unit_count + u, target * unit_count + group * 2 + u % 2))
        return lax.ppermute(value, ("exp", "unit"), pairs)

    def swap(value):
        return lax.ppermute(value, "unit", [(u, u ^ 1) for u in range(unit_count)])

    own, *sends = call(
        functools.partial(route_kernel, sizes, width),
        [((CAP, features), BF16)] + [((CAP, width), BF16)] * (IN_CHUNKS * (exp_count - 1)),
        [(tokens, None), (norm_gain.reshape(1, -1), None), (ids, None)],
        [pltpu.VMEM((tok_count, features), BF16)],
        flops=2 * tok_count * slots * features,
        moved=4 * tok_count * features,
    )
    padded = -(-EXPERTS * CAP // 128) * 128
    combine_high, combine_low, mask = call(
        functools.partial(prepare_kernel, sizes),
        [
            ((tok_count, padded), BF16),
            ((tok_count, padded), BF16),
            ((max(8, exp_count), unit_width), F32),
        ],
        [(ids, None), (weights, None), (active_blocks, pltpu.SMEM)],
        moved=1 << 20,
    )
    mine, other = [], []
    for chunk in range(IN_CHUNKS):
        batch = sends[chunk * (exp_count - 1) : (chunk + 1) * (exp_count - 1)]
        arrived = [shift(value, d + 1) for d, value in enumerate(batch)]
        mine.append(arrived)
        other.append([swap(value) for value in arrived])
    sums = None
    for chunk in range(IN_CHUNKS):
        first, last = chunk == 0, chunk == IN_CHUNKS - 1
        ins = [(own, None)] + [(v, None) for v in mine[chunk] + other[chunk]]
        ins += [(gate_weight, pl.ANY), (up_weight, pl.ANY)]
        if not first:
            ins += [(v, None) for v in sums]
        if last:
            ins += [(mask, None)]
        acc = ((slots, unit_width), F32)
        scratch = [
            pltpu.VMEM((2 * width // K_SLAB, slots, K_SLAB), BF16),
            pltpu.VMEM((K_DEPTH, K_SLAB, unit_width), BF16),
            pltpu.SemaphoreType.DMA((K_DEPTH,)),
        ]
        if last:
            scratch = [pltpu.VMEM(*acc), pltpu.VMEM(*acc)] + scratch
        sums = call(
            functools.partial(hidden_kernel, sizes, chunk, width, first, last),
            [((slots, unit_width), BF16)] if last else [acc, acc],
            ins,
            scratch,
            flops=2 * 2 * slots * 2 * width * unit_width,
            moved=2 * 2 * width * unit_width * 2,
        )
    hidden = sums[0]
    part = features // unit_count
    out_width = part // OUT_CHUNKS

    def output(chunk, keep, received):
        ins = [(hidden, None), (down_weight, pl.ANY)] + [(v, None) for v in received]
        outs = [((slots, out_width), BF16)] * groups
        if keep:
            outs = [((CAP, out_width), BF16)] * (groups * exp_count)
        return call(
            functools.partial(output_kernel, sizes, chunk, out_width, keep),
            outs,
            ins,
            [
                pltpu.VMEM((N_DEPTH, unit_width, N_SLAB), BF16),
                pltpu.SemaphoreType.DMA((N_DEPTH,)),
            ],
            flops=2 * slots * unit_width * groups * out_width,
            moved=2 * unit_width * groups * out_width,
        )

    given = [output(chunk, False, ()) for chunk in range(OUT_CHUNKS)]
    taken = [[swap(value) for value in values] for values in given]
    pieces = []
    for chunk in range(OUT_CHUNKS):
        kept = output(chunk, True, taken[chunk])
        for d in range(exp_count):
            for offset in range(groups):
                value = kept[offset * exp_count + d]
                pieces.append(shift(value, -d, offset) if d or offset else value)
    return call(
        functools.partial(combine_kernel, sizes),
        [((tok_count, part), BF16)],
        [(combine_high, None), (combine_low, None)] + [(v, None) for v in pieces],
        flops=4 * tok_count * EXPERTS * CAP * part,
        moved=4 * EXPERTS * CAP * part,
    )[0]


def per_device(*operands):
    tokens, gate_weight = operands[0], operands[5]
    exp_count, unit_count = lax.axis_size("exp"), lax.axis_size("unit")
    unit_width = gate_weight.shape[1]
    paired = (
        2 * unit_width == FF
        and unit_count % 2 == 0
        and exp_count * unit_count // 2 == EXPERTS
        and TILE % tokens.shape[0] == 0
    )
    return (paired_experts if paired else spread_experts)(*operands)


def solution(mesh):
    return jax.shard_map(
        per_device,
        mesh=mesh,
        in_specs=(
            P(("rep", "exp"), None),
            P(),
            P(("rep", "exp"), None),
            P(("rep", "exp"), None),
            P("rep", None, None),
            P(None, ("exp", "unit")),
            P(None, ("exp", "unit")),
            P(("exp", "unit"), None),
        ),
        out_specs=P(("rep", "exp"), "unit"),
        check_vma=False,
    )
```

```python
import functools

import jax
import jax.numpy as jnp
import numpy as np
from jax import lax
from jax.experimental import pallas as pl
from jax.experimental.pallas import tpu as pltpu
from jax.sharding import PartitionSpec as P

EXPERTS = 8
FF = 7168
BLK = 64
TILE = 256
CAP = 40

EPSILON = 1e-05

IN_CHUNKS = 2
OUT_CHUNKS = 2
K_SLAB = 512
K_DEPTH = 6
N_ROWS = 512
VMEM_LIMIT = 40 * 1024 * 1024

F32 = jnp.float32
BF16 = jnp.bfloat16


def normalize(tokens, norm_gain):
    values = tokens.astype(jnp.float32)
    inv_rms = lax.rsqrt(jnp.mean(values * values, axis=-1, keepdims=True) + EPSILON)
    return (values * inv_rms * norm_gain).astype(jnp.bfloat16)


def slot_numbers(entries, expert_count):
    onehot = (entries[..., None] == jnp.arange(expert_count, dtype=jnp.int32)).astype(jnp.int32)
    before = jnp.cumsum(onehot, axis=-2, dtype=jnp.int32) - onehot
    return jnp.sum(before * onehot, axis=-1)


def spread_experts(
    tokens, norm_gain, route_ids, route_weight, active_blocks, gate_weight, up_weight, down_weight
):
    exp_count = lax.axis_size("exp")
    unit_count = lax.axis_size("unit")
    tok_count, feature_width = tokens.shape
    unit_width = gate_weight.shape[1]
    row_units = unit_count * unit_width
    per_exp = max(1, row_units // FF)
    part_width = feature_width // unit_count
    block_count = unit_width // BLK
    tile_count = active_blocks.shape[0]
    exp_index = lax.axis_index("exp")
    unit_index = lax.axis_index("unit")
    first_unit = (exp_index * unit_count + unit_index) * unit_width
    own_expert = first_unit // FF
    first_block = first_unit % FF // BLK
    local_expert = own_expert - exp_index * row_units // FF
    normed = normalize(tokens, norm_gain)
    slot_index = slot_numbers(route_ids.reshape(1, -1), EXPERTS).reshape(tok_count, 2)
    positions = jnp.arange(tok_count, dtype=jnp.int32)
    tile_of = (exp_index * tok_count + positions) // TILE
    route_slot = (route_ids * CAP + slot_index).reshape(-1)
    token_source = (
        jnp.full((EXPERTS * CAP,), tok_count, jnp.int32)
        .at[route_slot]
        .set(jnp.repeat(positions, 2))
    )
    row_experts = np.arange(exp_count)[:, None] * row_units // FF + np.arange(per_exp)[None, :]
    slot_source = token_source.reshape(EXPERTS, CAP)[row_experts]
    padded_tiles = jnp.concatenate([tile_of, jnp.zeros((1,), jnp.int32)])
    slot_tiles = padded_tiles[slot_source]
    active_mine = lax.dynamic_index_in_dim(active_blocks, own_expert, 1, keepdims=False)
    local_blocks = first_block + jnp.arange(block_count, dtype=jnp.int32)
    block_on = jnp.any(active_mine[:, :, None] == local_blocks[None, None, :], axis=1).astype(
        jnp.float32
    )
    row_part = lax.dynamic_slice_in_dim(normed, unit_index * part_width, part_width, 1)
    padded_rows = jnp.concatenate([row_part, jnp.zeros((1, part_width), jnp.bfloat16)], 0)
    whole_rows = lax.all_gather(
        lax.all_to_all(padded_rows[slot_source], "exp", split_axis=0, concat_axis=0, tiled=True),
        "unit",
        axis=3,
        tiled=True,
    )
    slot_count = whole_rows.shape[2]
    own_rows = lax.dynamic_index_in_dim(whole_rows, local_expert, 1, keepdims=False).reshape(
        -1, feature_width
    )
    own_tiles = lax.dynamic_index_in_dim(
        lax.all_to_all(slot_tiles, "exp", split_axis=0, concat_axis=0, tiled=True),
        local_expert,
        1,
        keepdims=False,
    ).reshape(-1)
    tile_hot = (own_tiles[:, None] == jnp.arange(tile_count, dtype=jnp.int32)[None, :]).astype(
        jnp.float32
    )
    row_mask = jnp.dot(tile_hot, block_on, precision=lax.Precision.HIGHEST)
    gate_acts = jnp.dot(own_rows, gate_weight, preferred_element_type=jnp.float32)
    up_acts = jnp.dot(own_rows, up_weight, preferred_element_type=jnp.float32)
    hidden = jax.nn.relu(gate_acts) * jax.nn.relu(up_acts)
    hidden = (hidden.reshape(-1, block_count, BLK) * row_mask[:, :, None]).reshape(-1, unit_width)
    hidden = hidden.astype(jnp.bfloat16)
    partial_value = jnp.dot(hidden, down_weight, preferred_element_type=jnp.float32)
    partial_value = partial_value.reshape(exp_count, slot_count, feature_width)
    result = jnp.zeros((exp_count, per_exp, slot_count, feature_width), jnp.float32)
    partial_all = lax.dynamic_update_index_in_dim(result, partial_value, local_expert, 1)

    def by_expert(returned):
        last_width = returned.shape[-1]
        if per_exp == 1:
            grouped = returned.reshape(EXPERTS, exp_count // EXPERTS, CAP, last_width)
            return jnp.sum(grouped, axis=1, dtype=jnp.float32)
        return returned.reshape(EXPERTS, CAP, last_width).astype(jnp.float32)

    summed = lax.psum_scatter(
        partial_all.astype(jnp.bfloat16), "unit", scatter_dimension=3, tiled=True
    ).astype(jnp.float32)
    returned = lax.all_to_all(
        summed.astype(jnp.bfloat16), "exp", split_axis=0, concat_axis=0, tiled=True
    ).astype(summed.dtype)
    per_expert = by_expert(returned)
    last_width = per_expert.shape[-1]
    picked = per_expert.reshape(EXPERTS * CAP, last_width)[route_slot].reshape(
        tok_count, 2, last_width
    )
    mixed = jnp.sum(route_weight[:, :, None] * picked, axis=1)
    return mixed.astype(jnp.bfloat16)


def place(sizes):
    exp_count, groups = sizes
    return lax.axis_index("exp"), lax.axis_index("unit") // 2, lax.axis_index("unit") % 2


def pick_rows(named, before, d):
    rows = named.shape[1]
    place_of = jnp.where(named[d : d + 1, :] > 0, before[d : d + 1, :], -1)
    return (place_of == lax.broadcasted_iota(jnp.int32, (CAP, rows), 0)).astype(F32)


def count_earlier(ids, experts):
    rows = ids.shape[1]
    earlier = (
        lax.broadcasted_iota(jnp.int32, (rows, rows), 0)
        < lax.broadcasted_iota(jnp.int32, (rows, rows), 1)
    ).astype(BF16)
    named = ((ids[0:1, :] == experts) | (ids[1:2, :] == experts)).astype(jnp.int32)
    before = jnp.dot(named.astype(BF16), earlier, preferred_element_type=F32)
    return named, before.astype(jnp.int32)


def group_experts(exp_count, groups, z, g, rows):
    distance = lax.broadcasted_iota(jnp.int32, (max(8, exp_count), rows), 0)
    return lax.rem(z + distance, exp_count) * groups + g


def send_rows(normed, others, start, width, sends):
    found = jnp.dot(others, normed[:, pl.ds(start, width)], preferred_element_type=F32)
    for d, send in enumerate(sends):
        send[...] = found[d * CAP : (d + 1) * CAP, :].astype(BF16)


def route_kernel(sizes, width, tokens_hbm, gain_hbm, ids_hbm, normed, others, *rest):
    exp_count, groups = sizes
    sends, (tokens, gain, ids, sems) = rest[:-4], rest[-4:]
    pairs = ((tokens_hbm, tokens), (gain_hbm, gain), (ids_hbm, ids))
    copies = [pltpu.make_async_copy(a, b, sems.at[n]) for n, (a, b) in enumerate(pairs)]
    for copy in copies:
        copy.start()
    rows, features = tokens.shape
    z, g, s = place(sizes)
    for copy in copies:
        copy.wait()
    step = 16
    for first in range(0, rows, step):
        values = tokens[first : first + step, :].astype(F32)
        mean = jnp.sum(values * values, axis=1, keepdims=True) * (1.0 / features)
        inv_rms = lax.rsqrt(mean + EPSILON)
        normed[first : first + step, :] = (values * inv_rms * gain[...]).astype(BF16)
    named, before = count_earlier(ids, group_experts(exp_count, groups, z, g, rows))
    picks = [pick_rows(named, before, d) for d in range(1, exp_count)]
    others[...] = jnp.concatenate(picks, axis=0).astype(BF16)
    start = pl.multiple_of(s * (features // 2), 128)
    send_rows(normed, others[...], start, width, sends)


def prepare_kernel(sizes, width, normed, others, ids, weights, active, *rest):
    exp_count, groups = sizes
    own, combine_high, combine_low, mask = rest[:4]
    sends = rest[4:]
    rows, features = normed.shape
    z, g, s = place(sizes)
    for n in range(len(sends) // (exp_count - 1)):
        start = pl.multiple_of(s * (features // 2) + (n + 1) * width, 128)
        batch = sends[n * (exp_count - 1) : (n + 1) * (exp_count - 1)]
        send_rows(normed, others[...], start, width, batch)
    named, before = count_earlier(ids, group_experts(exp_count, groups, z, g, rows))
    own[...] = jnp.dot(
        pick_rows(named, before, 0).astype(BF16), normed[...], preferred_element_type=F32
    ).astype(BF16)
    zero = jnp.zeros((CAP, rows), F32)
    parts = []
    for d in range(exp_count):
        here = pick_rows(named, before, d) > 0
        expert = lax.rem(z + d, exp_count) * groups + g
        first = jnp.where(here & (ids[0:1, :] == expert), weights[0:1, :], zero)
        second = jnp.where(here & (ids[1:2, :] == expert), weights[1:2, :], zero)
        parts.append(first + second)
    padded = combine_high.shape[1]
    if padded > exp_count * CAP:
        parts.append(jnp.zeros((padded - exp_count * CAP, rows), F32))
    table = jnp.concatenate(parts, axis=0).T
    high = table.astype(BF16)
    combine_high[...] = high
    combine_low[...] = (table - high.astype(F32)).astype(BF16)
    unit_width = mask.shape[1]
    blocks = lax.broadcasted_iota(jnp.int32, mask.shape, 1) // BLK + s * (unit_width // BLK)
    source = lax.broadcasted_iota(jnp.int32, (mask.shape[0], 1), 0)
    own_expert = z * groups + g

    def add_entry(k, found):
        entry = jnp.full((mask.shape[0], 1), -1, jnp.int32)
        for d in range(exp_count):
            tile = lax.rem(z - d + exp_count, exp_count) * rows // TILE
            entry = jnp.where(source == d, active[tile, own_expert, k], entry)
        return jnp.where(blocks == entry, 1.0, found)

    mask[...] = lax.fori_loop(0, active.shape[2], add_entry, jnp.zeros(mask.shape, F32))


def hidden_kernel(sizes, chunk, width, first, last, *refs):
    exp_count, groups = sizes
    z, g, s = place(sizes)
    refs = list(refs)
    own = refs.pop(0)
    mine = [refs.pop(0) for _ in range(exp_count - 1)]
    other = [refs.pop(0) for _ in range(exp_count - 1)]
    gate, up = refs.pop(0), refs.pop(0)
    gate_in, up_in = (None, None) if first else (refs.pop(0), refs.pop(0))
    mask = refs.pop(0) if last else None
    if last:
        hidden = refs.pop(0)
        gate_sum, up_sum = refs.pop(0), refs.pop(0)
    else:
        gate_sum, up_sum = refs.pop(0), refs.pop(0)
    rows, slabs, sems = refs
    half = own.shape[1] // 2
    slab_count = width // K_SLAB
    total = 2 * slab_count
    depth = min(K_DEPTH, 2 * total)

    def copy(index, ref, which):
        side = jnp.where(index < slab_count, s, 1 - s)
        row = side * half + chunk * width + lax.rem(index, slab_count) * K_SLAB
        slot = lax.rem(index * 2 + which, depth)
        return pltpu.make_async_copy(
            ref.at[pl.ds(pl.multiple_of(row, K_SLAB), K_SLAB), :], slabs.at[slot], sems.at[slot]
        )

    for n in range(depth):
        copy(n // 2, (gate, up)[n % 2], n % 2).start()
    for side_of in range(2):
        source = (mine, other)[side_of]
        side = s if side_of == 0 else 1 - s
        start = pl.multiple_of(side * half + chunk * width, 128)
        pieces = [own[:, pl.ds(start, width)].astype(F32)] + [r[...].astype(F32) for r in source]
        whole = jnp.concatenate(pieces, axis=0).astype(BF16)
        for n in range(slab_count):
            rows[side_of * slab_count + n] = whole[:, n * K_SLAB : (n + 1) * K_SLAB]
    unit_width = gate.shape[1]
    n_tile = 512
    if first:
        gate_sum[...] = jnp.zeros_like(gate_sum)
        up_sum[...] = jnp.zeros_like(up_sum)
    else:
        gate_sum[...] = gate_in[...]
        up_sum[...] = up_in[...]

    def body(index, carry):
        left = rows[index]
        for which, (ref, acc) in enumerate(((gate, gate_sum), (up, up_sum))):
            copy(index, ref, which).wait()
            slot = lax.rem(index * 2 + which, depth)
            for col in range(0, unit_width, n_tile):
                end = min(col + n_tile, unit_width)
                acc[:, col:end] += jnp.dot(
                    left, slabs[slot, :, col:end], preferred_element_type=F32
                )

            @pl.when(index * 2 + which + depth < 2 * total)
            def _():
                copy(index + depth // 2, ref, which).start()

        return carry

    lax.fori_loop(0, total, body, 0)
    if last:
        for d in range(exp_count):
            lines = slice(d * CAP, (d + 1) * CAP)
            for col in range(0, unit_width, n_tile):
                cols = slice(col, min(col + n_tile, unit_width))
                product = jnp.maximum(gate_sum[lines, cols], 0.0) * jnp.maximum(
                    up_sum[lines, cols], 0.0
                )
                gate_sum[lines, cols] = product * mask[d : d + 1, cols]
        hidden[...] = gate_sum[...].astype(BF16)


def output_kernel(sizes, chunk, width, keep, *refs):
    exp_count, groups = sizes
    z, g, s = place(sizes)
    refs = list(refs)
    hidden, down = refs.pop(0), refs.pop(0)
    received = refs.pop(0) if keep else None
    total_sum, slabs, sems = refs[-3:]
    outs = refs[:-3]
    side = s if keep else 1 - s
    part = down.shape[1] // (2 * groups)
    pieces = down.shape[0] // N_ROWS

    def copy(index):
        group = lax.rem(g + index // pieces, groups)
        column = pl.multiple_of((group * 2 + side) * part + chunk * width, 128)
        lines = pl.ds(index % pieces * N_ROWS, N_ROWS)
        return pltpu.make_async_copy(
            down.at[lines, pl.ds(column, width)], slabs.at[index], sems.at[index]
        )

    for index in range(groups * pieces):
        copy(index).start()
    for offset in range(groups):
        for piece in range(pieces):
            index = offset * pieces + piece
            copy(index).wait()
            value = jnp.dot(
                hidden[:, piece * N_ROWS : (piece + 1) * N_ROWS],
                slabs[index],
                preferred_element_type=F32,
            )
            total_sum[...] = value if piece == 0 else total_sum[...] + value
        cols = slice(offset * width, (offset + 1) * width)
        if keep:
            for d in range(exp_count):
                lines = slice(d * CAP, (d + 1) * CAP)
                value = total_sum[lines, :] + received[:, cols].astype(F32)[lines, :]
                outs[d][:, cols] = value.astype(BF16)
        else:
            outs[0][:, cols] = total_sum[...].astype(BF16)


def combine_kernel(exp_count, high, low, *refs):
    pieces = [r[...].astype(F32) for r in refs[:exp_count]]
    kept, gives = refs[exp_count], refs[exp_count + 1 :]
    total = exp_count * CAP
    width = kept.shape[1]
    found = jnp.concatenate(pieces, axis=0).astype(BF16)
    value = jnp.dot(high[:, :total], found, preferred_element_type=F32)
    value = value + jnp.dot(low[:, :total], found, preferred_element_type=F32)
    kept[...] = value[:, :width]
    for n, give in enumerate(gives):
        give[...] = value[:, (n + 1) * width : (n + 2) * width].astype(BF16)


def finish_kernel(chunks, *refs):
    out = refs[-1]
    per_chunk = (len(refs) - 1) // chunks
    width = refs[0].shape[1]
    for chunk in range(chunks):
        kept, *others = refs[chunk * per_chunk : (chunk + 1) * per_chunk]
        value = kept[...]
        for other in others:
            value = value + other[...].astype(F32)
        out[:, chunk * width : (chunk + 1) * width] = value.astype(BF16)


def call(kernel, outs, ins, scratch=(), flops=0, moved=0, aliases=None):
    vmem = pl.BlockSpec(memory_space=pltpu.VMEM)
    arrays = [a for a, _ in ins]
    specs = [vmem if space is None else pl.BlockSpec(memory_space=space) for _, space in ins]
    return pl.pallas_call(
        kernel,
        out_shape=[jax.ShapeDtypeStruct(shape, kind) for shape, kind in outs],
        in_specs=specs,
        out_specs=[vmem] * len(outs),
        scratch_shapes=list(scratch),
        compiler_params=pltpu.CompilerParams(vmem_limit_bytes=VMEM_LIMIT),
        cost_estimate=pl.CostEstimate(flops=flops, bytes_accessed=moved, transcendentals=0),
    )(*arrays)


def paired_experts(
    tokens, norm_gain, route_ids, route_weight, active_blocks, gate_weight, up_weight, down_weight
):
    exp_count, unit_count = lax.axis_size("exp"), lax.axis_size("unit")
    groups = unit_count // 2
    sizes = (exp_count, groups)
    tok_count, features = tokens.shape
    unit_width = gate_weight.shape[1]
    slots = exp_count * CAP
    half = features // 2
    width = half // IN_CHUNKS
    ids = route_ids.T
    weights = route_weight.T

    def shift(value, distance, group_shift=0):
        pairs = []
        for z in range(exp_count):
            for u in range(unit_count):
                target = (z + distance) % exp_count
                group = (u // 2 + group_shift) % groups
                pairs.append((z * unit_count + u, target * unit_count + group * 2 + u % 2))
        return lax.ppermute(value, ("exp", "unit"), pairs)

    def swap(value):
        return lax.ppermute(value, "unit", [(u, u ^ 1) for u in range(unit_count)])

    batch = exp_count - 1
    normed, others, *sends = call(
        functools.partial(route_kernel, sizes, width),
        [((tok_count, features), BF16), ((batch * CAP, tok_count), BF16)]
        + [((CAP, width), BF16)] * batch,
        [
            (tokens, pltpu.HBM),
            (norm_gain.reshape(1, -1), pltpu.HBM),
            (ids, pltpu.HBM),
        ],
        [
            pltpu.VMEM((tok_count, features), BF16),
            pltpu.VMEM((1, features), F32),
            pltpu.VMEM(ids.shape, jnp.int32),
            pltpu.SemaphoreType.DMA((3,)),
        ],
        flops=2 * tok_count * slots * width,
        moved=4 * tok_count * features,
    )
    padded = -(-slots // 128) * 128
    own, combine_high, combine_low, mask, *more = call(
        functools.partial(prepare_kernel, sizes, width),
        [
            ((CAP, features), BF16),
            ((tok_count, padded), BF16),
            ((tok_count, padded), BF16),
            ((max(8, exp_count), unit_width), F32),
        ]
        + [((CAP, width), BF16)] * (batch * (IN_CHUNKS - 1)),
        [(normed, None), (others, None), (ids, None), (weights, None), (active_blocks, pltpu.SMEM)],
        flops=2 * tok_count * slots * features,
        moved=1 << 20,
    )
    sends = sends + more
    mine, other = [], []
    for chunk in range(IN_CHUNKS):
        ready = sends[chunk * batch : (chunk + 1) * batch]
        arrived = [shift(value, d + 1) for d, value in enumerate(ready)]
        mine.append(arrived)
        other.append([swap(value) for value in arrived])
    sums = None
    for chunk in range(IN_CHUNKS):
        first, last = chunk == 0, chunk == IN_CHUNKS - 1
        ins = [(own, None)] + [(v, None) for v in mine[chunk] + other[chunk]]
        ins += [(gate_weight, pltpu.HBM), (up_weight, pltpu.HBM)]
        if not first:
            ins += [(v, None) for v in sums]
        if last:
            ins += [(mask, None)]
        acc = ((slots, unit_width), F32)
        scratch = [
            pltpu.VMEM((2 * width // K_SLAB, slots, K_SLAB), BF16),
            pltpu.VMEM((K_DEPTH, K_SLAB, unit_width), BF16),
            pltpu.SemaphoreType.DMA((K_DEPTH,)),
        ]
        if last:
            scratch = [pltpu.VMEM(*acc), pltpu.VMEM(*acc)] + scratch
        sums = call(
            functools.partial(hidden_kernel, sizes, chunk, width, first, last),
            [((slots, unit_width), BF16)] if last else [acc, acc],
            ins,
            scratch,
            flops=2 * 2 * slots * 2 * width * unit_width,
            moved=2 * 2 * width * unit_width * 2,
        )
    hidden = sums[0]
    part = features // unit_count
    out_width = part // OUT_CHUNKS

    def output(chunk, keep, received):
        pieces = groups * (unit_width // N_ROWS)
        return call(
            functools.partial(output_kernel, sizes, chunk, out_width, keep),
            [((CAP, groups * out_width), BF16)] * exp_count
            if keep
            else [((slots, groups * out_width), BF16)],
            [(hidden, None), (down_weight, pltpu.HBM)] + [(v, None) for v in received],
            [
                pltpu.VMEM((slots, out_width), F32),
                pltpu.VMEM((pieces, N_ROWS, out_width), BF16),
                pltpu.SemaphoreType.DMA((pieces,)),
            ],
            flops=2 * slots * unit_width * groups * out_width,
            moved=2 * unit_width * groups * out_width,
        )

    given = [output(chunk, False, ())[0] for chunk in range(OUT_CHUNKS)]
    taken = [swap(value) for value in given]
    last = []
    for chunk in range(OUT_CHUNKS):
        kept = output(chunk, True, [taken[chunk]])
        home = [kept[0]] + [shift(kept[d], -d) for d in range(1, exp_count)]
        stay, *gives = call(
            functools.partial(combine_kernel, exp_count),
            [((tok_count, out_width), F32)] + [((tok_count, out_width), BF16)] * (groups - 1),
            [(combine_high, None), (combine_low, None)] + [(v, None) for v in home],
            flops=4 * tok_count * slots * groups * out_width,
            moved=1 << 20,
        )
        last += [stay] + [shift(value, 0, n + 1) for n, value in enumerate(gives)]
    return call(
        functools.partial(finish_kernel, OUT_CHUNKS),
        [((tok_count, part), BF16)],
        [(v, None) for v in last],
        moved=1 << 20,
    )[0]


def per_device(*operands):
    tokens, gate_weight = operands[0], operands[5]
    exp_count, unit_count = lax.axis_size("exp"), lax.axis_size("unit")
    unit_width = gate_weight.shape[1]
    paired = (
        2 * unit_width == FF
        and unit_count % 2 == 0
        and exp_count * unit_count // 2 == EXPERTS
        and TILE % tokens.shape[0] == 0
    )
    return (paired_experts if paired else spread_experts)(*operands)


def solution(mesh):
    return jax.shard_map(
        per_device,
        mesh=mesh,
        in_specs=(
            P(("rep", "exp"), None),
            P(),
            P(("rep", "exp"), None),
            P(("rep", "exp"), None),
            P("rep", None, None),
            P(None, ("exp", "unit")),
            P(None, ("exp", "unit")),
            P(("exp", "unit"), None),
        ),
        out_specs=P(("rep", "exp"), "unit"),
        check_vma=False,
    )
```

```python
import functools

import jax
import jax.numpy as jnp
import numpy as np
from jax import lax
from jax.experimental import pallas as pl
from jax.experimental.pallas import tpu as pltpu
from jax.sharding import PartitionSpec as P

EXPERTS = 8
FF = 7168
BLK = 64
TILE = 256
CAP = 40

EPSILON = 1e-05

OUT_CHUNKS = 2
K_SLAB = 512
K_DEPTH = 2
N_TILE = 512
NEAR_ROWS = 1024
GATE_NEAR = 4
UP_NEAR = 1
N_ROWS = 512

F32 = jnp.float32
BF16 = jnp.bfloat16


def normalize(tokens, norm_gain):
    values = tokens.astype(jnp.float32)
    inv_rms = lax.rsqrt(jnp.mean(values * values, axis=-1, keepdims=True) + EPSILON)
    return (values * inv_rms * norm_gain).astype(jnp.bfloat16)


def slot_numbers(entries, expert_count):
    onehot = (entries[..., None] == jnp.arange(expert_count, dtype=jnp.int32)).astype(jnp.int32)
    before = jnp.cumsum(onehot, axis=-2, dtype=jnp.int32) - onehot
    return jnp.sum(before * onehot, axis=-1)


def spread_experts(
    tokens, norm_gain, route_ids, route_weight, active_blocks, gate_weight, up_weight, down_weight
):
    exp_count = lax.axis_size("exp")
    unit_count = lax.axis_size("unit")
    tok_count, feature_width = tokens.shape
    unit_width = gate_weight.shape[1]
    row_units = unit_count * unit_width
    per_exp = max(1, row_units // FF)
    part_width = feature_width // unit_count
    block_count = unit_width // BLK
    tile_count = active_blocks.shape[0]
    exp_index = lax.axis_index("exp")
    unit_index = lax.axis_index("unit")
    first_unit = (exp_index * unit_count + unit_index) * unit_width
    own_expert = first_unit // FF
    first_block = first_unit % FF // BLK
    local_expert = own_expert - exp_index * row_units // FF
    normed = normalize(tokens, norm_gain)
    slot_index = slot_numbers(route_ids.reshape(1, -1), EXPERTS).reshape(tok_count, 2)
    positions = jnp.arange(tok_count, dtype=jnp.int32)
    tile_of = (exp_index * tok_count + positions) // TILE
    route_slot = (route_ids * CAP + slot_index).reshape(-1)
    token_source = (
        jnp.full((EXPERTS * CAP,), tok_count, jnp.int32)
        .at[route_slot]
        .set(jnp.repeat(positions, 2))
    )
    row_experts = np.arange(exp_count)[:, None] * row_units // FF + np.arange(per_exp)[None, :]
    slot_source = token_source.reshape(EXPERTS, CAP)[row_experts]
    padded_tiles = jnp.concatenate([tile_of, jnp.zeros((1,), jnp.int32)])
    slot_tiles = padded_tiles[slot_source]
    active_mine = lax.dynamic_index_in_dim(active_blocks, own_expert, 1, keepdims=False)
    local_blocks = first_block + jnp.arange(block_count, dtype=jnp.int32)
    block_on = jnp.any(active_mine[:, :, None] == local_blocks[None, None, :], axis=1).astype(
        jnp.float32
    )
    row_part = lax.dynamic_slice_in_dim(normed, unit_index * part_width, part_width, 1)
    padded_rows = jnp.concatenate([row_part, jnp.zeros((1, part_width), jnp.bfloat16)], 0)
    whole_rows = lax.all_gather(
        lax.all_to_all(padded_rows[slot_source], "exp", split_axis=0, concat_axis=0, tiled=True),
        "unit",
        axis=3,
        tiled=True,
    )
    slot_count = whole_rows.shape[2]
    own_rows = lax.dynamic_index_in_dim(whole_rows, local_expert, 1, keepdims=False).reshape(
        -1, feature_width
    )
    own_tiles = lax.dynamic_index_in_dim(
        lax.all_to_all(slot_tiles, "exp", split_axis=0, concat_axis=0, tiled=True),
        local_expert,
        1,
        keepdims=False,
    ).reshape(-1)
    tile_hot = (own_tiles[:, None] == jnp.arange(tile_count, dtype=jnp.int32)[None, :]).astype(
        jnp.float32
    )
    row_mask = jnp.dot(tile_hot, block_on, precision=lax.Precision.HIGHEST)
    gate_acts = jnp.dot(own_rows, gate_weight, preferred_element_type=jnp.float32)
    up_acts = jnp.dot(own_rows, up_weight, preferred_element_type=jnp.float32)
    hidden = jax.nn.relu(gate_acts) * jax.nn.relu(up_acts)
    hidden = (hidden.reshape(-1, block_count, BLK) * row_mask[:, :, None]).reshape(-1, unit_width)
    hidden = hidden.astype(jnp.bfloat16)
    partial_value = jnp.dot(hidden, down_weight, preferred_element_type=jnp.float32)
    partial_value = partial_value.reshape(exp_count, slot_count, feature_width)
    result = jnp.zeros((exp_count, per_exp, slot_count, feature_width), jnp.float32)
    partial_all = lax.dynamic_update_index_in_dim(result, partial_value, local_expert, 1)

    def by_expert(returned):
        last_width = returned.shape[-1]
        if per_exp == 1:
            grouped = returned.reshape(EXPERTS, exp_count // EXPERTS, CAP, last_width)
            return jnp.sum(grouped, axis=1, dtype=jnp.float32)
        return returned.reshape(EXPERTS, CAP, last_width).astype(jnp.float32)

    summed = lax.psum_scatter(
        partial_all.astype(jnp.bfloat16), "unit", scatter_dimension=3, tiled=True
    ).astype(jnp.float32)
    returned = lax.all_to_all(
        summed.astype(jnp.bfloat16), "exp", split_axis=0, concat_axis=0, tiled=True
    ).astype(summed.dtype)
    per_expert = by_expert(returned)
    last_width = per_expert.shape[-1]
    picked = per_expert.reshape(EXPERTS * CAP, last_width)[route_slot].reshape(
        tok_count, 2, last_width
    )
    mixed = jnp.sum(route_weight[:, :, None] * picked, axis=1)
    return mixed.astype(jnp.bfloat16)


def place(sizes):
    exp_count, groups = sizes
    return lax.axis_index("exp"), lax.axis_index("unit") // 2, lax.axis_index("unit") % 2


def pick_rows(named, before, d):
    rows = named.shape[1]
    place_of = jnp.where(named[d : d + 1, :] > 0, before[d : d + 1, :], -1)
    return (place_of == lax.broadcasted_iota(jnp.int32, (CAP, rows), 0)).astype(F32)


def count_earlier(ids, experts):
    rows = ids.shape[1]
    earlier = (
        lax.broadcasted_iota(jnp.int32, (rows, rows), 0)
        < lax.broadcasted_iota(jnp.int32, (rows, rows), 1)
    ).astype(BF16)
    named = ((ids[0:1, :] == experts) | (ids[1:2, :] == experts)).astype(jnp.int32)
    before = jnp.dot(named.astype(BF16), earlier, preferred_element_type=F32)
    return named, before.astype(jnp.int32)


def group_experts(exp_count, groups, z, g, rows):
    distance = lax.broadcasted_iota(jnp.int32, (max(8, exp_count), rows), 0)
    return lax.rem(z + distance, exp_count) * groups + g


def route_kernel(sizes, width, tokens_hbm, gain_hbm, ids_hbm, normed, *rest):
    exp_count, groups = sizes
    sends, (tokens, gain, ids, sems) = rest[:-4], rest[-4:]
    pairs = ((tokens_hbm, tokens), (gain_hbm, gain), (ids_hbm, ids))
    copies = [pltpu.make_async_copy(a, b, sems.at[n]) for n, (a, b) in enumerate(pairs)]
    for copy in copies:
        copy.start()
    rows, features = tokens.shape
    z, g, s = place(sizes)
    for copy in copies:
        copy.wait()
    step = 16
    for first in range(0, rows, step):
        values = tokens[first : first + step, :].astype(F32)
        mean = jnp.sum(values * values, axis=1, keepdims=True) * (1.0 / features)
        inv_rms = lax.rsqrt(mean + EPSILON)
        normed[first : first + step, :] = (values * inv_rms * gain[...]).astype(BF16)
    named, before = count_earlier(ids, group_experts(exp_count, groups, z, g, rows))
    picks = [pick_rows(named, before, d) for d in range(1, exp_count)]
    others = jnp.concatenate(picks, axis=0).astype(BF16)
    start = pl.multiple_of(s * (features // 2), 128)
    found = jnp.dot(others, normed[:, pl.ds(start, width)], preferred_element_type=F32)
    for d, send in enumerate(sends):
        send[...] = found[d * CAP : (d + 1) * CAP, :].astype(BF16)


def prepare_kernel(
    sizes, normed, ids, weights, active, gate, up, own, combine_high, combine_low, mask, *rest
):
    exp_count, groups = sizes
    rows, features = normed.shape
    z, g, s = place(sizes)
    copies = []
    *nears, sems = rest
    for n, near in enumerate(nears):
        source, piece = (gate, n) if n < GATE_NEAR else (up, n - GATE_NEAR)
        lines = pl.ds(piece * NEAR_ROWS, NEAR_ROWS)
        copies.append(pltpu.make_async_copy(source.at[lines, :], near, sems.at[n]))
    for copy in copies:
        copy.start()
    named, before = count_earlier(ids, group_experts(exp_count, groups, z, g, rows))
    own[...] = jnp.dot(
        pick_rows(named, before, 0).astype(BF16), normed[...], preferred_element_type=F32
    ).astype(BF16)
    zero = jnp.zeros((CAP, rows), F32)
    parts = []
    for d in range(exp_count):
        here = pick_rows(named, before, d) > 0
        expert = lax.rem(z + d, exp_count) * groups + g
        first = jnp.where(here & (ids[0:1, :] == expert), weights[0:1, :], zero)
        second = jnp.where(here & (ids[1:2, :] == expert), weights[1:2, :], zero)
        parts.append(first + second)
    padded = combine_high.shape[1]
    if padded > exp_count * CAP:
        parts.append(jnp.zeros((padded - exp_count * CAP, rows), F32))
    table = jnp.concatenate(parts, axis=0).T
    high = table.astype(BF16)
    combine_high[...] = high
    combine_low[...] = (table - high.astype(F32)).astype(BF16)
    unit_width = mask.shape[1]
    blocks = lax.broadcasted_iota(jnp.int32, mask.shape, 1) // BLK + s * (unit_width // BLK)
    source = lax.broadcasted_iota(jnp.int32, (mask.shape[0], 1), 0)
    own_expert = z * groups + g

    def add_entry(k, found):
        entry = jnp.full((mask.shape[0], 1), -1, jnp.int32)
        for d in range(exp_count):
            tile = lax.rem(z - d + exp_count, exp_count) * rows // TILE
            entry = jnp.where(source == d, active[tile, own_expert, k], entry)
        return jnp.where(blocks == entry, 1.0, found)

    mask[...] = lax.fori_loop(0, active.shape[2], add_entry, jnp.zeros(mask.shape, F32))
    for copy in copies:
        copy.wait()


def hidden_kernel(sizes, own, *refs):
    exp_count, groups = sizes
    z, g, s = place(sizes)
    refs = list(refs)
    mine = [refs.pop(0) for _ in range(exp_count - 1)]
    other = [refs.pop(0) for _ in range(exp_count - 1)]
    gate_near = [refs.pop(0) for _ in range(GATE_NEAR)]
    up_near = [refs.pop(0) for _ in range(UP_NEAR)]
    up, mask, hidden, gate_sum, up_sum, rows, slabs, sems = refs
    half = own.shape[1] // 2
    near, features = UP_NEAR * NEAR_ROWS, up.shape[0]
    unit_width = up.shape[1]
    far_count = (features - near) // K_SLAB

    def copy(index):
        slot = index % K_DEPTH
        return pltpu.make_async_copy(
            up.at[pl.ds(near + index * K_SLAB, K_SLAB), :], slabs.at[slot], sems.at[slot]
        )

    for n in range(min(K_DEPTH, far_count)):
        copy(n).start()
    for side_of in range(2):
        source = (mine, other)[side_of]
        side = s if side_of == 0 else 1 - s
        start = pl.multiple_of(side * half, 128)
        pieces = [own[:, pl.ds(start, half)].astype(F32)] + [r[...].astype(F32) for r in source]
        rows[:, pl.ds(start, half)] = jnp.concatenate(pieces, axis=0).astype(BF16)

    def each_tile(body):
        def step(n, carry):
            body(pl.ds(pl.multiple_of(n * N_TILE, N_TILE), N_TILE))
            return carry

        lax.fori_loop(0, unit_width // N_TILE, step, 0)

    def product(nears, cols):
        value = None
        for n, near in enumerate(nears):
            lines = slice(n * NEAR_ROWS, (n + 1) * NEAR_ROWS)
            term = jnp.dot(rows[:, lines], near[:, cols], preferred_element_type=F32)
            value = term if value is None else value + term
        return value

    def gate_tile(cols):
        gate_sum[:, cols] = jnp.maximum(product(gate_near, cols), 0.0)

    def near_tile(cols):
        up_sum[:, cols] = product(up_near, cols)

    each_tile(gate_tile)
    each_tile(near_tile)
    for n in range(far_count):
        copy(n).wait()
        left = slice(near + n * K_SLAB, near + (n + 1) * K_SLAB)

        def far_tile(cols):
            value = up_sum[:, cols] + jnp.dot(
                rows[:, left], slabs[n % K_DEPTH, :, cols], preferred_element_type=F32
            )
            if n < far_count - 1:
                up_sum[:, cols] = value
                return
            value = gate_sum[:, cols] * jnp.maximum(value, 0.0)
            parts = []
            for d in range(exp_count):
                parts.append(value[d * CAP : (d + 1) * CAP, :] * mask[d : d + 1, cols])
            hidden[:, cols] = jnp.concatenate(parts, axis=0).astype(BF16)

        each_tile(far_tile)
        if n + K_DEPTH < far_count:
            copy(n + K_DEPTH).start()


def output_kernel(sizes, chunk, width, keep, *refs):
    exp_count, groups = sizes
    z, g, s = place(sizes)
    refs = list(refs)
    hidden, down = refs.pop(0), refs.pop(0)
    received = refs.pop(0) if keep else None
    total_sum, slabs, sems = refs[-3:]
    outs = refs[:-3]
    side = s if keep else 1 - s
    part = down.shape[1] // (2 * groups)
    pieces = down.shape[0] // N_ROWS

    def copy(index):
        group = lax.rem(g + index // pieces, groups)
        column = pl.multiple_of((group * 2 + side) * part + chunk * width, 128)
        lines = pl.ds(index % pieces * N_ROWS, N_ROWS)
        return pltpu.make_async_copy(
            down.at[lines, pl.ds(column, width)], slabs.at[index], sems.at[index]
        )

    for index in range(groups * pieces):
        copy(index).start()
    for offset in range(groups):
        for piece in range(pieces):
            index = offset * pieces + piece
            copy(index).wait()
            value = jnp.dot(
                hidden[:, piece * N_ROWS : (piece + 1) * N_ROWS],
                slabs[index],
                preferred_element_type=F32,
            )
            total_sum[...] = value if piece == 0 else total_sum[...] + value
        cols = slice(offset * width, (offset + 1) * width)
        if keep:
            for d in range(exp_count):
                lines = slice(d * CAP, (d + 1) * CAP)
                value = total_sum[lines, :] + received[:, cols].astype(F32)[lines, :]
                outs[d][:, cols] = value.astype(BF16)
        else:
            outs[0][:, cols] = total_sum[...].astype(BF16)


def combine_kernel(exp_count, high, low, *refs):
    pieces = [r[...].astype(F32) for r in refs[:exp_count]]
    kept, gives = refs[exp_count], refs[exp_count + 1 :]
    total = exp_count * CAP
    width = kept.shape[1]
    found = jnp.concatenate(pieces, axis=0).astype(BF16)
    value = jnp.dot(high[:, :total], found, preferred_element_type=F32)
    value = value + jnp.dot(low[:, :total], found, preferred_element_type=F32)
    kept[...] = value[:, :width]
    for n, give in enumerate(gives):
        give[...] = value[:, (n + 1) * width : (n + 2) * width].astype(BF16)


def finish_kernel(chunks, *refs):
    out = refs[-1]
    per_chunk = (len(refs) - 1) // chunks
    width = refs[0].shape[1]
    for chunk in range(chunks):
        kept, *others = refs[chunk * per_chunk : (chunk + 1) * per_chunk]
        value = kept[...]
        for other in others:
            value = value + other[...].astype(F32)
        out[:, chunk * width : (chunk + 1) * width] = value.astype(BF16)


def call(kernel, outs, ins, scratch=(), flops=0, moved=0, limit=16):
    vmem = pl.BlockSpec(memory_space=pltpu.VMEM)
    arrays, specs = [], []
    for array, space in ins:
        if space in (pltpu.HBM, pltpu.VMEM):
            array = pltpu.with_memory_space_constraint(array, space)
        arrays.append(array)
        specs.append(vmem if space is None else pl.BlockSpec(memory_space=space))
    shapes = []
    for shape, kind, *space in outs:
        shapes.append(space[0](shape, kind) if space else jax.ShapeDtypeStruct(shape, kind))
    return pl.pallas_call(
        kernel,
        out_shape=shapes,
        in_specs=specs,
        out_specs=[vmem] * len(outs),
        scratch_shapes=list(scratch),
        compiler_params=pltpu.CompilerParams(vmem_limit_bytes=limit << 20),
        cost_estimate=pl.CostEstimate(flops=flops, bytes_accessed=moved, transcendentals=0),
    )(*arrays)


def paired_experts(
    tokens, norm_gain, route_ids, route_weight, active_blocks, gate_weight, up_weight, down_weight
):
    exp_count, unit_count = lax.axis_size("exp"), lax.axis_size("unit")
    groups = unit_count // 2
    sizes = (exp_count, groups)
    tok_count, features = tokens.shape
    unit_width = gate_weight.shape[1]
    slots = exp_count * CAP
    half = features // 2
    width = half
    ids = route_ids.T
    weights = route_weight.T

    def shift(value, distance, group_shift=0):
        pairs = []
        for z in range(exp_count):
            for u in range(unit_count):
                target = (z + distance) % exp_count
                group = (u // 2 + group_shift) % groups
                pairs.append((z * unit_count + u, target * unit_count + group * 2 + u % 2))
        return lax.ppermute(value, ("exp", "unit"), pairs)

    def swap(value):
        return lax.ppermute(value, "unit", [(u, u ^ 1) for u in range(unit_count)])

    batch = exp_count - 1
    normed, *sends = call(
        functools.partial(route_kernel, sizes, width),
        [((tok_count, features), BF16)] + [((CAP, width), BF16)] * batch,
        [
            (tokens, pltpu.HBM),
            (norm_gain.reshape(1, -1), pltpu.HBM),
            (ids, pltpu.HBM),
        ],
        [
            pltpu.VMEM((tok_count, features), BF16),
            pltpu.VMEM((1, features), F32),
            pltpu.VMEM(ids.shape, jnp.int32),
            pltpu.SemaphoreType.DMA((3,)),
        ],
        flops=2 * tok_count * slots * width,
        moved=4 * tok_count * features,
    )
    padded = -(-slots // 128) * 128
    own, combine_high, combine_low, mask, *nears = call(
        functools.partial(prepare_kernel, sizes),
        [
            ((CAP, features), BF16),
            ((tok_count, padded), BF16),
            ((tok_count, padded), BF16),
            ((max(8, exp_count), unit_width), F32),
        ]
        + [((NEAR_ROWS, unit_width), BF16, pltpu.VMEM)] * (GATE_NEAR + UP_NEAR),
        [
            (normed, None),
            (ids, None),
            (weights, None),
            (active_blocks, pltpu.SMEM),
            (gate_weight, pltpu.HBM),
            (up_weight, pltpu.HBM),
        ],
        [pltpu.SemaphoreType.DMA((GATE_NEAR + UP_NEAR,))],
        flops=2 * tok_count * slots * features,
        moved=2 * (GATE_NEAR + UP_NEAR) * NEAR_ROWS * unit_width,
        limit=16,
    )
    mine = [shift(value, d + 1) for d, value in enumerate(sends)]
    other = [swap(value) for value in mine]
    acc = ((slots, unit_width), F32)
    hidden = call(
        functools.partial(hidden_kernel, sizes),
        [((slots, unit_width), BF16)],
        [(v, None) for v in [own] + mine + other]
        + [(v, pltpu.VMEM) for v in nears]
        + [(up_weight, pltpu.HBM), (mask, None)],
        [
            pltpu.VMEM(*acc),
            pltpu.VMEM(*acc),
            pltpu.VMEM((slots, features), BF16),
            pltpu.VMEM((K_DEPTH, K_SLAB, unit_width), BF16),
            pltpu.SemaphoreType.DMA((K_DEPTH,)),
        ],
        flops=2 * 2 * slots * features * unit_width,
        moved=2 * features * unit_width * 2,
        limit=16,
    )[0]
    part = features // unit_count
    out_width = part // OUT_CHUNKS

    def output(chunk, keep, received):
        pieces = groups * (unit_width // N_ROWS)
        return call(
            functools.partial(output_kernel, sizes, chunk, out_width, keep),
            [((CAP, groups * out_width), BF16)] * exp_count
            if keep
            else [((slots, groups * out_width), BF16)],
            [(hidden, None), (down_weight, pltpu.HBM)] + [(v, None) for v in received],
            [
                pltpu.VMEM((slots, out_width), F32),
                pltpu.VMEM((pieces, N_ROWS, out_width), BF16),
                pltpu.SemaphoreType.DMA((pieces,)),
            ],
            flops=2 * slots * unit_width * groups * out_width,
            moved=2 * unit_width * groups * out_width,
        )

    given = [output(chunk, False, ())[0] for chunk in range(OUT_CHUNKS)]
    taken = [swap(value) for value in given]
    last = []
    for chunk in range(OUT_CHUNKS):
        kept = output(chunk, True, [taken[chunk]])
        home = [kept[0]] + [shift(kept[d], -d) for d in range(1, exp_count)]
        stay, *gives = call(
            functools.partial(combine_kernel, exp_count),
            [((tok_count, out_width), F32)] + [((tok_count, out_width), BF16)] * (groups - 1),
            [(combine_high, None), (combine_low, None)] + [(v, None) for v in home],
            flops=4 * tok_count * slots * groups * out_width,
            moved=1 << 20,
        )
        last += [stay] + [shift(value, 0, n + 1) for n, value in enumerate(gives)]
    return call(
        functools.partial(finish_kernel, OUT_CHUNKS),
        [((tok_count, part), BF16)],
        [(v, None) for v in last],
        moved=1 << 20,
    )[0]


def per_device(*operands):
    tokens, gate_weight = operands[0], operands[5]
    exp_count, unit_count = lax.axis_size("exp"), lax.axis_size("unit")
    unit_width = gate_weight.shape[1]
    paired = (
        2 * unit_width == FF
        and unit_count % 2 == 0
        and exp_count * unit_count // 2 == EXPERTS
        and TILE % tokens.shape[0] == 0
    )
    return (paired_experts if paired else spread_experts)(*operands)


def solution(mesh):
    return jax.shard_map(
        per_device,
        mesh=mesh,
        in_specs=(
            P(("rep", "exp"), None),
            P(),
            P(("rep", "exp"), None),
            P(("rep", "exp"), None),
            P("rep", None, None),
            P(None, ("exp", "unit")),
            P(None, ("exp", "unit")),
            P(("exp", "unit"), None),
        ),
        out_specs=P(("rep", "exp"), "unit"),
        check_vma=False,
    )
```

```python
import functools

import jax
import jax.numpy as jnp
import numpy as np
from jax import lax
from jax.experimental import pallas as pl
from jax.experimental.pallas import tpu as pltpu
from jax.sharding import PartitionSpec as P

EXPERTS = 8
FF = 7168
BLK = 64
TILE = 256
CAP = 40

EPSILON = 1e-05

OUT_CHUNKS = 2
K_SLAB = 512
K_DEPTH = 2
N_TILE = 512
NEAR_ROWS = 1024
GATE_NEAR = 4
UP_NEAR = 1
N_ROWS = 512

F32 = jnp.float32
BF16 = jnp.bfloat16


def normalize(tokens, norm_gain):
    values = tokens.astype(jnp.float32)
    inv_rms = lax.rsqrt(jnp.mean(values * values, axis=-1, keepdims=True) + EPSILON)
    return (values * inv_rms * norm_gain).astype(jnp.bfloat16)


def slot_numbers(entries, expert_count):
    onehot = (entries[..., None] == jnp.arange(expert_count, dtype=jnp.int32)).astype(jnp.int32)
    before = jnp.cumsum(onehot, axis=-2, dtype=jnp.int32) - onehot
    return jnp.sum(before * onehot, axis=-1)


def spread_experts(
    tokens, norm_gain, route_ids, route_weight, active_blocks, gate_weight, up_weight, down_weight
):
    exp_count = lax.axis_size("exp")
    unit_count = lax.axis_size("unit")
    tok_count, feature_width = tokens.shape
    unit_width = gate_weight.shape[1]
    row_units = unit_count * unit_width
    per_exp = max(1, row_units // FF)
    part_width = feature_width // unit_count
    block_count = unit_width // BLK
    tile_count = active_blocks.shape[0]
    exp_index = lax.axis_index("exp")
    unit_index = lax.axis_index("unit")
    first_unit = (exp_index * unit_count + unit_index) * unit_width
    own_expert = first_unit // FF
    first_block = first_unit % FF // BLK
    local_expert = own_expert - exp_index * row_units // FF
    normed = normalize(tokens, norm_gain)
    slot_index = slot_numbers(route_ids.reshape(1, -1), EXPERTS).reshape(tok_count, 2)
    positions = jnp.arange(tok_count, dtype=jnp.int32)
    tile_of = (exp_index * tok_count + positions) // TILE
    route_slot = (route_ids * CAP + slot_index).reshape(-1)
    token_source = (
        jnp.full((EXPERTS * CAP,), tok_count, jnp.int32)
        .at[route_slot]
        .set(jnp.repeat(positions, 2))
    )
    row_experts = np.arange(exp_count)[:, None] * row_units // FF + np.arange(per_exp)[None, :]
    slot_source = token_source.reshape(EXPERTS, CAP)[row_experts]
    padded_tiles = jnp.concatenate([tile_of, jnp.zeros((1,), jnp.int32)])
    slot_tiles = padded_tiles[slot_source]
    active_mine = lax.dynamic_index_in_dim(active_blocks, own_expert, 1, keepdims=False)
    local_blocks = first_block + jnp.arange(block_count, dtype=jnp.int32)
    block_on = jnp.any(active_mine[:, :, None] == local_blocks[None, None, :], axis=1).astype(
        jnp.float32
    )
    row_part = lax.dynamic_slice_in_dim(normed, unit_index * part_width, part_width, 1)
    padded_rows = jnp.concatenate([row_part, jnp.zeros((1, part_width), jnp.bfloat16)], 0)
    whole_rows = lax.all_gather(
        lax.all_to_all(padded_rows[slot_source], "exp", split_axis=0, concat_axis=0, tiled=True),
        "unit",
        axis=3,
        tiled=True,
    )
    slot_count = whole_rows.shape[2]
    own_rows = lax.dynamic_index_in_dim(whole_rows, local_expert, 1, keepdims=False).reshape(
        -1, feature_width
    )
    own_tiles = lax.dynamic_index_in_dim(
        lax.all_to_all(slot_tiles, "exp", split_axis=0, concat_axis=0, tiled=True),
        local_expert,
        1,
        keepdims=False,
    ).reshape(-1)
    tile_hot = (own_tiles[:, None] == jnp.arange(tile_count, dtype=jnp.int32)[None, :]).astype(
        jnp.float32
    )
    row_mask = jnp.dot(tile_hot, block_on, precision=lax.Precision.HIGHEST)
    gate_acts = jnp.dot(own_rows, gate_weight, preferred_element_type=jnp.float32)
    up_acts = jnp.dot(own_rows, up_weight, preferred_element_type=jnp.float32)
    hidden = jax.nn.relu(gate_acts) * jax.nn.relu(up_acts)
    hidden = (hidden.reshape(-1, block_count, BLK) * row_mask[:, :, None]).reshape(-1, unit_width)
    hidden = hidden.astype(jnp.bfloat16)
    partial_value = jnp.dot(hidden, down_weight, preferred_element_type=jnp.float32)
    partial_value = partial_value.reshape(exp_count, slot_count, feature_width)
    result = jnp.zeros((exp_count, per_exp, slot_count, feature_width), jnp.float32)
    partial_all = lax.dynamic_update_index_in_dim(result, partial_value, local_expert, 1)

    def by_expert(returned):
        last_width = returned.shape[-1]
        if per_exp == 1:
            grouped = returned.reshape(EXPERTS, exp_count // EXPERTS, CAP, last_width)
            return jnp.sum(grouped, axis=1, dtype=jnp.float32)
        return returned.reshape(EXPERTS, CAP, last_width).astype(jnp.float32)

    summed = lax.psum_scatter(
        partial_all.astype(jnp.bfloat16), "unit", scatter_dimension=3, tiled=True
    ).astype(jnp.float32)
    returned = lax.all_to_all(
        summed.astype(jnp.bfloat16), "exp", split_axis=0, concat_axis=0, tiled=True
    ).astype(summed.dtype)
    per_expert = by_expert(returned)
    last_width = per_expert.shape[-1]
    picked = per_expert.reshape(EXPERTS * CAP, last_width)[route_slot].reshape(
        tok_count, 2, last_width
    )
    mixed = jnp.sum(route_weight[:, :, None] * picked, axis=1)
    return mixed.astype(jnp.bfloat16)


def place(sizes):
    exp_count, groups = sizes
    return lax.axis_index("exp"), lax.axis_index("unit") // 2, lax.axis_index("unit") % 2


def pick_rows(named, before, d):
    rows = named.shape[1]
    place_of = jnp.where(named[d : d + 1, :] > 0, before[d : d + 1, :], -1)
    return (place_of == lax.broadcasted_iota(jnp.int32, (CAP, rows), 0)).astype(F32)


def count_earlier(ids, experts):
    rows = ids.shape[1]
    earlier = (
        lax.broadcasted_iota(jnp.int32, (rows, rows), 0)
        < lax.broadcasted_iota(jnp.int32, (rows, rows), 1)
    ).astype(BF16)
    named = ((ids[0:1, :] == experts) | (ids[1:2, :] == experts)).astype(jnp.int32)
    before = jnp.dot(named.astype(BF16), earlier, preferred_element_type=F32)
    return named, before.astype(jnp.int32)


def group_experts(exp_count, groups, z, g, rows):
    distance = lax.broadcasted_iota(jnp.int32, (max(8, exp_count), rows), 0)
    return lax.rem(z + distance, exp_count) * groups + g


def route_kernel(sizes, width, tokens_hbm, gain_hbm, ids_hbm, normed, *rest):
    exp_count, groups = sizes
    sends, (tokens, gain, ids, sems) = rest[:-4], rest[-4:]
    pairs = ((tokens_hbm, tokens), (gain_hbm, gain), (ids_hbm, ids))
    copies = [pltpu.make_async_copy(a, b, sems.at[n]) for n, (a, b) in enumerate(pairs)]
    for copy in copies:
        copy.start()
    rows, features = tokens.shape
    z, g, s = place(sizes)
    for copy in copies:
        copy.wait()
    step = 16
    for first in range(0, rows, step):
        values = tokens[first : first + step, :].astype(F32)
        mean = jnp.sum(values * values, axis=1, keepdims=True) * (1.0 / features)
        inv_rms = lax.rsqrt(mean + EPSILON)
        normed[first : first + step, :] = (values * inv_rms * gain[...]).astype(BF16)
    named, before = count_earlier(ids, group_experts(exp_count, groups, z, g, rows))
    picks = [pick_rows(named, before, d) for d in range(1, exp_count)]
    others = jnp.concatenate(picks, axis=0).astype(BF16)
    start = pl.multiple_of(s * (features // 2), 128)
    found = jnp.dot(others, normed[:, pl.ds(start, width)], preferred_element_type=F32)
    for d, send in enumerate(sends):
        send[...] = found[d * CAP : (d + 1) * CAP, :].astype(BF16)


def prepare_kernel(
    sizes, normed, ids, weights, active, gate, up, own, combine_high, combine_low, mask, *rest
):
    exp_count, groups = sizes
    rows, features = normed.shape
    z, g, s = place(sizes)
    copies = []
    *nears, sems = rest
    for n, near in enumerate(nears):
        source, piece = (gate, n) if n < GATE_NEAR else (up, n - GATE_NEAR)
        lines = pl.ds(piece * NEAR_ROWS, NEAR_ROWS)
        copies.append(pltpu.make_async_copy(source.at[lines, :], near, sems.at[n]))
    for copy in copies:
        copy.start()
    named, before = count_earlier(ids, group_experts(exp_count, groups, z, g, rows))
    own[...] = jnp.dot(
        pick_rows(named, before, 0).astype(BF16), normed[...], preferred_element_type=F32
    ).astype(BF16)
    zero = jnp.zeros((CAP, rows), F32)
    parts = []
    for d in range(exp_count):
        here = pick_rows(named, before, d) > 0
        expert = lax.rem(z + d, exp_count) * groups + g
        first = jnp.where(here & (ids[0:1, :] == expert), weights[0:1, :], zero)
        second = jnp.where(here & (ids[1:2, :] == expert), weights[1:2, :], zero)
        parts.append(first + second)
    padded = combine_high.shape[1]
    if padded > exp_count * CAP:
        parts.append(jnp.zeros((padded - exp_count * CAP, rows), F32))
    table = jnp.concatenate(parts, axis=0).T
    high = table.astype(BF16)
    combine_high[...] = high
    combine_low[...] = (table - high.astype(F32)).astype(BF16)
    unit_width = mask.shape[1]
    blocks = lax.broadcasted_iota(jnp.int32, mask.shape, 1) // BLK + s * (unit_width // BLK)
    source = lax.broadcasted_iota(jnp.int32, (mask.shape[0], 1), 0)
    own_expert = z * groups + g

    def add_entry(k, found):
        entry = jnp.full((mask.shape[0], 1), -1, jnp.int32)
        for d in range(exp_count):
            tile = lax.rem(z - d + exp_count, exp_count) * rows // TILE
            entry = jnp.where(source == d, active[tile, own_expert, k], entry)
        return jnp.where(blocks == entry, 1.0, found)

    mask[...] = lax.fori_loop(0, active.shape[2], add_entry, jnp.zeros(mask.shape, F32))
    for copy in copies:
        copy.wait()


def join_kernel(after, *refs):
    pieces = [r[...].astype(F32) for r in refs[:-1]]
    refs[-1][...] = jnp.concatenate(pieces, axis=0).astype(BF16)


def hidden_kernel(sizes, own, mine, other, *refs):
    exp_count, groups = sizes
    z, g, s = place(sizes)
    refs = list(refs)
    gate_near = [refs.pop(0) for _ in range(GATE_NEAR)]
    up_near = [refs.pop(0) for _ in range(UP_NEAR)]
    up, mask, hidden, gate_sum, up_sum, rows, slabs, sems = refs
    half = own.shape[1] // 2
    near, features = UP_NEAR * NEAR_ROWS, up.shape[0]
    unit_width = up.shape[1]
    far_count = (features - near) // K_SLAB

    def copy(index):
        slot = index % K_DEPTH
        return pltpu.make_async_copy(
            up.at[pl.ds(near + index * K_SLAB, K_SLAB), :], slabs.at[slot], sems.at[slot]
        )

    for n in range(min(K_DEPTH, far_count)):
        copy(n).start()
    for source, side in ((mine, s), (other, 1 - s)):
        cols = pl.ds(pl.multiple_of(side * half, 128), half)
        pieces = [own[:, cols].astype(F32), source[...].astype(F32)]
        rows[:, cols] = jnp.concatenate(pieces, axis=0).astype(BF16)

    def each_tile(body):
        def step(n, carry):
            body(pl.ds(pl.multiple_of(n * N_TILE, N_TILE), N_TILE))
            return carry

        lax.fori_loop(0, unit_width // N_TILE, step, 0)

    def product(nears, cols):
        value = None
        for n, near in enumerate(nears):
            lines = slice(n * NEAR_ROWS, (n + 1) * NEAR_ROWS)
            term = jnp.dot(rows[:, lines], near[:, cols], preferred_element_type=F32)
            value = term if value is None else value + term
        return value

    def gate_tile(cols):
        gate_sum[:, cols] = jnp.maximum(product(gate_near, cols), 0.0)

    def near_tile(cols):
        up_sum[:, cols] = product(up_near, cols)

    each_tile(gate_tile)
    each_tile(near_tile)
    for n in range(far_count):
        copy(n).wait()
        left = slice(near + n * K_SLAB, near + (n + 1) * K_SLAB)

        def far_tile(cols):
            value = up_sum[:, cols] + jnp.dot(
                rows[:, left], slabs[n % K_DEPTH, :, cols], preferred_element_type=F32
            )
            if n < far_count - 1:
                up_sum[:, cols] = value
                return
            value = gate_sum[:, cols] * jnp.maximum(value, 0.0)
            parts = []
            for d in range(exp_count):
                parts.append(value[d * CAP : (d + 1) * CAP, :] * mask[d : d + 1, cols])
            hidden[:, cols] = jnp.concatenate(parts, axis=0).astype(BF16)

        each_tile(far_tile)
        if n + K_DEPTH < far_count:
            copy(n + K_DEPTH).start()


def output_kernel(sizes, chunk, width, keep, *refs):
    exp_count, groups = sizes
    z, g, s = place(sizes)
    refs = list(refs)
    hidden, down = refs.pop(0), refs.pop(0)
    received = refs.pop(0) if keep else None
    total_sum, slabs, sems = refs[-3:]
    outs = refs[:-3]
    side = s if keep else 1 - s
    part = down.shape[1] // (2 * groups)
    pieces = down.shape[0] // N_ROWS

    def copy(index):
        group = lax.rem(g + index // pieces, groups)
        column = pl.multiple_of((group * 2 + side) * part + chunk * width, 128)
        lines = pl.ds(index % pieces * N_ROWS, N_ROWS)
        return pltpu.make_async_copy(
            down.at[lines, pl.ds(column, width)], slabs.at[index], sems.at[index]
        )

    for index in range(groups * pieces):
        copy(index).start()
    for offset in range(groups):
        for piece in range(pieces):
            index = offset * pieces + piece
            copy(index).wait()
            value = jnp.dot(
                hidden[:, piece * N_ROWS : (piece + 1) * N_ROWS],
                slabs[index],
                preferred_element_type=F32,
            )
            total_sum[...] = value if piece == 0 else total_sum[...] + value
        cols = slice(offset * width, (offset + 1) * width)
        if keep:
            for d in range(exp_count):
                lines = slice(d * CAP, (d + 1) * CAP)
                value = total_sum[lines, :] + received[:, cols].astype(F32)[lines, :]
                outs[d][:, cols] = value.astype(BF16)
        else:
            outs[0][:, cols] = total_sum[...].astype(BF16)


def combine_kernel(exp_count, high, low, *refs):
    pieces = [r[...].astype(F32) for r in refs[:exp_count]]
    kept, gives = refs[exp_count], refs[exp_count + 1 :]
    total = exp_count * CAP
    width = kept.shape[1]
    found = jnp.concatenate(pieces, axis=0).astype(BF16)
    value = jnp.dot(high[:, :total], found, preferred_element_type=F32)
    value = value + jnp.dot(low[:, :total], found, preferred_element_type=F32)
    kept[...] = value[:, :width]
    for n, give in enumerate(gives):
        give[...] = value[:, (n + 1) * width : (n + 2) * width].astype(BF16)


def finish_kernel(chunks, *refs):
    out = refs[-1]
    per_chunk = (len(refs) - 1) // chunks
    width = refs[0].shape[1]
    for chunk in range(chunks):
        kept, *others = refs[chunk * per_chunk : (chunk + 1) * per_chunk]
        value = kept[...]
        for other in others:
            value = value + other[...].astype(F32)
        out[:, chunk * width : (chunk + 1) * width] = value.astype(BF16)


def call(kernel, outs, ins, scratch=(), flops=0, moved=0, limit=16):
    vmem = pl.BlockSpec(memory_space=pltpu.VMEM)
    arrays, specs = [], []
    for array, space in ins:
        if space in (pltpu.HBM, pltpu.VMEM):
            array = pltpu.with_memory_space_constraint(array, space)
        arrays.append(array)
        specs.append(vmem if space is None else pl.BlockSpec(memory_space=space))
    shapes = []
    for shape, kind, *space in outs:
        shapes.append(space[0](shape, kind) if space else jax.ShapeDtypeStruct(shape, kind))
    return pl.pallas_call(
        kernel,
        out_shape=shapes,
        in_specs=specs,
        out_specs=[vmem] * len(outs),
        scratch_shapes=list(scratch),
        compiler_params=pltpu.CompilerParams(vmem_limit_bytes=limit << 20),
        cost_estimate=pl.CostEstimate(flops=flops, bytes_accessed=moved, transcendentals=0),
    )(*arrays)


def paired_experts(
    tokens, norm_gain, route_ids, route_weight, active_blocks, gate_weight, up_weight, down_weight
):
    exp_count, unit_count = lax.axis_size("exp"), lax.axis_size("unit")
    groups = unit_count // 2
    sizes = (exp_count, groups)
    tok_count, features = tokens.shape
    unit_width = gate_weight.shape[1]
    slots = exp_count * CAP
    half = features // 2
    width = half
    ids = route_ids.T
    weights = route_weight.T

    def shift(value, distance, group_shift=0):
        pairs = []
        for z in range(exp_count):
            for u in range(unit_count):
                target = (z + distance) % exp_count
                group = (u // 2 + group_shift) % groups
                pairs.append((z * unit_count + u, target * unit_count + group * 2 + u % 2))
        return lax.ppermute(value, ("exp", "unit"), pairs)

    def swap(value):
        return lax.ppermute(value, "unit", [(u, u ^ 1) for u in range(unit_count)])

    batch = exp_count - 1
    normed, *sends = call(
        functools.partial(route_kernel, sizes, width),
        [((tok_count, features), BF16)] + [((CAP, width), BF16)] * batch,
        [
            (tokens, pltpu.HBM),
            (norm_gain.reshape(1, -1), pltpu.HBM),
            (ids, pltpu.HBM),
        ],
        [
            pltpu.VMEM((tok_count, features), BF16),
            pltpu.VMEM((1, features), F32),
            pltpu.VMEM(ids.shape, jnp.int32),
            pltpu.SemaphoreType.DMA((3,)),
        ],
        flops=2 * tok_count * slots * width,
        moved=4 * tok_count * features,
    )
    padded = -(-slots // 128) * 128
    own, combine_high, combine_low, mask, *nears = call(
        functools.partial(prepare_kernel, sizes),
        [
            ((CAP, features), BF16),
            ((tok_count, padded), BF16),
            ((tok_count, padded), BF16),
            ((max(8, exp_count), unit_width), F32),
        ]
        + [((NEAR_ROWS, unit_width), BF16, pltpu.VMEM)] * (GATE_NEAR + UP_NEAR),
        [
            (normed, None),
            (ids, None),
            (weights, None),
            (active_blocks, pltpu.SMEM),
            (gate_weight, pltpu.HBM),
            (up_weight, pltpu.HBM),
        ],
        [pltpu.SemaphoreType.DMA((GATE_NEAR + UP_NEAR,))],
        flops=2 * tok_count * slots * features,
        moved=2 * (GATE_NEAR + UP_NEAR) * NEAR_ROWS * unit_width,
        limit=16,
    )
    arrived = [shift(value, d + 1) for d, value in enumerate(sends)]
    mine = call(
        join_kernel,
        [((batch * CAP, width), BF16)],
        [(mask, pl.ANY)] + [(v, None) for v in arrived],
        moved=1 << 20,
    )[0]
    other = swap(mine)
    acc = ((slots, unit_width), F32)
    hidden = call(
        functools.partial(hidden_kernel, sizes),
        [((slots, unit_width), BF16)],
        [(own, None), (mine, None), (other, None)]
        + [(v, pltpu.VMEM) for v in nears]
        + [(up_weight, pltpu.HBM), (mask, None)],
        [
            pltpu.VMEM(*acc),
            pltpu.VMEM(*acc),
            pltpu.VMEM((slots, features), BF16),
            pltpu.VMEM((K_DEPTH, K_SLAB, unit_width), BF16),
            pltpu.SemaphoreType.DMA((K_DEPTH,)),
        ],
        flops=2 * 2 * slots * features * unit_width,
        moved=2 * features * unit_width * 2,
        limit=16,
    )[0]
    part = features // unit_count
    out_width = part // OUT_CHUNKS

    def output(chunk, keep, received):
        pieces = groups * (unit_width // N_ROWS)
        return call(
            functools.partial(output_kernel, sizes, chunk, out_width, keep),
            [((CAP, groups * out_width), BF16)] * exp_count
            if keep
            else [((slots, groups * out_width), BF16)],
            [(hidden, None), (down_weight, pltpu.HBM)] + [(v, None) for v in received],
            [
                pltpu.VMEM((slots, out_width), F32),
                pltpu.VMEM((pieces, N_ROWS, out_width), BF16),
                pltpu.SemaphoreType.DMA((pieces,)),
            ],
            flops=2 * slots * unit_width * groups * out_width,
            moved=2 * unit_width * groups * out_width,
        )

    given = [output(chunk, False, ())[0] for chunk in range(OUT_CHUNKS)]
    taken = [swap(value) for value in given]
    last = []
    for chunk in range(OUT_CHUNKS):
        kept = output(chunk, True, [taken[chunk]])
        home = [kept[0]] + [shift(kept[d], -d) for d in range(1, exp_count)]
        stay, *gives = call(
            functools.partial(combine_kernel, exp_count),
            [((tok_count, out_width), F32)] + [((tok_count, out_width), BF16)] * (groups - 1),
            [(combine_high, None), (combine_low, None)] + [(v, None) for v in home],
            flops=4 * tok_count * slots * groups * out_width,
            moved=1 << 20,
        )
        last += [stay] + [shift(value, 0, n + 1) for n, value in enumerate(gives)]
    return call(
        functools.partial(finish_kernel, OUT_CHUNKS),
        [((tok_count, part), BF16)],
        [(v, None) for v in last],
        moved=1 << 20,
    )[0]


def per_device(*operands):
    tokens, gate_weight = operands[0], operands[5]
    exp_count, unit_count = lax.axis_size("exp"), lax.axis_size("unit")
    unit_width = gate_weight.shape[1]
    paired = (
        2 * unit_width == FF
        and unit_count % 2 == 0
        and exp_count * unit_count // 2 == EXPERTS
        and TILE % tokens.shape[0] == 0
    )
    return (paired_experts if paired else spread_experts)(*operands)


def solution(mesh):
    return jax.shard_map(
        per_device,
        mesh=mesh,
        in_specs=(
            P(("rep", "exp"), None),
            P(),
            P(("rep", "exp"), None),
            P(("rep", "exp"), None),
            P("rep", None, None),
            P(None, ("exp", "unit")),
            P(None, ("exp", "unit")),
            P(("exp", "unit"), None),
        ),
        out_specs=P(("rep", "exp"), "unit"),
        check_vma=False,
    )
```

```python
import functools

import jax
import jax.numpy as jnp
import numpy as np
from jax import lax
from jax.experimental import pallas as pl
from jax.experimental.pallas import tpu as pltpu
from jax.sharding import PartitionSpec as P

EXPERTS = 8
FF = 7168
BLK = 64
TILE = 256
CAP = 40

EPSILON = 1e-05

OUT_CHUNKS = 2
BLOCK = 512
K_BLOCKS = 2
READY = 4
BUFFERS = 5
LIMIT = 8

F32 = jnp.float32
BF16 = jnp.bfloat16


def normalize(tokens, norm_gain):
    values = tokens.astype(jnp.float32)
    inv_rms = lax.rsqrt(jnp.mean(values * values, axis=-1, keepdims=True) + EPSILON)
    return (values * inv_rms * norm_gain).astype(jnp.bfloat16)


def slot_numbers(entries, expert_count):
    onehot = (entries[..., None] == jnp.arange(expert_count, dtype=jnp.int32)).astype(jnp.int32)
    before = jnp.cumsum(onehot, axis=-2, dtype=jnp.int32) - onehot
    return jnp.sum(before * onehot, axis=-1)


def spread_experts(
    tokens, norm_gain, route_ids, route_weight, active_blocks, gate_weight, up_weight, down_weight
):
    exp_count = lax.axis_size("exp")
    unit_count = lax.axis_size("unit")
    tok_count, feature_width = tokens.shape
    unit_width = gate_weight.shape[1]
    row_units = unit_count * unit_width
    per_exp = max(1, row_units // FF)
    part_width = feature_width // unit_count
    block_count = unit_width // BLK
    tile_count = active_blocks.shape[0]
    exp_index = lax.axis_index("exp")
    unit_index = lax.axis_index("unit")
    first_unit = (exp_index * unit_count + unit_index) * unit_width
    own_expert = first_unit // FF
    first_block = first_unit % FF // BLK
    local_expert = own_expert - exp_index * row_units // FF
    normed = normalize(tokens, norm_gain)
    slot_index = slot_numbers(route_ids.reshape(1, -1), EXPERTS).reshape(tok_count, 2)
    positions = jnp.arange(tok_count, dtype=jnp.int32)
    tile_of = (exp_index * tok_count + positions) // TILE
    route_slot = (route_ids * CAP + slot_index).reshape(-1)
    token_source = (
        jnp.full((EXPERTS * CAP,), tok_count, jnp.int32)
        .at[route_slot]
        .set(jnp.repeat(positions, 2))
    )
    row_experts = np.arange(exp_count)[:, None] * row_units // FF + np.arange(per_exp)[None, :]
    slot_source = token_source.reshape(EXPERTS, CAP)[row_experts]
    padded_tiles = jnp.concatenate([tile_of, jnp.zeros((1,), jnp.int32)])
    slot_tiles = padded_tiles[slot_source]
    active_mine = lax.dynamic_index_in_dim(active_blocks, own_expert, 1, keepdims=False)
    local_blocks = first_block + jnp.arange(block_count, dtype=jnp.int32)
    block_on = jnp.any(active_mine[:, :, None] == local_blocks[None, None, :], axis=1).astype(
        jnp.float32
    )
    row_part = lax.dynamic_slice_in_dim(normed, unit_index * part_width, part_width, 1)
    padded_rows = jnp.concatenate([row_part, jnp.zeros((1, part_width), jnp.bfloat16)], 0)
    whole_rows = lax.all_gather(
        lax.all_to_all(padded_rows[slot_source], "exp", split_axis=0, concat_axis=0, tiled=True),
        "unit",
        axis=3,
        tiled=True,
    )
    slot_count = whole_rows.shape[2]
    own_rows = lax.dynamic_index_in_dim(whole_rows, local_expert, 1, keepdims=False).reshape(
        -1, feature_width
    )
    own_tiles = lax.dynamic_index_in_dim(
        lax.all_to_all(slot_tiles, "exp", split_axis=0, concat_axis=0, tiled=True),
        local_expert,
        1,
        keepdims=False,
    ).reshape(-1)
    tile_hot = (own_tiles[:, None] == jnp.arange(tile_count, dtype=jnp.int32)[None, :]).astype(
        jnp.float32
    )
    row_mask = jnp.dot(tile_hot, block_on, precision=lax.Precision.HIGHEST)
    gate_acts = jnp.dot(own_rows, gate_weight, preferred_element_type=jnp.float32)
    up_acts = jnp.dot(own_rows, up_weight, preferred_element_type=jnp.float32)
    hidden = jax.nn.relu(gate_acts) * jax.nn.relu(up_acts)
    hidden = (hidden.reshape(-1, block_count, BLK) * row_mask[:, :, None]).reshape(-1, unit_width)
    hidden = hidden.astype(jnp.bfloat16)
    partial_value = jnp.dot(hidden, down_weight, preferred_element_type=jnp.float32)
    partial_value = partial_value.reshape(exp_count, slot_count, feature_width)
    result = jnp.zeros((exp_count, per_exp, slot_count, feature_width), jnp.float32)
    partial_all = lax.dynamic_update_index_in_dim(result, partial_value, local_expert, 1)

    def by_expert(returned):
        last_width = returned.shape[-1]
        if per_exp == 1:
            grouped = returned.reshape(EXPERTS, exp_count // EXPERTS, CAP, last_width)
            return jnp.sum(grouped, axis=1, dtype=jnp.float32)
        return returned.reshape(EXPERTS, CAP, last_width).astype(jnp.float32)

    summed = lax.psum_scatter(
        partial_all.astype(jnp.bfloat16), "unit", scatter_dimension=3, tiled=True
    ).astype(jnp.float32)
    returned = lax.all_to_all(
        summed.astype(jnp.bfloat16), "exp", split_axis=0, concat_axis=0, tiled=True
    ).astype(summed.dtype)
    per_expert = by_expert(returned)
    last_width = per_expert.shape[-1]
    picked = per_expert.reshape(EXPERTS * CAP, last_width)[route_slot].reshape(
        tok_count, 2, last_width
    )
    mixed = jnp.sum(route_weight[:, :, None] * picked, axis=1)
    return mixed.astype(jnp.bfloat16)


def place(sizes):
    exp_count, groups = sizes
    return lax.axis_index("exp"), lax.axis_index("unit") // 2, lax.axis_index("unit") % 2


def pick_rows(named, before, d):
    rows = named.shape[1]
    place_of = jnp.where(named[d : d + 1, :] > 0, before[d : d + 1, :], -1)
    return (place_of == lax.broadcasted_iota(jnp.int32, (CAP, rows), 0)).astype(F32)


def count_earlier(ids, experts):
    rows = ids.shape[1]
    earlier = (
        lax.broadcasted_iota(jnp.int32, (rows, rows), 0)
        < lax.broadcasted_iota(jnp.int32, (rows, rows), 1)
    ).astype(BF16)
    named = ((ids[0:1, :] == experts) | (ids[1:2, :] == experts)).astype(jnp.int32)
    before = jnp.dot(named.astype(BF16), earlier, preferred_element_type=F32)
    return named, before.astype(jnp.int32)


def group_experts(exp_count, groups, z, g, rows):
    distance = lax.broadcasted_iota(jnp.int32, (max(8, exp_count), rows), 0)
    return lax.rem(z + distance, exp_count) * groups + g


def route_kernel(sizes, width, tokens_hbm, gain_hbm, ids_hbm, own, *rest):
    exp_count, groups = sizes
    sends, (tokens, normed, gain, ids, sems) = rest[:-5], rest[-5:]
    pairs = ((tokens_hbm, tokens), (gain_hbm, gain), (ids_hbm, ids))
    copies = [pltpu.make_async_copy(a, b, sems.at[n]) for n, (a, b) in enumerate(pairs)]
    for copy in copies:
        copy.start()
    rows, features = tokens.shape
    z, g, s = place(sizes)
    for copy in copies:
        copy.wait()
    step = 16
    for first in range(0, rows, step):
        values = tokens[first : first + step, :].astype(F32)
        mean = jnp.sum(values * values, axis=1, keepdims=True) * (1.0 / features)
        inv_rms = lax.rsqrt(mean + EPSILON)
        normed[first : first + step, :] = (values * inv_rms * gain[...]).astype(BF16)
    named, before = count_earlier(ids, group_experts(exp_count, groups, z, g, rows))
    picks = [pick_rows(named, before, d) for d in range(exp_count)]
    others = jnp.concatenate(picks[1:], axis=0).astype(BF16)
    start = pl.multiple_of(s * (features // 2), 128)
    found = jnp.dot(others, normed[:, pl.ds(start, width)], preferred_element_type=F32)
    for d, send in enumerate(sends):
        send[...] = found[d * CAP : (d + 1) * CAP, :].astype(BF16)
    own[...] = jnp.dot(
        picks[0].astype(BF16), normed[...], preferred_element_type=F32
    ).astype(BF16)


def fetch_rows(weight, piece, buffer, sem):
    def start(index, carry):
        line = piece * K_BLOCKS + lax.rem(index, K_BLOCKS)
        column = index // K_BLOCKS
        pltpu.make_async_copy(
            weight.at[
                pl.ds(pl.multiple_of(line * BLOCK, BLOCK), BLOCK),
                pl.ds(pl.multiple_of(column * BLOCK, BLOCK), BLOCK),
            ],
            buffer.at[index],
            sem,
        ).start()
        return carry

    lax.fori_loop(0, buffer.shape[0], start, 0)


def fetch_columns(sizes, down, chunk, keep, buffer, sem):
    exp_count, groups = sizes
    z, g, s = place(sizes)
    side = s if keep else 1 - s
    part = down.shape[1] // (2 * groups)
    lines = down.shape[0] // BLOCK

    def start(index, carry):
        group = lax.rem(g + index // lines, groups)
        column = (group * 2 + side) * part + chunk * BLOCK
        pltpu.make_async_copy(
            down.at[
                pl.ds(pl.multiple_of(lax.rem(index, lines) * BLOCK, BLOCK), BLOCK),
                pl.ds(pl.multiple_of(column, BLOCK), BLOCK),
            ],
            buffer.at[index],
            sem,
        ).start()
        return carry

    lax.fori_loop(0, buffer.shape[0], start, 0)


def await_all(buffer, sem):
    pltpu.make_async_copy(buffer, buffer, sem).wait()


def stacked(buffer, column, count):
    blocks = buffer[column * count : (column + 1) * count]
    return blocks.reshape(count * BLOCK, BLOCK)


def table_kernel(sizes, ids_hbm, weights_hbm, after, combine_high, combine_low, ids, weights, sems):
    exp_count, groups = sizes
    pairs = ((ids_hbm, ids), (weights_hbm, weights))
    copies = [pltpu.make_async_copy(a, b, sems.at[n]) for n, (a, b) in enumerate(pairs)]
    for copy in copies:
        copy.start()
    for copy in copies:
        copy.wait()
    rows = ids.shape[1]
    z, g, s = place(sizes)
    named, before = count_earlier(ids, group_experts(exp_count, groups, z, g, rows))
    zero = jnp.zeros((CAP, rows), F32)
    parts = []
    for d in range(exp_count):
        here = pick_rows(named, before, d) > 0
        expert = lax.rem(z + d, exp_count) * groups + g
        first = jnp.where(here & (ids[0:1, :] == expert), weights[0:1, :], zero)
        second = jnp.where(here & (ids[1:2, :] == expert), weights[1:2, :], zero)
        parts.append(first + second)
    padded = combine_high.shape[1]
    if padded > exp_count * CAP:
        parts.append(jnp.zeros((padded - exp_count * CAP, rows), F32))
    table = jnp.concatenate(parts, axis=0).T
    high = table.astype(BF16)
    combine_high[...] = high
    combine_low[...] = (table - high.astype(F32)).astype(BF16)


def prepare_kernel(sizes, rows, active_hbm, gate, after, mask, *rest):
    exp_count, groups = sizes
    *buffers, active, small_sem, sems = rest
    z, g, s = place(sizes)
    small = pltpu.make_async_copy(active_hbm, active, small_sem)
    small.start()
    for n, buffer in enumerate(buffers[:READY]):
        fetch_rows(gate, n, buffer, sems.at[n])
    small.wait()
    unit_width = mask.shape[1]
    blocks = lax.broadcasted_iota(jnp.int32, mask.shape, 1) // BLK + s * (unit_width // BLK)
    source = lax.broadcasted_iota(jnp.int32, (mask.shape[0], 1), 0)
    own_expert = z * groups + g

    def add_entry(k, found):
        entry = jnp.full((mask.shape[0], 1), -1, jnp.int32)
        for d in range(exp_count):
            tile = lax.rem(z - d + exp_count, exp_count) * rows // TILE
            entry = jnp.where(source == d, active[tile, own_expert, k], entry)
        return jnp.where(blocks == entry, 1.0, found)

    mask[...] = lax.fori_loop(0, active.shape[2], add_entry, jnp.zeros(mask.shape, F32))
    for n, buffer in enumerate(buffers[:READY]):
        await_all(buffer, sems.at[n])


def join_kernel(after, *refs):
    pieces = [r[...].astype(F32) for r in refs[:-1]]
    refs[-1][...] = jnp.concatenate(pieces, axis=0).astype(BF16)


def hidden_kernel(sizes, own, mine, other, *refs):
    exp_count, groups = sizes
    z, g, s = place(sizes)
    refs = list(refs)
    refs = refs[BUFFERS:]
    up, down, mask, hidden = [refs.pop(0) for _ in range(4)]
    buffers = [refs.pop(0) for _ in range(BUFFERS)]
    gate_sum, up_sum, rows, sems = refs
    half = own.shape[1] // 2
    features, unit_width = up.shape
    columns = unit_width // BLOCK
    pieces = features // (K_BLOCKS * BLOCK)
    count = len(buffers)

    def fetch(piece):
        buffer, sem = buffers[piece % count], sems.at[piece % count]
        if piece < 2 * pieces:
            fetch_rows(up, piece - pieces, buffer, sem)
        elif piece < 2 * pieces + OUT_CHUNKS:
            fetch_columns(sizes, down, piece - 2 * pieces, False, buffer, sem)

    for piece in range(READY, count):
        fetch(piece)
    for source, side in ((mine, s), (other, 1 - s)):
        cols = pl.ds(pl.multiple_of(side * half, 128), half)
        joined = [own[:, cols].astype(F32), source[...].astype(F32)]
        rows[:, cols] = jnp.concatenate(joined, axis=0).astype(BF16)
    for piece in range(2 * pieces):
        buffer = buffers[piece % count]
        if piece >= READY:
            await_all(buffer, sems.at[piece % count])
        step = piece % pieces
        total = gate_sum if piece < pieces else up_sum
        left = rows[:, step * K_BLOCKS * BLOCK : (step + 1) * K_BLOCKS * BLOCK]
        for column in range(columns):
            cols = slice(column * BLOCK, (column + 1) * BLOCK)
            value = jnp.dot(left, stacked(buffer, column, K_BLOCKS), preferred_element_type=F32)
            if step > 0:
                value = total[:, cols] + value
            if piece < 2 * pieces - 1:
                total[:, cols] = value
                continue
            value = jnp.maximum(gate_sum[:, cols], 0.0) * jnp.maximum(value, 0.0)
            parts = []
            for d in range(exp_count):
                parts.append(value[d * CAP : (d + 1) * CAP, :] * mask[d : d + 1, cols])
            hidden[:, cols] = jnp.concatenate(parts, axis=0).astype(BF16)
        fetch(piece + count)
    for piece in range(2 * pieces, 2 * pieces + OUT_CHUNKS):
        await_all(buffers[piece % count], sems.at[piece % count])


def give_kernel(sizes, chunk, hidden, weights, down, given, kept_weights, sem):
    exp_count, groups = sizes
    fetch_columns(sizes, down, chunk, True, kept_weights, sem)
    lines = down.shape[0] // BLOCK
    for offset in range(groups):
        value = jnp.dot(
            hidden[...], stacked(weights, offset, lines), preferred_element_type=F32
        )
        given[:, offset * BLOCK : (offset + 1) * BLOCK] = value.astype(BF16)
    await_all(kept_weights, sem)


def keep_kernel(sizes, hidden, weights, received, *outs):
    exp_count, groups = sizes
    lines = hidden.shape[1] // BLOCK
    for offset in range(groups):
        cols = slice(offset * BLOCK, (offset + 1) * BLOCK)
        value = jnp.dot(
            hidden[...], stacked(weights, offset, lines), preferred_element_type=F32
        )
        value = value + received[:, cols].astype(F32)
        for d in range(exp_count):
            outs[d][:, cols] = value[d * CAP : (d + 1) * CAP, :].astype(BF16)


def combine_kernel(exp_count, high, low, *refs):
    pieces = [r[...].astype(F32) for r in refs[:exp_count]]
    kept, gives = refs[exp_count], refs[exp_count + 1 :]
    total = exp_count * CAP
    width = kept.shape[1]
    found = jnp.concatenate(pieces, axis=0).astype(BF16)
    value = jnp.dot(high[:, :total], found, preferred_element_type=F32)
    value = value + jnp.dot(low[:, :total], found, preferred_element_type=F32)
    kept[...] = value[:, :width]
    for n, give in enumerate(gives):
        give[...] = value[:, (n + 1) * width : (n + 2) * width].astype(BF16)


def finish_kernel(chunks, *refs):
    out = refs[-1]
    per_chunk = (len(refs) - 1) // chunks
    width = refs[0].shape[1]
    for chunk in range(chunks):
        kept, *others = refs[chunk * per_chunk : (chunk + 1) * per_chunk]
        value = kept[...]
        for other in others:
            value = value + other[...].astype(F32)
        out[:, chunk * width : (chunk + 1) * width] = value.astype(BF16)


def call(kernel, outs, ins, scratch=(), flops=0, moved=0, aliases=None):
    vmem = pl.BlockSpec(memory_space=pltpu.VMEM)
    arrays, specs = [], []
    for array, space in ins:
        if space in (pltpu.HBM, pltpu.VMEM):
            array = pltpu.with_memory_space_constraint(array, space)
        arrays.append(array)
        specs.append(vmem if space is None else pl.BlockSpec(memory_space=space))
    shapes = []
    for shape, kind, *space in outs:
        shapes.append(space[0](shape, kind) if space else jax.ShapeDtypeStruct(shape, kind))
    return pl.pallas_call(
        kernel,
        out_shape=shapes,
        in_specs=specs,
        out_specs=[vmem] * len(outs),
        scratch_shapes=list(scratch),
        input_output_aliases=aliases or {},
        compiler_params=pltpu.CompilerParams(vmem_limit_bytes=LIMIT << 20),
        cost_estimate=pl.CostEstimate(flops=flops, bytes_accessed=moved, transcendentals=0),
    )(*arrays)


def paired_experts(
    tokens, norm_gain, route_ids, route_weight, active_blocks, gate_weight, up_weight, down_weight
):
    exp_count, unit_count = lax.axis_size("exp"), lax.axis_size("unit")
    groups = unit_count // 2
    sizes = (exp_count, groups)
    tok_count, features = tokens.shape
    unit_width = gate_weight.shape[1]
    slots = exp_count * CAP
    half = features // 2
    width = half
    ids = route_ids.T
    weights = route_weight.T

    def shift(value, distance, group_shift=0):
        pairs = []
        for z in range(exp_count):
            for u in range(unit_count):
                target = (z + distance) % exp_count
                group = (u // 2 + group_shift) % groups
                pairs.append((z * unit_count + u, target * unit_count + group * 2 + u % 2))
        return lax.ppermute(value, ("exp", "unit"), pairs)

    def swap(value):
        return lax.ppermute(value, "unit", [(u, u ^ 1) for u in range(unit_count)])

    batch = exp_count - 1
    own, *sends = call(
        functools.partial(route_kernel, sizes, width),
        [((CAP, features), BF16)] + [((CAP, width), BF16)] * batch,
        [
            (tokens, pltpu.HBM),
            (norm_gain.reshape(1, -1), pltpu.HBM),
            (ids, pltpu.HBM),
        ],
        [
            pltpu.VMEM((tok_count, features), BF16),
            pltpu.VMEM((tok_count, features), BF16),
            pltpu.VMEM((1, features), F32),
            pltpu.VMEM(ids.shape, jnp.int32),
            pltpu.SemaphoreType.DMA((3,)),
        ],
        flops=2 * tok_count * slots * width,
        moved=4 * tok_count * features,
    )
    blocks = K_BLOCKS * unit_width // BLOCK
    buffer = ((blocks, BLOCK, BLOCK), BF16, pltpu.VMEM)
    piece_bytes = 2 * blocks * BLOCK * BLOCK
    mask, *ready = call(
        functools.partial(prepare_kernel, sizes, tok_count),
        [((max(8, exp_count), unit_width), F32)] + [buffer] * BUFFERS,
        [(active_blocks, pltpu.HBM), (gate_weight, pltpu.HBM), (own, pl.ANY)],
        [
            pltpu.SMEM(active_blocks.shape, jnp.int32),
            pltpu.SemaphoreType.DMA,
            pltpu.SemaphoreType.DMA((READY,)),
        ],
        flops=2 * tok_count * slots * features,
        moved=READY * piece_bytes,
    )
    arrived = [shift(value, d + 1) for d, value in enumerate(sends)]
    mine = call(
        join_kernel,
        [((batch * CAP, width), BF16)],
        [(mask, pl.ANY)] + [(v, None) for v in arrived],
        moved=1 << 20,
    )[0]
    other = swap(mine)
    padded = -(-slots // 128) * 128
    combine_high, combine_low = call(
        functools.partial(table_kernel, sizes),
        [((tok_count, padded), BF16)] * 2,
        [(ids, pltpu.HBM), (weights, pltpu.HBM), (mine, pl.ANY)],
        [
            pltpu.VMEM(ids.shape, jnp.int32),
            pltpu.VMEM(weights.shape, F32),
            pltpu.SemaphoreType.DMA((2,)),
        ],
        moved=1 << 21,
    )
    acc = pltpu.VMEM((slots, unit_width), F32)
    hidden, *buffers = call(
        functools.partial(hidden_kernel, sizes),
        [((slots, unit_width), BF16)] + [buffer] * BUFFERS,
        [(own, None), (mine, None), (other, None)]
        + [(v, pltpu.VMEM) for v in ready]
        + [(up_weight, pltpu.HBM), (down_weight, pltpu.HBM), (mask, None)],
        [
            acc,
            acc,
            pltpu.VMEM((slots, features), BF16),
            pltpu.SemaphoreType.DMA((BUFFERS,)),
        ],
        flops=2 * 2 * slots * features * unit_width,
        moved=6 * piece_bytes,
        aliases={3 + n: 1 + n for n in range(BUFFERS)},
    )
    first = 2 * features // (K_BLOCKS * BLOCK)
    part = features // unit_count
    out_width = BLOCK
    given, kept_weights = [], []
    for chunk in range(OUT_CHUNKS):
        value, kept = call(
            functools.partial(give_kernel, sizes, chunk),
            [((slots, groups * BLOCK), BF16), buffer],
            [
                (hidden, None),
                (buffers[(first + chunk) % BUFFERS], pltpu.VMEM),
                (down_weight, pltpu.HBM),
            ],
            [pltpu.SemaphoreType.DMA],
            flops=2 * slots * unit_width * groups * BLOCK,
            moved=piece_bytes,
        )
        given.append(value)
        kept_weights.append(kept)
    taken = [swap(value) for value in given]
    last = []
    for chunk in range(OUT_CHUNKS):
        kept = call(
            functools.partial(keep_kernel, sizes),
            [((CAP, groups * BLOCK), BF16)] * exp_count,
            [(hidden, None), (kept_weights[chunk], pltpu.VMEM), (taken[chunk], None)],
            flops=2 * slots * unit_width * groups * BLOCK,
            moved=piece_bytes,
        )
        home = [kept[0]] + [shift(kept[d], -d) for d in range(1, exp_count)]
        stay, *gives = call(
            functools.partial(combine_kernel, exp_count),
            [((tok_count, out_width), F32)] + [((tok_count, out_width), BF16)] * (groups - 1),
            [(combine_high, None), (combine_low, None)] + [(v, None) for v in home],
            flops=4 * tok_count * slots * groups * out_width,
            moved=1 << 20,
        )
        last += [stay] + [shift(value, 0, n + 1) for n, value in enumerate(gives)]
    return call(
        functools.partial(finish_kernel, OUT_CHUNKS),
        [((tok_count, part), BF16)],
        [(v, None) for v in last],
        moved=1 << 20,
    )[0]


def per_device(*operands):
    tokens, gate_weight = operands[0], operands[5]
    exp_count, unit_count = lax.axis_size("exp"), lax.axis_size("unit")
    unit_width = gate_weight.shape[1]
    paired = (
        2 * unit_width == FF
        and unit_count % 2 == 0
        and exp_count * unit_count // 2 == EXPERTS
        and TILE % tokens.shape[0] == 0
        and unit_width % BLOCK == 0
        and tokens.shape[1] == unit_count * OUT_CHUNKS * BLOCK == READY * K_BLOCKS * BLOCK
        and unit_count // 2 == K_BLOCKS
    )
    return (paired_experts if paired else spread_experts)(*operands)


def solution(mesh):
    return jax.shard_map(
        per_device,
        mesh=mesh,
        in_specs=(
            P(("rep", "exp"), None),
            P(),
            P(("rep", "exp"), None),
            P(("rep", "exp"), None),
            P("rep", None, None),
            P(None, ("exp", "unit")),
            P(None, ("exp", "unit")),
            P(("exp", "unit"), None),
        ),
        out_specs=P(("rep", "exp"), "unit"),
        check_vma=False,
    )
```

```python
import functools

import jax
import jax.numpy as jnp
import numpy as np
from jax import lax
from jax.experimental import pallas as pl
from jax.experimental.pallas import tpu as pltpu
from jax.sharding import PartitionSpec as P

EXPERTS = 8
FF = 7168
BLK = 64
TILE = 256
CAP = 40

EPSILON = 1e-05

BLOCK = 512
K_BLOCKS = 2
READY = 4
BUFFERS = 5
LIMIT = 8

F32 = jnp.float32
BF16 = jnp.bfloat16


def normalize(tokens, norm_gain):
    values = tokens.astype(jnp.float32)
    inv_rms = lax.rsqrt(jnp.mean(values * values, axis=-1, keepdims=True) + EPSILON)
    return (values * inv_rms * norm_gain).astype(jnp.bfloat16)


def slot_numbers(entries, expert_count):
    onehot = (entries[..., None] == jnp.arange(expert_count, dtype=jnp.int32)).astype(jnp.int32)
    before = jnp.cumsum(onehot, axis=-2, dtype=jnp.int32) - onehot
    return jnp.sum(before * onehot, axis=-1)


def spread_experts(
    tokens, norm_gain, route_ids, route_weight, active_blocks, gate_weight, up_weight, down_weight
):
    exp_count = lax.axis_size("exp")
    unit_count = lax.axis_size("unit")
    tok_count, feature_width = tokens.shape
    unit_width = gate_weight.shape[1]
    row_units = unit_count * unit_width
    per_exp = max(1, row_units // FF)
    part_width = feature_width // unit_count
    block_count = unit_width // BLK
    tile_count = active_blocks.shape[0]
    exp_index = lax.axis_index("exp")
    unit_index = lax.axis_index("unit")
    first_unit = (exp_index * unit_count + unit_index) * unit_width
    own_expert = first_unit // FF
    first_block = first_unit % FF // BLK
    local_expert = own_expert - exp_index * row_units // FF
    normed = normalize(tokens, norm_gain)
    slot_index = slot_numbers(route_ids.reshape(1, -1), EXPERTS).reshape(tok_count, 2)
    positions = jnp.arange(tok_count, dtype=jnp.int32)
    tile_of = (exp_index * tok_count + positions) // TILE
    route_slot = (route_ids * CAP + slot_index).reshape(-1)
    token_source = (
        jnp.full((EXPERTS * CAP,), tok_count, jnp.int32)
        .at[route_slot]
        .set(jnp.repeat(positions, 2))
    )
    row_experts = np.arange(exp_count)[:, None] * row_units // FF + np.arange(per_exp)[None, :]
    slot_source = token_source.reshape(EXPERTS, CAP)[row_experts]
    padded_tiles = jnp.concatenate([tile_of, jnp.zeros((1,), jnp.int32)])
    slot_tiles = padded_tiles[slot_source]
    active_mine = lax.dynamic_index_in_dim(active_blocks, own_expert, 1, keepdims=False)
    local_blocks = first_block + jnp.arange(block_count, dtype=jnp.int32)
    block_on = jnp.any(active_mine[:, :, None] == local_blocks[None, None, :], axis=1).astype(
        jnp.float32
    )
    row_part = lax.dynamic_slice_in_dim(normed, unit_index * part_width, part_width, 1)
    padded_rows = jnp.concatenate([row_part, jnp.zeros((1, part_width), jnp.bfloat16)], 0)
    whole_rows = lax.all_gather(
        lax.all_to_all(padded_rows[slot_source], "exp", split_axis=0, concat_axis=0, tiled=True),
        "unit",
        axis=3,
        tiled=True,
    )
    slot_count = whole_rows.shape[2]
    own_rows = lax.dynamic_index_in_dim(whole_rows, local_expert, 1, keepdims=False).reshape(
        -1, feature_width
    )
    own_tiles = lax.dynamic_index_in_dim(
        lax.all_to_all(slot_tiles, "exp", split_axis=0, concat_axis=0, tiled=True),
        local_expert,
        1,
        keepdims=False,
    ).reshape(-1)
    tile_hot = (own_tiles[:, None] == jnp.arange(tile_count, dtype=jnp.int32)[None, :]).astype(
        jnp.float32
    )
    row_mask = jnp.dot(tile_hot, block_on, precision=lax.Precision.HIGHEST)
    gate_acts = jnp.dot(own_rows, gate_weight, preferred_element_type=jnp.float32)
    up_acts = jnp.dot(own_rows, up_weight, preferred_element_type=jnp.float32)
    hidden = jax.nn.relu(gate_acts) * jax.nn.relu(up_acts)
    hidden = (hidden.reshape(-1, block_count, BLK) * row_mask[:, :, None]).reshape(-1, unit_width)
    hidden = hidden.astype(jnp.bfloat16)
    partial_value = jnp.dot(hidden, down_weight, preferred_element_type=jnp.float32)
    partial_value = partial_value.reshape(exp_count, slot_count, feature_width)
    result = jnp.zeros((exp_count, per_exp, slot_count, feature_width), jnp.float32)
    partial_all = lax.dynamic_update_index_in_dim(result, partial_value, local_expert, 1)

    def by_expert(returned):
        last_width = returned.shape[-1]
        if per_exp == 1:
            grouped = returned.reshape(EXPERTS, exp_count // EXPERTS, CAP, last_width)
            return jnp.sum(grouped, axis=1, dtype=jnp.float32)
        return returned.reshape(EXPERTS, CAP, last_width).astype(jnp.float32)

    summed = lax.psum_scatter(
        partial_all.astype(jnp.bfloat16), "unit", scatter_dimension=3, tiled=True
    ).astype(jnp.float32)
    returned = lax.all_to_all(
        summed.astype(jnp.bfloat16), "exp", split_axis=0, concat_axis=0, tiled=True
    ).astype(summed.dtype)
    per_expert = by_expert(returned)
    last_width = per_expert.shape[-1]
    picked = per_expert.reshape(EXPERTS * CAP, last_width)[route_slot].reshape(
        tok_count, 2, last_width
    )
    mixed = jnp.sum(route_weight[:, :, None] * picked, axis=1)
    return mixed.astype(jnp.bfloat16)


def place(sizes):
    exp_count, groups = sizes
    return lax.axis_index("exp"), lax.axis_index("unit") // 2, lax.axis_index("unit") % 2


def pick_rows(named, before, d):
    rows = named.shape[1]
    place_of = jnp.where(named[d : d + 1, :] > 0, before[d : d + 1, :], -1)
    return (place_of == lax.broadcasted_iota(jnp.int32, (CAP, rows), 0)).astype(F32)


def count_earlier(ids, experts):
    rows = ids.shape[1]
    earlier = (
        lax.broadcasted_iota(jnp.int32, (rows, rows), 0)
        < lax.broadcasted_iota(jnp.int32, (rows, rows), 1)
    ).astype(BF16)
    named = ((ids[0:1, :] == experts) | (ids[1:2, :] == experts)).astype(jnp.int32)
    before = jnp.dot(named.astype(BF16), earlier, preferred_element_type=F32)
    return named, before.astype(jnp.int32)


def group_experts(exp_count, groups, z, g, rows):
    distance = lax.broadcasted_iota(jnp.int32, (max(8, exp_count), rows), 0)
    return lax.rem(z + distance, exp_count) * groups + g


def route_kernel(sizes, width, tokens_hbm, gain_hbm, ids_hbm, own, *rest):
    exp_count, groups = sizes
    sends, (tokens, normed, gain, ids, sems) = rest[:-5], rest[-5:]
    pairs = ((tokens_hbm, tokens), (gain_hbm, gain), (ids_hbm, ids))
    copies = [pltpu.make_async_copy(a, b, sems.at[n]) for n, (a, b) in enumerate(pairs)]
    for copy in copies:
        copy.start()
    rows, features = tokens.shape
    z, g, s = place(sizes)
    for copy in copies:
        copy.wait()
    step = 16
    for first in range(0, rows, step):
        values = tokens[first : first + step, :].astype(F32)
        mean = jnp.sum(values * values, axis=1, keepdims=True) * (1.0 / features)
        inv_rms = lax.rsqrt(mean + EPSILON)
        normed[first : first + step, :] = (values * inv_rms * gain[...]).astype(BF16)
    named, before = count_earlier(ids, group_experts(exp_count, groups, z, g, rows))
    picks = [pick_rows(named, before, d) for d in range(exp_count)]
    others = jnp.concatenate(picks[1:], axis=0).astype(BF16)
    start = pl.multiple_of(s * (features // 2), 128)
    found = jnp.dot(others, normed[:, pl.ds(start, width)], preferred_element_type=F32)
    for d, send in enumerate(sends):
        send[...] = found[d * CAP : (d + 1) * CAP, :].astype(BF16)
    own[...] = jnp.dot(
        picks[0].astype(BF16), normed[...], preferred_element_type=F32
    ).astype(BF16)


def fetch_rows(weight, piece, buffer, sem):
    def start(index, carry):
        line = piece * K_BLOCKS + lax.rem(index, K_BLOCKS)
        column = index // K_BLOCKS
        pltpu.make_async_copy(
            weight.at[
                pl.ds(pl.multiple_of(line * BLOCK, BLOCK), BLOCK),
                pl.ds(pl.multiple_of(column * BLOCK, BLOCK), BLOCK),
            ],
            buffer.at[index],
            sem,
        ).start()
        return carry

    lax.fori_loop(0, buffer.shape[0], start, 0)


def fetch_columns(sizes, down, offset, keep, buffer, sem):
    exp_count, groups = sizes
    z, g, s = place(sizes)
    side = s if keep else 1 - s
    part = down.shape[1] // (2 * groups)
    lines = down.shape[0] // BLOCK
    first = (lax.rem(g + offset, groups) * 2 + side) * part

    def start(index, carry):
        column = first + index // lines * BLOCK
        pltpu.make_async_copy(
            down.at[
                pl.ds(pl.multiple_of(lax.rem(index, lines) * BLOCK, BLOCK), BLOCK),
                pl.ds(pl.multiple_of(column, BLOCK), BLOCK),
            ],
            buffer.at[index],
            sem,
        ).start()
        return carry

    lax.fori_loop(0, buffer.shape[0], start, 0)


def await_all(buffer, sem):
    pltpu.make_async_copy(buffer, buffer, sem).wait()


def stacked(buffer, column, count):
    blocks = buffer[column * count : (column + 1) * count]
    return blocks.reshape(count * BLOCK, BLOCK)


def table_kernel(sizes, ids_hbm, weights_hbm, after, combine_high, combine_low, ids, weights, sems):
    exp_count, groups = sizes
    pairs = ((ids_hbm, ids), (weights_hbm, weights))
    copies = [pltpu.make_async_copy(a, b, sems.at[n]) for n, (a, b) in enumerate(pairs)]
    for copy in copies:
        copy.start()
    for copy in copies:
        copy.wait()
    rows = ids.shape[1]
    z, g, s = place(sizes)
    zero = jnp.zeros((CAP, rows), F32)
    padded = combine_high.shape[2]
    for order in range(groups):
        group = lax.rem(g - (order + 1) % groups + groups, groups)
        named, before = count_earlier(ids, group_experts(exp_count, groups, z, group, rows))
        parts = []
        for d in range(exp_count):
            here = pick_rows(named, before, d) > 0
            expert = lax.rem(z + d, exp_count) * groups + group
            first = jnp.where(here & (ids[0:1, :] == expert), weights[0:1, :], zero)
            second = jnp.where(here & (ids[1:2, :] == expert), weights[1:2, :], zero)
            parts.append(first + second)
        if padded > exp_count * CAP:
            parts.append(jnp.zeros((padded - exp_count * CAP, rows), F32))
        table = jnp.concatenate(parts, axis=0).T
        high = table.astype(BF16)
        combine_high[order] = high
        combine_low[order] = (table - high.astype(F32)).astype(BF16)


def prepare_kernel(sizes, rows, active_hbm, gate, after, mask, *rest):
    exp_count, groups = sizes
    *buffers, active, small_sem, sems = rest
    z, g, s = place(sizes)
    small = pltpu.make_async_copy(active_hbm, active, small_sem)
    small.start()
    for n, buffer in enumerate(buffers[:READY]):
        fetch_rows(gate, n, buffer, sems.at[n])
    small.wait()
    unit_width = mask.shape[1]
    blocks = lax.broadcasted_iota(jnp.int32, mask.shape, 1) // BLK + s * (unit_width // BLK)
    source = lax.broadcasted_iota(jnp.int32, (mask.shape[0], 1), 0)
    own_expert = z * groups + g

    def add_entry(k, found):
        entry = jnp.full((mask.shape[0], 1), -1, jnp.int32)
        for d in range(exp_count):
            tile = lax.rem(z - d + exp_count, exp_count) * rows // TILE
            entry = jnp.where(source == d, active[tile, own_expert, k], entry)
        return jnp.where(blocks == entry, 1.0, found)

    mask[...] = lax.fori_loop(0, active.shape[2], add_entry, jnp.zeros(mask.shape, F32))
    for n, buffer in enumerate(buffers[:READY]):
        await_all(buffer, sems.at[n])


def join_kernel(after, *refs):
    pieces = [r[...].astype(F32) for r in refs[:-1]]
    refs[-1][...] = jnp.concatenate(pieces, axis=0).astype(BF16)


def hidden_kernel(sizes, own, mine, other, *refs):
    exp_count, groups = sizes
    z, g, s = place(sizes)
    refs = list(refs)
    refs = refs[BUFFERS:]
    up, down, mask, hidden = [refs.pop(0) for _ in range(4)]
    buffers = [refs.pop(0) for _ in range(BUFFERS)]
    gate_sum, up_sum, rows, sems = refs
    half = own.shape[1] // 2
    features, unit_width = up.shape
    columns = unit_width // BLOCK
    pieces = features // (K_BLOCKS * BLOCK)
    count = len(buffers)

    def fetch(piece):
        buffer, sem = buffers[piece % count], sems.at[piece % count]
        if piece < 2 * pieces:
            fetch_rows(up, piece - pieces, buffer, sem)
        elif piece < 2 * pieces + groups:
            fetch_columns(sizes, down, piece - 2 * pieces + 1, False, buffer, sem)

    for piece in range(READY, count):
        fetch(piece)
    for source, side in ((mine, s), (other, 1 - s)):
        cols = pl.ds(pl.multiple_of(side * half, 128), half)
        joined = [own[:, cols].astype(F32), source[...].astype(F32)]
        rows[:, cols] = jnp.concatenate(joined, axis=0).astype(BF16)
    for piece in range(2 * pieces):
        buffer = buffers[piece % count]
        if piece >= READY:
            await_all(buffer, sems.at[piece % count])
        step = piece % pieces
        total = gate_sum if piece < pieces else up_sum
        left = rows[:, step * K_BLOCKS * BLOCK : (step + 1) * K_BLOCKS * BLOCK]
        for column in range(columns):
            cols = slice(column * BLOCK, (column + 1) * BLOCK)
            value = jnp.dot(left, stacked(buffer, column, K_BLOCKS), preferred_element_type=F32)
            if step > 0:
                value = total[:, cols] + value
            if piece < 2 * pieces - 1:
                total[:, cols] = value
                continue
            value = jnp.maximum(gate_sum[:, cols], 0.0) * jnp.maximum(value, 0.0)
            parts = []
            for d in range(exp_count):
                parts.append(value[d * CAP : (d + 1) * CAP, :] * mask[d : d + 1, cols])
            hidden[:, cols] = jnp.concatenate(parts, axis=0).astype(BF16)
        fetch(piece + count)
    for piece in range(2 * pieces, 2 * pieces + groups):
        await_all(buffers[piece % count], sems.at[piece % count])


def give_kernel(sizes, offset, hidden, weights, down, given, kept_weights, sem):
    fetch_columns(sizes, down, offset, True, kept_weights, sem)
    lines = down.shape[0] // BLOCK
    for column in range(given.shape[1] // BLOCK):
        value = jnp.dot(hidden[...], stacked(weights, column, lines), preferred_element_type=F32)
        given[:, column * BLOCK : (column + 1) * BLOCK] = value.astype(BF16)
    await_all(kept_weights, sem)


def keep_kernel(sizes, hidden, weights, received, *outs):
    exp_count, groups = sizes
    lines = hidden.shape[1] // BLOCK
    for column in range(received.shape[1] // BLOCK):
        cols = slice(column * BLOCK, (column + 1) * BLOCK)
        value = jnp.dot(hidden[...], stacked(weights, column, lines), preferred_element_type=F32)
        value = value + received[:, cols].astype(F32)
        for d in range(exp_count):
            outs[d][:, cols] = value[d * CAP : (d + 1) * CAP, :].astype(BF16)


def combine_kernel(order, high, low, *refs):
    refs = list(refs)
    out = refs.pop()
    before = refs.pop(0) if order > 0 else None
    found = jnp.concatenate([r[...].astype(F32) for r in refs], axis=0).astype(BF16)
    count = found.shape[0]
    value = jnp.dot(high[order, :, :count], found, preferred_element_type=F32)
    value = value + jnp.dot(low[order, :, :count], found, preferred_element_type=F32)
    if before is not None:
        value = before[...] + value
    out[...] = value.astype(out.dtype)


def call(kernel, outs, ins, scratch=(), flops=0, moved=0, aliases=None):
    vmem = pl.BlockSpec(memory_space=pltpu.VMEM)
    arrays, specs = [], []
    for array, space in ins:
        if space in (pltpu.HBM, pltpu.VMEM):
            array = pltpu.with_memory_space_constraint(array, space)
        arrays.append(array)
        specs.append(vmem if space is None else pl.BlockSpec(memory_space=space))
    shapes = []
    for shape, kind, *space in outs:
        shapes.append(space[0](shape, kind) if space else jax.ShapeDtypeStruct(shape, kind))
    return pl.pallas_call(
        kernel,
        out_shape=shapes,
        in_specs=specs,
        out_specs=[vmem] * len(outs),
        scratch_shapes=list(scratch),
        input_output_aliases=aliases or {},
        compiler_params=pltpu.CompilerParams(vmem_limit_bytes=LIMIT << 20),
        cost_estimate=pl.CostEstimate(flops=flops, bytes_accessed=moved, transcendentals=0),
    )(*arrays)


def paired_experts(
    tokens, norm_gain, route_ids, route_weight, active_blocks, gate_weight, up_weight, down_weight
):
    exp_count, unit_count = lax.axis_size("exp"), lax.axis_size("unit")
    groups = unit_count // 2
    sizes = (exp_count, groups)
    tok_count, features = tokens.shape
    unit_width = gate_weight.shape[1]
    slots = exp_count * CAP
    half = features // 2
    width = half
    ids = route_ids.T
    weights = route_weight.T

    def shift(value, distance, group_shift=0):
        pairs = []
        for z in range(exp_count):
            for u in range(unit_count):
                target = (z + distance) % exp_count
                group = (u // 2 + group_shift) % groups
                pairs.append((z * unit_count + u, target * unit_count + group * 2 + u % 2))
        return lax.ppermute(value, ("exp", "unit"), pairs)

    def swap(value):
        return lax.ppermute(value, "unit", [(u, u ^ 1) for u in range(unit_count)])

    batch = exp_count - 1
    own, *sends = call(
        functools.partial(route_kernel, sizes, width),
        [((CAP, features), BF16)] + [((CAP, width), BF16)] * batch,
        [
            (tokens, pltpu.HBM),
            (norm_gain.reshape(1, -1), pltpu.HBM),
            (ids, pltpu.HBM),
        ],
        [
            pltpu.VMEM((tok_count, features), BF16),
            pltpu.VMEM((tok_count, features), BF16),
            pltpu.VMEM((1, features), F32),
            pltpu.VMEM(ids.shape, jnp.int32),
            pltpu.SemaphoreType.DMA((3,)),
        ],
        flops=2 * tok_count * slots * width,
        moved=4 * tok_count * features,
    )
    blocks = K_BLOCKS * unit_width // BLOCK
    buffer = ((blocks, BLOCK, BLOCK), BF16, pltpu.VMEM)
    piece_bytes = 2 * blocks * BLOCK * BLOCK
    mask, *ready = call(
        functools.partial(prepare_kernel, sizes, tok_count),
        [((max(8, exp_count), unit_width), F32)] + [buffer] * BUFFERS,
        [(active_blocks, pltpu.HBM), (gate_weight, pltpu.HBM), (own, pl.ANY)],
        [
            pltpu.SMEM(active_blocks.shape, jnp.int32),
            pltpu.SemaphoreType.DMA,
            pltpu.SemaphoreType.DMA((READY,)),
        ],
        flops=2 * tok_count * slots * features,
        moved=READY * piece_bytes,
    )
    arrived = [shift(value, d + 1) for d, value in enumerate(sends)]
    mine = call(
        join_kernel,
        [((batch * CAP, width), BF16)],
        [(mask, pl.ANY)] + [(v, None) for v in arrived],
        moved=1 << 20,
    )[0]
    other = swap(mine)
    padded = -(-slots // 128) * 128
    combine_high, combine_low = call(
        functools.partial(table_kernel, sizes),
        [((groups, tok_count, padded), BF16)] * 2,
        [(ids, pltpu.HBM), (weights, pltpu.HBM), (mine, pl.ANY)],
        [
            pltpu.VMEM(ids.shape, jnp.int32),
            pltpu.VMEM(weights.shape, F32),
            pltpu.SemaphoreType.DMA((2,)),
        ],
        moved=1 << 21,
    )
    acc = pltpu.VMEM((slots, unit_width), F32)
    hidden, *buffers = call(
        functools.partial(hidden_kernel, sizes),
        [((slots, unit_width), BF16)] + [buffer] * BUFFERS,
        [(own, None), (mine, None), (other, None)]
        + [(v, pltpu.VMEM) for v in ready]
        + [(up_weight, pltpu.HBM), (down_weight, pltpu.HBM), (mask, None)],
        [
            acc,
            acc,
            pltpu.VMEM((slots, features), BF16),
            pltpu.SemaphoreType.DMA((BUFFERS,)),
        ],
        flops=2 * 2 * slots * features * unit_width,
        moved=6 * piece_bytes,
        aliases={3 + n: 1 + n for n in range(BUFFERS)},
    )
    first = 2 * features // (K_BLOCKS * BLOCK)
    part = features // unit_count
    offsets = [(order + 1) % groups for order in range(groups)]
    given, kept_weights = [], []
    for order, offset in enumerate(offsets):
        value, kept = call(
            functools.partial(give_kernel, sizes, offset),
            [((slots, part), BF16), buffer],
            [
                (hidden, None),
                (buffers[(first + order) % BUFFERS], pltpu.VMEM),
                (down_weight, pltpu.HBM),
            ],
            [pltpu.SemaphoreType.DMA],
            flops=2 * slots * unit_width * part,
            moved=piece_bytes,
        )
        given.append(value)
        kept_weights.append(kept)
    taken = [swap(value) for value in given]
    homes = []
    for order, offset in enumerate(offsets):
        kept = call(
            functools.partial(keep_kernel, sizes),
            [((CAP, part), BF16)] * exp_count,
            [(hidden, None), (kept_weights[order], pltpu.VMEM), (taken[order], None)],
            flops=2 * slots * unit_width * part,
            moved=piece_bytes,
        )
        homes.append(
            [shift(v, -d, offset) if d or offset else v for d, v in enumerate(kept)]
        )
    mixed = None
    for order, home in enumerate(homes):
        last = order == groups - 1
        mixed = call(
            functools.partial(combine_kernel, order),
            [((tok_count, part), BF16 if last else F32)],
            [(combine_high, None), (combine_low, None)]
            + ([(mixed, None)] if order else [])
            + [(v, None) for v in home],
            flops=4 * tok_count * slots * part,
            moved=1 << 20,
        )[0]
    return mixed


def per_device(*operands):
    tokens, gate_weight = operands[0], operands[5]
    exp_count, unit_count = lax.axis_size("exp"), lax.axis_size("unit")
    unit_width = gate_weight.shape[1]
    paired = (
        2 * unit_width == FF
        and unit_count % 2 == 0
        and exp_count * unit_count // 2 == EXPERTS
        and TILE % tokens.shape[0] == 0
        and unit_width % BLOCK == 0
        and tokens.shape[1] == READY * K_BLOCKS * BLOCK == unit_count * K_BLOCKS * BLOCK
    )
    return (paired_experts if paired else spread_experts)(*operands)


def solution(mesh):
    return jax.shard_map(
        per_device,
        mesh=mesh,
        in_specs=(
            P(("rep", "exp"), None),
            P(),
            P(("rep", "exp"), None),
            P(("rep", "exp"), None),
            P("rep", None, None),
            P(None, ("exp", "unit")),
            P(None, ("exp", "unit")),
            P(("exp", "unit"), None),
        ),
        out_specs=P(("rep", "exp"), "unit"),
        check_vma=False,
    )
```

```python
import functools

import jax
import jax.numpy as jnp
import numpy as np
from jax import lax
from jax.experimental import pallas as pl
from jax.experimental.pallas import tpu as pltpu
from jax.sharding import PartitionSpec as P

EXPERTS = 8
FF = 7168
BLK = 64
TILE = 256
CAP = 40

EPSILON = 1e-05

BLOCK = 512
READY = 10
BUFFERS = 12
LIMIT = 8

F32 = jnp.float32
BF16 = jnp.bfloat16


def normalize(tokens, norm_gain):
    values = tokens.astype(jnp.float32)
    inv_rms = lax.rsqrt(jnp.mean(values * values, axis=-1, keepdims=True) + EPSILON)
    return (values * inv_rms * norm_gain).astype(jnp.bfloat16)


def slot_numbers(entries, expert_count):
    onehot = (entries[..., None] == jnp.arange(expert_count, dtype=jnp.int32)).astype(jnp.int32)
    before = jnp.cumsum(onehot, axis=-2, dtype=jnp.int32) - onehot
    return jnp.sum(before * onehot, axis=-1)


def spread_experts(
    tokens, norm_gain, route_ids, route_weight, active_blocks, gate_weight, up_weight, down_weight
):
    exp_count = lax.axis_size("exp")
    unit_count = lax.axis_size("unit")
    tok_count, feature_width = tokens.shape
    unit_width = gate_weight.shape[1]
    row_units = unit_count * unit_width
    per_exp = max(1, row_units // FF)
    part_width = feature_width // unit_count
    block_count = unit_width // BLK
    tile_count = active_blocks.shape[0]
    exp_index = lax.axis_index("exp")
    unit_index = lax.axis_index("unit")
    first_unit = (exp_index * unit_count + unit_index) * unit_width
    own_expert = first_unit // FF
    first_block = first_unit % FF // BLK
    local_expert = own_expert - exp_index * row_units // FF
    normed = normalize(tokens, norm_gain)
    slot_index = slot_numbers(route_ids.reshape(1, -1), EXPERTS).reshape(tok_count, 2)
    positions = jnp.arange(tok_count, dtype=jnp.int32)
    tile_of = (exp_index * tok_count + positions) // TILE
    route_slot = (route_ids * CAP + slot_index).reshape(-1)
    token_source = (
        jnp.full((EXPERTS * CAP,), tok_count, jnp.int32)
        .at[route_slot]
        .set(jnp.repeat(positions, 2))
    )
    row_experts = np.arange(exp_count)[:, None] * row_units // FF + np.arange(per_exp)[None, :]
    slot_source = token_source.reshape(EXPERTS, CAP)[row_experts]
    padded_tiles = jnp.concatenate([tile_of, jnp.zeros((1,), jnp.int32)])
    slot_tiles = padded_tiles[slot_source]
    active_mine = lax.dynamic_index_in_dim(active_blocks, own_expert, 1, keepdims=False)
    local_blocks = first_block + jnp.arange(block_count, dtype=jnp.int32)
    block_on = jnp.any(active_mine[:, :, None] == local_blocks[None, None, :], axis=1).astype(
        jnp.float32
    )
    row_part = lax.dynamic_slice_in_dim(normed, unit_index * part_width, part_width, 1)
    padded_rows = jnp.concatenate([row_part, jnp.zeros((1, part_width), jnp.bfloat16)], 0)
    whole_rows = lax.all_gather(
        lax.all_to_all(padded_rows[slot_source], "exp", split_axis=0, concat_axis=0, tiled=True),
        "unit",
        axis=3,
        tiled=True,
    )
    slot_count = whole_rows.shape[2]
    own_rows = lax.dynamic_index_in_dim(whole_rows, local_expert, 1, keepdims=False).reshape(
        -1, feature_width
    )
    own_tiles = lax.dynamic_index_in_dim(
        lax.all_to_all(slot_tiles, "exp", split_axis=0, concat_axis=0, tiled=True),
        local_expert,
        1,
        keepdims=False,
    ).reshape(-1)
    tile_hot = (own_tiles[:, None] == jnp.arange(tile_count, dtype=jnp.int32)[None, :]).astype(
        jnp.float32
    )
    row_mask = jnp.dot(tile_hot, block_on, precision=lax.Precision.HIGHEST)
    gate_acts = jnp.dot(own_rows, gate_weight, preferred_element_type=jnp.float32)
    up_acts = jnp.dot(own_rows, up_weight, preferred_element_type=jnp.float32)
    hidden = jax.nn.relu(gate_acts) * jax.nn.relu(up_acts)
    hidden = (hidden.reshape(-1, block_count, BLK) * row_mask[:, :, None]).reshape(-1, unit_width)
    hidden = hidden.astype(jnp.bfloat16)
    partial_value = jnp.dot(hidden, down_weight, preferred_element_type=jnp.float32)
    partial_value = partial_value.reshape(exp_count, slot_count, feature_width)
    result = jnp.zeros((exp_count, per_exp, slot_count, feature_width), jnp.float32)
    partial_all = lax.dynamic_update_index_in_dim(result, partial_value, local_expert, 1)

    def by_expert(returned):
        last_width = returned.shape[-1]
        if per_exp == 1:
            grouped = returned.reshape(EXPERTS, exp_count // EXPERTS, CAP, last_width)
            return jnp.sum(grouped, axis=1, dtype=jnp.float32)
        return returned.reshape(EXPERTS, CAP, last_width).astype(jnp.float32)

    summed = lax.psum_scatter(
        partial_all.astype(jnp.bfloat16), "unit", scatter_dimension=3, tiled=True
    ).astype(jnp.float32)
    returned = lax.all_to_all(
        summed.astype(jnp.bfloat16), "exp", split_axis=0, concat_axis=0, tiled=True
    ).astype(summed.dtype)
    per_expert = by_expert(returned)
    last_width = per_expert.shape[-1]
    picked = per_expert.reshape(EXPERTS * CAP, last_width)[route_slot].reshape(
        tok_count, 2, last_width
    )
    mixed = jnp.sum(route_weight[:, :, None] * picked, axis=1)
    return mixed.astype(jnp.bfloat16)


def place(sizes):
    exp_count, groups = sizes
    return lax.axis_index("exp"), lax.axis_index("unit") // 2, lax.axis_index("unit") % 2


def pick_rows(named, before, d):
    rows = named.shape[1]
    place_of = jnp.where(named[d : d + 1, :] > 0, before[d : d + 1, :], -1)
    return (place_of == lax.broadcasted_iota(jnp.int32, (CAP, rows), 0)).astype(F32)


def count_earlier(ids, experts):
    rows = ids.shape[1]
    earlier = (
        lax.broadcasted_iota(jnp.int32, (rows, rows), 0)
        < lax.broadcasted_iota(jnp.int32, (rows, rows), 1)
    ).astype(BF16)
    named = ((ids[0:1, :] == experts) | (ids[1:2, :] == experts)).astype(jnp.int32)
    before = jnp.dot(named.astype(BF16), earlier, preferred_element_type=F32)
    return named, before.astype(jnp.int32)


def group_experts(exp_count, groups, z, g, rows):
    distance = lax.broadcasted_iota(jnp.int32, (max(8, exp_count), rows), 0)
    return lax.rem(z + distance, exp_count) * groups + g


def route_kernel(sizes, width, tokens_hbm, gain_hbm, ids_hbm, own, *rest):
    exp_count, groups = sizes
    sends, (tokens, normed, gain, ids, sems) = rest[:-5], rest[-5:]
    pairs = ((tokens_hbm, tokens), (gain_hbm, gain), (ids_hbm, ids))
    copies = [pltpu.make_async_copy(a, b, sems.at[n]) for n, (a, b) in enumerate(pairs)]
    for copy in copies:
        copy.start()
    rows, features = tokens.shape
    z, g, s = place(sizes)
    for copy in copies:
        copy.wait()
    step = 16
    for first in range(0, rows, step):
        values = tokens[first : first + step, :].astype(F32)
        mean = jnp.sum(values * values, axis=1, keepdims=True) * (1.0 / features)
        inv_rms = lax.rsqrt(mean + EPSILON)
        normed[first : first + step, :] = (values * inv_rms * gain[...]).astype(BF16)
    named, before = count_earlier(ids, group_experts(exp_count, groups, z, g, rows))
    picks = [pick_rows(named, before, d) for d in range(exp_count)]
    others = jnp.concatenate(picks[1:], axis=0).astype(BF16)
    start = pl.multiple_of(s * (features // 2), 128)
    found = jnp.dot(others, normed[:, pl.ds(start, width)], preferred_element_type=F32)
    for d, send in enumerate(sends):
        send[...] = found[d * CAP : (d + 1) * CAP, :].astype(BF16)
    own[...] = jnp.dot(
        picks[0].astype(BF16), normed[...], preferred_element_type=F32
    ).astype(BF16)


def fetch_rows(weight, line, buffer, sem):
    def start(index, carry):
        pltpu.make_async_copy(
            weight.at[
                pl.ds(line * BLOCK, BLOCK), pl.ds(pl.multiple_of(index * BLOCK, BLOCK), BLOCK)
            ],
            buffer.at[index],
            sem,
        ).start()
        return carry

    lax.fori_loop(0, buffer.shape[0], start, 0)


def fetch_columns(sizes, down, offset, keep, step, buffer, sem):
    exp_count, groups = sizes
    z, g, s = place(sizes)
    side = s if keep else 1 - s
    part = down.shape[1] // (2 * groups)
    column = (lax.rem(g + offset, groups) * 2 + side) * part + step * BLOCK

    def start(index, carry):
        pltpu.make_async_copy(
            down.at[
                pl.ds(pl.multiple_of(index * BLOCK, BLOCK), BLOCK),
                pl.ds(pl.multiple_of(column, BLOCK), BLOCK),
            ],
            buffer.at[index],
            sem,
        ).start()
        return carry

    lax.fori_loop(0, buffer.shape[0], start, 0)


def await_all(buffer, sem):
    pltpu.make_async_copy(buffer, buffer, sem).wait()


def stacked(buffer):
    return buffer[...].reshape(buffer.shape[0] * BLOCK, BLOCK)


def table_kernel(sizes, ids_hbm, weights_hbm, after, combine_high, combine_low, ids, weights, sems):
    exp_count, groups = sizes
    pairs = ((ids_hbm, ids), (weights_hbm, weights))
    copies = [pltpu.make_async_copy(a, b, sems.at[n]) for n, (a, b) in enumerate(pairs)]
    for copy in copies:
        copy.start()
    for copy in copies:
        copy.wait()
    rows = ids.shape[1]
    z, g, s = place(sizes)
    zero = jnp.zeros((CAP, rows), F32)
    padded = combine_high.shape[2]
    for order in range(groups):
        group = lax.rem(g - (order + 1) % groups + groups, groups)
        named, before = count_earlier(ids, group_experts(exp_count, groups, z, group, rows))
        parts = []
        for d in range(exp_count):
            here = pick_rows(named, before, d) > 0
            expert = lax.rem(z + d, exp_count) * groups + group
            first = jnp.where(here & (ids[0:1, :] == expert), weights[0:1, :], zero)
            second = jnp.where(here & (ids[1:2, :] == expert), weights[1:2, :], zero)
            parts.append(first + second)
        if padded > exp_count * CAP:
            parts.append(jnp.zeros((padded - exp_count * CAP, rows), F32))
        table = jnp.concatenate(parts, axis=0).T
        high = table.astype(BF16)
        combine_high[order] = high
        combine_low[order] = (table - high.astype(F32)).astype(BF16)


def prepare_kernel(sizes, rows, active_hbm, gate, up, after, mask, *rest):
    exp_count, groups = sizes
    *buffers, active, small_sem, sems = rest
    z, g, s = place(sizes)
    small = pltpu.make_async_copy(active_hbm, active, small_sem)
    small.start()
    lines = gate.shape[0] // BLOCK
    for n, buffer in enumerate(buffers[:READY]):
        fetch_rows(gate if n < lines else up, n % lines, buffer, sems.at[n])
    small.wait()
    unit_width = mask.shape[1]
    blocks = lax.broadcasted_iota(jnp.int32, mask.shape, 1) // BLK + s * (unit_width // BLK)
    source = lax.broadcasted_iota(jnp.int32, (mask.shape[0], 1), 0)
    own_expert = z * groups + g

    def add_entry(k, found):
        entry = jnp.full((mask.shape[0], 1), -1, jnp.int32)
        for d in range(exp_count):
            tile = lax.rem(z - d + exp_count, exp_count) * rows // TILE
            entry = jnp.where(source == d, active[tile, own_expert, k], entry)
        return jnp.where(blocks == entry, 1.0, found)

    mask[...] = lax.fori_loop(0, active.shape[2], add_entry, jnp.zeros(mask.shape, F32))
    for n, buffer in enumerate(buffers[:READY]):
        await_all(buffer, sems.at[n])


def join_kernel(after, *refs):
    pieces = [r[...].astype(F32) for r in refs[:-1]]
    refs[-1][...] = jnp.concatenate(pieces, axis=0).astype(BF16)


def hidden_kernel(sizes, own, mine, other, *refs):
    exp_count, groups = sizes
    z, g, s = place(sizes)
    refs = list(refs)
    refs = refs[BUFFERS:]
    up, down, mask, hidden = [refs.pop(0) for _ in range(4)]
    buffers = [refs.pop(0) for _ in range(BUFFERS)]
    gate_sum, up_sum, rows, sems = refs
    half = own.shape[1] // 2
    features, unit_width = up.shape
    columns, lines = unit_width // BLOCK, features // BLOCK
    given = features // (2 * groups) // BLOCK
    count = len(buffers)

    def fetch(index):
        buffer, sem = buffers[index % count], sems.at[index % count]
        if index < 2 * lines:
            fetch_rows(up, index - lines, buffer, sem)
        elif index < 2 * lines + groups * given:
            order, step = divmod(index - 2 * lines, given)
            fetch_columns(sizes, down, order + 1, False, step, buffer, sem)

    for index in range(READY, count):
        fetch(index)
    for source, side in ((mine, s), (other, 1 - s)):
        cols = pl.ds(pl.multiple_of(side * half, 128), half)
        joined = [own[:, cols].astype(F32), source[...].astype(F32)]
        rows[:, cols] = jnp.concatenate(joined, axis=0).astype(BF16)
    for index in range(0, 2 * lines, 2):
        pair = [buffers[(index + n) % count] for n in range(2)]
        for n in range(2):
            if index + n >= READY:
                await_all(pair[n], sems.at[(index + n) % count])
        line = index % lines
        total = gate_sum if index < lines else up_sum
        left = [rows[:, (line + n) * BLOCK : (line + n + 1) * BLOCK] for n in range(2)]
        for column in range(columns):
            cols = slice(column * BLOCK, (column + 1) * BLOCK)
            value = jnp.dot(left[0], pair[0][column], preferred_element_type=F32)
            value = value + jnp.dot(left[1], pair[1][column], preferred_element_type=F32)
            if line > 0:
                value = total[:, cols] + value
            if index < 2 * lines - 2:
                total[:, cols] = value
                continue
            value = jnp.maximum(gate_sum[:, cols], 0.0) * jnp.maximum(value, 0.0)
            parts = []
            for d in range(exp_count):
                parts.append(value[d * CAP : (d + 1) * CAP, :] * mask[d : d + 1, cols])
            hidden[:, cols] = jnp.concatenate(parts, axis=0).astype(BF16)
        for n in range(2):
            fetch(index + n + count)
    for index in range(2 * lines, 2 * lines + groups * given):
        await_all(buffers[index % count], sems.at[index % count])


def give_kernel(sizes, offset, hidden, *refs):
    exp_count, groups = sizes
    steps = (len(refs) - 3) // 2
    weights, (down, given), kept_weights, sems = (
        refs[:steps],
        refs[steps : steps + 2],
        refs[steps + 2 : -1],
        refs[-1],
    )
    for step, buffer in enumerate(kept_weights):
        fetch_columns(sizes, down, offset, True, step, buffer, sems.at[step])
    for step, buffer in enumerate(weights):
        value = jnp.dot(hidden[...], stacked(buffer), preferred_element_type=F32)
        given[:, step * BLOCK : (step + 1) * BLOCK] = value.astype(BF16)
    for step, buffer in enumerate(kept_weights):
        await_all(buffer, sems.at[step])


def keep_kernel(sizes, hidden, received, *refs):
    exp_count, groups = sizes
    weights, outs = refs[:-exp_count], refs[-exp_count:]
    for step, buffer in enumerate(weights):
        cols = slice(step * BLOCK, (step + 1) * BLOCK)
        value = jnp.dot(hidden[...], stacked(buffer), preferred_element_type=F32)
        value = value + received[:, cols].astype(F32)
        for d in range(exp_count):
            outs[d][:, cols] = value[d * CAP : (d + 1) * CAP, :].astype(BF16)


def combine_kernel(order, high, low, *refs):
    refs = list(refs)
    out = refs.pop()
    before = refs.pop(0) if order > 0 else None
    found = jnp.concatenate([r[...].astype(F32) for r in refs], axis=0).astype(BF16)
    count = found.shape[0]
    value = jnp.dot(high[order, :, :count], found, preferred_element_type=F32)
    value = value + jnp.dot(low[order, :, :count], found, preferred_element_type=F32)
    if before is not None:
        value = before[...] + value
    out[...] = value.astype(out.dtype)


def call(kernel, outs, ins, scratch=(), flops=0, moved=0, aliases=None):
    vmem = pl.BlockSpec(memory_space=pltpu.VMEM)
    arrays, specs = [], []
    for array, space in ins:
        if space in (pltpu.HBM, pltpu.VMEM):
            array = pltpu.with_memory_space_constraint(array, space)
        arrays.append(array)
        specs.append(vmem if space is None else pl.BlockSpec(memory_space=space))
    shapes = []
    for shape, kind, *space in outs:
        shapes.append(space[0](shape, kind) if space else jax.ShapeDtypeStruct(shape, kind))
    return pl.pallas_call(
        kernel,
        out_shape=shapes,
        in_specs=specs,
        out_specs=[vmem] * len(outs),
        scratch_shapes=list(scratch),
        input_output_aliases=aliases or {},
        compiler_params=pltpu.CompilerParams(vmem_limit_bytes=LIMIT << 20),
        cost_estimate=pl.CostEstimate(flops=flops, bytes_accessed=moved, transcendentals=0),
    )(*arrays)


def paired_experts(
    tokens, norm_gain, route_ids, route_weight, active_blocks, gate_weight, up_weight, down_weight
):
    exp_count, unit_count = lax.axis_size("exp"), lax.axis_size("unit")
    groups = unit_count // 2
    sizes = (exp_count, groups)
    tok_count, features = tokens.shape
    unit_width = gate_weight.shape[1]
    slots = exp_count * CAP
    half = features // 2
    width = half
    ids = route_ids.T
    weights = route_weight.T

    def shift(value, distance, group_shift=0):
        pairs = []
        for z in range(exp_count):
            for u in range(unit_count):
                target = (z + distance) % exp_count
                group = (u // 2 + group_shift) % groups
                pairs.append((z * unit_count + u, target * unit_count + group * 2 + u % 2))
        return lax.ppermute(value, ("exp", "unit"), pairs)

    def swap(value):
        return lax.ppermute(value, "unit", [(u, u ^ 1) for u in range(unit_count)])

    batch = exp_count - 1
    own, *sends = call(
        functools.partial(route_kernel, sizes, width),
        [((CAP, features), BF16)] + [((CAP, width), BF16)] * batch,
        [
            (tokens, pltpu.HBM),
            (norm_gain.reshape(1, -1), pltpu.HBM),
            (ids, pltpu.HBM),
        ],
        [
            pltpu.VMEM((tok_count, features), BF16),
            pltpu.VMEM((tok_count, features), BF16),
            pltpu.VMEM((1, features), F32),
            pltpu.VMEM(ids.shape, jnp.int32),
            pltpu.SemaphoreType.DMA((3,)),
        ],
        flops=2 * tok_count * slots * width,
        moved=4 * tok_count * features,
    )
    blocks = unit_width // BLOCK
    buffer = ((blocks, BLOCK, BLOCK), BF16, pltpu.VMEM)
    piece_bytes = 2 * blocks * BLOCK * BLOCK
    mask, *ready = call(
        functools.partial(prepare_kernel, sizes, tok_count),
        [((max(8, exp_count), unit_width), F32)] + [buffer] * BUFFERS,
        [
            (active_blocks, pltpu.HBM),
            (gate_weight, pltpu.HBM),
            (up_weight, pltpu.HBM),
            (own, pl.ANY),
        ],
        [
            pltpu.SMEM(active_blocks.shape, jnp.int32),
            pltpu.SemaphoreType.DMA,
            pltpu.SemaphoreType.DMA((READY,)),
        ],
        flops=2 * tok_count * slots * features,
        moved=READY * piece_bytes,
    )
    arrived = [shift(value, d + 1) for d, value in enumerate(sends)]
    mine = call(
        join_kernel,
        [((batch * CAP, width), BF16)],
        [(mask, pl.ANY)] + [(v, None) for v in arrived],
        moved=1 << 20,
    )[0]
    other = swap(mine)
    padded = -(-slots // 128) * 128
    combine_high, combine_low = call(
        functools.partial(table_kernel, sizes),
        [((groups, tok_count, padded), BF16)] * 2,
        [(ids, pltpu.HBM), (weights, pltpu.HBM), (mine, pl.ANY)],
        [
            pltpu.VMEM(ids.shape, jnp.int32),
            pltpu.VMEM(weights.shape, F32),
            pltpu.SemaphoreType.DMA((2,)),
        ],
        moved=1 << 21,
    )
    acc = pltpu.VMEM((slots, unit_width), F32)
    hidden, *buffers = call(
        functools.partial(hidden_kernel, sizes),
        [((slots, unit_width), BF16)] + [buffer] * BUFFERS,
        [(own, None), (mine, None), (other, None)]
        + [(v, pltpu.VMEM) for v in ready]
        + [(up_weight, pltpu.HBM), (down_weight, pltpu.HBM), (mask, None)],
        [
            acc,
            acc,
            pltpu.VMEM((slots, features), BF16),
            pltpu.SemaphoreType.DMA((BUFFERS,)),
        ],
        flops=2 * 2 * slots * features * unit_width,
        moved=10 * piece_bytes,
        aliases={3 + n: 1 + n for n in range(BUFFERS)},
    )
    part = features // unit_count
    steps = part // BLOCK
    offsets = [(order + 1) % groups for order in range(groups)]
    given, kept_weights = [], []
    for order, offset in enumerate(offsets):
        first = 2 * features // BLOCK + order * steps
        value, *kept = call(
            functools.partial(give_kernel, sizes, offset),
            [((slots, part), BF16)] + [buffer] * steps,
            [(hidden, None)]
            + [(buffers[(first + step) % BUFFERS], pltpu.VMEM) for step in range(steps)]
            + [(down_weight, pltpu.HBM)],
            [pltpu.SemaphoreType.DMA((steps,))],
            flops=2 * slots * unit_width * part,
            moved=steps * piece_bytes,
        )
        given.append(value)
        kept_weights.append(kept)
    taken = [swap(value) for value in given]
    homes = []
    for order, offset in enumerate(offsets):
        kept = call(
            functools.partial(keep_kernel, sizes),
            [((CAP, part), BF16)] * exp_count,
            [(hidden, None), (taken[order], None)]
            + [(v, pltpu.VMEM) for v in kept_weights[order]],
            flops=2 * slots * unit_width * part,
            moved=piece_bytes,
        )
        homes.append(
            [shift(v, -d, offset) if d or offset else v for d, v in enumerate(kept)]
        )
    mixed = None
    for order, home in enumerate(homes):
        last = order == groups - 1
        mixed = call(
            functools.partial(combine_kernel, order),
            [((tok_count, part), BF16 if last else F32)],
            [(combine_high, None), (combine_low, None)]
            + ([(mixed, None)] if order else [])
            + [(v, None) for v in home],
            flops=4 * tok_count * slots * part,
            moved=1 << 20,
        )[0]
    return mixed


def per_device(*operands):
    tokens, gate_weight = operands[0], operands[5]
    exp_count, unit_count = lax.axis_size("exp"), lax.axis_size("unit")
    unit_width = gate_weight.shape[1]
    paired = (
        2 * unit_width == FF
        and unit_count % 2 == 0
        and exp_count * unit_count // 2 == EXPERTS
        and TILE % tokens.shape[0] == 0
        and unit_width % BLOCK == 0
        and tokens.shape[1] % (unit_count * BLOCK) == 0
        and tokens.shape[1] <= READY * BLOCK <= 2 * tokens.shape[1]
    )
    return (paired_experts if paired else spread_experts)(*operands)


def solution(mesh):
    return jax.shard_map(
        per_device,
        mesh=mesh,
        in_specs=(
            P(("rep", "exp"), None),
            P(),
            P(("rep", "exp"), None),
            P(("rep", "exp"), None),
            P("rep", None, None),
            P(None, ("exp", "unit")),
            P(None, ("exp", "unit")),
            P(("exp", "unit"), None),
        ),
        out_specs=P(("rep", "exp"), "unit"),
        check_vma=False,
    )
```

```python
import functools

import jax
import jax.numpy as jnp
import numpy as np
from jax import lax
from jax.experimental import pallas as pl
from jax.experimental.pallas import tpu as pltpu
from jax.sharding import PartitionSpec as P

EXPERTS = 8
FF = 7168
BLK = 64
TILE = 256
CAP = 40

EPSILON = 1e-05

BLOCK = 512
READY = 11
BUFFERS = 12
LIMIT = 8

F32 = jnp.float32
BF16 = jnp.bfloat16


def normalize(tokens, norm_gain):
    values = tokens.astype(jnp.float32)
    inv_rms = lax.rsqrt(jnp.mean(values * values, axis=-1, keepdims=True) + EPSILON)
    return (values * inv_rms * norm_gain).astype(jnp.bfloat16)


def slot_numbers(entries, expert_count):
    onehot = (entries[..., None] == jnp.arange(expert_count, dtype=jnp.int32)).astype(jnp.int32)
    before = jnp.cumsum(onehot, axis=-2, dtype=jnp.int32) - onehot
    return jnp.sum(before * onehot, axis=-1)


def spread_experts(
    tokens, norm_gain, route_ids, route_weight, active_blocks, gate_weight, up_weight, down_weight
):
    exp_count = lax.axis_size("exp")
    unit_count = lax.axis_size("unit")
    tok_count, feature_width = tokens.shape
    unit_width = gate_weight.shape[1]
    row_units = unit_count * unit_width
    per_exp = max(1, row_units // FF)
    part_width = feature_width // unit_count
    block_count = unit_width // BLK
    tile_count = active_blocks.shape[0]
    exp_index = lax.axis_index("exp")
    unit_index = lax.axis_index("unit")
    first_unit = (exp_index * unit_count + unit_index) * unit_width
    own_expert = first_unit // FF
    first_block = first_unit % FF // BLK
    local_expert = own_expert - exp_index * row_units // FF
    normed = normalize(tokens, norm_gain)
    slot_index = slot_numbers(route_ids.reshape(1, -1), EXPERTS).reshape(tok_count, 2)
    positions = jnp.arange(tok_count, dtype=jnp.int32)
    tile_of = (exp_index * tok_count + positions) // TILE
    route_slot = (route_ids * CAP + slot_index).reshape(-1)
    token_source = (
        jnp.full((EXPERTS * CAP,), tok_count, jnp.int32)
        .at[route_slot]
        .set(jnp.repeat(positions, 2))
    )
    row_experts = np.arange(exp_count)[:, None] * row_units // FF + np.arange(per_exp)[None, :]
    slot_source = token_source.reshape(EXPERTS, CAP)[row_experts]
    padded_tiles = jnp.concatenate([tile_of, jnp.zeros((1,), jnp.int32)])
    slot_tiles = padded_tiles[slot_source]
    active_mine = lax.dynamic_index_in_dim(active_blocks, own_expert, 1, keepdims=False)
    local_blocks = first_block + jnp.arange(block_count, dtype=jnp.int32)
    block_on = jnp.any(active_mine[:, :, None] == local_blocks[None, None, :], axis=1).astype(
        jnp.float32
    )
    row_part = lax.dynamic_slice_in_dim(normed, unit_index * part_width, part_width, 1)
    padded_rows = jnp.concatenate([row_part, jnp.zeros((1, part_width), jnp.bfloat16)], 0)
    whole_rows = lax.all_gather(
        lax.all_to_all(padded_rows[slot_source], "exp", split_axis=0, concat_axis=0, tiled=True),
        "unit",
        axis=3,
        tiled=True,
    )
    slot_count = whole_rows.shape[2]
    own_rows = lax.dynamic_index_in_dim(whole_rows, local_expert, 1, keepdims=False).reshape(
        -1, feature_width
    )
    own_tiles = lax.dynamic_index_in_dim(
        lax.all_to_all(slot_tiles, "exp", split_axis=0, concat_axis=0, tiled=True),
        local_expert,
        1,
        keepdims=False,
    ).reshape(-1)
    tile_hot = (own_tiles[:, None] == jnp.arange(tile_count, dtype=jnp.int32)[None, :]).astype(
        jnp.float32
    )
    row_mask = jnp.dot(tile_hot, block_on, precision=lax.Precision.HIGHEST)
    gate_acts = jnp.dot(own_rows, gate_weight, preferred_element_type=jnp.float32)
    up_acts = jnp.dot(own_rows, up_weight, preferred_element_type=jnp.float32)
    hidden = jax.nn.relu(gate_acts) * jax.nn.relu(up_acts)
    hidden = (hidden.reshape(-1, block_count, BLK) * row_mask[:, :, None]).reshape(-1, unit_width)
    hidden = hidden.astype(jnp.bfloat16)
    partial_value = jnp.dot(hidden, down_weight, preferred_element_type=jnp.float32)
    partial_value = partial_value.reshape(exp_count, slot_count, feature_width)
    result = jnp.zeros((exp_count, per_exp, slot_count, feature_width), jnp.float32)
    partial_all = lax.dynamic_update_index_in_dim(result, partial_value, local_expert, 1)

    def by_expert(returned):
        last_width = returned.shape[-1]
        if per_exp == 1:
            grouped = returned.reshape(EXPERTS, exp_count // EXPERTS, CAP, last_width)
            return jnp.sum(grouped, axis=1, dtype=jnp.float32)
        return returned.reshape(EXPERTS, CAP, last_width).astype(jnp.float32)

    summed = lax.psum_scatter(
        partial_all.astype(jnp.bfloat16), "unit", scatter_dimension=3, tiled=True
    ).astype(jnp.float32)
    returned = lax.all_to_all(
        summed.astype(jnp.bfloat16), "exp", split_axis=0, concat_axis=0, tiled=True
    ).astype(summed.dtype)
    per_expert = by_expert(returned)
    last_width = per_expert.shape[-1]
    picked = per_expert.reshape(EXPERTS * CAP, last_width)[route_slot].reshape(
        tok_count, 2, last_width
    )
    mixed = jnp.sum(route_weight[:, :, None] * picked, axis=1)
    return mixed.astype(jnp.bfloat16)


def place(sizes):
    exp_count, groups = sizes
    return lax.axis_index("exp"), lax.axis_index("unit") // 2, lax.axis_index("unit") % 2


def pick_rows(named, before, d):
    rows = named.shape[1]
    place_of = jnp.where(named[d : d + 1, :] > 0, before[d : d + 1, :], -1)
    return (place_of == lax.broadcasted_iota(jnp.int32, (CAP, rows), 0)).astype(F32)


def count_earlier(ids, experts):
    rows = ids.shape[1]
    earlier = (
        lax.broadcasted_iota(jnp.int32, (rows, rows), 0)
        < lax.broadcasted_iota(jnp.int32, (rows, rows), 1)
    ).astype(BF16)
    named = ((ids[0:1, :] == experts) | (ids[1:2, :] == experts)).astype(jnp.int32)
    before = jnp.dot(named.astype(BF16), earlier, preferred_element_type=F32)
    return named, before.astype(jnp.int32)


def group_experts(exp_count, groups, z, g, rows):
    distance = lax.broadcasted_iota(jnp.int32, (max(8, exp_count), rows), 0)
    return lax.rem(z + distance, exp_count) * groups + g


def fetch_rows(weight, line, buffer, sem):
    def start(index, carry):
        pltpu.make_async_copy(
            weight.at[
                pl.ds(line * BLOCK, BLOCK), pl.ds(pl.multiple_of(index * BLOCK, BLOCK), BLOCK)
            ],
            buffer.at[index],
            sem,
        ).start()
        return carry

    lax.fori_loop(0, buffer.shape[0], start, 0)


def fetch_columns(sizes, down, offset, keep, step, buffer, sem):
    exp_count, groups = sizes
    z, g, s = place(sizes)
    side = s if keep else 1 - s
    part = down.shape[1] // (2 * groups)
    column = (lax.rem(g + offset, groups) * 2 + side) * part + step * BLOCK

    def start(index, carry):
        pltpu.make_async_copy(
            down.at[
                pl.ds(pl.multiple_of(index * BLOCK, BLOCK), BLOCK),
                pl.ds(pl.multiple_of(column, BLOCK), BLOCK),
            ],
            buffer.at[index],
            sem,
        ).start()
        return carry

    lax.fori_loop(0, buffer.shape[0], start, 0)


def await_all(buffer, sem):
    pltpu.make_async_copy(buffer, buffer, sem).wait()


def stacked(buffer):
    return buffer[...].reshape(buffer.shape[0] * BLOCK, BLOCK)


def route_kernel(sizes, width, tokens_hbm, gain_hbm, ids_hbm, gate, own, buffer, *rest):
    exp_count, groups = sizes
    sends, (tokens, normed, gain, ids, sems, gate_sem) = rest[:-6], rest[-6:]
    rows, features = tokens.shape
    count = 4
    lines = [pl.ds(n * (rows // count), rows // count) for n in range(count)]
    pairs = [(gain_hbm, gain), (ids_hbm, ids)]
    pairs += [(tokens_hbm.at[part, :], tokens.at[part, :]) for part in lines]
    copies = [pltpu.make_async_copy(a, b, sems.at[n]) for n, (a, b) in enumerate(pairs)]
    for copy in copies:
        copy.start()
    fetch_rows(gate, 0, buffer, gate_sem)
    z, g, s = place(sizes)
    copies[0].wait()
    copies[1].wait()
    named, before = count_earlier(ids, group_experts(exp_count, groups, z, g, rows))
    picks = [pick_rows(named, before, d) for d in range(exp_count)]
    others = jnp.concatenate(picks[1:], axis=0).astype(BF16)
    step = 16
    for first in range(0, rows, step):
        if first % (rows // count) == 0:
            copies[2 + first // (rows // count)].wait()
        values = tokens[first : first + step, :].astype(F32)
        mean = jnp.sum(values * values, axis=1, keepdims=True) * (1.0 / features)
        inv_rms = lax.rsqrt(mean + EPSILON)
        normed[first : first + step, :] = (values * inv_rms * gain[...]).astype(BF16)
    start = pl.multiple_of(s * (features // 2), 128)
    found = jnp.dot(others, normed[:, pl.ds(start, width)], preferred_element_type=F32)
    for d, send in enumerate(sends):
        send[...] = found[d * CAP : (d + 1) * CAP, :].astype(BF16)
    own[...] = jnp.dot(
        picks[0].astype(BF16), normed[...], preferred_element_type=F32
    ).astype(BF16)
    await_all(buffer, gate_sem)


def arrivals(sizes):
    exp_count, groups = sizes
    early = [(o, d) for o in range(1, groups) for d in range(1, exp_count)] + [(0, 0)]
    late = [(0, d) for d in range(1, exp_count)] + [(o, 0) for o in range(1, groups)]
    return early, late


def table_kernel(sizes, ids_hbm, weights_hbm, after, combine_high, combine_low, ids, weights, sems):
    exp_count, groups = sizes
    pairs = ((ids_hbm, ids), (weights_hbm, weights))
    copies = [pltpu.make_async_copy(a, b, sems.at[n]) for n, (a, b) in enumerate(pairs)]
    for copy in copies:
        copy.start()
    for copy in copies:
        copy.wait()
    rows = ids.shape[1]
    z, g, s = place(sizes)
    zero = jnp.zeros((CAP, rows), F32)
    padded = combine_high.shape[2]
    batches = arrivals(sizes)
    experts = [
        lax.rem(z + d, exp_count) * groups + lax.rem(g - o + groups, groups)
        for batch in batches
        for o, d in batch
    ]
    line = lax.broadcasted_iota(jnp.int32, (max(8, len(experts)), rows), 0)
    listed = jnp.full(line.shape, -1, jnp.int32)
    for n, expert in enumerate(experts):
        listed = jnp.where(line == n, expert, listed)
    named, before = count_earlier(ids, listed)
    for order, batch in enumerate(batches):
        parts = []
        for n in range(len(batch)):
            entry = order * len(batch) + n
            here = pick_rows(named, before, entry) > 0
            first = jnp.where(here & (ids[0:1, :] == experts[entry]), weights[0:1, :], zero)
            second = jnp.where(here & (ids[1:2, :] == experts[entry]), weights[1:2, :], zero)
            parts.append(first + second)
        if padded > len(batch) * CAP:
            parts.append(jnp.zeros((padded - len(batch) * CAP, rows), F32))
        table = jnp.concatenate(parts, axis=0).T
        high = table.astype(BF16)
        combine_high[order] = high
        combine_low[order] = (table - high.astype(F32)).astype(BF16)


def prepare_kernel(sizes, rows, active_hbm, gate, up, after, _, mask, *rest):
    exp_count, groups = sizes
    *buffers, active, small_sem, sems = rest
    z, g, s = place(sizes)
    small = pltpu.make_async_copy(active_hbm, active, small_sem)
    small.start()
    lines = gate.shape[0] // BLOCK
    for n, buffer in enumerate(buffers[1:READY], 1):
        fetch_rows(gate if n < lines else up, n % lines, buffer, sems.at[n])
    small.wait()
    unit_width = mask.shape[1]
    blocks = lax.broadcasted_iota(jnp.int32, mask.shape, 1) // BLK + s * (unit_width // BLK)
    source = lax.broadcasted_iota(jnp.int32, (mask.shape[0], 1), 0)
    own_expert = z * groups + g

    def add_entry(k, found):
        entry = jnp.full((mask.shape[0], 1), -1, jnp.int32)
        for d in range(exp_count):
            tile = lax.rem(z - d + exp_count, exp_count) * rows // TILE
            entry = jnp.where(source == d, active[tile, own_expert, k], entry)
        return jnp.where(blocks == entry, 1.0, found)

    mask[...] = lax.fori_loop(0, active.shape[2], add_entry, jnp.zeros(mask.shape, F32))
    for n, buffer in enumerate(buffers[1:READY], 1):
        await_all(buffer, sems.at[n])


def join_kernel(after, *refs):
    pieces = [r[...].astype(F32) for r in refs[:-1]]
    refs[-1][...] = jnp.concatenate(pieces, axis=0).astype(BF16)


def hidden_kernel(sizes, own, mine, other, *refs):
    exp_count, groups = sizes
    z, g, s = place(sizes)
    refs = list(refs)
    refs = refs[BUFFERS:]
    up, down, mask, hidden = [refs.pop(0) for _ in range(4)]
    buffers = [refs.pop(0) for _ in range(BUFFERS)]
    gate_sum, up_sum, rows, sems = refs
    half = own.shape[1] // 2
    features, unit_width = up.shape
    columns, lines = unit_width // BLOCK, features // BLOCK
    given = features // (2 * groups) // BLOCK
    count = len(buffers)

    def fetch(index):
        buffer, sem = buffers[index % count], sems.at[index % count]
        if index < 2 * lines:
            fetch_rows(up, index - lines, buffer, sem)
        elif index < 2 * lines + groups * given:
            order, step = divmod(index - 2 * lines, given)
            fetch_columns(sizes, down, order + 1, False, step, buffer, sem)

    for index in range(READY, count):
        fetch(index)
    for source, side in ((mine, s), (other, 1 - s)):
        cols = pl.ds(pl.multiple_of(side * half, 128), half)
        joined = [own[:, cols].astype(F32), source[...].astype(F32)]
        rows[:, cols] = jnp.concatenate(joined, axis=0).astype(BF16)
    for index in range(0, 2 * lines, 2):
        pair = [buffers[(index + n) % count] for n in range(2)]
        for n in range(2):
            if index + n >= READY:
                await_all(pair[n], sems.at[(index + n) % count])
        line = index % lines
        total = gate_sum if index < lines else up_sum
        left = [rows[:, (line + n) * BLOCK : (line + n + 1) * BLOCK] for n in range(2)]
        for column in range(columns):
            cols = slice(column * BLOCK, (column + 1) * BLOCK)
            value = jnp.dot(left[0], pair[0][column], preferred_element_type=F32)
            value = value + jnp.dot(left[1], pair[1][column], preferred_element_type=F32)
            if line > 0:
                value = total[:, cols] + value
            if index < 2 * lines - 2:
                total[:, cols] = value
                continue
            value = jnp.maximum(gate_sum[:, cols], 0.0) * jnp.maximum(value, 0.0)
            parts = []
            for d in range(exp_count):
                parts.append(value[d * CAP : (d + 1) * CAP, :] * mask[d : d + 1, cols])
            hidden[:, cols] = jnp.concatenate(parts, axis=0).astype(BF16)
        for n in range(2):
            fetch(index + n + count)
    for index in range(2 * lines, 2 * lines + groups * given):
        await_all(buffers[index % count], sems.at[index % count])


def give_kernel(sizes, offset, hidden, *refs):
    exp_count, groups = sizes
    steps = (len(refs) - 3) // 2
    weights, (down, given), kept_weights, sems = (
        refs[:steps],
        refs[steps : steps + 2],
        refs[steps + 2 : -1],
        refs[-1],
    )
    for step, buffer in enumerate(kept_weights):
        fetch_columns(sizes, down, offset, True, step, buffer, sems.at[step])
    for step, buffer in enumerate(weights):
        value = jnp.dot(hidden[...], stacked(buffer), preferred_element_type=F32)
        given[:, step * BLOCK : (step + 1) * BLOCK] = value.astype(BF16)
    for step, buffer in enumerate(kept_weights):
        await_all(buffer, sems.at[step])


def keep_kernel(sizes, hidden, received, *refs):
    exp_count, groups = sizes
    passed = (len(refs) - received.shape[1] // BLOCK - exp_count) // 2
    weights = refs[: received.shape[1] // BLOCK]
    handed = refs[len(weights) : len(weights) + passed]
    outs = refs[len(weights) + passed :]
    for step, buffer in enumerate(weights):
        cols = slice(step * BLOCK, (step + 1) * BLOCK)
        value = jnp.dot(hidden[...], stacked(buffer), preferred_element_type=F32)
        value = value + received[:, cols].astype(F32)
        for d in range(exp_count):
            outs[d][:, cols] = value[d * CAP : (d + 1) * CAP, :].astype(BF16)
    for given, out in zip(handed, outs[exp_count:]):
        out[...] = given[...]


def combine_kernel(order, high, low, *refs):
    refs = list(refs)
    out = refs.pop()
    before = refs.pop(0) if order > 0 else None
    found = jnp.concatenate([r[...].astype(F32) for r in refs], axis=0).astype(BF16)
    count = found.shape[0]
    value = jnp.dot(high[order, :, :count], found, preferred_element_type=F32)
    value = value + jnp.dot(low[order, :, :count], found, preferred_element_type=F32)
    if before is not None:
        value = before[...] + value
    out[...] = value.astype(out.dtype)


def call(kernel, outs, ins, scratch=(), flops=0, moved=0, aliases=None):
    vmem = pl.BlockSpec(memory_space=pltpu.VMEM)
    arrays, specs = [], []
    for array, space in ins:
        if space in (pltpu.HBM, pltpu.VMEM):
            array = pltpu.with_memory_space_constraint(array, space)
        arrays.append(array)
        specs.append(vmem if space is None else pl.BlockSpec(memory_space=space))
    shapes = []
    for shape, kind, *space in outs:
        shapes.append(space[0](shape, kind) if space else jax.ShapeDtypeStruct(shape, kind))
    return pl.pallas_call(
        kernel,
        out_shape=shapes,
        in_specs=specs,
        out_specs=[vmem] * len(outs),
        scratch_shapes=list(scratch),
        input_output_aliases=aliases or {},
        compiler_params=pltpu.CompilerParams(vmem_limit_bytes=LIMIT << 20),
        cost_estimate=pl.CostEstimate(flops=flops, bytes_accessed=moved, transcendentals=0),
    )(*arrays)


def paired_experts(
    tokens, norm_gain, route_ids, route_weight, active_blocks, gate_weight, up_weight, down_weight
):
    exp_count, unit_count = lax.axis_size("exp"), lax.axis_size("unit")
    groups = unit_count // 2
    sizes = (exp_count, groups)
    tok_count, features = tokens.shape
    unit_width = gate_weight.shape[1]
    slots = exp_count * CAP
    half = features // 2
    width = half
    ids = route_ids.T
    weights = route_weight.T

    def shift(value, distance, group_shift=0):
        pairs = []
        for z in range(exp_count):
            for u in range(unit_count):
                target = (z + distance) % exp_count
                group = (u // 2 + group_shift) % groups
                pairs.append((z * unit_count + u, target * unit_count + group * 2 + u % 2))
        return lax.ppermute(value, ("exp", "unit"), pairs)

    def swap(value):
        return lax.ppermute(value, "unit", [(u, u ^ 1) for u in range(unit_count)])

    batch = exp_count - 1
    buffer = ((unit_width // BLOCK, BLOCK, BLOCK), BF16, pltpu.VMEM)
    piece_bytes = 2 * unit_width * BLOCK
    own, ready, *sends = call(
        functools.partial(route_kernel, sizes, width),
        [((CAP, features), BF16), buffer] + [((CAP, width), BF16)] * batch,
        [
            (tokens, pltpu.HBM),
            (norm_gain.reshape(1, -1), pltpu.HBM),
            (ids, pltpu.HBM),
            (gate_weight, pltpu.HBM),
        ],
        [
            pltpu.VMEM((tok_count, features), BF16),
            pltpu.VMEM((tok_count, features), BF16),
            pltpu.VMEM((1, features), F32),
            pltpu.VMEM(ids.shape, jnp.int32),
            pltpu.SemaphoreType.DMA((6,)),
            pltpu.SemaphoreType.DMA,
        ],
        flops=2 * tok_count * slots * width,
        moved=4 * tok_count * features + piece_bytes,
    )
    mask, *ready = call(
        functools.partial(prepare_kernel, sizes, tok_count),
        [((max(8, exp_count), unit_width), F32)] + [buffer] * BUFFERS,
        [
            (active_blocks, pltpu.HBM),
            (gate_weight, pltpu.HBM),
            (up_weight, pltpu.HBM),
            (own, pl.ANY),
            (ready, pltpu.VMEM),
        ],
        [
            pltpu.SMEM(active_blocks.shape, jnp.int32),
            pltpu.SemaphoreType.DMA,
            pltpu.SemaphoreType.DMA((READY,)),
        ],
        flops=2 * tok_count * slots * features,
        moved=(READY - 1) * piece_bytes,
        aliases={4: 1},
    )
    arrived = [shift(value, d + 1) for d, value in enumerate(sends)]
    mine = call(
        join_kernel,
        [((batch * CAP, width), BF16)],
        [(mask, pl.ANY)] + [(v, None) for v in arrived],
        moved=1 << 20,
    )[0]
    other = swap(mine)
    padded = -(-slots // 128) * 128
    combine_high, combine_low = call(
        functools.partial(table_kernel, sizes),
        [((2, tok_count, padded), BF16)] * 2,
        [(ids, pltpu.HBM), (weights, pltpu.HBM), (mine, pl.ANY)],
        [
            pltpu.VMEM(ids.shape, jnp.int32),
            pltpu.VMEM(weights.shape, F32),
            pltpu.SemaphoreType.DMA((2,)),
        ],
        moved=1 << 21,
    )
    acc = pltpu.VMEM((slots, unit_width), F32)
    hidden, *buffers = call(
        functools.partial(hidden_kernel, sizes),
        [((slots, unit_width), BF16)] + [buffer] * BUFFERS,
        [(own, None), (mine, None), (other, None)]
        + [(v, pltpu.VMEM) for v in ready]
        + [(up_weight, pltpu.HBM), (down_weight, pltpu.HBM), (mask, None)],
        [
            acc,
            acc,
            pltpu.VMEM((slots, features), BF16),
            pltpu.SemaphoreType.DMA((BUFFERS,)),
        ],
        flops=2 * 2 * slots * features * unit_width,
        moved=10 * piece_bytes,
        aliases={3 + n: 1 + n for n in range(BUFFERS)},
    )
    part = features // unit_count
    steps = part // BLOCK
    offsets = [(order + 1) % groups for order in range(groups)]
    given, kept_weights = [], []
    for order, offset in enumerate(offsets):
        first = 2 * features // BLOCK + order * steps
        value, *kept = call(
            functools.partial(give_kernel, sizes, offset),
            [((slots, part), BF16)] + [buffer] * steps,
            [(hidden, None)]
            + [(buffers[(first + step) % BUFFERS], pltpu.VMEM) for step in range(steps)]
            + [(down_weight, pltpu.HBM)],
            [pltpu.SemaphoreType.DMA((steps,))],
            flops=2 * slots * unit_width * part,
            moved=steps * piece_bytes,
        )
        given.append(value)
        kept_weights.append(kept)
    taken = [swap(value) for value in given]
    kept, stays = {}, []
    for order, offset in enumerate(offsets):
        last = order == groups - 1
        outs = call(
            functools.partial(keep_kernel, sizes),
            [((CAP, part), BF16)] * (exp_count + (len(stays) if last else 0)),
            [(hidden, None), (taken[order], None)]
            + [(v, pltpu.VMEM) for v in kept_weights[order]]
            + [(v, None) for v in (stays if last else [])],
            flops=2 * slots * unit_width * part,
            moved=piece_bytes,
        )
        for d in range(exp_count):
            kept[offset, d] = outs[d]
        if last:
            for n, other_offset in enumerate(offsets[:-1]):
                kept[other_offset, 0] = outs[exp_count + n]
        else:
            stays.append(outs[0])
    home = {(o, d): shift(v, -d, o) if o or d else v for (o, d), v in kept.items()}
    mixed = None
    for order, batch in enumerate(arrivals(sizes)):
        last = order == 1
        mixed = call(
            functools.partial(combine_kernel, order),
            [((tok_count, part), BF16 if last else F32)],
            [(combine_high, None), (combine_low, None)]
            + ([(mixed, None)] if order else [])
            + [(home[key], None) for key in batch],
            flops=4 * tok_count * slots * part,
            moved=1 << 20,
        )[0]
    return mixed


def per_device(*operands):
    tokens, gate_weight = operands[0], operands[5]
    exp_count, unit_count = lax.axis_size("exp"), lax.axis_size("unit")
    unit_width = gate_weight.shape[1]
    paired = (
        2 * unit_width == FF
        and unit_count % 2 == 0
        and exp_count * unit_count // 2 == EXPERTS
        and TILE % tokens.shape[0] == 0
        and unit_width % BLOCK == 0
        and unit_count == 4
        and tokens.shape[1] % (unit_count * BLOCK) == 0
        and tokens.shape[1] <= READY * BLOCK <= 2 * tokens.shape[1]
    )
    return (paired_experts if paired else spread_experts)(*operands)


def solution(mesh):
    return jax.shard_map(
        per_device,
        mesh=mesh,
        in_specs=(
            P(("rep", "exp"), None),
            P(),
            P(("rep", "exp"), None),
            P(("rep", "exp"), None),
            P("rep", None, None),
            P(None, ("exp", "unit")),
            P(None, ("exp", "unit")),
            P(("exp", "unit"), None),
        ),
        out_specs=P(("rep", "exp"), "unit"),
        check_vma=False,
    )
```

```python
import functools

import jax
import jax.numpy as jnp
import numpy as np
from jax import lax
from jax.experimental import pallas as pl
from jax.experimental.pallas import tpu as pltpu
from jax.sharding import PartitionSpec as P

EXPERTS = 8
FF = 7168
BLK = 64
TILE = 256
CAP = 40

EPSILON = 1e-05

BLOCK = 512
READY = 11
BUFFERS = 12
LIMIT = 8

F32 = jnp.float32
BF16 = jnp.bfloat16


def normalize(tokens, norm_gain):
    values = tokens.astype(jnp.float32)
    inv_rms = lax.rsqrt(jnp.mean(values * values, axis=-1, keepdims=True) + EPSILON)
    return (values * inv_rms * norm_gain).astype(jnp.bfloat16)


def slot_numbers(entries, expert_count):
    onehot = (entries[..., None] == jnp.arange(expert_count, dtype=jnp.int32)).astype(jnp.int32)
    before = jnp.cumsum(onehot, axis=-2, dtype=jnp.int32) - onehot
    return jnp.sum(before * onehot, axis=-1)


def spread_experts(
    tokens, norm_gain, route_ids, route_weight, active_blocks, gate_weight, up_weight, down_weight
):
    exp_count = lax.axis_size("exp")
    unit_count = lax.axis_size("unit")
    tok_count, feature_width = tokens.shape
    unit_width = gate_weight.shape[1]
    row_units = unit_count * unit_width
    per_exp = max(1, row_units // FF)
    part_width = feature_width // unit_count
    block_count = unit_width // BLK
    tile_count = active_blocks.shape[0]
    exp_index = lax.axis_index("exp")
    unit_index = lax.axis_index("unit")
    first_unit = (exp_index * unit_count + unit_index) * unit_width
    own_expert = first_unit // FF
    first_block = first_unit % FF // BLK
    local_expert = own_expert - exp_index * row_units // FF
    normed = normalize(tokens, norm_gain)
    slot_index = slot_numbers(route_ids.reshape(1, -1), EXPERTS).reshape(tok_count, 2)
    positions = jnp.arange(tok_count, dtype=jnp.int32)
    tile_of = (exp_index * tok_count + positions) // TILE
    route_slot = (route_ids * CAP + slot_index).reshape(-1)
    token_source = (
        jnp.full((EXPERTS * CAP,), tok_count, jnp.int32)
        .at[route_slot]
        .set(jnp.repeat(positions, 2))
    )
    row_experts = np.arange(exp_count)[:, None] * row_units // FF + np.arange(per_exp)[None, :]
    slot_source = token_source.reshape(EXPERTS, CAP)[row_experts]
    padded_tiles = jnp.concatenate([tile_of, jnp.zeros((1,), jnp.int32)])
    slot_tiles = padded_tiles[slot_source]
    active_mine = lax.dynamic_index_in_dim(active_blocks, own_expert, 1, keepdims=False)
    local_blocks = first_block + jnp.arange(block_count, dtype=jnp.int32)
    block_on = jnp.any(active_mine[:, :, None] == local_blocks[None, None, :], axis=1).astype(
        jnp.float32
    )
    row_part = lax.dynamic_slice_in_dim(normed, unit_index * part_width, part_width, 1)
    padded_rows = jnp.concatenate([row_part, jnp.zeros((1, part_width), jnp.bfloat16)], 0)
    whole_rows = lax.all_gather(
        lax.all_to_all(padded_rows[slot_source], "exp", split_axis=0, concat_axis=0, tiled=True),
        "unit",
        axis=3,
        tiled=True,
    )
    slot_count = whole_rows.shape[2]
    own_rows = lax.dynamic_index_in_dim(whole_rows, local_expert, 1, keepdims=False).reshape(
        -1, feature_width
    )
    own_tiles = lax.dynamic_index_in_dim(
        lax.all_to_all(slot_tiles, "exp", split_axis=0, concat_axis=0, tiled=True),
        local_expert,
        1,
        keepdims=False,
    ).reshape(-1)
    tile_hot = (own_tiles[:, None] == jnp.arange(tile_count, dtype=jnp.int32)[None, :]).astype(
        jnp.float32
    )
    row_mask = jnp.dot(tile_hot, block_on, precision=lax.Precision.HIGHEST)
    gate_acts = jnp.dot(own_rows, gate_weight, preferred_element_type=jnp.float32)
    up_acts = jnp.dot(own_rows, up_weight, preferred_element_type=jnp.float32)
    hidden = jax.nn.relu(gate_acts) * jax.nn.relu(up_acts)
    hidden = (hidden.reshape(-1, block_count, BLK) * row_mask[:, :, None]).reshape(-1, unit_width)
    hidden = hidden.astype(jnp.bfloat16)
    partial_value = jnp.dot(hidden, down_weight, preferred_element_type=jnp.float32)
    partial_value = partial_value.reshape(exp_count, slot_count, feature_width)
    result = jnp.zeros((exp_count, per_exp, slot_count, feature_width), jnp.float32)
    partial_all = lax.dynamic_update_index_in_dim(result, partial_value, local_expert, 1)

    def by_expert(returned):
        last_width = returned.shape[-1]
        if per_exp == 1:
            grouped = returned.reshape(EXPERTS, exp_count // EXPERTS, CAP, last_width)
            return jnp.sum(grouped, axis=1, dtype=jnp.float32)
        return returned.reshape(EXPERTS, CAP, last_width).astype(jnp.float32)

    summed = lax.psum_scatter(
        partial_all.astype(jnp.bfloat16), "unit", scatter_dimension=3, tiled=True
    ).astype(jnp.float32)
    returned = lax.all_to_all(
        summed.astype(jnp.bfloat16), "exp", split_axis=0, concat_axis=0, tiled=True
    ).astype(summed.dtype)
    per_expert = by_expert(returned)
    last_width = per_expert.shape[-1]
    picked = per_expert.reshape(EXPERTS * CAP, last_width)[route_slot].reshape(
        tok_count, 2, last_width
    )
    mixed = jnp.sum(route_weight[:, :, None] * picked, axis=1)
    return mixed.astype(jnp.bfloat16)


def place(sizes):
    exp_count, groups = sizes
    return lax.axis_index("exp"), lax.axis_index("unit") // 2, lax.axis_index("unit") % 2


def pick_rows(named, before, d):
    rows = named.shape[1]
    place_of = jnp.where(named[d : d + 1, :] > 0, before[d : d + 1, :], -1)
    return (place_of == lax.broadcasted_iota(jnp.int32, (CAP, rows), 0)).astype(F32)


def count_earlier(ids, experts):
    rows = ids.shape[1]
    earlier = (
        lax.broadcasted_iota(jnp.int32, (rows, rows), 0)
        < lax.broadcasted_iota(jnp.int32, (rows, rows), 1)
    ).astype(BF16)
    named = ((ids[0:1, :] == experts) | (ids[1:2, :] == experts)).astype(jnp.int32)
    before = jnp.dot(named.astype(BF16), earlier, preferred_element_type=F32)
    return named, before.astype(jnp.int32)


def group_experts(exp_count, groups, z, g, rows):
    distance = lax.broadcasted_iota(jnp.int32, (max(8, exp_count), rows), 0)
    return lax.rem(z + distance, exp_count) * groups + g


def fetch_rows(weight, line, buffer, sem):
    def start(index, carry):
        pltpu.make_async_copy(
            weight.at[
                pl.ds(line * BLOCK, BLOCK), pl.ds(pl.multiple_of(index * BLOCK, BLOCK), BLOCK)
            ],
            buffer.at[index],
            sem,
        ).start()
        return carry

    lax.fori_loop(0, buffer.shape[0], start, 0)


def fetch_columns(sizes, down, offset, keep, step, buffer, sem):
    exp_count, groups = sizes
    z, g, s = place(sizes)
    side = s if keep else 1 - s
    part = down.shape[1] // (2 * groups)
    column = (lax.rem(g + offset, groups) * 2 + side) * part + step * BLOCK

    def start(index, carry):
        pltpu.make_async_copy(
            down.at[
                pl.ds(pl.multiple_of(index * BLOCK, BLOCK), BLOCK),
                pl.ds(pl.multiple_of(column, BLOCK), BLOCK),
            ],
            buffer.at[index],
            sem,
        ).start()
        return carry

    lax.fori_loop(0, buffer.shape[0], start, 0)


def await_all(buffer, sem):
    pltpu.make_async_copy(buffer, buffer, sem).wait()


def stacked(buffer):
    return buffer[...].reshape(buffer.shape[0] * BLOCK, BLOCK)


def route_kernel(sizes, width, tokens_hbm, gain_hbm, ids_hbm, gate, own, buffer, *rest):
    exp_count, groups = sizes
    sends, (tokens, normed, gain, ids, sems, gate_sem) = rest[:-6], rest[-6:]
    rows, features = tokens.shape
    count = 4
    lines = [pl.ds(n * (rows // count), rows // count) for n in range(count)]
    pairs = [(gain_hbm, gain), (ids_hbm, ids)]
    pairs += [(tokens_hbm.at[part, :], tokens.at[part, :]) for part in lines]
    copies = [pltpu.make_async_copy(a, b, sems.at[n]) for n, (a, b) in enumerate(pairs)]
    for copy in copies:
        copy.start()
    fetch_rows(gate, 0, buffer, gate_sem)
    z, g, s = place(sizes)
    copies[0].wait()
    copies[1].wait()
    named, before = count_earlier(ids, group_experts(exp_count, groups, z, g, rows))
    picks = [pick_rows(named, before, d) for d in range(exp_count)]
    others = jnp.concatenate(picks[1:], axis=0).astype(BF16)
    step = 16
    for first in range(0, rows, step):
        if first % (rows // count) == 0:
            copies[2 + first // (rows // count)].wait()
        values = tokens[first : first + step, :].astype(F32)
        mean = jnp.sum(values * values, axis=1, keepdims=True) * (1.0 / features)
        inv_rms = lax.rsqrt(mean + EPSILON)
        normed[first : first + step, :] = (values * inv_rms * gain[...]).astype(BF16)
    start = pl.multiple_of(s * (features // 2), 128)
    found = jnp.dot(others, normed[:, pl.ds(start, width)], preferred_element_type=F32)
    for d, send in enumerate(sends):
        send[...] = found[d * CAP : (d + 1) * CAP, :].astype(BF16)
    own[...] = jnp.dot(
        picks[0].astype(BF16), normed[...], preferred_element_type=F32
    ).astype(BF16)
    await_all(buffer, gate_sem)


def arrivals(sizes):
    exp_count, groups = sizes
    order = list(range(1, exp_count)) + [0]
    early = [(o, d) for o in range(1, groups) for d in order]
    late = [(0, d) for d in order]
    return early, late


def table_kernel(sizes, ids_hbm, weights_hbm, after, combine_high, combine_low, ids, weights, sems):
    exp_count, groups = sizes
    pairs = ((ids_hbm, ids), (weights_hbm, weights))
    copies = [pltpu.make_async_copy(a, b, sems.at[n]) for n, (a, b) in enumerate(pairs)]
    for copy in copies:
        copy.start()
    for copy in copies:
        copy.wait()
    rows = ids.shape[1]
    z, g, s = place(sizes)
    zero = jnp.zeros((CAP, rows), F32)
    padded = combine_high.shape[2]
    batches = arrivals(sizes)
    experts = [
        lax.rem(z + d, exp_count) * groups + lax.rem(g - o + groups, groups)
        for batch in batches
        for o, d in batch
    ]
    line = lax.broadcasted_iota(jnp.int32, (max(8, len(experts)), rows), 0)
    listed = jnp.full(line.shape, -1, jnp.int32)
    for n, expert in enumerate(experts):
        listed = jnp.where(line == n, expert, listed)
    named, before = count_earlier(ids, listed)
    for order, batch in enumerate(batches):
        parts = []
        for n in range(len(batch)):
            entry = order * len(batch) + n
            here = pick_rows(named, before, entry) > 0
            first = jnp.where(here & (ids[0:1, :] == experts[entry]), weights[0:1, :], zero)
            second = jnp.where(here & (ids[1:2, :] == experts[entry]), weights[1:2, :], zero)
            parts.append(first + second)
        if padded > len(batch) * CAP:
            parts.append(jnp.zeros((padded - len(batch) * CAP, rows), F32))
        table = jnp.concatenate(parts, axis=0).T
        high = table.astype(BF16)
        combine_high[order] = high
        combine_low[order] = (table - high.astype(F32)).astype(BF16)


def prepare_kernel(sizes, rows, active_hbm, gate, up, after, _, mask, *rest):
    exp_count, groups = sizes
    *buffers, active, small_sem, sems = rest
    z, g, s = place(sizes)
    small = pltpu.make_async_copy(active_hbm, active, small_sem)
    small.start()
    lines = gate.shape[0] // BLOCK
    for n, buffer in enumerate(buffers[1:READY], 1):
        fetch_rows(gate if n < lines else up, n % lines, buffer, sems.at[n])
    small.wait()
    unit_width = mask.shape[1]
    blocks = lax.broadcasted_iota(jnp.int32, mask.shape, 1) // BLK + s * (unit_width // BLK)
    source = lax.broadcasted_iota(jnp.int32, (mask.shape[0], 1), 0)
    own_expert = z * groups + g

    def add_entry(k, found):
        entry = jnp.full((mask.shape[0], 1), -1, jnp.int32)
        for d in range(exp_count):
            tile = lax.rem(z - d + exp_count, exp_count) * rows // TILE
            entry = jnp.where(source == d, active[tile, own_expert, k], entry)
        return jnp.where(blocks == entry, 1.0, found)

    mask[...] = lax.fori_loop(0, active.shape[2], add_entry, jnp.zeros(mask.shape, F32))
    for n, buffer in enumerate(buffers[1:READY], 1):
        await_all(buffer, sems.at[n])


def join_kernel(after, *refs):
    pieces = [r[...].astype(F32) for r in refs[:-1]]
    refs[-1][...] = jnp.concatenate(pieces, axis=0).astype(BF16)


def hidden_kernel(sizes, own, mine, other, *refs):
    exp_count, groups = sizes
    z, g, s = place(sizes)
    refs = list(refs)
    refs = refs[BUFFERS:]
    up, down, mask, _, hidden = [refs.pop(0) for _ in range(5)]
    buffers = [refs.pop(0) for _ in range(BUFFERS)]
    gate_sum, up_sum, rows, sems = refs
    half = own.shape[1] // 2
    features, unit_width = up.shape
    columns, lines = unit_width // BLOCK, features // BLOCK
    given = features // (2 * groups) // BLOCK
    count = len(buffers)

    def fetch(index):
        buffer, sem = buffers[index % count], sems.at[index % count]
        if index < 2 * lines:
            fetch_rows(up, index - lines, buffer, sem)
        elif index < 2 * lines + groups * given:
            order, step = divmod(index - 2 * lines, given)
            fetch_columns(sizes, down, order + 1, False, step, buffer, sem)

    for index in range(READY, count):
        fetch(index)
    for source, side in ((mine, s), (other, 1 - s)):
        cols = pl.ds(pl.multiple_of(side * half, 128), half)
        joined = [own[:, cols].astype(F32), source[...].astype(F32)]
        rows[:, cols] = jnp.concatenate(joined, axis=0).astype(BF16)
    for index in range(0, 2 * lines, 2):
        pair = [buffers[(index + n) % count] for n in range(2)]
        for n in range(2):
            if index + n >= READY:
                await_all(pair[n], sems.at[(index + n) % count])
        line = index % lines
        total = gate_sum if index < lines else up_sum
        left = [rows[:, (line + n) * BLOCK : (line + n + 1) * BLOCK] for n in range(2)]
        for column in range(columns):
            cols = slice(column * BLOCK, (column + 1) * BLOCK)
            value = jnp.dot(left[0], pair[0][column], preferred_element_type=F32)
            value = value + jnp.dot(left[1], pair[1][column], preferred_element_type=F32)
            if line > 0:
                value = total[:, cols] + value
            if index < 2 * lines - 2:
                total[:, cols] = value
                continue
            value = jnp.maximum(gate_sum[:, cols], 0.0) * jnp.maximum(value, 0.0)
            parts = []
            for d in range(exp_count):
                parts.append(value[d * CAP : (d + 1) * CAP, :] * mask[d : d + 1, cols])
            hidden[:, cols] = jnp.concatenate(parts, axis=0).astype(BF16)
        for n in range(2):
            fetch(index + n + count)
    for index in range(2 * lines, 2 * lines + groups * given):
        await_all(buffers[index % count], sems.at[index % count])


def give_kernel(sizes, offset, hidden, *refs):
    exp_count, groups = sizes
    steps = (len(refs) - 3) // 2
    weights, (down, given), kept_weights, sems = (
        refs[:steps],
        refs[steps : steps + 2],
        refs[steps + 2 : -1],
        refs[-1],
    )
    for step, buffer in enumerate(kept_weights):
        fetch_columns(sizes, down, offset, True, step, buffer, sems.at[step])
    for step, buffer in enumerate(weights):
        value = jnp.dot(hidden[...], stacked(buffer), preferred_element_type=F32)
        given[:, step * BLOCK : (step + 1) * BLOCK] = value.astype(BF16)
    for step, buffer in enumerate(kept_weights):
        await_all(buffer, sems.at[step])


def keep_kernel(sizes, hidden, received, *refs):
    exp_count, groups = sizes
    weights, outs = refs[:-exp_count], refs[-exp_count:]
    for step, buffer in enumerate(weights):
        cols = slice(step * BLOCK, (step + 1) * BLOCK)
        value = jnp.dot(hidden[...], stacked(buffer), preferred_element_type=F32)
        value = value + received[:, cols].astype(F32)
        for d in range(exp_count):
            outs[d][:, cols] = value[d * CAP : (d + 1) * CAP, :].astype(BF16)


def combine_kernel(order, high, low, *refs):
    refs = list(refs)
    out = refs.pop()
    before = refs.pop(0) if order > 0 else None
    found = jnp.concatenate([r[...].astype(F32) for r in refs], axis=0).astype(BF16)
    count = found.shape[0]
    value = jnp.dot(high[order, :, :count], found, preferred_element_type=F32)
    value = value + jnp.dot(low[order, :, :count], found, preferred_element_type=F32)
    if before is not None:
        value = before[...] + value
    out[...] = value.astype(out.dtype)


def call(kernel, outs, ins, scratch=(), flops=0, moved=0, aliases=None):
    vmem = pl.BlockSpec(memory_space=pltpu.VMEM)
    arrays, specs = [], []
    for array, space in ins:
        if space in (pltpu.HBM, pltpu.VMEM):
            array = pltpu.with_memory_space_constraint(array, space)
        arrays.append(array)
        specs.append(vmem if space is None else pl.BlockSpec(memory_space=space))
    shapes = []
    for shape, kind, *space in outs:
        shapes.append(space[0](shape, kind) if space else jax.ShapeDtypeStruct(shape, kind))
    return pl.pallas_call(
        kernel,
        out_shape=shapes,
        in_specs=specs,
        out_specs=[vmem] * len(outs),
        scratch_shapes=list(scratch),
        input_output_aliases=aliases or {},
        compiler_params=pltpu.CompilerParams(vmem_limit_bytes=LIMIT << 20),
        cost_estimate=pl.CostEstimate(flops=flops, bytes_accessed=moved, transcendentals=0),
    )(*arrays)


def paired_experts(
    tokens, norm_gain, route_ids, route_weight, active_blocks, gate_weight, up_weight, down_weight
):
    exp_count, unit_count = lax.axis_size("exp"), lax.axis_size("unit")
    groups = unit_count // 2
    sizes = (exp_count, groups)
    tok_count, features = tokens.shape
    unit_width = gate_weight.shape[1]
    slots = exp_count * CAP
    half = features // 2
    width = half
    ids = route_ids.T
    weights = route_weight.T

    def shift(value, distance, group_shift=0):
        pairs = []
        for z in range(exp_count):
            for u in range(unit_count):
                target = (z + distance) % exp_count
                group = (u // 2 + group_shift) % groups
                pairs.append((z * unit_count + u, target * unit_count + group * 2 + u % 2))
        return lax.ppermute(value, ("exp", "unit"), pairs)

    def swap(value):
        return lax.ppermute(value, "unit", [(u, u ^ 1) for u in range(unit_count)])

    batch = exp_count - 1
    buffer = ((unit_width // BLOCK, BLOCK, BLOCK), BF16, pltpu.VMEM)
    piece_bytes = 2 * unit_width * BLOCK
    own, ready, *sends = call(
        functools.partial(route_kernel, sizes, width),
        [((CAP, features), BF16), buffer] + [((CAP, width), BF16)] * batch,
        [
            (tokens, pltpu.HBM),
            (norm_gain.reshape(1, -1), pltpu.HBM),
            (ids, pltpu.HBM),
            (gate_weight, pltpu.HBM),
        ],
        [
            pltpu.VMEM((tok_count, features), BF16),
            pltpu.VMEM((tok_count, features), BF16),
            pltpu.VMEM((1, features), F32),
            pltpu.VMEM(ids.shape, jnp.int32),
            pltpu.SemaphoreType.DMA((6,)),
            pltpu.SemaphoreType.DMA,
        ],
        flops=2 * tok_count * slots * width,
        moved=4 * tok_count * features + piece_bytes,
    )
    mask, *ready = call(
        functools.partial(prepare_kernel, sizes, tok_count),
        [((max(8, exp_count), unit_width), F32)] + [buffer] * BUFFERS,
        [
            (active_blocks, pltpu.HBM),
            (gate_weight, pltpu.HBM),
            (up_weight, pltpu.HBM),
            (own, pl.ANY),
            (ready, pltpu.VMEM),
        ],
        [
            pltpu.SMEM(active_blocks.shape, jnp.int32),
            pltpu.SemaphoreType.DMA,
            pltpu.SemaphoreType.DMA((READY,)),
        ],
        flops=2 * tok_count * slots * features,
        moved=(READY - 1) * piece_bytes,
        aliases={4: 1},
    )
    arrived = [shift(value, d + 1) for d, value in enumerate(sends)]
    mine = call(
        join_kernel,
        [((batch * CAP, width), BF16)],
        [(mask, pl.ANY)] + [(v, None) for v in arrived],
        moved=1 << 20,
    )[0]
    other = swap(mine)
    padded = -(-slots // 128) * 128
    combine_high, combine_low = call(
        functools.partial(table_kernel, sizes),
        [((2, tok_count, padded), BF16)] * 2,
        [(ids, pltpu.HBM), (weights, pltpu.HBM), (mine, pl.ANY)],
        [
            pltpu.VMEM(ids.shape, jnp.int32),
            pltpu.VMEM(weights.shape, F32),
            pltpu.SemaphoreType.DMA((2,)),
        ],
        moved=1 << 21,
    )
    acc = pltpu.VMEM((slots, unit_width), F32)
    hidden, *buffers = call(
        functools.partial(hidden_kernel, sizes),
        [((slots, unit_width), BF16)] + [buffer] * BUFFERS,
        [(own, None), (mine, None), (other, None)]
        + [(v, pltpu.VMEM) for v in ready]
        + [(up_weight, pltpu.HBM), (down_weight, pltpu.HBM), (mask, None)]
        + [(combine_low, pl.ANY)],
        [
            acc,
            acc,
            pltpu.VMEM((slots, features), BF16),
            pltpu.SemaphoreType.DMA((BUFFERS,)),
        ],
        flops=2 * 2 * slots * features * unit_width,
        moved=10 * piece_bytes,
        aliases={3 + n: 1 + n for n in range(BUFFERS)},
    )
    part = features // unit_count
    steps = part // BLOCK
    offsets = [(order + 1) % groups for order in range(groups)]
    given, kept_weights = [], []
    for order, offset in enumerate(offsets):
        first = 2 * features // BLOCK + order * steps
        value, *kept = call(
            functools.partial(give_kernel, sizes, offset),
            [((slots, part), BF16)] + [buffer] * steps,
            [(hidden, None)]
            + [(buffers[(first + step) % BUFFERS], pltpu.VMEM) for step in range(steps)]
            + [(down_weight, pltpu.HBM)],
            [pltpu.SemaphoreType.DMA((steps,))],
            flops=2 * slots * unit_width * part,
            moved=steps * piece_bytes,
        )
        given.append(value)
        kept_weights.append(kept)
    taken = [swap(value) for value in given]
    home = {}
    for order, offset in enumerate(offsets):
        kept = call(
            functools.partial(keep_kernel, sizes),
            [((CAP, part), BF16)] * exp_count,
            [(hidden, None), (taken[order], None)]
            + [(v, pltpu.VMEM) for v in kept_weights[order]],
            flops=2 * slots * unit_width * part,
            moved=piece_bytes,
        )
        for d in list(range(1, exp_count)) + [0]:
            home[offset, d] = shift(kept[d], -d, offset) if d or offset else kept[d]
    mixed = None
    for order, batch in enumerate(arrivals(sizes)):
        last = order == 1
        mixed = call(
            functools.partial(combine_kernel, order),
            [((tok_count, part), BF16 if last else F32)],
            [(combine_high, None), (combine_low, None)]
            + ([(mixed, None)] if order else [])
            + [(home[key], None) for key in batch],
            flops=4 * tok_count * slots * part,
            moved=1 << 20,
        )[0]
    return mixed


def per_device(*operands):
    tokens, gate_weight = operands[0], operands[5]
    exp_count, unit_count = lax.axis_size("exp"), lax.axis_size("unit")
    unit_width = gate_weight.shape[1]
    paired = (
        2 * unit_width == FF
        and unit_count % 2 == 0
        and exp_count * unit_count // 2 == EXPERTS
        and TILE % tokens.shape[0] == 0
        and unit_width % BLOCK == 0
        and unit_count == 4
        and tokens.shape[1] % (unit_count * BLOCK) == 0
        and tokens.shape[1] <= READY * BLOCK <= 2 * tokens.shape[1]
    )
    return (paired_experts if paired else spread_experts)(*operands)


def solution(mesh):
    return jax.shard_map(
        per_device,
        mesh=mesh,
        in_specs=(
            P(("rep", "exp"), None),
            P(),
            P(("rep", "exp"), None),
            P(("rep", "exp"), None),
            P("rep", None, None),
            P(None, ("exp", "unit")),
            P(None, ("exp", "unit")),
            P(("exp", "unit"), None),
        ),
        out_specs=P(("rep", "exp"), "unit"),
        check_vma=False,
    )
```

```python
import functools

import jax
import jax.numpy as jnp
import numpy as np
from jax import lax
from jax.experimental import pallas as pl
from jax.experimental.pallas import tpu as pltpu
from jax.sharding import PartitionSpec as P

EXPERTS = 8
FF = 7168
BLK = 64
TILE = 256
CAP = 40

EPSILON = 1e-05

BLOCK = 512
READY = 11
BUFFERS = 12
LIMIT = 8

F32 = jnp.float32
BF16 = jnp.bfloat16


def normalize(tokens, norm_gain):
    values = tokens.astype(jnp.float32)
    inv_rms = lax.rsqrt(jnp.mean(values * values, axis=-1, keepdims=True) + EPSILON)
    return (values * inv_rms * norm_gain).astype(jnp.bfloat16)


def slot_numbers(entries, expert_count):
    onehot = (entries[..., None] == jnp.arange(expert_count, dtype=jnp.int32)).astype(jnp.int32)
    before = jnp.cumsum(onehot, axis=-2, dtype=jnp.int32) - onehot
    return jnp.sum(before * onehot, axis=-1)


def spread_experts(
    tokens, norm_gain, route_ids, route_weight, active_blocks, gate_weight, up_weight, down_weight
):
    exp_count = lax.axis_size("exp")
    unit_count = lax.axis_size("unit")
    tok_count, feature_width = tokens.shape
    unit_width = gate_weight.shape[1]
    row_units = unit_count * unit_width
    per_exp = max(1, row_units // FF)
    part_width = feature_width // unit_count
    block_count = unit_width // BLK
    tile_count = active_blocks.shape[0]
    exp_index = lax.axis_index("exp")
    unit_index = lax.axis_index("unit")
    first_unit = (exp_index * unit_count + unit_index) * unit_width
    own_expert = first_unit // FF
    first_block = first_unit % FF // BLK
    local_expert = own_expert - exp_index * row_units // FF
    normed = normalize(tokens, norm_gain)
    slot_index = slot_numbers(route_ids.reshape(1, -1), EXPERTS).reshape(tok_count, 2)
    positions = jnp.arange(tok_count, dtype=jnp.int32)
    tile_of = (exp_index * tok_count + positions) // TILE
    route_slot = (route_ids * CAP + slot_index).reshape(-1)
    token_source = (
        jnp.full((EXPERTS * CAP,), tok_count, jnp.int32)
        .at[route_slot]
        .set(jnp.repeat(positions, 2))
    )
    row_experts = np.arange(exp_count)[:, None] * row_units // FF + np.arange(per_exp)[None, :]
    slot_source = token_source.reshape(EXPERTS, CAP)[row_experts]
    padded_tiles = jnp.concatenate([tile_of, jnp.zeros((1,), jnp.int32)])
    slot_tiles = padded_tiles[slot_source]
    active_mine = lax.dynamic_index_in_dim(active_blocks, own_expert, 1, keepdims=False)
    local_blocks = first_block + jnp.arange(block_count, dtype=jnp.int32)
    block_on = jnp.any(active_mine[:, :, None] == local_blocks[None, None, :], axis=1).astype(
        jnp.float32
    )
    row_part = lax.dynamic_slice_in_dim(normed, unit_index * part_width, part_width, 1)
    padded_rows = jnp.concatenate([row_part, jnp.zeros((1, part_width), jnp.bfloat16)], 0)
    whole_rows = lax.all_gather(
        lax.all_to_all(padded_rows[slot_source], "exp", split_axis=0, concat_axis=0, tiled=True),
        "unit",
        axis=3,
        tiled=True,
    )
    slot_count = whole_rows.shape[2]
    own_rows = lax.dynamic_index_in_dim(whole_rows, local_expert, 1, keepdims=False).reshape(
        -1, feature_width
    )
    own_tiles = lax.dynamic_index_in_dim(
        lax.all_to_all(slot_tiles, "exp", split_axis=0, concat_axis=0, tiled=True),
        local_expert,
        1,
        keepdims=False,
    ).reshape(-1)
    tile_hot = (own_tiles[:, None] == jnp.arange(tile_count, dtype=jnp.int32)[None, :]).astype(
        jnp.float32
    )
    row_mask = jnp.dot(tile_hot, block_on, precision=lax.Precision.HIGHEST)
    gate_acts = jnp.dot(own_rows, gate_weight, preferred_element_type=jnp.float32)
    up_acts = jnp.dot(own_rows, up_weight, preferred_element_type=jnp.float32)
    hidden = jax.nn.relu(gate_acts) * jax.nn.relu(up_acts)
    hidden = (hidden.reshape(-1, block_count, BLK) * row_mask[:, :, None]).reshape(-1, unit_width)
    hidden = hidden.astype(jnp.bfloat16)
    partial_value = jnp.dot(hidden, down_weight, preferred_element_type=jnp.float32)
    partial_value = partial_value.reshape(exp_count, slot_count, feature_width)
    result = jnp.zeros((exp_count, per_exp, slot_count, feature_width), jnp.float32)
    partial_all = lax.dynamic_update_index_in_dim(result, partial_value, local_expert, 1)

    def by_expert(returned):
        last_width = returned.shape[-1]
        if per_exp == 1:
            grouped = returned.reshape(EXPERTS, exp_count // EXPERTS, CAP, last_width)
            return jnp.sum(grouped, axis=1, dtype=jnp.float32)
        return returned.reshape(EXPERTS, CAP, last_width).astype(jnp.float32)

    summed = lax.psum_scatter(
        partial_all.astype(jnp.bfloat16), "unit", scatter_dimension=3, tiled=True
    ).astype(jnp.float32)
    returned = lax.all_to_all(
        summed.astype(jnp.bfloat16), "exp", split_axis=0, concat_axis=0, tiled=True
    ).astype(summed.dtype)
    per_expert = by_expert(returned)
    last_width = per_expert.shape[-1]
    picked = per_expert.reshape(EXPERTS * CAP, last_width)[route_slot].reshape(
        tok_count, 2, last_width
    )
    mixed = jnp.sum(route_weight[:, :, None] * picked, axis=1)
    return mixed.astype(jnp.bfloat16)


def place(sizes):
    exp_count, groups = sizes
    return lax.axis_index("exp"), lax.axis_index("unit") // 2, lax.axis_index("unit") % 2


def pick_rows(named, before, d):
    rows = named.shape[1]
    place_of = jnp.where(named[d : d + 1, :] > 0, before[d : d + 1, :], -1)
    return (place_of == lax.broadcasted_iota(jnp.int32, (CAP, rows), 0)).astype(F32)


def count_earlier(ids, experts):
    rows = ids.shape[1]
    earlier = (
        lax.broadcasted_iota(jnp.int32, (rows, rows), 0)
        < lax.broadcasted_iota(jnp.int32, (rows, rows), 1)
    ).astype(BF16)
    named = ((ids[0:1, :] == experts) | (ids[1:2, :] == experts)).astype(jnp.int32)
    before = jnp.dot(named.astype(BF16), earlier, preferred_element_type=F32)
    return named, before.astype(jnp.int32)


def group_experts(exp_count, groups, z, g, rows):
    distance = lax.broadcasted_iota(jnp.int32, (max(8, exp_count), rows), 0)
    return lax.rem(z + distance, exp_count) * groups + g


def fetch_rows(weight, line, buffer, sem):
    def start(index, carry):
        pltpu.make_async_copy(
            weight.at[
                pl.ds(line * BLOCK, BLOCK), pl.ds(pl.multiple_of(index * BLOCK, BLOCK), BLOCK)
            ],
            buffer.at[index],
            sem,
        ).start()
        return carry

    lax.fori_loop(0, buffer.shape[0], start, 0)


def fetch_columns(sizes, down, offset, keep, step, buffer, sem):
    exp_count, groups = sizes
    z, g, s = place(sizes)
    side = s if keep else 1 - s
    part = down.shape[1] // (2 * groups)
    column = (lax.rem(g + offset, groups) * 2 + side) * part + step * BLOCK

    def start(index, carry):
        pltpu.make_async_copy(
            down.at[
                pl.ds(pl.multiple_of(index * BLOCK, BLOCK), BLOCK),
                pl.ds(pl.multiple_of(column, BLOCK), BLOCK),
            ],
            buffer.at[index],
            sem,
        ).start()
        return carry

    lax.fori_loop(0, buffer.shape[0], start, 0)


def await_all(buffer, sem):
    pltpu.make_async_copy(buffer, buffer, sem).wait()


def stacked(buffer):
    return buffer[...].reshape(buffer.shape[0] * BLOCK, BLOCK)


def route_kernel(sizes, width, tokens_hbm, gain_hbm, ids_hbm, gate, own, buffer, *rest):
    exp_count, groups = sizes
    sends, (tokens, normed, gain, ids, sems, gate_sem) = rest[:-6], rest[-6:]
    rows, features = tokens.shape
    count = 4
    lines = [pl.ds(n * (rows // count), rows // count) for n in range(count)]
    pairs = [(gain_hbm, gain), (ids_hbm, ids)]
    pairs += [(tokens_hbm.at[part, :], tokens.at[part, :]) for part in lines]
    copies = [pltpu.make_async_copy(a, b, sems.at[n]) for n, (a, b) in enumerate(pairs)]
    for copy in copies:
        copy.start()
    fetch_rows(gate, 0, buffer, gate_sem)
    z, g, s = place(sizes)
    copies[0].wait()
    copies[1].wait()
    named, before = count_earlier(ids, group_experts(exp_count, groups, z, g, rows))
    picks = [pick_rows(named, before, d) for d in range(exp_count)]
    others = jnp.concatenate(picks[1:], axis=0).astype(BF16)
    step = 16
    for first in range(0, rows, step):
        if first % (rows // count) == 0:
            copies[2 + first // (rows // count)].wait()
        values = tokens[first : first + step, :].astype(F32)
        mean = jnp.sum(values * values, axis=1, keepdims=True) * (1.0 / features)
        inv_rms = lax.rsqrt(mean + EPSILON)
        normed[first : first + step, :] = (values * inv_rms * gain[...]).astype(BF16)
    start = pl.multiple_of(s * (features // 2), 128)
    found = jnp.dot(others, normed[:, pl.ds(start, width)], preferred_element_type=F32)
    for d, send in enumerate(sends):
        send[...] = found[d * CAP : (d + 1) * CAP, :].astype(BF16)
    own[...] = jnp.dot(
        picks[0].astype(BF16), normed[...], preferred_element_type=F32
    ).astype(BF16)
    await_all(buffer, gate_sem)


def arrivals(sizes):
    exp_count, groups = sizes
    order = list(range(1, exp_count)) + [0]
    early = [(o, d) for o in range(1, groups) for d in order]
    late = [(0, d) for d in order]
    return early, late


def table_kernel(sizes, ids_hbm, weights_hbm, after, combine_high, combine_low, ids, weights, sems):
    exp_count, groups = sizes
    pairs = ((ids_hbm, ids), (weights_hbm, weights))
    copies = [pltpu.make_async_copy(a, b, sems.at[n]) for n, (a, b) in enumerate(pairs)]
    for copy in copies:
        copy.start()
    for copy in copies:
        copy.wait()
    rows = ids.shape[1]
    z, g, s = place(sizes)
    zero = jnp.zeros((CAP, rows), F32)
    padded = combine_high.shape[2]
    batches = arrivals(sizes)
    experts = [
        lax.rem(z + d, exp_count) * groups + lax.rem(g - o + groups, groups)
        for batch in batches
        for o, d in batch
    ]
    line = lax.broadcasted_iota(jnp.int32, (max(8, len(experts)), rows), 0)
    listed = jnp.full(line.shape, -1, jnp.int32)
    for n, expert in enumerate(experts):
        listed = jnp.where(line == n, expert, listed)
    named, before = count_earlier(ids, listed)
    for order, batch in enumerate(batches):
        parts = []
        for n in range(len(batch)):
            entry = order * len(batch) + n
            here = pick_rows(named, before, entry) > 0
            first = jnp.where(here & (ids[0:1, :] == experts[entry]), weights[0:1, :], zero)
            second = jnp.where(here & (ids[1:2, :] == experts[entry]), weights[1:2, :], zero)
            parts.append(first + second)
        if padded > len(batch) * CAP:
            parts.append(jnp.zeros((padded - len(batch) * CAP, rows), F32))
        table = jnp.concatenate(parts, axis=0).T
        high = table.astype(BF16)
        combine_high[order] = high
        combine_low[order] = (table - high.astype(F32)).astype(BF16)


def prepare_kernel(sizes, rows, active_hbm, gate, up, after, _, mask, *rest):
    exp_count, groups = sizes
    *buffers, active, small_sem, sems = rest
    z, g, s = place(sizes)
    small = pltpu.make_async_copy(active_hbm, active, small_sem)
    small.start()
    lines = gate.shape[0] // BLOCK
    for n, buffer in enumerate(buffers[1:READY], 1):
        fetch_rows(gate if n < lines else up, n % lines, buffer, sems.at[n])
    small.wait()
    unit_width = mask.shape[1]
    blocks = lax.broadcasted_iota(jnp.int32, mask.shape, 1) // BLK + s * (unit_width // BLK)
    source = lax.broadcasted_iota(jnp.int32, (mask.shape[0], 1), 0)
    own_expert = z * groups + g

    def add_entry(k, found):
        entry = jnp.full((mask.shape[0], 1), -1, jnp.int32)
        for d in range(exp_count):
            tile = lax.rem(z - d + exp_count, exp_count) * rows // TILE
            entry = jnp.where(source == d, active[tile, own_expert, k], entry)
        return jnp.where(blocks == entry, 1.0, found)

    mask[...] = lax.fori_loop(0, active.shape[2], add_entry, jnp.zeros(mask.shape, F32))
    for n, buffer in enumerate(buffers[1:READY], 1):
        await_all(buffer, sems.at[n])


def join_kernel(after, *refs):
    pieces = [r[...].astype(F32) for r in refs[:-1]]
    refs[-1][...] = jnp.concatenate(pieces, axis=0).astype(BF16)


def hidden_kernel(sizes, own, mine, other, *refs):
    exp_count, groups = sizes
    z, g, s = place(sizes)
    refs = list(refs)
    refs = refs[BUFFERS:]
    up, down, mask, _, hidden, gives = [refs.pop(0) for _ in range(6)]
    buffers = [refs.pop(0) for _ in range(BUFFERS)]
    gate_sum, up_sum, rows, sems = refs
    half = own.shape[1] // 2
    features, unit_width = up.shape
    columns, lines = unit_width // BLOCK, features // BLOCK
    given = features // (2 * groups) // BLOCK
    count = len(buffers)

    def fetch(index):
        buffer, sem = buffers[index % count], sems.at[index % count]
        if index < 2 * lines:
            fetch_rows(up, index - lines, buffer, sem)
        elif index < 2 * lines + groups * given:
            order, step = divmod(index - 2 * lines, given)
            fetch_columns(sizes, down, order + 1, False, step, buffer, sem)
        elif index < 2 * lines + (groups + 1) * given:
            step = index - 2 * lines - groups * given
            fetch_columns(sizes, down, 1, True, step, buffer, sem)

    for index in range(READY, count):
        fetch(index)
    for source, side in ((mine, s), (other, 1 - s)):
        cols = pl.ds(pl.multiple_of(side * half, 128), half)
        joined = [own[:, cols].astype(F32), source[...].astype(F32)]
        rows[:, cols] = jnp.concatenate(joined, axis=0).astype(BF16)
    for index in range(0, 2 * lines, 2):
        pair = [buffers[(index + n) % count] for n in range(2)]
        for n in range(2):
            if index + n >= READY:
                await_all(pair[n], sems.at[(index + n) % count])
        line = index % lines
        total = gate_sum if index < lines else up_sum
        left = [rows[:, (line + n) * BLOCK : (line + n + 1) * BLOCK] for n in range(2)]
        for column in range(columns):
            cols = slice(column * BLOCK, (column + 1) * BLOCK)
            value = jnp.dot(left[0], pair[0][column], preferred_element_type=F32)
            value = value + jnp.dot(left[1], pair[1][column], preferred_element_type=F32)
            if line > 0:
                value = total[:, cols] + value
            if index < 2 * lines - 2:
                total[:, cols] = value
                continue
            value = jnp.maximum(gate_sum[:, cols], 0.0) * jnp.maximum(value, 0.0)
            parts = []
            for d in range(exp_count):
                parts.append(value[d * CAP : (d + 1) * CAP, :] * mask[d : d + 1, cols])
            hidden[:, cols] = jnp.concatenate(parts, axis=0).astype(BF16)
        for n in range(2):
            fetch(index + n + count)
    for index in range(2 * lines, 2 * lines + (groups + 1) * given):
        buffer = buffers[index % count]
        await_all(buffer, sems.at[index % count])
        step = index - 2 * lines
        if step < given:
            value = jnp.dot(hidden[...], stacked(buffer), preferred_element_type=F32)
            gives[:, step * BLOCK : (step + 1) * BLOCK] = value.astype(BF16)


def give_kernel(sizes, offset, hidden, *refs):
    exp_count, groups = sizes
    steps = (len(refs) - 3) // 2
    weights, (down, given), kept_weights, sems = (
        refs[:steps],
        refs[steps : steps + 2],
        refs[steps + 2 : -1],
        refs[-1],
    )
    for step, buffer in enumerate(kept_weights):
        fetch_columns(sizes, down, offset, True, step, buffer, sems.at[step])
    for step, buffer in enumerate(weights):
        value = jnp.dot(hidden[...], stacked(buffer), preferred_element_type=F32)
        given[:, step * BLOCK : (step + 1) * BLOCK] = value.astype(BF16)
    for step, buffer in enumerate(kept_weights):
        await_all(buffer, sems.at[step])


def keep_kernel(sizes, hidden, received, *refs):
    exp_count, groups = sizes
    weights, outs = refs[:-exp_count], refs[-exp_count:]
    for step, buffer in enumerate(weights):
        cols = slice(step * BLOCK, (step + 1) * BLOCK)
        value = jnp.dot(hidden[...], stacked(buffer), preferred_element_type=F32)
        value = value + received[:, cols].astype(F32)
        for d in range(exp_count):
            outs[d][:, cols] = value[d * CAP : (d + 1) * CAP, :].astype(BF16)


def combine_kernel(order, high, low, *refs):
    refs = list(refs)
    out = refs.pop()
    before = refs.pop(0) if order > 0 else None
    found = jnp.concatenate([r[...].astype(F32) for r in refs], axis=0).astype(BF16)
    count = found.shape[0]
    value = jnp.dot(high[order, :, :count], found, preferred_element_type=F32)
    value = value + jnp.dot(low[order, :, :count], found, preferred_element_type=F32)
    if before is not None:
        value = before[...] + value
    out[...] = value.astype(out.dtype)


def call(kernel, outs, ins, scratch=(), flops=0, moved=0, aliases=None):
    vmem = pl.BlockSpec(memory_space=pltpu.VMEM)
    arrays, specs = [], []
    for array, space in ins:
        if space in (pltpu.HBM, pltpu.VMEM):
            array = pltpu.with_memory_space_constraint(array, space)
        arrays.append(array)
        specs.append(vmem if space is None else pl.BlockSpec(memory_space=space))
    shapes = []
    for shape, kind, *space in outs:
        shapes.append(space[0](shape, kind) if space else jax.ShapeDtypeStruct(shape, kind))
    return pl.pallas_call(
        kernel,
        out_shape=shapes,
        in_specs=specs,
        out_specs=[vmem] * len(outs),
        scratch_shapes=list(scratch),
        input_output_aliases=aliases or {},
        compiler_params=pltpu.CompilerParams(vmem_limit_bytes=LIMIT << 20),
        cost_estimate=pl.CostEstimate(flops=flops, bytes_accessed=moved, transcendentals=0),
    )(*arrays)


def paired_experts(
    tokens, norm_gain, route_ids, route_weight, active_blocks, gate_weight, up_weight, down_weight
):
    exp_count, unit_count = lax.axis_size("exp"), lax.axis_size("unit")
    groups = unit_count // 2
    sizes = (exp_count, groups)
    tok_count, features = tokens.shape
    unit_width = gate_weight.shape[1]
    slots = exp_count * CAP
    half = features // 2
    width = half
    ids = route_ids.T
    weights = route_weight.T

    def shift(value, distance, group_shift=0):
        pairs = []
        for z in range(exp_count):
            for u in range(unit_count):
                target = (z + distance) % exp_count
                group = (u // 2 + group_shift) % groups
                pairs.append((z * unit_count + u, target * unit_count + group * 2 + u % 2))
        return lax.ppermute(value, ("exp", "unit"), pairs)

    def swap(value):
        return lax.ppermute(value, "unit", [(u, u ^ 1) for u in range(unit_count)])

    batch = exp_count - 1
    buffer = ((unit_width // BLOCK, BLOCK, BLOCK), BF16, pltpu.VMEM)
    piece_bytes = 2 * unit_width * BLOCK
    own, ready, *sends = call(
        functools.partial(route_kernel, sizes, width),
        [((CAP, features), BF16), buffer] + [((CAP, width), BF16)] * batch,
        [
            (tokens, pltpu.HBM),
            (norm_gain.reshape(1, -1), pltpu.HBM),
            (ids, pltpu.HBM),
            (gate_weight, pltpu.HBM),
        ],
        [
            pltpu.VMEM((tok_count, features), BF16),
            pltpu.VMEM((tok_count, features), BF16),
            pltpu.VMEM((1, features), F32),
            pltpu.VMEM(ids.shape, jnp.int32),
            pltpu.SemaphoreType.DMA((6,)),
            pltpu.SemaphoreType.DMA,
        ],
        flops=2 * tok_count * slots * width,
        moved=4 * tok_count * features + piece_bytes,
    )
    mask, *ready = call(
        functools.partial(prepare_kernel, sizes, tok_count),
        [((max(8, exp_count), unit_width), F32)] + [buffer] * BUFFERS,
        [
            (active_blocks, pltpu.HBM),
            (gate_weight, pltpu.HBM),
            (up_weight, pltpu.HBM),
            (own, pl.ANY),
            (ready, pltpu.VMEM),
        ],
        [
            pltpu.SMEM(active_blocks.shape, jnp.int32),
            pltpu.SemaphoreType.DMA,
            pltpu.SemaphoreType.DMA((READY,)),
        ],
        flops=2 * tok_count * slots * features,
        moved=(READY - 1) * piece_bytes,
        aliases={4: 1},
    )
    arrived = [shift(value, d + 1) for d, value in enumerate(sends)]
    mine = call(
        join_kernel,
        [((batch * CAP, width), BF16)],
        [(mask, pl.ANY)] + [(v, None) for v in arrived],
        moved=1 << 20,
    )[0]
    other = swap(mine)
    padded = -(-slots // 128) * 128
    combine_high, combine_low = call(
        functools.partial(table_kernel, sizes),
        [((2, tok_count, padded), BF16)] * 2,
        [(ids, pltpu.HBM), (weights, pltpu.HBM), (mine, pl.ANY)],
        [
            pltpu.VMEM(ids.shape, jnp.int32),
            pltpu.VMEM(weights.shape, F32),
            pltpu.SemaphoreType.DMA((2,)),
        ],
        moved=1 << 21,
    )
    acc = pltpu.VMEM((slots, unit_width), F32)
    part = features // unit_count
    hidden, first_given, *buffers = call(
        functools.partial(hidden_kernel, sizes),
        [((slots, unit_width), BF16), ((slots, part), BF16)] + [buffer] * BUFFERS,
        [(own, None), (mine, None), (other, None)]
        + [(v, pltpu.VMEM) for v in ready]
        + [(up_weight, pltpu.HBM), (down_weight, pltpu.HBM), (mask, None)]
        + [(combine_low, pl.ANY)],
        [
            acc,
            acc,
            pltpu.VMEM((slots, features), BF16),
            pltpu.SemaphoreType.DMA((BUFFERS,)),
        ],
        flops=2 * 2 * slots * features * unit_width,
        moved=10 * piece_bytes,
        aliases={3 + n: 2 + n for n in range(BUFFERS)},
    )
    steps = part // BLOCK
    offsets = [(order + 1) % groups for order in range(groups)]
    first = 2 * features // BLOCK + groups * steps
    given = [first_given]
    kept_weights = [[buffers[(first + step) % BUFFERS] for step in range(steps)]]
    for order, offset in list(enumerate(offsets))[1:]:
        first = 2 * features // BLOCK + order * steps
        value, *kept = call(
            functools.partial(give_kernel, sizes, offset),
            [((slots, part), BF16)] + [buffer] * steps,
            [(hidden, None)]
            + [(buffers[(first + step) % BUFFERS], pltpu.VMEM) for step in range(steps)]
            + [(down_weight, pltpu.HBM)],
            [pltpu.SemaphoreType.DMA((steps,))],
            flops=2 * slots * unit_width * part,
            moved=steps * piece_bytes,
        )
        given.append(value)
        kept_weights.append(kept)
    taken = [swap(value) for value in given]
    home = {}
    for order, offset in enumerate(offsets):
        kept = call(
            functools.partial(keep_kernel, sizes),
            [((CAP, part), BF16)] * exp_count,
            [(hidden, None), (taken[order], None)]
            + [(v, pltpu.VMEM) for v in kept_weights[order]],
            flops=2 * slots * unit_width * part,
            moved=piece_bytes,
        )
        for d in list(range(1, exp_count)) + [0]:
            home[offset, d] = shift(kept[d], -d, offset) if d or offset else kept[d]
    mixed = None
    for order, batch in enumerate(arrivals(sizes)):
        last = order == 1
        mixed = call(
            functools.partial(combine_kernel, order),
            [((tok_count, part), BF16 if last else F32)],
            [(combine_high, None), (combine_low, None)]
            + ([(mixed, None)] if order else [])
            + [(home[key], None) for key in batch],
            flops=4 * tok_count * slots * part,
            moved=1 << 20,
        )[0]
    return mixed


def per_device(*operands):
    tokens, gate_weight = operands[0], operands[5]
    exp_count, unit_count = lax.axis_size("exp"), lax.axis_size("unit")
    unit_width = gate_weight.shape[1]
    paired = (
        2 * unit_width == FF
        and unit_count % 2 == 0
        and exp_count * unit_count // 2 == EXPERTS
        and TILE % tokens.shape[0] == 0
        and unit_width % BLOCK == 0
        and unit_count == 4
        and tokens.shape[1] % (unit_count * BLOCK) == 0
        and tokens.shape[1] <= READY * BLOCK <= 2 * tokens.shape[1]
    )
    return (paired_experts if paired else spread_experts)(*operands)


def solution(mesh):
    return jax.shard_map(
        per_device,
        mesh=mesh,
        in_specs=(
            P(("rep", "exp"), None),
            P(),
            P(("rep", "exp"), None),
            P(("rep", "exp"), None),
            P("rep", None, None),
            P(None, ("exp", "unit")),
            P(None, ("exp", "unit")),
            P(("exp", "unit"), None),
        ),
        out_specs=P(("rep", "exp"), "unit"),
        check_vma=False,
    )
```

```python
import functools

import jax
import jax.numpy as jnp
import numpy as np
from jax import lax
from jax.experimental import pallas as pl
from jax.experimental.pallas import tpu as pltpu
from jax.sharding import PartitionSpec as P

EXPERTS = 8
FF = 7168
BLK = 64
TILE = 256
CAP = 40

EPSILON = 1e-05

BLOCK = 512
READY = 11
BUFFERS = 12
LIMIT = 8

F32 = jnp.float32
BF16 = jnp.bfloat16


def normalize(tokens, norm_gain):
    values = tokens.astype(jnp.float32)
    inv_rms = lax.rsqrt(jnp.mean(values * values, axis=-1, keepdims=True) + EPSILON)
    return (values * inv_rms * norm_gain).astype(jnp.bfloat16)


def slot_numbers(entries, expert_count):
    onehot = (entries[..., None] == jnp.arange(expert_count, dtype=jnp.int32)).astype(jnp.int32)
    before = jnp.cumsum(onehot, axis=-2, dtype=jnp.int32) - onehot
    return jnp.sum(before * onehot, axis=-1)


def spread_experts(
    tokens, norm_gain, route_ids, route_weight, active_blocks, gate_weight, up_weight, down_weight
):
    exp_count = lax.axis_size("exp")
    unit_count = lax.axis_size("unit")
    tok_count, feature_width = tokens.shape
    unit_width = gate_weight.shape[1]
    row_units = unit_count * unit_width
    per_exp = max(1, row_units // FF)
    part_width = feature_width // unit_count
    block_count = unit_width // BLK
    tile_count = active_blocks.shape[0]
    exp_index = lax.axis_index("exp")
    unit_index = lax.axis_index("unit")
    first_unit = (exp_index * unit_count + unit_index) * unit_width
    own_expert = first_unit // FF
    first_block = first_unit % FF // BLK
    local_expert = own_expert - exp_index * row_units // FF
    normed = normalize(tokens, norm_gain)
    slot_index = slot_numbers(route_ids.reshape(1, -1), EXPERTS).reshape(tok_count, 2)
    positions = jnp.arange(tok_count, dtype=jnp.int32)
    tile_of = (exp_index * tok_count + positions) // TILE
    route_slot = (route_ids * CAP + slot_index).reshape(-1)
    token_source = (
        jnp.full((EXPERTS * CAP,), tok_count, jnp.int32)
        .at[route_slot]
        .set(jnp.repeat(positions, 2))
    )
    row_experts = np.arange(exp_count)[:, None] * row_units // FF + np.arange(per_exp)[None, :]
    slot_source = token_source.reshape(EXPERTS, CAP)[row_experts]
    padded_tiles = jnp.concatenate([tile_of, jnp.zeros((1,), jnp.int32)])
    slot_tiles = padded_tiles[slot_source]
    active_mine = lax.dynamic_index_in_dim(active_blocks, own_expert, 1, keepdims=False)
    local_blocks = first_block + jnp.arange(block_count, dtype=jnp.int32)
    block_on = jnp.any(active_mine[:, :, None] == local_blocks[None, None, :], axis=1).astype(
        jnp.float32
    )
    row_part = lax.dynamic_slice_in_dim(normed, unit_index * part_width, part_width, 1)
    padded_rows = jnp.concatenate([row_part, jnp.zeros((1, part_width), jnp.bfloat16)], 0)
    whole_rows = lax.all_gather(
        lax.all_to_all(padded_rows[slot_source], "exp", split_axis=0, concat_axis=0, tiled=True),
        "unit",
        axis=3,
        tiled=True,
    )
    slot_count = whole_rows.shape[2]
    own_rows = lax.dynamic_index_in_dim(whole_rows, local_expert, 1, keepdims=False).reshape(
        -1, feature_width
    )
    own_tiles = lax.dynamic_index_in_dim(
        lax.all_to_all(slot_tiles, "exp", split_axis=0, concat_axis=0, tiled=True),
        local_expert,
        1,
        keepdims=False,
    ).reshape(-1)
    tile_hot = (own_tiles[:, None] == jnp.arange(tile_count, dtype=jnp.int32)[None, :]).astype(
        jnp.float32
    )
    row_mask = jnp.dot(tile_hot, block_on, precision=lax.Precision.HIGHEST)
    gate_acts = jnp.dot(own_rows, gate_weight, preferred_element_type=jnp.float32)
    up_acts = jnp.dot(own_rows, up_weight, preferred_element_type=jnp.float32)
    hidden = jax.nn.relu(gate_acts) * jax.nn.relu(up_acts)
    hidden = (hidden.reshape(-1, block_count, BLK) * row_mask[:, :, None]).reshape(-1, unit_width)
    hidden = hidden.astype(jnp.bfloat16)
    partial_value = jnp.dot(hidden, down_weight, preferred_element_type=jnp.float32)
    partial_value = partial_value.reshape(exp_count, slot_count, feature_width)
    result = jnp.zeros((exp_count, per_exp, slot_count, feature_width), jnp.float32)
    partial_all = lax.dynamic_update_index_in_dim(result, partial_value, local_expert, 1)

    def by_expert(returned):
        last_width = returned.shape[-1]
        if per_exp == 1:
            grouped = returned.reshape(EXPERTS, exp_count // EXPERTS, CAP, last_width)
            return jnp.sum(grouped, axis=1, dtype=jnp.float32)
        return returned.reshape(EXPERTS, CAP, last_width).astype(jnp.float32)

    summed = lax.psum_scatter(
        partial_all.astype(jnp.bfloat16), "unit", scatter_dimension=3, tiled=True
    ).astype(jnp.float32)
    returned = lax.all_to_all(
        summed.astype(jnp.bfloat16), "exp", split_axis=0, concat_axis=0, tiled=True
    ).astype(summed.dtype)
    per_expert = by_expert(returned)
    last_width = per_expert.shape[-1]
    picked = per_expert.reshape(EXPERTS * CAP, last_width)[route_slot].reshape(
        tok_count, 2, last_width
    )
    mixed = jnp.sum(route_weight[:, :, None] * picked, axis=1)
    return mixed.astype(jnp.bfloat16)


def place(sizes):
    exp_count, groups = sizes
    return lax.axis_index("exp"), lax.axis_index("unit") // 2, lax.axis_index("unit") % 2


def pick_rows(named, before, d):
    rows = named.shape[1]
    place_of = jnp.where(named[d : d + 1, :] > 0, before[d : d + 1, :], -1)
    return (place_of == lax.broadcasted_iota(jnp.int32, (CAP, rows), 0)).astype(F32)


def count_earlier(ids, experts):
    rows = ids.shape[1]
    earlier = (
        lax.broadcasted_iota(jnp.int32, (rows, rows), 0)
        < lax.broadcasted_iota(jnp.int32, (rows, rows), 1)
    ).astype(BF16)
    named = ((ids[0:1, :] == experts) | (ids[1:2, :] == experts)).astype(jnp.int32)
    before = jnp.dot(named.astype(BF16), earlier, preferred_element_type=F32)
    return named, before.astype(jnp.int32)


def group_experts(exp_count, groups, z, g, rows):
    distance = lax.broadcasted_iota(jnp.int32, (max(8, exp_count), rows), 0)
    return lax.rem(z + distance, exp_count) * groups + g


def fetch_rows(weight, line, buffer, sem):
    def start(index, carry):
        pltpu.make_async_copy(
            weight.at[
                pl.ds(line * BLOCK, BLOCK), pl.ds(pl.multiple_of(index * BLOCK, BLOCK), BLOCK)
            ],
            buffer.at[index],
            sem,
        ).start()
        return carry

    lax.fori_loop(0, buffer.shape[0], start, 0)


def fetch_columns(sizes, down, offset, keep, step, buffer, sem):
    exp_count, groups = sizes
    z, g, s = place(sizes)
    side = s if keep else 1 - s
    part = down.shape[1] // (2 * groups)
    column = (lax.rem(g + offset, groups) * 2 + side) * part + step * BLOCK

    def start(index, carry):
        pltpu.make_async_copy(
            down.at[
                pl.ds(pl.multiple_of(index * BLOCK, BLOCK), BLOCK),
                pl.ds(pl.multiple_of(column, BLOCK), BLOCK),
            ],
            buffer.at[index],
            sem,
        ).start()
        return carry

    lax.fori_loop(0, buffer.shape[0], start, 0)


def await_all(buffer, sem):
    pltpu.make_async_copy(buffer, buffer, sem).wait()


def stacked(buffer):
    return buffer[...].reshape(buffer.shape[0] * BLOCK, BLOCK)


def route_kernel(sizes, width, tokens_hbm, gain_hbm, ids_hbm, gate, own, buffer, *rest):
    exp_count, groups = sizes
    sends, (tokens, normed, gain, ids, sems, gate_sem) = rest[:-6], rest[-6:]
    rows, features = tokens.shape
    count = 4
    lines = [pl.ds(n * (rows // count), rows // count) for n in range(count)]
    pairs = [(gain_hbm, gain), (ids_hbm, ids)]
    pairs += [(tokens_hbm.at[part, :], tokens.at[part, :]) for part in lines]
    copies = [pltpu.make_async_copy(a, b, sems.at[n]) for n, (a, b) in enumerate(pairs)]
    for copy in copies:
        copy.start()
    fetch_rows(gate, 0, buffer, gate_sem)
    z, g, s = place(sizes)
    copies[0].wait()
    copies[1].wait()
    named, before = count_earlier(ids, group_experts(exp_count, groups, z, g, rows))
    picks = [pick_rows(named, before, d) for d in range(exp_count)]
    others = jnp.concatenate(picks[1:], axis=0).astype(BF16)
    step = 16
    for first in range(0, rows, step):
        if first % (rows // count) == 0:
            copies[2 + first // (rows // count)].wait()
        values = tokens[first : first + step, :].astype(F32)
        mean = jnp.sum(values * values, axis=1, keepdims=True) * (1.0 / features)
        inv_rms = lax.rsqrt(mean + EPSILON)
        normed[first : first + step, :] = (values * inv_rms * gain[...]).astype(BF16)
    start = pl.multiple_of(s * (features // 2), 128)
    found = jnp.dot(others, normed[:, pl.ds(start, width)], preferred_element_type=F32)
    for d, send in enumerate(sends):
        send[...] = found[d * CAP : (d + 1) * CAP, :].astype(BF16)
    own[...] = jnp.dot(
        picks[0].astype(BF16), normed[...], preferred_element_type=F32
    ).astype(BF16)
    await_all(buffer, gate_sem)


def distances(exp_count):
    middle = exp_count // 2
    return [middle] + [d for d in range(1, exp_count) if d != middle]


def arrivals(sizes):
    exp_count, groups = sizes
    order = distances(exp_count) + [0]
    early = [(o, d) for o in range(1, groups) for d in order]
    late = [(0, d) for d in order]
    return early, late


def table_kernel(sizes, ids_hbm, weights_hbm, after, combine_high, combine_low, ids, weights, sems):
    exp_count, groups = sizes
    pairs = ((ids_hbm, ids), (weights_hbm, weights))
    copies = [pltpu.make_async_copy(a, b, sems.at[n]) for n, (a, b) in enumerate(pairs)]
    for copy in copies:
        copy.start()
    for copy in copies:
        copy.wait()
    rows = ids.shape[1]
    z, g, s = place(sizes)
    zero = jnp.zeros((CAP, rows), F32)
    padded = combine_high.shape[2]
    batches = arrivals(sizes)
    experts = [
        lax.rem(z + d, exp_count) * groups + lax.rem(g - o + groups, groups)
        for batch in batches
        for o, d in batch
    ]
    line = lax.broadcasted_iota(jnp.int32, (max(8, len(experts)), rows), 0)
    listed = jnp.full(line.shape, -1, jnp.int32)
    for n, expert in enumerate(experts):
        listed = jnp.where(line == n, expert, listed)
    named, before = count_earlier(ids, listed)
    for order, batch in enumerate(batches):
        parts = []
        for n in range(len(batch)):
            entry = order * len(batch) + n
            here = pick_rows(named, before, entry) > 0
            first = jnp.where(here & (ids[0:1, :] == experts[entry]), weights[0:1, :], zero)
            second = jnp.where(here & (ids[1:2, :] == experts[entry]), weights[1:2, :], zero)
            parts.append(first + second)
        if padded > len(batch) * CAP:
            parts.append(jnp.zeros((padded - len(batch) * CAP, rows), F32))
        table = jnp.concatenate(parts, axis=0).T
        high = table.astype(BF16)
        combine_high[order] = high
        combine_low[order] = (table - high.astype(F32)).astype(BF16)


def prepare_kernel(sizes, rows, active_hbm, gate, up, after, _, mask, *rest):
    exp_count, groups = sizes
    *buffers, active, small_sem, sems = rest
    z, g, s = place(sizes)
    small = pltpu.make_async_copy(active_hbm, active, small_sem)
    small.start()
    lines = gate.shape[0] // BLOCK
    for n, buffer in enumerate(buffers[1:READY], 1):
        fetch_rows(gate if n < lines else up, n % lines, buffer, sems.at[n])
    small.wait()
    unit_width = mask.shape[1]
    blocks = lax.broadcasted_iota(jnp.int32, mask.shape, 1) // BLK + s * (unit_width // BLK)
    source = lax.broadcasted_iota(jnp.int32, (mask.shape[0], 1), 0)
    own_expert = z * groups + g

    def add_entry(k, found):
        entry = jnp.full((mask.shape[0], 1), -1, jnp.int32)
        for d in range(exp_count):
            tile = lax.rem(z - d + exp_count, exp_count) * rows // TILE
            entry = jnp.where(source == d, active[tile, own_expert, k], entry)
        return jnp.where(blocks == entry, 1.0, found)

    mask[...] = lax.fori_loop(0, active.shape[2], add_entry, jnp.zeros(mask.shape, F32))
    for n, buffer in enumerate(buffers[1:READY], 1):
        await_all(buffer, sems.at[n])


def join_kernel(order, after, *refs):
    pieces = [refs[order.index(d + 1)][...].astype(F32) for d in range(len(order))]
    refs[-1][...] = jnp.concatenate(pieces, axis=0).astype(BF16)


def hidden_kernel(sizes, own, mine, other, *refs):
    exp_count, groups = sizes
    z, g, s = place(sizes)
    refs = list(refs)
    refs = refs[BUFFERS:]
    up, down, mask, _, hidden, gives = [refs.pop(0) for _ in range(6)]
    buffers = [refs.pop(0) for _ in range(BUFFERS)]
    gate_sum, up_sum, rows, sems = refs
    half = own.shape[1] // 2
    features, unit_width = up.shape
    columns, lines = unit_width // BLOCK, features // BLOCK
    given = features // (2 * groups) // BLOCK
    count = len(buffers)

    def fetch(index):
        buffer, sem = buffers[index % count], sems.at[index % count]
        if index < 2 * lines:
            fetch_rows(up, index - lines, buffer, sem)
        elif index < 2 * lines + groups * given:
            order, step = divmod(index - 2 * lines, given)
            fetch_columns(sizes, down, order + 1, False, step, buffer, sem)
        elif index < 2 * lines + (groups + 1) * given:
            step = index - 2 * lines - groups * given
            fetch_columns(sizes, down, 1, True, step, buffer, sem)

    for index in range(READY, count):
        fetch(index)
    for source, side in ((mine, s), (other, 1 - s)):
        cols = pl.ds(pl.multiple_of(side * half, 128), half)
        joined = [own[:, cols].astype(F32), source[...].astype(F32)]
        rows[:, cols] = jnp.concatenate(joined, axis=0).astype(BF16)
    for index in range(0, 2 * lines, 2):
        pair = [buffers[(index + n) % count] for n in range(2)]
        for n in range(2):
            if index + n >= READY:
                await_all(pair[n], sems.at[(index + n) % count])
        line = index % lines
        total = gate_sum if index < lines else up_sum
        left = [rows[:, (line + n) * BLOCK : (line + n + 1) * BLOCK] for n in range(2)]
        for column in range(columns):
            cols = slice(column * BLOCK, (column + 1) * BLOCK)
            value = jnp.dot(left[0], pair[0][column], preferred_element_type=F32)
            value = value + jnp.dot(left[1], pair[1][column], preferred_element_type=F32)
            if line > 0:
                value = total[:, cols] + value
            if index < 2 * lines - 2:
                total[:, cols] = value
                continue
            value = jnp.maximum(gate_sum[:, cols], 0.0) * jnp.maximum(value, 0.0)
            parts = []
            for d in range(exp_count):
                parts.append(value[d * CAP : (d + 1) * CAP, :] * mask[d : d + 1, cols])
            hidden[:, cols] = jnp.concatenate(parts, axis=0).astype(BF16)
        for n in range(2):
            fetch(index + n + count)
    for index in range(2 * lines, 2 * lines + (groups + 1) * given):
        buffer = buffers[index % count]
        await_all(buffer, sems.at[index % count])
        step = index - 2 * lines
        if step < given:
            value = jnp.dot(hidden[...], stacked(buffer), preferred_element_type=F32)
            gives[:, step * BLOCK : (step + 1) * BLOCK] = value.astype(BF16)


def give_kernel(sizes, offset, hidden, *refs):
    exp_count, groups = sizes
    *weights, down, given, kept_weights, sem = refs
    fetch_columns(sizes, down, offset, True, 0, kept_weights, sem)
    for step, buffer in enumerate(weights):
        value = jnp.dot(hidden[...], stacked(buffer), preferred_element_type=F32)
        given[:, step * BLOCK : (step + 1) * BLOCK] = value.astype(BF16)
    await_all(kept_weights, sem)


def keep_kernel(sizes, ahead, hidden, received, *refs):
    exp_count, groups = sizes
    refs = list(refs)
    if ahead is not None:
        sem, down = refs.pop(), refs.pop(0)
        next_weights = refs[received.shape[1] // BLOCK + exp_count :]
        for step, buffer in enumerate(next_weights, 1):
            fetch_columns(sizes, down, ahead, True, step, buffer, sem.at[step - 1])
    weights = refs[: received.shape[1] // BLOCK]
    outs = refs[len(weights) : len(weights) + exp_count]
    for step, buffer in enumerate(weights):
        cols = slice(step * BLOCK, (step + 1) * BLOCK)
        value = jnp.dot(hidden[...], stacked(buffer), preferred_element_type=F32)
        value = value + received[:, cols].astype(F32)
        for d in range(exp_count):
            outs[d][:, cols] = value[d * CAP : (d + 1) * CAP, :].astype(BF16)
    if ahead is not None:
        for step, buffer in enumerate(next_weights, 1):
            await_all(buffer, sem.at[step - 1])


def combine_kernel(order, high, low, *refs):
    refs = list(refs)
    out = refs.pop()
    before = refs.pop(0) if order > 0 else None
    found = jnp.concatenate([r[...].astype(F32) for r in refs], axis=0).astype(BF16)
    count = found.shape[0]
    value = jnp.dot(high[order, :, :count], found, preferred_element_type=F32)
    value = value + jnp.dot(low[order, :, :count], found, preferred_element_type=F32)
    if before is not None:
        value = before[...] + value
    out[...] = value.astype(out.dtype)


def call(kernel, outs, ins, scratch=(), flops=0, moved=0, aliases=None):
    vmem = pl.BlockSpec(memory_space=pltpu.VMEM)
    arrays, specs = [], []
    for array, space in ins:
        if space in (pltpu.HBM, pltpu.VMEM):
            array = pltpu.with_memory_space_constraint(array, space)
        arrays.append(array)
        specs.append(vmem if space is None else pl.BlockSpec(memory_space=space))
    shapes = []
    for shape, kind, *space in outs:
        shapes.append(space[0](shape, kind) if space else jax.ShapeDtypeStruct(shape, kind))
    return pl.pallas_call(
        kernel,
        out_shape=shapes,
        in_specs=specs,
        out_specs=[vmem] * len(outs),
        scratch_shapes=list(scratch),
        input_output_aliases=aliases or {},
        compiler_params=pltpu.CompilerParams(vmem_limit_bytes=LIMIT << 20),
        cost_estimate=pl.CostEstimate(flops=flops, bytes_accessed=moved, transcendentals=0),
    )(*arrays)


def paired_experts(
    tokens, norm_gain, route_ids, route_weight, active_blocks, gate_weight, up_weight, down_weight
):
    exp_count, unit_count = lax.axis_size("exp"), lax.axis_size("unit")
    groups = unit_count // 2
    sizes = (exp_count, groups)
    tok_count, features = tokens.shape
    unit_width = gate_weight.shape[1]
    slots = exp_count * CAP
    half = features // 2
    width = half
    ids = route_ids.T
    weights = route_weight.T

    def shift(value, distance, group_shift=0):
        pairs = []
        for z in range(exp_count):
            for u in range(unit_count):
                target = (z + distance) % exp_count
                group = (u // 2 + group_shift) % groups
                pairs.append((z * unit_count + u, target * unit_count + group * 2 + u % 2))
        return lax.ppermute(value, ("exp", "unit"), pairs)

    def swap(value):
        return lax.ppermute(value, "unit", [(u, u ^ 1) for u in range(unit_count)])

    batch = exp_count - 1
    buffer = ((unit_width // BLOCK, BLOCK, BLOCK), BF16, pltpu.VMEM)
    piece_bytes = 2 * unit_width * BLOCK
    own, ready, *sends = call(
        functools.partial(route_kernel, sizes, width),
        [((CAP, features), BF16), buffer] + [((CAP, width), BF16)] * batch,
        [
            (tokens, pltpu.HBM),
            (norm_gain.reshape(1, -1), pltpu.HBM),
            (ids, pltpu.HBM),
            (gate_weight, pltpu.HBM),
        ],
        [
            pltpu.VMEM((tok_count, features), BF16),
            pltpu.VMEM((tok_count, features), BF16),
            pltpu.VMEM((1, features), F32),
            pltpu.VMEM(ids.shape, jnp.int32),
            pltpu.SemaphoreType.DMA((6,)),
            pltpu.SemaphoreType.DMA,
        ],
        flops=2 * tok_count * slots * width,
        moved=4 * tok_count * features + piece_bytes,
    )
    mask, *ready = call(
        functools.partial(prepare_kernel, sizes, tok_count),
        [((max(8, exp_count), unit_width), F32)] + [buffer] * BUFFERS,
        [
            (active_blocks, pltpu.HBM),
            (gate_weight, pltpu.HBM),
            (up_weight, pltpu.HBM),
            (own, pl.ANY),
            (ready, pltpu.VMEM),
        ],
        [
            pltpu.SMEM(active_blocks.shape, jnp.int32),
            pltpu.SemaphoreType.DMA,
            pltpu.SemaphoreType.DMA((READY,)),
        ],
        flops=2 * tok_count * slots * features,
        moved=(READY - 1) * piece_bytes,
        aliases={4: 1},
    )
    arrived = [shift(sends[d - 1], d) for d in distances(exp_count)]
    mine = call(
        functools.partial(join_kernel, distances(exp_count)),
        [((batch * CAP, width), BF16)],
        [(mask, pl.ANY)] + [(v, None) for v in arrived],
        moved=1 << 20,
    )[0]
    other = swap(mine)
    padded = -(-slots // 128) * 128
    combine_high, combine_low = call(
        functools.partial(table_kernel, sizes),
        [((2, tok_count, padded), BF16)] * 2,
        [(ids, pltpu.HBM), (weights, pltpu.HBM), (mine, pl.ANY)],
        [
            pltpu.VMEM(ids.shape, jnp.int32),
            pltpu.VMEM(weights.shape, F32),
            pltpu.SemaphoreType.DMA((2,)),
        ],
        moved=1 << 21,
    )
    acc = pltpu.VMEM((slots, unit_width), F32)
    part = features // unit_count
    hidden, first_given, *buffers = call(
        functools.partial(hidden_kernel, sizes),
        [((slots, unit_width), BF16), ((slots, part), BF16)] + [buffer] * BUFFERS,
        [(own, None), (mine, None), (other, None)]
        + [(v, pltpu.VMEM) for v in ready]
        + [(up_weight, pltpu.HBM), (down_weight, pltpu.HBM), (mask, None)]
        + [(combine_low, pl.ANY)],
        [
            acc,
            acc,
            pltpu.VMEM((slots, features), BF16),
            pltpu.SemaphoreType.DMA((BUFFERS,)),
        ],
        flops=2 * 2 * slots * features * unit_width,
        moved=10 * piece_bytes,
        aliases={3 + n: 2 + n for n in range(BUFFERS)},
    )
    steps = part // BLOCK
    offsets = [(order + 1) % groups for order in range(groups)]
    first = 2 * features // BLOCK + groups * steps
    given = [first_given]
    kept_weights = [[buffers[(first + step) % BUFFERS] for step in range(steps)]]
    for order, offset in list(enumerate(offsets))[1:]:
        first = 2 * features // BLOCK + order * steps
        value, *kept = call(
            functools.partial(give_kernel, sizes, offset),
            [((slots, part), BF16), buffer],
            [(hidden, None)]
            + [(buffers[(first + step) % BUFFERS], pltpu.VMEM) for step in range(steps)]
            + [(down_weight, pltpu.HBM)],
            [pltpu.SemaphoreType.DMA],
            flops=2 * slots * unit_width * part,
            moved=piece_bytes,
        )
        given.append(value)
        kept_weights.append(kept)
    taken = [swap(value) for value in given]
    home = {}
    for order, offset in enumerate(offsets):
        more = order < groups - 1
        outs = call(
            functools.partial(keep_kernel, sizes, offsets[order + 1] if more else None),
            [((CAP, part), BF16)] * exp_count + [buffer] * (steps - 1 if more else 0),
            [(hidden, None), (taken[order], None)]
            + ([(down_weight, pltpu.HBM)] if more else [])
            + [(v, pltpu.VMEM) for v in kept_weights[order]],
            [pltpu.SemaphoreType.DMA((steps - 1,))] if more else [],
            flops=2 * slots * unit_width * part,
            moved=piece_bytes,
        )
        kept = outs[:exp_count]
        if more:
            kept_weights[order + 1] = list(kept_weights[order + 1]) + list(outs[exp_count:])
        for d in distances(exp_count) + [0]:
            home[offset, d] = shift(kept[d], -d, offset) if d or offset else kept[d]
    mixed = None
    for order, batch in enumerate(arrivals(sizes)):
        last = order == 1
        mixed = call(
            functools.partial(combine_kernel, order),
            [((tok_count, part), BF16 if last else F32)],
            [(combine_high, None), (combine_low, None)]
            + ([(mixed, None)] if order else [])
            + [(home[key], None) for key in batch],
            flops=4 * tok_count * slots * part,
            moved=1 << 20,
        )[0]
    return mixed


def per_device(*operands):
    tokens, gate_weight = operands[0], operands[5]
    exp_count, unit_count = lax.axis_size("exp"), lax.axis_size("unit")
    unit_width = gate_weight.shape[1]
    paired = (
        2 * unit_width == FF
        and unit_count % 2 == 0
        and exp_count * unit_count // 2 == EXPERTS
        and TILE % tokens.shape[0] == 0
        and unit_width % BLOCK == 0
        and unit_count == 4
        and tokens.shape[1] % (unit_count * BLOCK) == 0
        and tokens.shape[1] <= READY * BLOCK <= 2 * tokens.shape[1]
    )
    return (paired_experts if paired else spread_experts)(*operands)


def solution(mesh):
    return jax.shard_map(
        per_device,
        mesh=mesh,
        in_specs=(
            P(("rep", "exp"), None),
            P(),
            P(("rep", "exp"), None),
            P(("rep", "exp"), None),
            P("rep", None, None),
            P(None, ("exp", "unit")),
            P(None, ("exp", "unit")),
            P(("exp", "unit"), None),
        ),
        out_specs=P(("rep", "exp"), "unit"),
        check_vma=False,
    )
```

```python
import functools

import jax
import jax.numpy as jnp
import numpy as np
from jax import lax
from jax.experimental import pallas as pl
from jax.experimental.pallas import tpu as pltpu
from jax.sharding import PartitionSpec as P

EXPERTS = 8
FF = 7168
BLK = 64
TILE = 256
CAP = 40

EPSILON = 1e-05

BLOCK = 512
READY = 11
BUFFERS = 12
LIMIT = 8

F32 = jnp.float32
BF16 = jnp.bfloat16


def normalize(tokens, norm_gain):
    values = tokens.astype(jnp.float32)
    inv_rms = lax.rsqrt(jnp.mean(values * values, axis=-1, keepdims=True) + EPSILON)
    return (values * inv_rms * norm_gain).astype(jnp.bfloat16)


def slot_numbers(entries, expert_count):
    onehot = (entries[..., None] == jnp.arange(expert_count, dtype=jnp.int32)).astype(jnp.int32)
    before = jnp.cumsum(onehot, axis=-2, dtype=jnp.int32) - onehot
    return jnp.sum(before * onehot, axis=-1)


def spread_experts(
    tokens, norm_gain, route_ids, route_weight, active_blocks, gate_weight, up_weight, down_weight
):
    exp_count = lax.axis_size("exp")
    unit_count = lax.axis_size("unit")
    tok_count, feature_width = tokens.shape
    unit_width = gate_weight.shape[1]
    row_units = unit_count * unit_width
    per_exp = max(1, row_units // FF)
    part_width = feature_width // unit_count
    block_count = unit_width // BLK
    tile_count = active_blocks.shape[0]
    exp_index = lax.axis_index("exp")
    unit_index = lax.axis_index("unit")
    first_unit = (exp_index * unit_count + unit_index) * unit_width
    own_expert = first_unit // FF
    first_block = first_unit % FF // BLK
    local_expert = own_expert - exp_index * row_units // FF
    normed = normalize(tokens, norm_gain)
    slot_index = slot_numbers(route_ids.reshape(1, -1), EXPERTS).reshape(tok_count, 2)
    positions = jnp.arange(tok_count, dtype=jnp.int32)
    tile_of = (exp_index * tok_count + positions) // TILE
    route_slot = (route_ids * CAP + slot_index).reshape(-1)
    token_source = (
        jnp.full((EXPERTS * CAP,), tok_count, jnp.int32)
        .at[route_slot]
        .set(jnp.repeat(positions, 2))
    )
    row_experts = np.arange(exp_count)[:, None] * row_units // FF + np.arange(per_exp)[None, :]
    slot_source = token_source.reshape(EXPERTS, CAP)[row_experts]
    padded_tiles = jnp.concatenate([tile_of, jnp.zeros((1,), jnp.int32)])
    slot_tiles = padded_tiles[slot_source]
    active_mine = lax.dynamic_index_in_dim(active_blocks, own_expert, 1, keepdims=False)
    local_blocks = first_block + jnp.arange(block_count, dtype=jnp.int32)
    block_on = jnp.any(active_mine[:, :, None] == local_blocks[None, None, :], axis=1).astype(
        jnp.float32
    )
    row_part = lax.dynamic_slice_in_dim(normed, unit_index * part_width, part_width, 1)
    padded_rows = jnp.concatenate([row_part, jnp.zeros((1, part_width), jnp.bfloat16)], 0)
    whole_rows = lax.all_gather(
        lax.all_to_all(padded_rows[slot_source], "exp", split_axis=0, concat_axis=0, tiled=True),
        "unit",
        axis=3,
        tiled=True,
    )
    slot_count = whole_rows.shape[2]
    own_rows = lax.dynamic_index_in_dim(whole_rows, local_expert, 1, keepdims=False).reshape(
        -1, feature_width
    )
    own_tiles = lax.dynamic_index_in_dim(
        lax.all_to_all(slot_tiles, "exp", split_axis=0, concat_axis=0, tiled=True),
        local_expert,
        1,
        keepdims=False,
    ).reshape(-1)
    tile_hot = (own_tiles[:, None] == jnp.arange(tile_count, dtype=jnp.int32)[None, :]).astype(
        jnp.float32
    )
    row_mask = jnp.dot(tile_hot, block_on, precision=lax.Precision.HIGHEST)
    gate_acts = jnp.dot(own_rows, gate_weight, preferred_element_type=jnp.float32)
    up_acts = jnp.dot(own_rows, up_weight, preferred_element_type=jnp.float32)
    hidden = jax.nn.relu(gate_acts) * jax.nn.relu(up_acts)
    hidden = (hidden.reshape(-1, block_count, BLK) * row_mask[:, :, None]).reshape(-1, unit_width)
    hidden = hidden.astype(jnp.bfloat16)
    partial_value = jnp.dot(hidden, down_weight, preferred_element_type=jnp.float32)
    partial_value = partial_value.reshape(exp_count, slot_count, feature_width)
    result = jnp.zeros((exp_count, per_exp, slot_count, feature_width), jnp.float32)
    partial_all = lax.dynamic_update_index_in_dim(result, partial_value, local_expert, 1)

    def by_expert(returned):
        last_width = returned.shape[-1]
        if per_exp == 1:
            grouped = returned.reshape(EXPERTS, exp_count // EXPERTS, CAP, last_width)
            return jnp.sum(grouped, axis=1, dtype=jnp.float32)
        return returned.reshape(EXPERTS, CAP, last_width).astype(jnp.float32)

    summed = lax.psum_scatter(
        partial_all.astype(jnp.bfloat16), "unit", scatter_dimension=3, tiled=True
    ).astype(jnp.float32)
    returned = lax.all_to_all(
        summed.astype(jnp.bfloat16), "exp", split_axis=0, concat_axis=0, tiled=True
    ).astype(summed.dtype)
    per_expert = by_expert(returned)
    last_width = per_expert.shape[-1]
    picked = per_expert.reshape(EXPERTS * CAP, last_width)[route_slot].reshape(
        tok_count, 2, last_width
    )
    mixed = jnp.sum(route_weight[:, :, None] * picked, axis=1)
    return mixed.astype(jnp.bfloat16)


def place(sizes):
    exp_count, groups = sizes
    return lax.axis_index("exp"), lax.axis_index("unit") // 2, lax.axis_index("unit") % 2


def pick_rows(named, before, d):
    rows = named.shape[1]
    place_of = jnp.where(named[d : d + 1, :] > 0, before[d : d + 1, :], -1)
    return (place_of == lax.broadcasted_iota(jnp.int32, (CAP, rows), 0)).astype(F32)


def count_earlier(ids, experts):
    rows = ids.shape[1]
    earlier = (
        lax.broadcasted_iota(jnp.int32, (rows, rows), 0)
        < lax.broadcasted_iota(jnp.int32, (rows, rows), 1)
    ).astype(BF16)
    named = ((ids[0:1, :] == experts) | (ids[1:2, :] == experts)).astype(jnp.int32)
    before = jnp.dot(named.astype(BF16), earlier, preferred_element_type=F32)
    return named, before.astype(jnp.int32)


def group_experts(exp_count, groups, z, g, rows):
    distance = lax.broadcasted_iota(jnp.int32, (max(8, exp_count), rows), 0)
    return lax.rem(z + distance, exp_count) * groups + g


def fetch_rows(weight, line, buffer, sem):
    def start(index, carry):
        pltpu.make_async_copy(
            weight.at[
                pl.ds(line * BLOCK, BLOCK), pl.ds(pl.multiple_of(index * BLOCK, BLOCK), BLOCK)
            ],
            buffer.at[index],
            sem,
        ).start()
        return carry

    lax.fori_loop(0, buffer.shape[0], start, 0)


def fetch_columns(sizes, down, offset, keep, step, buffer, sem):
    exp_count, groups = sizes
    z, g, s = place(sizes)
    side = s if keep else 1 - s
    part = down.shape[1] // (2 * groups)
    column = (lax.rem(g + offset, groups) * 2 + side) * part + step * BLOCK

    def start(index, carry):
        pltpu.make_async_copy(
            down.at[
                pl.ds(pl.multiple_of(index * BLOCK, BLOCK), BLOCK),
                pl.ds(pl.multiple_of(column, BLOCK), BLOCK),
            ],
            buffer.at[index],
            sem,
        ).start()
        return carry

    lax.fori_loop(0, buffer.shape[0], start, 0)


def await_all(buffer, sem):
    pltpu.make_async_copy(buffer, buffer, sem).wait()


def stacked(buffer):
    return buffer[...].reshape(buffer.shape[0] * BLOCK, BLOCK)


def route_kernel(sizes, width, tokens_hbm, gain_hbm, ids_hbm, gate, own, buffer, *rest):
    exp_count, groups = sizes
    sends, (tokens, normed, gain, ids, sems, gate_sem) = rest[:-6], rest[-6:]
    rows, features = tokens.shape
    count = 4
    lines = [pl.ds(n * (rows // count), rows // count) for n in range(count)]
    pairs = [(gain_hbm, gain), (ids_hbm, ids)]
    pairs += [(tokens_hbm.at[part, :], tokens.at[part, :]) for part in lines]
    copies = [pltpu.make_async_copy(a, b, sems.at[n]) for n, (a, b) in enumerate(pairs)]
    for copy in copies:
        copy.start()
    fetch_rows(gate, 0, buffer, gate_sem)
    z, g, s = place(sizes)
    copies[0].wait()
    copies[1].wait()
    named, before = count_earlier(ids, group_experts(exp_count, groups, z, g, rows))
    picks = [pick_rows(named, before, d) for d in range(exp_count)]
    others = jnp.concatenate(picks[1:], axis=0).astype(BF16)
    step = 16
    for first in range(0, rows, step):
        if first % (rows // count) == 0:
            copies[2 + first // (rows // count)].wait()
        values = tokens[first : first + step, :].astype(F32)
        mean = jnp.sum(values * values, axis=1, keepdims=True) * (1.0 / features)
        inv_rms = lax.rsqrt(mean + EPSILON)
        normed[first : first + step, :] = (values * inv_rms * gain[...]).astype(BF16)
    start = pl.multiple_of(s * (features // 2), 128)
    found = jnp.dot(others, normed[:, pl.ds(start, width)], preferred_element_type=F32)
    for d, send in enumerate(sends):
        send[...] = found[d * CAP : (d + 1) * CAP, :].astype(BF16)
    own[...] = jnp.dot(
        picks[0].astype(BF16), normed[...], preferred_element_type=F32
    ).astype(BF16)
    await_all(buffer, gate_sem)


def distances(exp_count):
    middle = exp_count // 2
    return [middle] + [d for d in range(1, exp_count) if d != middle]


def arrivals(sizes):
    exp_count, groups = sizes
    order = distances(exp_count) + [0]
    early = [(o, d) for o in range(1, groups) for d in order]
    late = [(0, d) for d in order]
    return early, late


def table_kernel(
    sizes, ids_hbm, weights_hbm, after, gate, up, _, combine_high, combine_low, buffer, ids, weights,
    sems, sem
):
    exp_count, groups = sizes
    lines = gate.shape[0] // BLOCK
    last = READY - 1
    fetch_rows(gate if last < lines else up, last % lines, buffer, sem)
    pairs = ((ids_hbm, ids), (weights_hbm, weights))
    copies = [pltpu.make_async_copy(a, b, sems.at[n]) for n, (a, b) in enumerate(pairs)]
    for copy in copies:
        copy.start()
    for copy in copies:
        copy.wait()
    rows = ids.shape[1]
    z, g, s = place(sizes)
    zero = jnp.zeros((CAP, rows), F32)
    padded = combine_high.shape[2]
    batches = arrivals(sizes)
    experts = [
        lax.rem(z + d, exp_count) * groups + lax.rem(g - o + groups, groups)
        for batch in batches
        for o, d in batch
    ]
    line = lax.broadcasted_iota(jnp.int32, (max(8, len(experts)), rows), 0)
    listed = jnp.full(line.shape, -1, jnp.int32)
    for n, expert in enumerate(experts):
        listed = jnp.where(line == n, expert, listed)
    named, before = count_earlier(ids, listed)
    for order, batch in enumerate(batches):
        parts = []
        for n in range(len(batch)):
            entry = order * len(batch) + n
            here = pick_rows(named, before, entry) > 0
            first = jnp.where(here & (ids[0:1, :] == experts[entry]), weights[0:1, :], zero)
            second = jnp.where(here & (ids[1:2, :] == experts[entry]), weights[1:2, :], zero)
            parts.append(first + second)
        if padded > len(batch) * CAP:
            parts.append(jnp.zeros((padded - len(batch) * CAP, rows), F32))
        table = jnp.concatenate(parts, axis=0).T
        high = table.astype(BF16)
        combine_high[order] = high
        combine_low[order] = (table - high.astype(F32)).astype(BF16)
    await_all(buffer, sem)


def prepare_kernel(sizes, rows, active_hbm, gate, up, after, _, mask, *rest):
    exp_count, groups = sizes
    *buffers, active, small_sem, sems = rest
    z, g, s = place(sizes)
    small = pltpu.make_async_copy(active_hbm, active, small_sem)
    small.start()
    lines = gate.shape[0] // BLOCK
    for n, buffer in enumerate(buffers[1 : READY - 1], 1):
        fetch_rows(gate if n < lines else up, n % lines, buffer, sems.at[n])
    small.wait()
    unit_width = mask.shape[1]
    blocks = lax.broadcasted_iota(jnp.int32, mask.shape, 1) // BLK + s * (unit_width // BLK)
    source = lax.broadcasted_iota(jnp.int32, (mask.shape[0], 1), 0)
    own_expert = z * groups + g

    def add_entry(k, found):
        entry = jnp.full((mask.shape[0], 1), -1, jnp.int32)
        for d in range(exp_count):
            tile = lax.rem(z - d + exp_count, exp_count) * rows // TILE
            entry = jnp.where(source == d, active[tile, own_expert, k], entry)
        return jnp.where(blocks == entry, 1.0, found)

    mask[...] = lax.fori_loop(0, active.shape[2], add_entry, jnp.zeros(mask.shape, F32))
    for n, buffer in enumerate(buffers[1 : READY - 1], 1):
        await_all(buffer, sems.at[n])


def join_kernel(order, after, *refs):
    pieces = [refs[order.index(d + 1)][...].astype(F32) for d in range(len(order))]
    refs[-1][...] = jnp.concatenate(pieces, axis=0).astype(BF16)


def hidden_kernel(sizes, own, mine, other, *refs):
    exp_count, groups = sizes
    z, g, s = place(sizes)
    refs = list(refs)
    refs = refs[BUFFERS:]
    up, down, mask, _, hidden, gives = [refs.pop(0) for _ in range(6)]
    buffers = [refs.pop(0) for _ in range(BUFFERS)]
    gate_sum, up_sum, rows, sems = refs
    half = own.shape[1] // 2
    features, unit_width = up.shape
    columns, lines = unit_width // BLOCK, features // BLOCK
    given = features // (2 * groups) // BLOCK
    count = len(buffers)

    def fetch(index):
        buffer, sem = buffers[index % count], sems.at[index % count]
        if index < 2 * lines:
            fetch_rows(up, index - lines, buffer, sem)
        elif index < 2 * lines + groups * given:
            order, step = divmod(index - 2 * lines, given)
            fetch_columns(sizes, down, order + 1, False, step, buffer, sem)
        elif index < 2 * lines + (groups + 1) * given:
            step = index - 2 * lines - groups * given
            fetch_columns(sizes, down, 1, True, step, buffer, sem)

    for index in range(READY, count):
        fetch(index)
    for source, side in ((mine, s), (other, 1 - s)):
        cols = pl.ds(pl.multiple_of(side * half, 128), half)
        joined = [own[:, cols].astype(F32), source[...].astype(F32)]
        rows[:, cols] = jnp.concatenate(joined, axis=0).astype(BF16)
    for index in range(0, 2 * lines, 2):
        pair = [buffers[(index + n) % count] for n in range(2)]
        for n in range(2):
            if index + n >= READY:
                await_all(pair[n], sems.at[(index + n) % count])
        line = index % lines
        total = gate_sum if index < lines else up_sum
        left = [rows[:, (line + n) * BLOCK : (line + n + 1) * BLOCK] for n in range(2)]
        for column in range(columns):
            cols = slice(column * BLOCK, (column + 1) * BLOCK)
            value = jnp.dot(left[0], pair[0][column], preferred_element_type=F32)
            value = value + jnp.dot(left[1], pair[1][column], preferred_element_type=F32)
            if line > 0:
                value = total[:, cols] + value
            if index < 2 * lines - 2:
                total[:, cols] = value
                continue
            value = jnp.maximum(gate_sum[:, cols], 0.0) * jnp.maximum(value, 0.0)
            parts = []
            for d in range(exp_count):
                parts.append(value[d * CAP : (d + 1) * CAP, :] * mask[d : d + 1, cols])
            hidden[:, cols] = jnp.concatenate(parts, axis=0).astype(BF16)
        for n in range(2):
            fetch(index + n + count)
    for index in range(2 * lines, 2 * lines + (groups + 1) * given):
        buffer = buffers[index % count]
        await_all(buffer, sems.at[index % count])
        step = index - 2 * lines
        if step < given:
            value = jnp.dot(hidden[...], stacked(buffer), preferred_element_type=F32)
            gives[:, step * BLOCK : (step + 1) * BLOCK] = value.astype(BF16)


def give_kernel(sizes, offset, hidden, *refs):
    exp_count, groups = sizes
    *weights, down, given, kept_weights, sem = refs
    fetch_columns(sizes, down, offset, True, 0, kept_weights, sem)
    for step, buffer in enumerate(weights):
        value = jnp.dot(hidden[...], stacked(buffer), preferred_element_type=F32)
        given[:, step * BLOCK : (step + 1) * BLOCK] = value.astype(BF16)
    await_all(kept_weights, sem)


def keep_kernel(sizes, ahead, hidden, received, *refs):
    exp_count, groups = sizes
    refs = list(refs)
    if ahead is not None:
        sem, down = refs.pop(), refs.pop(0)
        next_weights = refs[received.shape[1] // BLOCK + exp_count :]
        for step, buffer in enumerate(next_weights, 1):
            fetch_columns(sizes, down, ahead, True, step, buffer, sem.at[step - 1])
    weights = refs[: received.shape[1] // BLOCK]
    outs = refs[len(weights) : len(weights) + exp_count]
    for step, buffer in enumerate(weights):
        cols = slice(step * BLOCK, (step + 1) * BLOCK)
        value = jnp.dot(hidden[...], stacked(buffer), preferred_element_type=F32)
        value = value + received[:, cols].astype(F32)
        for d in range(exp_count):
            outs[d][:, cols] = value[d * CAP : (d + 1) * CAP, :].astype(BF16)
    if ahead is not None:
        for step, buffer in enumerate(next_weights, 1):
            await_all(buffer, sem.at[step - 1])


def combine_kernel(order, high, low, *refs):
    refs = list(refs)
    out = refs.pop()
    before = refs.pop(0) if order > 0 else None
    found = jnp.concatenate([r[...].astype(F32) for r in refs], axis=0).astype(BF16)
    count = found.shape[0]
    value = jnp.dot(high[order, :, :count], found, preferred_element_type=F32)
    value = value + jnp.dot(low[order, :, :count], found, preferred_element_type=F32)
    if before is not None:
        value = before[...] + value
    out[...] = value.astype(out.dtype)


def call(kernel, outs, ins, scratch=(), flops=0, moved=0, aliases=None):
    vmem = pl.BlockSpec(memory_space=pltpu.VMEM)
    arrays, specs = [], []
    for array, space in ins:
        if space in (pltpu.HBM, pltpu.VMEM):
            array = pltpu.with_memory_space_constraint(array, space)
        arrays.append(array)
        specs.append(vmem if space is None else pl.BlockSpec(memory_space=space))
    shapes = []
    for shape, kind, *space in outs:
        shapes.append(space[0](shape, kind) if space else jax.ShapeDtypeStruct(shape, kind))
    return pl.pallas_call(
        kernel,
        out_shape=shapes,
        in_specs=specs,
        out_specs=[vmem] * len(outs),
        scratch_shapes=list(scratch),
        input_output_aliases=aliases or {},
        compiler_params=pltpu.CompilerParams(vmem_limit_bytes=LIMIT << 20),
        cost_estimate=pl.CostEstimate(flops=flops, bytes_accessed=moved, transcendentals=0),
    )(*arrays)


def paired_experts(
    tokens, norm_gain, route_ids, route_weight, active_blocks, gate_weight, up_weight, down_weight
):
    exp_count, unit_count = lax.axis_size("exp"), lax.axis_size("unit")
    groups = unit_count // 2
    sizes = (exp_count, groups)
    tok_count, features = tokens.shape
    unit_width = gate_weight.shape[1]
    slots = exp_count * CAP
    half = features // 2
    width = half
    ids = route_ids.T
    weights = route_weight.T

    def shift(value, distance, group_shift=0):
        pairs = []
        for z in range(exp_count):
            for u in range(unit_count):
                target = (z + distance) % exp_count
                group = (u // 2 + group_shift) % groups
                pairs.append((z * unit_count + u, target * unit_count + group * 2 + u % 2))
        return lax.ppermute(value, ("exp", "unit"), pairs)

    def swap(value):
        return lax.ppermute(value, "unit", [(u, u ^ 1) for u in range(unit_count)])

    batch = exp_count - 1
    buffer = ((unit_width // BLOCK, BLOCK, BLOCK), BF16, pltpu.VMEM)
    piece_bytes = 2 * unit_width * BLOCK
    own, ready, *sends = call(
        functools.partial(route_kernel, sizes, width),
        [((CAP, features), BF16), buffer] + [((CAP, width), BF16)] * batch,
        [
            (tokens, pltpu.HBM),
            (norm_gain.reshape(1, -1), pltpu.HBM),
            (ids, pltpu.HBM),
            (gate_weight, pltpu.HBM),
        ],
        [
            pltpu.VMEM((tok_count, features), BF16),
            pltpu.VMEM((tok_count, features), BF16),
            pltpu.VMEM((1, features), F32),
            pltpu.VMEM(ids.shape, jnp.int32),
            pltpu.SemaphoreType.DMA((6,)),
            pltpu.SemaphoreType.DMA,
        ],
        flops=2 * tok_count * slots * width,
        moved=4 * tok_count * features + piece_bytes,
    )
    mask, *ready = call(
        functools.partial(prepare_kernel, sizes, tok_count),
        [((max(8, exp_count), unit_width), F32)] + [buffer] * BUFFERS,
        [
            (active_blocks, pltpu.HBM),
            (gate_weight, pltpu.HBM),
            (up_weight, pltpu.HBM),
            (own, pl.ANY),
            (ready, pltpu.VMEM),
        ],
        [
            pltpu.SMEM(active_blocks.shape, jnp.int32),
            pltpu.SemaphoreType.DMA,
            pltpu.SemaphoreType.DMA((READY,)),
        ],
        flops=2 * tok_count * slots * features,
        moved=(READY - 2) * piece_bytes,
        aliases={4: 1},
    )
    order = list(range(exp_count - 1, 0, -1))
    arrived = [shift(sends[d - 1], d) for d in order]
    mine = call(
        functools.partial(join_kernel, order),
        [((batch * CAP, width), BF16)],
        [(mask, pl.ANY)] + [(v, None) for v in arrived],
        moved=1 << 20,
    )[0]
    other = swap(mine)
    padded = -(-slots // 128) * 128
    combine_high, combine_low, ready[READY - 1] = call(
        functools.partial(table_kernel, sizes),
        [((2, tok_count, padded), BF16)] * 2 + [buffer],
        [
            (ids, pltpu.HBM),
            (weights, pltpu.HBM),
            (mine, pl.ANY),
            (gate_weight, pltpu.HBM),
            (up_weight, pltpu.HBM),
            (ready[READY - 1], pltpu.VMEM),
        ],
        [
            pltpu.VMEM(ids.shape, jnp.int32),
            pltpu.VMEM(weights.shape, F32),
            pltpu.SemaphoreType.DMA((2,)),
            pltpu.SemaphoreType.DMA,
        ],
        moved=1 << 22,
        aliases={5: 2},
    )
    acc = pltpu.VMEM((slots, unit_width), F32)
    part = features // unit_count
    hidden, first_given, *buffers = call(
        functools.partial(hidden_kernel, sizes),
        [((slots, unit_width), BF16), ((slots, part), BF16)] + [buffer] * BUFFERS,
        [(own, None), (mine, None), (other, None)]
        + [(v, pltpu.VMEM) for v in ready]
        + [(up_weight, pltpu.HBM), (down_weight, pltpu.HBM), (mask, None)]
        + [(combine_low, pl.ANY)],
        [
            acc,
            acc,
            pltpu.VMEM((slots, features), BF16),
            pltpu.SemaphoreType.DMA((BUFFERS,)),
        ],
        flops=2 * 2 * slots * features * unit_width,
        moved=10 * piece_bytes,
        aliases={3 + n: 2 + n for n in range(BUFFERS)},
    )
    steps = part // BLOCK
    offsets = [(order + 1) % groups for order in range(groups)]
    first = 2 * features // BLOCK + groups * steps
    given = [first_given]
    kept_weights = [[buffers[(first + step) % BUFFERS] for step in range(steps)]]
    for order, offset in list(enumerate(offsets))[1:]:
        first = 2 * features // BLOCK + order * steps
        value, *kept = call(
            functools.partial(give_kernel, sizes, offset),
            [((slots, part), BF16), buffer],
            [(hidden, None)]
            + [(buffers[(first + step) % BUFFERS], pltpu.VMEM) for step in range(steps)]
            + [(down_weight, pltpu.HBM)],
            [pltpu.SemaphoreType.DMA],
            flops=2 * slots * unit_width * part,
            moved=piece_bytes,
        )
        given.append(value)
        kept_weights.append(kept)
    taken = [swap(value) for value in given]
    home = {}
    for order, offset in enumerate(offsets):
        more = order < groups - 1
        outs = call(
            functools.partial(keep_kernel, sizes, offsets[order + 1] if more else None),
            [((CAP, part), BF16)] * exp_count + [buffer] * (steps - 1 if more else 0),
            [(hidden, None), (taken[order], None)]
            + ([(down_weight, pltpu.HBM)] if more else [])
            + [(v, pltpu.VMEM) for v in kept_weights[order]],
            [pltpu.SemaphoreType.DMA((steps - 1,))] if more else [],
            flops=2 * slots * unit_width * part,
            moved=piece_bytes,
        )
        kept = outs[:exp_count]
        if more:
            kept_weights[order + 1] = list(kept_weights[order + 1]) + list(outs[exp_count:])
        for d in distances(exp_count) + [0]:
            home[offset, d] = shift(kept[d], -d, offset) if d or offset else kept[d]
    mixed = None
    for order, batch in enumerate(arrivals(sizes)):
        last = order == 1
        mixed = call(
            functools.partial(combine_kernel, order),
            [((tok_count, part), BF16 if last else F32)],
            [(combine_high, None), (combine_low, None)]
            + ([(mixed, None)] if order else [])
            + [(home[key], None) for key in batch],
            flops=4 * tok_count * slots * part,
            moved=1 << 20,
        )[0]
    return mixed


def per_device(*operands):
    tokens, gate_weight = operands[0], operands[5]
    exp_count, unit_count = lax.axis_size("exp"), lax.axis_size("unit")
    unit_width = gate_weight.shape[1]
    paired = (
        2 * unit_width == FF
        and unit_count % 2 == 0
        and exp_count * unit_count // 2 == EXPERTS
        and TILE % tokens.shape[0] == 0
        and unit_width % BLOCK == 0
        and unit_count == 4
        and tokens.shape[1] % (unit_count * BLOCK) == 0
        and tokens.shape[1] <= READY * BLOCK <= 2 * tokens.shape[1]
    )
    return (paired_experts if paired else spread_experts)(*operands)


def solution(mesh):
    return jax.shard_map(
        per_device,
        mesh=mesh,
        in_specs=(
            P(("rep", "exp"), None),
            P(),
            P(("rep", "exp"), None),
            P(("rep", "exp"), None),
            P("rep", None, None),
            P(None, ("exp", "unit")),
            P(None, ("exp", "unit")),
            P(("exp", "unit"), None),
        ),
        out_specs=P(("rep", "exp"), "unit"),
        check_vma=False,
    )
```

```python
import functools

import jax
import jax.numpy as jnp
import numpy as np
from jax import lax
from jax.experimental import pallas as pl
from jax.experimental.pallas import tpu as pltpu
from jax.sharding import PartitionSpec as P

EXPERTS = 8
FF = 7168
BLK = 64
TILE = 256
CAP = 40

EPSILON = 1e-05

BLOCK = 512
READY = 11
BUFFERS = 12
LIMIT = 8

F32 = jnp.float32
BF16 = jnp.bfloat16


def normalize(tokens, norm_gain):
    values = tokens.astype(jnp.float32)
    inv_rms = lax.rsqrt(jnp.mean(values * values, axis=-1, keepdims=True) + EPSILON)
    return (values * inv_rms * norm_gain).astype(jnp.bfloat16)


def slot_numbers(entries, expert_count):
    onehot = (entries[..., None] == jnp.arange(expert_count, dtype=jnp.int32)).astype(jnp.int32)
    before = jnp.cumsum(onehot, axis=-2, dtype=jnp.int32) - onehot
    return jnp.sum(before * onehot, axis=-1)


def spread_experts(
    tokens, norm_gain, route_ids, route_weight, active_blocks, gate_weight, up_weight, down_weight
):
    exp_count = lax.axis_size("exp")
    unit_count = lax.axis_size("unit")
    tok_count, feature_width = tokens.shape
    unit_width = gate_weight.shape[1]
    row_units = unit_count * unit_width
    per_exp = max(1, row_units // FF)
    part_width = feature_width // unit_count
    block_count = unit_width // BLK
    tile_count = active_blocks.shape[0]
    exp_index = lax.axis_index("exp")
    unit_index = lax.axis_index("unit")
    first_unit = (exp_index * unit_count + unit_index) * unit_width
    own_expert = first_unit // FF
    first_block = first_unit % FF // BLK
    local_expert = own_expert - exp_index * row_units // FF
    normed = normalize(tokens, norm_gain)
    slot_index = slot_numbers(route_ids.reshape(1, -1), EXPERTS).reshape(tok_count, 2)
    positions = jnp.arange(tok_count, dtype=jnp.int32)
    tile_of = (exp_index * tok_count + positions) // TILE
    route_slot = (route_ids * CAP + slot_index).reshape(-1)
    token_source = (
        jnp.full((EXPERTS * CAP,), tok_count, jnp.int32)
        .at[route_slot]
        .set(jnp.repeat(positions, 2))
    )
    row_experts = np.arange(exp_count)[:, None] * row_units // FF + np.arange(per_exp)[None, :]
    slot_source = token_source.reshape(EXPERTS, CAP)[row_experts]
    padded_tiles = jnp.concatenate([tile_of, jnp.zeros((1,), jnp.int32)])
    slot_tiles = padded_tiles[slot_source]
    active_mine = lax.dynamic_index_in_dim(active_blocks, own_expert, 1, keepdims=False)
    local_blocks = first_block + jnp.arange(block_count, dtype=jnp.int32)
    block_on = jnp.any(active_mine[:, :, None] == local_blocks[None, None, :], axis=1).astype(
        jnp.float32
    )
    row_part = lax.dynamic_slice_in_dim(normed, unit_index * part_width, part_width, 1)
    padded_rows = jnp.concatenate([row_part, jnp.zeros((1, part_width), jnp.bfloat16)], 0)
    whole_rows = lax.all_gather(
        lax.all_to_all(padded_rows[slot_source], "exp", split_axis=0, concat_axis=0, tiled=True),
        "unit",
        axis=3,
        tiled=True,
    )
    slot_count = whole_rows.shape[2]
    own_rows = lax.dynamic_index_in_dim(whole_rows, local_expert, 1, keepdims=False).reshape(
        -1, feature_width
    )
    own_tiles = lax.dynamic_index_in_dim(
        lax.all_to_all(slot_tiles, "exp", split_axis=0, concat_axis=0, tiled=True),
        local_expert,
        1,
        keepdims=False,
    ).reshape(-1)
    tile_hot = (own_tiles[:, None] == jnp.arange(tile_count, dtype=jnp.int32)[None, :]).astype(
        jnp.float32
    )
    row_mask = jnp.dot(tile_hot, block_on, precision=lax.Precision.HIGHEST)
    gate_acts = jnp.dot(own_rows, gate_weight, preferred_element_type=jnp.float32)
    up_acts = jnp.dot(own_rows, up_weight, preferred_element_type=jnp.float32)
    hidden = jax.nn.relu(gate_acts) * jax.nn.relu(up_acts)
    hidden = (hidden.reshape(-1, block_count, BLK) * row_mask[:, :, None]).reshape(-1, unit_width)
    hidden = hidden.astype(jnp.bfloat16)
    partial_value = jnp.dot(hidden, down_weight, preferred_element_type=jnp.float32)
    partial_value = partial_value.reshape(exp_count, slot_count, feature_width)
    result = jnp.zeros((exp_count, per_exp, slot_count, feature_width), jnp.float32)
    partial_all = lax.dynamic_update_index_in_dim(result, partial_value, local_expert, 1)

    def by_expert(returned):
        last_width = returned.shape[-1]
        if per_exp == 1:
            grouped = returned.reshape(EXPERTS, exp_count // EXPERTS, CAP, last_width)
            return jnp.sum(grouped, axis=1, dtype=jnp.float32)
        return returned.reshape(EXPERTS, CAP, last_width).astype(jnp.float32)

    summed = lax.psum_scatter(
        partial_all.astype(jnp.bfloat16), "unit", scatter_dimension=3, tiled=True
    ).astype(jnp.float32)
    returned = lax.all_to_all(
        summed.astype(jnp.bfloat16), "exp", split_axis=0, concat_axis=0, tiled=True
    ).astype(summed.dtype)
    per_expert = by_expert(returned)
    last_width = per_expert.shape[-1]
    picked = per_expert.reshape(EXPERTS * CAP, last_width)[route_slot].reshape(
        tok_count, 2, last_width
    )
    mixed = jnp.sum(route_weight[:, :, None] * picked, axis=1)
    return mixed.astype(jnp.bfloat16)


def place(sizes):
    exp_count, groups = sizes
    return lax.axis_index("exp"), lax.axis_index("unit") // 2, lax.axis_index("unit") % 2


def pick_rows(named, before, d):
    rows = named.shape[1]
    place_of = jnp.where(named[d : d + 1, :] > 0, before[d : d + 1, :], -1)
    return (place_of == lax.broadcasted_iota(jnp.int32, (CAP, rows), 0)).astype(F32)


def count_earlier(ids, experts):
    rows = ids.shape[1]
    earlier = (
        lax.broadcasted_iota(jnp.int32, (rows, rows), 0)
        < lax.broadcasted_iota(jnp.int32, (rows, rows), 1)
    ).astype(BF16)
    named = ((ids[0:1, :] == experts) | (ids[1:2, :] == experts)).astype(jnp.int32)
    before = jnp.dot(named.astype(BF16), earlier, preferred_element_type=F32)
    return named, before.astype(jnp.int32)


def group_experts(exp_count, groups, z, g, rows):
    distance = lax.broadcasted_iota(jnp.int32, (max(8, exp_count), rows), 0)
    return lax.rem(z + distance, exp_count) * groups + g


def fetch_rows(weight, line, buffer, sem):
    def start(index, carry):
        pltpu.make_async_copy(
            weight.at[
                pl.ds(line * BLOCK, BLOCK), pl.ds(pl.multiple_of(index * BLOCK, BLOCK), BLOCK)
            ],
            buffer.at[index],
            sem,
        ).start()
        return carry

    lax.fori_loop(0, buffer.shape[0], start, 0)


def fetch_columns(sizes, down, offset, keep, step, buffer, sem):
    exp_count, groups = sizes
    z, g, s = place(sizes)
    side = s if keep else 1 - s
    part = down.shape[1] // (2 * groups)
    column = (lax.rem(g + offset, groups) * 2 + side) * part + step * BLOCK

    def start(index, carry):
        pltpu.make_async_copy(
            down.at[
                pl.ds(pl.multiple_of(index * BLOCK, BLOCK), BLOCK),
                pl.ds(pl.multiple_of(column, BLOCK), BLOCK),
            ],
            buffer.at[index],
            sem,
        ).start()
        return carry

    lax.fori_loop(0, buffer.shape[0], start, 0)


def await_all(buffer, sem):
    pltpu.make_async_copy(buffer, buffer, sem).wait()


def stacked(buffer):
    return buffer[...].reshape(buffer.shape[0] * BLOCK, BLOCK)


def route_kernel(sizes, width, tokens_hbm, gain_hbm, ids_hbm, gate, own, buffer, *rest):
    exp_count, groups = sizes
    sends, (tokens, normed, gain, ids, sems, gate_sem) = rest[:-6], rest[-6:]
    rows, features = tokens.shape
    count = 4
    lines = [pl.ds(n * (rows // count), rows // count) for n in range(count)]
    pairs = [(gain_hbm, gain), (ids_hbm, ids)]
    pairs += [(tokens_hbm.at[part, :], tokens.at[part, :]) for part in lines]
    copies = [pltpu.make_async_copy(a, b, sems.at[n]) for n, (a, b) in enumerate(pairs)]
    for copy in copies:
        copy.start()
    fetch_rows(gate, 0, buffer, gate_sem)
    z, g, s = place(sizes)
    copies[0].wait()
    copies[1].wait()
    named, before = count_earlier(ids, group_experts(exp_count, groups, z, g, rows))
    picks = [pick_rows(named, before, d) for d in range(exp_count)]
    others = jnp.concatenate(picks[1:], axis=0).astype(BF16)
    step = 16
    for first in range(0, rows, step):
        if first % (rows // count) == 0:
            copies[2 + first // (rows // count)].wait()
        values = tokens[first : first + step, :].astype(F32)
        mean = jnp.sum(values * values, axis=1, keepdims=True) * (1.0 / features)
        inv_rms = lax.rsqrt(mean + EPSILON)
        normed[first : first + step, :] = (values * inv_rms * gain[...]).astype(BF16)
    start = pl.multiple_of(s * (features // 2), 128)
    found = jnp.dot(others, normed[:, pl.ds(start, width)], preferred_element_type=F32)
    for d, send in enumerate(sends):
        send[...] = found[d * CAP : (d + 1) * CAP, :].astype(BF16)
    own[...] = jnp.dot(
        picks[0].astype(BF16), normed[...], preferred_element_type=F32
    ).astype(BF16)
    await_all(buffer, gate_sem)


def distances(exp_count):
    middle = exp_count // 2
    return [middle] + [d for d in range(1, exp_count) if d != middle]


def arrivals(sizes):
    exp_count, groups = sizes
    order = distances(exp_count) + [0]
    early = [(o, d) for o in range(1, groups) for d in order]
    late = [(0, d) for d in order]
    return early, late


def table_kernel(
    sizes, ids_hbm, weights_hbm, after, gate, up, _, combine_high, combine_low, buffer, ids, weights,
    sems, sem
):
    exp_count, groups = sizes
    lines = gate.shape[0] // BLOCK
    last = READY - 1
    fetch_rows(gate if last < lines else up, last % lines, buffer, sem)
    pairs = ((ids_hbm, ids), (weights_hbm, weights))
    copies = [pltpu.make_async_copy(a, b, sems.at[n]) for n, (a, b) in enumerate(pairs)]
    for copy in copies:
        copy.start()
    for copy in copies:
        copy.wait()
    rows = ids.shape[1]
    z, g, s = place(sizes)
    zero = jnp.zeros((CAP, rows), F32)
    padded = combine_high.shape[2]
    batches = arrivals(sizes)
    experts = [
        lax.rem(z + d, exp_count) * groups + lax.rem(g - o + groups, groups)
        for batch in batches
        for o, d in batch
    ]
    line = lax.broadcasted_iota(jnp.int32, (max(8, len(experts)), rows), 0)
    listed = jnp.full(line.shape, -1, jnp.int32)
    for n, expert in enumerate(experts):
        listed = jnp.where(line == n, expert, listed)
    named, before = count_earlier(ids, listed)
    for order, batch in enumerate(batches):
        parts = []
        for n in range(len(batch)):
            entry = order * len(batch) + n
            here = pick_rows(named, before, entry) > 0
            first = jnp.where(here & (ids[0:1, :] == experts[entry]), weights[0:1, :], zero)
            second = jnp.where(here & (ids[1:2, :] == experts[entry]), weights[1:2, :], zero)
            parts.append(first + second)
        if padded > len(batch) * CAP:
            parts.append(jnp.zeros((padded - len(batch) * CAP, rows), F32))
        table = jnp.concatenate(parts, axis=0).T
        high = table.astype(BF16)
        combine_high[order] = high
        combine_low[order] = (table - high.astype(F32)).astype(BF16)
    await_all(buffer, sem)


def prepare_kernel(sizes, rows, active_hbm, gate, up, after, _, mask, *rest):
    exp_count, groups = sizes
    *buffers, active, small_sem, sems = rest
    z, g, s = place(sizes)
    small = pltpu.make_async_copy(active_hbm, active, small_sem)
    small.start()
    lines = gate.shape[0] // BLOCK
    for n, buffer in enumerate(buffers[1 : READY - 1], 1):
        fetch_rows(gate if n < lines else up, n % lines, buffer, sems.at[n])
    small.wait()
    unit_width = mask.shape[1]
    blocks = lax.broadcasted_iota(jnp.int32, mask.shape, 1) // BLK + s * (unit_width // BLK)
    source = lax.broadcasted_iota(jnp.int32, (mask.shape[0], 1), 0)
    own_expert = z * groups + g

    def add_entry(k, found):
        entry = jnp.full((mask.shape[0], 1), -1, jnp.int32)
        for d in range(exp_count):
            tile = lax.rem(z - d + exp_count, exp_count) * rows // TILE
            entry = jnp.where(source == d, active[tile, own_expert, k], entry)
        return jnp.where(blocks == entry, 1.0, found)

    mask[...] = lax.fori_loop(0, active.shape[2], add_entry, jnp.zeros(mask.shape, F32))
    for n, buffer in enumerate(buffers[1 : READY - 1], 1):
        await_all(buffer, sems.at[n])


def join_kernel(order, after, *refs):
    pieces = [refs[order.index(d + 1)][...].astype(F32) for d in range(len(order))]
    refs[-1][...] = jnp.concatenate(pieces, axis=0).astype(BF16)


def hidden_kernel(sizes, own, mine, other, *refs):
    exp_count, groups = sizes
    z, g, s = place(sizes)
    refs = list(refs)
    refs = refs[BUFFERS:]
    up, down, mask, _, hidden, gives = [refs.pop(0) for _ in range(6)]
    buffers = [refs.pop(0) for _ in range(BUFFERS)]
    gate_sum, up_sum, rows, sems = refs
    half = own.shape[1] // 2
    features, unit_width = up.shape
    columns, lines = unit_width // BLOCK, features // BLOCK
    given = features // (2 * groups) // BLOCK
    count = len(buffers)

    def fetch(index):
        buffer, sem = buffers[index % count], sems.at[index % count]
        if index < 2 * lines:
            fetch_rows(up, index - lines, buffer, sem)
        elif index < 2 * lines + groups * given:
            order, step = divmod(index - 2 * lines, given)
            fetch_columns(sizes, down, order + 1, False, step, buffer, sem)
        elif index < 2 * lines + (groups + 1) * given:
            step = index - 2 * lines - groups * given
            fetch_columns(sizes, down, 1, True, step, buffer, sem)

    for index in range(READY, count):
        fetch(index)
    for source, side in ((mine, s), (other, 1 - s)):
        cols = pl.ds(pl.multiple_of(side * half, 128), half)
        joined = [own[:, cols].astype(F32), source[...].astype(F32)]
        rows[:, cols] = jnp.concatenate(joined, axis=0).astype(BF16)
    for index in range(0, 2 * lines, 2):
        pair = [buffers[(index + n) % count] for n in range(2)]
        for n in range(2):
            if index + n >= READY:
                await_all(pair[n], sems.at[(index + n) % count])
        line = index % lines
        total = gate_sum if index < lines else up_sum
        left = [rows[:, (line + n) * BLOCK : (line + n + 1) * BLOCK] for n in range(2)]
        for column in range(columns):
            cols = slice(column * BLOCK, (column + 1) * BLOCK)
            value = jnp.dot(left[0], pair[0][column], preferred_element_type=F32)
            value = value + jnp.dot(left[1], pair[1][column], preferred_element_type=F32)
            if line > 0:
                value = total[:, cols] + value
            if index < 2 * lines - 2:
                total[:, cols] = value
                continue
            value = jnp.maximum(gate_sum[:, cols], 0.0) * jnp.maximum(value, 0.0)
            parts = []
            for d in range(exp_count):
                parts.append(value[d * CAP : (d + 1) * CAP, :] * mask[d : d + 1, cols])
            hidden[:, cols] = jnp.concatenate(parts, axis=0).astype(BF16)
        for n in range(2):
            fetch(index + n + count)
    for index in range(2 * lines, 2 * lines + (groups + 1) * given):
        buffer = buffers[index % count]
        await_all(buffer, sems.at[index % count])
        step = index - 2 * lines
        if step < given:
            value = jnp.dot(hidden[...], stacked(buffer), preferred_element_type=F32)
            gives[:, step * BLOCK : (step + 1) * BLOCK] = value.astype(BF16)


def give_kernel(sizes, offset, hidden, *refs):
    exp_count, groups = sizes
    *weights, down, given, kept_weights, sem = refs
    fetch_columns(sizes, down, offset, True, 0, kept_weights, sem)
    for step, buffer in enumerate(weights):
        value = jnp.dot(hidden[...], stacked(buffer), preferred_element_type=F32)
        given[:, step * BLOCK : (step + 1) * BLOCK] = value.astype(BF16)
    await_all(kept_weights, sem)


def keep_kernel(sizes, ahead, hidden, received, *refs):
    exp_count, groups = sizes
    refs = list(refs)
    if ahead is not None:
        sem, down = refs.pop(), refs.pop(0)
        next_weights = refs[received.shape[1] // BLOCK + exp_count :]
        for step, buffer in enumerate(next_weights, 1):
            fetch_columns(sizes, down, ahead, True, step, buffer, sem.at[step - 1])
    weights = refs[: received.shape[1] // BLOCK]
    outs = refs[len(weights) : len(weights) + exp_count]
    for step, buffer in enumerate(weights):
        cols = slice(step * BLOCK, (step + 1) * BLOCK)
        value = jnp.dot(hidden[...], stacked(buffer), preferred_element_type=F32)
        value = value + received[:, cols].astype(F32)
        for d in range(exp_count):
            outs[d][:, cols] = value[d * CAP : (d + 1) * CAP, :].astype(BF16)
    if ahead is not None:
        for step, buffer in enumerate(next_weights, 1):
            await_all(buffer, sem.at[step - 1])


def combine_kernel(order, high, low, *refs):
    refs = list(refs)
    out = refs.pop()
    before = refs.pop(0) if order > 0 else None
    found = jnp.concatenate([r[...].astype(F32) for r in refs], axis=0).astype(BF16)
    count = found.shape[0]
    value = jnp.dot(high[order, :, :count], found, preferred_element_type=F32)
    value = value + jnp.dot(low[order, :, :count], found, preferred_element_type=F32)
    if before is not None:
        value = before[...] + value
    out[...] = value.astype(out.dtype)


def call(kernel, outs, ins, scratch=(), flops=0, moved=0, aliases=None):
    vmem = pl.BlockSpec(memory_space=pltpu.VMEM)
    arrays, specs = [], []
    for array, space in ins:
        if space in (pltpu.HBM, pltpu.VMEM):
            array = pltpu.with_memory_space_constraint(array, space)
        arrays.append(array)
        specs.append(vmem if space is None else pl.BlockSpec(memory_space=space))
    shapes = []
    for shape, kind, *space in outs:
        shapes.append(space[0](shape, kind) if space else jax.ShapeDtypeStruct(shape, kind))
    return pl.pallas_call(
        kernel,
        out_shape=shapes,
        in_specs=specs,
        out_specs=[vmem] * len(outs),
        scratch_shapes=list(scratch),
        input_output_aliases=aliases or {},
        compiler_params=pltpu.CompilerParams(vmem_limit_bytes=LIMIT << 20),
        cost_estimate=pl.CostEstimate(flops=flops, bytes_accessed=moved, transcendentals=0),
    )(*arrays)


def paired_experts(
    tokens, norm_gain, route_ids, route_weight, active_blocks, gate_weight, up_weight, down_weight
):
    exp_count, unit_count = lax.axis_size("exp"), lax.axis_size("unit")
    groups = unit_count // 2
    sizes = (exp_count, groups)
    tok_count, features = tokens.shape
    unit_width = gate_weight.shape[1]
    slots = exp_count * CAP
    half = features // 2
    width = half
    ids = route_ids.T
    weights = route_weight.T

    def shift(value, distance, group_shift=0):
        pairs = []
        for z in range(exp_count):
            for u in range(unit_count):
                target = (z + distance) % exp_count
                group = (u // 2 + group_shift) % groups
                pairs.append((z * unit_count + u, target * unit_count + group * 2 + u % 2))
        return lax.ppermute(value, ("exp", "unit"), pairs)

    def swap(value):
        return lax.ppermute(value, "unit", [(u, u ^ 1) for u in range(unit_count)])

    batch = exp_count - 1
    buffer = ((unit_width // BLOCK, BLOCK, BLOCK), BF16, pltpu.VMEM)
    piece_bytes = 2 * unit_width * BLOCK
    own, ready, *sends = call(
        functools.partial(route_kernel, sizes, width),
        [((CAP, features), BF16), buffer] + [((CAP, width), BF16)] * batch,
        [
            (tokens, pltpu.HBM),
            (norm_gain.reshape(1, -1), pltpu.HBM),
            (ids, pltpu.HBM),
            (gate_weight, pltpu.HBM),
        ],
        [
            pltpu.VMEM((tok_count, features), BF16),
            pltpu.VMEM((tok_count, features), BF16),
            pltpu.VMEM((1, features), F32),
            pltpu.VMEM(ids.shape, jnp.int32),
            pltpu.SemaphoreType.DMA((6,)),
            pltpu.SemaphoreType.DMA,
        ],
        flops=2 * tok_count * slots * width,
        moved=4 * tok_count * features + piece_bytes,
    )
    mask, *ready = call(
        functools.partial(prepare_kernel, sizes, tok_count),
        [((max(8, exp_count), unit_width), F32)] + [buffer] * BUFFERS,
        [
            (active_blocks, pltpu.HBM),
            (gate_weight, pltpu.HBM),
            (up_weight, pltpu.HBM),
            (own, pl.ANY),
            (ready, pltpu.VMEM),
        ],
        [
            pltpu.SMEM(active_blocks.shape, jnp.int32),
            pltpu.SemaphoreType.DMA,
            pltpu.SemaphoreType.DMA((READY,)),
        ],
        flops=2 * tok_count * slots * features,
        moved=(READY - 2) * piece_bytes,
        aliases={4: 1},
    )
    order = distances(exp_count)
    arrived = [shift(sends[d - 1], d) for d in order]
    mine = call(
        functools.partial(join_kernel, order),
        [((batch * CAP, width), BF16)],
        [(mask, pl.ANY)] + [(v, None) for v in arrived],
        moved=1 << 20,
    )[0]
    other = swap(mine)
    padded = -(-slots // 128) * 128
    combine_high, combine_low, ready[READY - 1] = call(
        functools.partial(table_kernel, sizes),
        [((2, tok_count, padded), BF16)] * 2 + [buffer],
        [
            (ids, pltpu.HBM),
            (weights, pltpu.HBM),
            (mine, pl.ANY),
            (gate_weight, pltpu.HBM),
            (up_weight, pltpu.HBM),
            (ready[READY - 1], pltpu.VMEM),
        ],
        [
            pltpu.VMEM(ids.shape, jnp.int32),
            pltpu.VMEM(weights.shape, F32),
            pltpu.SemaphoreType.DMA((2,)),
            pltpu.SemaphoreType.DMA,
        ],
        moved=1 << 22,
        aliases={5: 2},
    )
    acc = pltpu.VMEM((slots, unit_width), F32)
    part = features // unit_count
    hidden, first_given, *buffers = call(
        functools.partial(hidden_kernel, sizes),
        [((slots, unit_width), BF16), ((slots, part), BF16)] + [buffer] * BUFFERS,
        [(own, None), (mine, None), (other, None)]
        + [(v, pltpu.VMEM) for v in ready]
        + [(up_weight, pltpu.HBM), (down_weight, pltpu.HBM), (mask, None)]
        + [(combine_low, pl.ANY)],
        [
            acc,
            acc,
            pltpu.VMEM((slots, features), BF16),
            pltpu.SemaphoreType.DMA((BUFFERS,)),
        ],
        flops=2 * 2 * slots * features * unit_width,
        moved=10 * piece_bytes,
        aliases={3 + n: 2 + n for n in range(BUFFERS)},
    )
    steps = part // BLOCK
    offsets = [(order + 1) % groups for order in range(groups)]
    first = 2 * features // BLOCK + groups * steps
    given = [first_given]
    kept_weights = [[buffers[(first + step) % BUFFERS] for step in range(steps)]]
    for order, offset in list(enumerate(offsets))[1:]:
        first = 2 * features // BLOCK + order * steps
        value, *kept = call(
            functools.partial(give_kernel, sizes, offset),
            [((slots, part), BF16), buffer],
            [(hidden, None)]
            + [(buffers[(first + step) % BUFFERS], pltpu.VMEM) for step in range(steps)]
            + [(down_weight, pltpu.HBM)],
            [pltpu.SemaphoreType.DMA],
            flops=2 * slots * unit_width * part,
            moved=piece_bytes,
        )
        given.append(value)
        kept_weights.append(kept)
    taken = [swap(value) for value in given]
    home = {}
    for order, offset in enumerate(offsets):
        more = order < groups - 1
        outs = call(
            functools.partial(keep_kernel, sizes, offsets[order + 1] if more else None),
            [((CAP, part), BF16)] * exp_count + [buffer] * (steps - 1 if more else 0),
            [(hidden, None), (taken[order], None)]
            + ([(down_weight, pltpu.HBM)] if more else [])
            + [(v, pltpu.VMEM) for v in kept_weights[order]],
            [pltpu.SemaphoreType.DMA((steps - 1,))] if more else [],
            flops=2 * slots * unit_width * part,
            moved=piece_bytes,
        )
        kept = outs[:exp_count]
        if more:
            kept_weights[order + 1] = list(kept_weights[order + 1]) + list(outs[exp_count:])
        for d in distances(exp_count) + [0]:
            home[offset, d] = shift(kept[d], -d, offset) if d or offset else kept[d]
    mixed = None
    for order, batch in enumerate(arrivals(sizes)):
        last = order == 1
        mixed = call(
            functools.partial(combine_kernel, order),
            [((tok_count, part), BF16 if last else F32)],
            [(combine_high, None), (combine_low, None)]
            + ([(mixed, None)] if order else [])
            + [(home[key], None) for key in batch],
            flops=4 * tok_count * slots * part,
            moved=1 << 20,
        )[0]
    return mixed


def per_device(*operands):
    tokens, gate_weight = operands[0], operands[5]
    exp_count, unit_count = lax.axis_size("exp"), lax.axis_size("unit")
    unit_width = gate_weight.shape[1]
    paired = (
        2 * unit_width == FF
        and unit_count % 2 == 0
        and exp_count * unit_count // 2 == EXPERTS
        and TILE % tokens.shape[0] == 0
        and unit_width % BLOCK == 0
        and unit_count == 4
        and tokens.shape[1] % (unit_count * BLOCK) == 0
        and tokens.shape[1] <= READY * BLOCK <= 2 * tokens.shape[1]
    )
    return (paired_experts if paired else spread_experts)(*operands)


def solution(mesh):
    return jax.shard_map(
        per_device,
        mesh=mesh,
        in_specs=(
            P(("rep", "exp"), None),
            P(),
            P(("rep", "exp"), None),
            P(("rep", "exp"), None),
            P("rep", None, None),
            P(None, ("exp", "unit")),
            P(None, ("exp", "unit")),
            P(("exp", "unit"), None),
        ),
        out_specs=P(("rep", "exp"), "unit"),
        check_vma=False,
    )
```

```python
import functools

import jax
import jax.numpy as jnp
import numpy as np
from jax import lax
from jax.experimental import pallas as pl
from jax.experimental.pallas import tpu as pltpu
from jax.sharding import PartitionSpec as P

EXPERTS = 8
FF = 7168
BLK = 64
TILE = 256
CAP = 40

EPSILON = 1e-05

BLOCK = 512
READY = 12
BUFFERS = 13
LIMIT = 5

F32 = jnp.float32
BF16 = jnp.bfloat16


def normalize(tokens, norm_gain):
    values = tokens.astype(jnp.float32)
    inv_rms = lax.rsqrt(jnp.mean(values * values, axis=-1, keepdims=True) + EPSILON)
    return (values * inv_rms * norm_gain).astype(jnp.bfloat16)


def slot_numbers(entries, expert_count):
    onehot = (entries[..., None] == jnp.arange(expert_count, dtype=jnp.int32)).astype(jnp.int32)
    before = jnp.cumsum(onehot, axis=-2, dtype=jnp.int32) - onehot
    return jnp.sum(before * onehot, axis=-1)


def spread_experts(
    tokens, norm_gain, route_ids, route_weight, active_blocks, gate_weight, up_weight, down_weight
):
    exp_count = lax.axis_size("exp")
    unit_count = lax.axis_size("unit")
    tok_count, feature_width = tokens.shape
    unit_width = gate_weight.shape[1]
    row_units = unit_count * unit_width
    per_exp = max(1, row_units // FF)
    part_width = feature_width // unit_count
    block_count = unit_width // BLK
    tile_count = active_blocks.shape[0]
    exp_index = lax.axis_index("exp")
    unit_index = lax.axis_index("unit")
    first_unit = (exp_index * unit_count + unit_index) * unit_width
    own_expert = first_unit // FF
    first_block = first_unit % FF // BLK
    local_expert = own_expert - exp_index * row_units // FF
    normed = normalize(tokens, norm_gain)
    slot_index = slot_numbers(route_ids.reshape(1, -1), EXPERTS).reshape(tok_count, 2)
    positions = jnp.arange(tok_count, dtype=jnp.int32)
    tile_of = (exp_index * tok_count + positions) // TILE
    route_slot = (route_ids * CAP + slot_index).reshape(-1)
    token_source = (
        jnp.full((EXPERTS * CAP,), tok_count, jnp.int32)
        .at[route_slot]
        .set(jnp.repeat(positions, 2))
    )
    row_experts = np.arange(exp_count)[:, None] * row_units // FF + np.arange(per_exp)[None, :]
    slot_source = token_source.reshape(EXPERTS, CAP)[row_experts]
    padded_tiles = jnp.concatenate([tile_of, jnp.zeros((1,), jnp.int32)])
    slot_tiles = padded_tiles[slot_source]
    active_mine = lax.dynamic_index_in_dim(active_blocks, own_expert, 1, keepdims=False)
    local_blocks = first_block + jnp.arange(block_count, dtype=jnp.int32)
    block_on = jnp.any(active_mine[:, :, None] == local_blocks[None, None, :], axis=1).astype(
        jnp.float32
    )
    row_part = lax.dynamic_slice_in_dim(normed, unit_index * part_width, part_width, 1)
    padded_rows = jnp.concatenate([row_part, jnp.zeros((1, part_width), jnp.bfloat16)], 0)
    whole_rows = lax.all_gather(
        lax.all_to_all(padded_rows[slot_source], "exp", split_axis=0, concat_axis=0, tiled=True),
        "unit",
        axis=3,
        tiled=True,
    )
    slot_count = whole_rows.shape[2]
    own_rows = lax.dynamic_index_in_dim(whole_rows, local_expert, 1, keepdims=False).reshape(
        -1, feature_width
    )
    own_tiles = lax.dynamic_index_in_dim(
        lax.all_to_all(slot_tiles, "exp", split_axis=0, concat_axis=0, tiled=True),
        local_expert,
        1,
        keepdims=False,
    ).reshape(-1)
    tile_hot = (own_tiles[:, None] == jnp.arange(tile_count, dtype=jnp.int32)[None, :]).astype(
        jnp.float32
    )
    row_mask = jnp.dot(tile_hot, block_on, precision=lax.Precision.HIGHEST)
    gate_acts = jnp.dot(own_rows, gate_weight, preferred_element_type=jnp.float32)
    up_acts = jnp.dot(own_rows, up_weight, preferred_element_type=jnp.float32)
    hidden = jax.nn.relu(gate_acts) * jax.nn.relu(up_acts)
    hidden = (hidden.reshape(-1, block_count, BLK) * row_mask[:, :, None]).reshape(-1, unit_width)
    hidden = hidden.astype(jnp.bfloat16)
    partial_value = jnp.dot(hidden, down_weight, preferred_element_type=jnp.float32)
    partial_value = partial_value.reshape(exp_count, slot_count, feature_width)
    result = jnp.zeros((exp_count, per_exp, slot_count, feature_width), jnp.float32)
    partial_all = lax.dynamic_update_index_in_dim(result, partial_value, local_expert, 1)

    def by_expert(returned):
        last_width = returned.shape[-1]
        if per_exp == 1:
            grouped = returned.reshape(EXPERTS, exp_count // EXPERTS, CAP, last_width)
            return jnp.sum(grouped, axis=1, dtype=jnp.float32)
        return returned.reshape(EXPERTS, CAP, last_width).astype(jnp.float32)

    summed = lax.psum_scatter(
        partial_all.astype(jnp.bfloat16), "unit", scatter_dimension=3, tiled=True
    ).astype(jnp.float32)
    returned = lax.all_to_all(
        summed.astype(jnp.bfloat16), "exp", split_axis=0, concat_axis=0, tiled=True
    ).astype(summed.dtype)
    per_expert = by_expert(returned)
    last_width = per_expert.shape[-1]
    picked = per_expert.reshape(EXPERTS * CAP, last_width)[route_slot].reshape(
        tok_count, 2, last_width
    )
    mixed = jnp.sum(route_weight[:, :, None] * picked, axis=1)
    return mixed.astype(jnp.bfloat16)


def place(sizes):
    exp_count, groups = sizes
    return lax.axis_index("exp"), lax.axis_index("unit") // 2, lax.axis_index("unit") % 2


def pick_rows(named, before, d):
    rows = named.shape[1]
    place_of = jnp.where(named[d : d + 1, :] > 0, before[d : d + 1, :], -1)
    return (place_of == lax.broadcasted_iota(jnp.int32, (CAP, rows), 0)).astype(F32)


def count_earlier(ids, experts):
    rows = ids.shape[1]
    earlier = (
        lax.broadcasted_iota(jnp.int32, (rows, rows), 0)
        < lax.broadcasted_iota(jnp.int32, (rows, rows), 1)
    ).astype(BF16)
    named = ((ids[0:1, :] == experts) | (ids[1:2, :] == experts)).astype(jnp.int32)
    before = jnp.dot(named.astype(BF16), earlier, preferred_element_type=F32)
    return named, before.astype(jnp.int32)


def group_experts(exp_count, groups, z, g, rows):
    distance = lax.broadcasted_iota(jnp.int32, (max(8, exp_count), rows), 0)
    return lax.rem(z + distance, exp_count) * groups + g


def fetch_rows(weight, line, buffer, sem):
    def start(index, carry):
        pltpu.make_async_copy(
            weight.at[
                pl.ds(line * BLOCK, BLOCK), pl.ds(pl.multiple_of(index * BLOCK, BLOCK), BLOCK)
            ],
            buffer.at[index],
            sem,
        ).start()
        return carry

    lax.fori_loop(0, buffer.shape[0], start, 0)


def fetch_columns(sizes, down, offset, keep, step, buffer, sem):
    exp_count, groups = sizes
    z, g, s = place(sizes)
    side = s if keep else 1 - s
    part = down.shape[1] // (2 * groups)
    column = (lax.rem(g + offset, groups) * 2 + side) * part + step * BLOCK

    def start(index, carry):
        pltpu.make_async_copy(
            down.at[
                pl.ds(pl.multiple_of(index * BLOCK, BLOCK), BLOCK),
                pl.ds(pl.multiple_of(column, BLOCK), BLOCK),
            ],
            buffer.at[index],
            sem,
        ).start()
        return carry

    lax.fori_loop(0, buffer.shape[0], start, 0)


def await_all(buffer, sem):
    pltpu.make_async_copy(buffer, buffer, sem).wait()


def stacked(buffer):
    return buffer[...].reshape(buffer.shape[0] * BLOCK, BLOCK)


def route_kernel(sizes, width, tokens_hbm, gain_hbm, ids_hbm, gate, own, buffer, *rest):
    exp_count, groups = sizes
    sends, (tokens, normed, gain, ids, sems, gate_sem) = rest[:-6], rest[-6:]
    rows, features = tokens.shape
    count = 4
    lines = [pl.ds(n * (rows // count), rows // count) for n in range(count)]
    pairs = [(gain_hbm, gain), (ids_hbm, ids)]
    pairs += [(tokens_hbm.at[part, :], tokens.at[part, :]) for part in lines]
    copies = [pltpu.make_async_copy(a, b, sems.at[n]) for n, (a, b) in enumerate(pairs)]
    for copy in copies:
        copy.start()
    fetch_rows(gate, 0, buffer, gate_sem)
    z, g, s = place(sizes)
    copies[0].wait()
    copies[1].wait()
    named, before = count_earlier(ids, group_experts(exp_count, groups, z, g, rows))
    picks = [pick_rows(named, before, d) for d in range(exp_count)]
    others = jnp.concatenate(picks[1:], axis=0).astype(BF16)
    step = 16
    for first in range(0, rows, step):
        if first % (rows // count) == 0:
            copies[2 + first // (rows // count)].wait()
        values = tokens[first : first + step, :].astype(F32)
        mean = jnp.sum(values * values, axis=1, keepdims=True) * (1.0 / features)
        inv_rms = lax.rsqrt(mean + EPSILON)
        normed[first : first + step, :] = (values * inv_rms * gain[...]).astype(BF16)
    start = pl.multiple_of(s * (features // 2), 128)
    found = jnp.dot(others, normed[:, pl.ds(start, width)], preferred_element_type=F32)
    for d, send in enumerate(sends):
        send[...] = found[d * CAP : (d + 1) * CAP, :].astype(BF16)
    own[...] = jnp.dot(
        picks[0].astype(BF16), normed[...], preferred_element_type=F32
    ).astype(BF16)
    await_all(buffer, gate_sem)


def distances(exp_count):
    middle = exp_count // 2
    return [middle] + [d for d in range(1, exp_count) if d != middle]


def arrivals(sizes):
    exp_count, groups = sizes
    order = distances(exp_count) + [0]
    early = [(o, d) for o in range(1, groups) for d in order]
    late = [(0, d) for d in order]
    return early, late


def table_kernel(
    sizes, ids_hbm, weights_hbm, after, gate, up, _, combine_high, combine_low, buffer, ids, weights,
    sems, sem
):
    exp_count, groups = sizes
    lines = gate.shape[0] // BLOCK
    last = READY - 1
    fetch_rows(gate if last < lines else up, last % lines, buffer, sem)
    pairs = ((ids_hbm, ids), (weights_hbm, weights))
    copies = [pltpu.make_async_copy(a, b, sems.at[n]) for n, (a, b) in enumerate(pairs)]
    for copy in copies:
        copy.start()
    for copy in copies:
        copy.wait()
    rows = ids.shape[1]
    z, g, s = place(sizes)
    zero = jnp.zeros((CAP, rows), F32)
    padded = combine_high.shape[2]
    batches = arrivals(sizes)
    experts = [
        lax.rem(z + d, exp_count) * groups + lax.rem(g - o + groups, groups)
        for batch in batches
        for o, d in batch
    ]
    line = lax.broadcasted_iota(jnp.int32, (max(8, len(experts)), rows), 0)
    listed = jnp.full(line.shape, -1, jnp.int32)
    for n, expert in enumerate(experts):
        listed = jnp.where(line == n, expert, listed)
    named, before = count_earlier(ids, listed)
    for order, batch in enumerate(batches):
        parts = []
        for n in range(len(batch)):
            entry = order * len(batch) + n
            here = pick_rows(named, before, entry) > 0
            first = jnp.where(here & (ids[0:1, :] == experts[entry]), weights[0:1, :], zero)
            second = jnp.where(here & (ids[1:2, :] == experts[entry]), weights[1:2, :], zero)
            parts.append(first + second)
        if padded > len(batch) * CAP:
            parts.append(jnp.zeros((padded - len(batch) * CAP, rows), F32))
        table = jnp.concatenate(parts, axis=0).T
        high = table.astype(BF16)
        combine_high[order] = high
        combine_low[order] = (table - high.astype(F32)).astype(BF16)
    await_all(buffer, sem)


def prepare_kernel(sizes, rows, active_hbm, gate, up, after, _, mask, *rest):
    exp_count, groups = sizes
    *buffers, active, small_sem, sems = rest
    z, g, s = place(sizes)
    small = pltpu.make_async_copy(active_hbm, active, small_sem)
    small.start()
    lines = gate.shape[0] // BLOCK
    for n, buffer in enumerate(buffers[1 : READY - 1], 1):
        fetch_rows(gate if n < lines else up, n % lines, buffer, sems.at[n])
    small.wait()
    unit_width = mask.shape[1]
    blocks = lax.broadcasted_iota(jnp.int32, mask.shape, 1) // BLK + s * (unit_width // BLK)
    source = lax.broadcasted_iota(jnp.int32, (mask.shape[0], 1), 0)
    own_expert = z * groups + g

    def add_entry(k, found):
        entry = jnp.full((mask.shape[0], 1), -1, jnp.int32)
        for d in range(exp_count):
            tile = lax.rem(z - d + exp_count, exp_count) * rows // TILE
            entry = jnp.where(source == d, active[tile, own_expert, k], entry)
        return jnp.where(blocks == entry, 1.0, found)

    mask[...] = lax.fori_loop(0, active.shape[2], add_entry, jnp.zeros(mask.shape, F32))
    for n, buffer in enumerate(buffers[1 : READY - 1], 1):
        await_all(buffer, sems.at[n])


def join_kernel(order, after, *refs):
    pieces = [refs[order.index(d + 1)][...].astype(F32) for d in range(len(order))]
    refs[-1][...] = jnp.concatenate(pieces, axis=0).astype(BF16)


def hidden_kernel(sizes, own, mine, other, *refs):
    exp_count, groups = sizes
    z, g, s = place(sizes)
    refs = list(refs)
    refs = refs[BUFFERS:]
    up, down, mask, _, hidden, gives = [refs.pop(0) for _ in range(6)]
    buffers = [refs.pop(0) for _ in range(BUFFERS)]
    total, rows, sems = refs
    half = own.shape[1] // 2
    features, unit_width = up.shape
    columns, lines = unit_width // BLOCK, features // BLOCK
    given = features // (2 * groups) // BLOCK
    count = len(buffers)

    def fetch(index):
        buffer, sem = buffers[index % count], sems.at[index % count]
        if index < 2 * lines:
            fetch_rows(up, index - lines, buffer, sem)
        elif index < 2 * lines + groups * given:
            order, step = divmod(index - 2 * lines, given)
            fetch_columns(sizes, down, order + 1, False, step, buffer, sem)
        elif index < 2 * lines + (groups + 1) * given:
            step = index - 2 * lines - groups * given
            fetch_columns(sizes, down, 1, True, step, buffer, sem)

    for index in range(READY, count):
        fetch(index)
    for source, side in ((mine, s), (other, 1 - s)):
        cols = pl.ds(pl.multiple_of(side * half, 128), half)
        joined = [own[:, cols].astype(F32), source[...].astype(F32)]
        rows[:, cols] = jnp.concatenate(joined, axis=0).astype(BF16)
    for index in range(0, 2 * lines, 2):
        pair = [buffers[(index + n) % count] for n in range(2)]
        for n in range(2):
            if index + n >= READY:
                await_all(pair[n], sems.at[(index + n) % count])
        line = index % lines
        left = [rows[:, (line + n) * BLOCK : (line + n + 1) * BLOCK] for n in range(2)]
        for column in range(columns):
            cols = slice(column * BLOCK, (column + 1) * BLOCK)
            value = jnp.dot(left[0], pair[0][column], preferred_element_type=F32)
            value = value + jnp.dot(left[1], pair[1][column], preferred_element_type=F32)
            if line > 0:
                value = total[:, cols] + value
            if line < lines - 2:
                total[:, cols] = value
                continue
            if index < lines:
                hidden[:, cols] = jnp.maximum(value, 0.0).astype(BF16)
                continue
            value = hidden[:, cols].astype(F32) * jnp.maximum(value, 0.0)
            parts = []
            for d in range(exp_count):
                parts.append(value[d * CAP : (d + 1) * CAP, :] * mask[d : d + 1, cols])
            hidden[:, cols] = jnp.concatenate(parts, axis=0).astype(BF16)
        for n in range(2):
            fetch(index + n + count)
    for index in range(2 * lines, 2 * lines + (groups + 1) * given):
        buffer = buffers[index % count]
        await_all(buffer, sems.at[index % count])
        step = index - 2 * lines
        if step < given:
            value = jnp.dot(hidden[...], stacked(buffer), preferred_element_type=F32)
            gives[:, step * BLOCK : (step + 1) * BLOCK] = value.astype(BF16)


def give_kernel(sizes, offset, hidden, *refs):
    exp_count, groups = sizes
    *weights, down, given, kept_weights, sem = refs
    fetch_columns(sizes, down, offset, True, 0, kept_weights, sem)
    for step, buffer in enumerate(weights):
        value = jnp.dot(hidden[...], stacked(buffer), preferred_element_type=F32)
        given[:, step * BLOCK : (step + 1) * BLOCK] = value.astype(BF16)
    await_all(kept_weights, sem)


def keep_kernel(sizes, ahead, hidden, received, *refs):
    exp_count, groups = sizes
    refs = list(refs)
    if ahead is not None:
        sem, down = refs.pop(), refs.pop(0)
        next_weights = refs[received.shape[1] // BLOCK + exp_count :]
        for step, buffer in enumerate(next_weights, 1):
            fetch_columns(sizes, down, ahead, True, step, buffer, sem.at[step - 1])
    weights = refs[: received.shape[1] // BLOCK]
    outs = refs[len(weights) : len(weights) + exp_count]
    for step, buffer in enumerate(weights):
        cols = slice(step * BLOCK, (step + 1) * BLOCK)
        value = jnp.dot(hidden[...], stacked(buffer), preferred_element_type=F32)
        value = value + received[:, cols].astype(F32)
        for d in range(exp_count):
            outs[d][:, cols] = value[d * CAP : (d + 1) * CAP, :].astype(BF16)
    if ahead is not None:
        for step, buffer in enumerate(next_weights, 1):
            await_all(buffer, sem.at[step - 1])


def combine_kernel(order, high, low, *refs):
    refs = list(refs)
    out = refs.pop()
    before = refs.pop(0) if order > 0 else None
    found = jnp.concatenate([r[...].astype(F32) for r in refs], axis=0).astype(BF16)
    count = found.shape[0]
    value = jnp.dot(high[order, :, :count], found, preferred_element_type=F32)
    value = value + jnp.dot(low[order, :, :count], found, preferred_element_type=F32)
    if before is not None:
        value = before[...] + value
    out[...] = value.astype(out.dtype)


def call(kernel, outs, ins, scratch=(), flops=0, moved=0, aliases=None):
    vmem = pl.BlockSpec(memory_space=pltpu.VMEM)
    arrays, specs = [], []
    for array, space in ins:
        if space in (pltpu.HBM, pltpu.VMEM):
            array = pltpu.with_memory_space_constraint(array, space)
        arrays.append(array)
        specs.append(vmem if space is None else pl.BlockSpec(memory_space=space))
    shapes = []
    for shape, kind, *space in outs:
        shapes.append(space[0](shape, kind) if space else jax.ShapeDtypeStruct(shape, kind))
    return pl.pallas_call(
        kernel,
        out_shape=shapes,
        in_specs=specs,
        out_specs=[vmem] * len(outs),
        scratch_shapes=list(scratch),
        input_output_aliases=aliases or {},
        compiler_params=pltpu.CompilerParams(vmem_limit_bytes=LIMIT << 20),
        cost_estimate=pl.CostEstimate(flops=flops, bytes_accessed=moved, transcendentals=0),
    )(*arrays)


def paired_experts(
    tokens, norm_gain, route_ids, route_weight, active_blocks, gate_weight, up_weight, down_weight
):
    exp_count, unit_count = lax.axis_size("exp"), lax.axis_size("unit")
    groups = unit_count // 2
    sizes = (exp_count, groups)
    tok_count, features = tokens.shape
    unit_width = gate_weight.shape[1]
    slots = exp_count * CAP
    half = features // 2
    width = half
    ids = route_ids.T
    weights = route_weight.T

    def shift(value, distance, group_shift=0):
        pairs = []
        for z in range(exp_count):
            for u in range(unit_count):
                target = (z + distance) % exp_count
                group = (u // 2 + group_shift) % groups
                pairs.append((z * unit_count + u, target * unit_count + group * 2 + u % 2))
        return lax.ppermute(value, ("exp", "unit"), pairs)

    def swap(value):
        return lax.ppermute(value, "unit", [(u, u ^ 1) for u in range(unit_count)])

    batch = exp_count - 1
    buffer = ((unit_width // BLOCK, BLOCK, BLOCK), BF16, pltpu.VMEM)
    piece_bytes = 2 * unit_width * BLOCK
    own, ready, *sends = call(
        functools.partial(route_kernel, sizes, width),
        [((CAP, features), BF16), buffer] + [((CAP, width), BF16)] * batch,
        [
            (tokens, pltpu.HBM),
            (norm_gain.reshape(1, -1), pltpu.HBM),
            (ids, pltpu.HBM),
            (gate_weight, pltpu.HBM),
        ],
        [
            pltpu.VMEM((tok_count, features), BF16),
            pltpu.VMEM((tok_count, features), BF16),
            pltpu.VMEM((1, features), F32),
            pltpu.VMEM(ids.shape, jnp.int32),
            pltpu.SemaphoreType.DMA((6,)),
            pltpu.SemaphoreType.DMA,
        ],
        flops=2 * tok_count * slots * width,
        moved=4 * tok_count * features + piece_bytes,
    )
    mask, *ready = call(
        functools.partial(prepare_kernel, sizes, tok_count),
        [((max(8, exp_count), unit_width), F32)] + [buffer] * BUFFERS,
        [
            (active_blocks, pltpu.HBM),
            (gate_weight, pltpu.HBM),
            (up_weight, pltpu.HBM),
            (own, pl.ANY),
            (ready, pltpu.VMEM),
        ],
        [
            pltpu.SMEM(active_blocks.shape, jnp.int32),
            pltpu.SemaphoreType.DMA,
            pltpu.SemaphoreType.DMA((READY,)),
        ],
        flops=2 * tok_count * slots * features,
        moved=(READY - 2) * piece_bytes,
        aliases={4: 1},
    )
    order = distances(exp_count)
    arrived = [shift(sends[d - 1], d) for d in order]
    mine = call(
        functools.partial(join_kernel, order),
        [((batch * CAP, width), BF16)],
        [(mask, pl.ANY)] + [(v, None) for v in arrived],
        moved=1 << 20,
    )[0]
    other = swap(mine)
    padded = -(-slots // 128) * 128
    combine_high, combine_low, ready[READY - 1] = call(
        functools.partial(table_kernel, sizes),
        [((2, tok_count, padded), BF16)] * 2 + [buffer],
        [
            (ids, pltpu.HBM),
            (weights, pltpu.HBM),
            (mine, pl.ANY),
            (gate_weight, pltpu.HBM),
            (up_weight, pltpu.HBM),
            (ready[READY - 1], pltpu.VMEM),
        ],
        [
            pltpu.VMEM(ids.shape, jnp.int32),
            pltpu.VMEM(weights.shape, F32),
            pltpu.SemaphoreType.DMA((2,)),
            pltpu.SemaphoreType.DMA,
        ],
        moved=1 << 22,
        aliases={5: 2},
    )
    part = features // unit_count
    hidden, first_given, *buffers = call(
        functools.partial(hidden_kernel, sizes),
        [((slots, unit_width), BF16), ((slots, part), BF16)] + [buffer] * BUFFERS,
        [(own, None), (mine, None), (other, None)]
        + [(v, pltpu.VMEM) for v in ready]
        + [(up_weight, pltpu.HBM), (down_weight, pltpu.HBM), (mask, None)]
        + [(combine_low, pl.ANY)],
        [
            pltpu.VMEM((slots, unit_width), F32),
            pltpu.VMEM((slots, features), BF16),
            pltpu.SemaphoreType.DMA((BUFFERS,)),
        ],
        flops=2 * 2 * slots * features * unit_width,
        moved=10 * piece_bytes,
        aliases={3 + n: 2 + n for n in range(BUFFERS)},
    )
    steps = part // BLOCK
    offsets = [(order + 1) % groups for order in range(groups)]
    first = 2 * features // BLOCK + groups * steps
    given = [first_given]
    kept_weights = [[buffers[(first + step) % BUFFERS] for step in range(steps)]]
    for order, offset in list(enumerate(offsets))[1:]:
        first = 2 * features // BLOCK + order * steps
        value, *kept = call(
            functools.partial(give_kernel, sizes, offset),
            [((slots, part), BF16), buffer],
            [(hidden, None)]
            + [(buffers[(first + step) % BUFFERS], pltpu.VMEM) for step in range(steps)]
            + [(down_weight, pltpu.HBM)],
            [pltpu.SemaphoreType.DMA],
            flops=2 * slots * unit_width * part,
            moved=piece_bytes,
        )
        given.append(value)
        kept_weights.append(kept)
    taken = [swap(value) for value in given]
    home = {}
    for order, offset in enumerate(offsets):
        more = order < groups - 1
        outs = call(
            functools.partial(keep_kernel, sizes, offsets[order + 1] if more else None),
            [((CAP, part), BF16)] * exp_count + [buffer] * (steps - 1 if more else 0),
            [(hidden, None), (taken[order], None)]
            + ([(down_weight, pltpu.HBM)] if more else [])
            + [(v, pltpu.VMEM) for v in kept_weights[order]],
            [pltpu.SemaphoreType.DMA((steps - 1,))] if more else [],
            flops=2 * slots * unit_width * part,
            moved=piece_bytes,
        )
        kept = outs[:exp_count]
        if more:
            kept_weights[order + 1] = list(kept_weights[order + 1]) + list(outs[exp_count:])
        for d in distances(exp_count) + [0]:
            home[offset, d] = shift(kept[d], -d, offset) if d or offset else kept[d]
    mixed = None
    for order, batch in enumerate(arrivals(sizes)):
        last = order == 1
        mixed = call(
            functools.partial(combine_kernel, order),
            [((tok_count, part), BF16 if last else F32)],
            [(combine_high, None), (combine_low, None)]
            + ([(mixed, None)] if order else [])
            + [(home[key], None) for key in batch],
            flops=4 * tok_count * slots * part,
            moved=1 << 20,
        )[0]
    return mixed


def per_device(*operands):
    tokens, gate_weight = operands[0], operands[5]
    exp_count, unit_count = lax.axis_size("exp"), lax.axis_size("unit")
    unit_width = gate_weight.shape[1]
    paired = (
        2 * unit_width == FF
        and unit_count % 2 == 0
        and exp_count * unit_count // 2 == EXPERTS
        and TILE % tokens.shape[0] == 0
        and unit_width % BLOCK == 0
        and unit_count == 4
        and tokens.shape[1] % (unit_count * BLOCK) == 0
        and tokens.shape[1] <= READY * BLOCK <= 2 * tokens.shape[1]
    )
    return (paired_experts if paired else spread_experts)(*operands)


def solution(mesh):
    return jax.shard_map(
        per_device,
        mesh=mesh,
        in_specs=(
            P(("rep", "exp"), None),
            P(),
            P(("rep", "exp"), None),
            P(("rep", "exp"), None),
            P("rep", None, None),
            P(None, ("exp", "unit")),
            P(None, ("exp", "unit")),
            P(("exp", "unit"), None),
        ),
        out_specs=P(("rep", "exp"), "unit"),
        check_vma=False,
    )
```

```python
import functools

import jax
import jax.numpy as jnp
import numpy as np
from jax import lax
from jax.experimental import pallas as pl
from jax.experimental.pallas import tpu as pltpu
from jax.sharding import PartitionSpec as P

EXPERTS = 8
FF = 7168
BLK = 64
TILE = 256
CAP = 40

EPSILON = 1e-05

BLOCK = 512
READY = 12
BUFFERS = 13
LIMIT = 5

F32 = jnp.float32
BF16 = jnp.bfloat16


def normalize(tokens, norm_gain):
    values = tokens.astype(jnp.float32)
    inv_rms = lax.rsqrt(jnp.mean(values * values, axis=-1, keepdims=True) + EPSILON)
    return (values * inv_rms * norm_gain).astype(jnp.bfloat16)


def slot_numbers(entries, expert_count):
    onehot = (entries[..., None] == jnp.arange(expert_count, dtype=jnp.int32)).astype(jnp.int32)
    before = jnp.cumsum(onehot, axis=-2, dtype=jnp.int32) - onehot
    return jnp.sum(before * onehot, axis=-1)


def spread_experts(
    tokens, norm_gain, route_ids, route_weight, active_blocks, gate_weight, up_weight, down_weight
):
    exp_count = lax.axis_size("exp")
    unit_count = lax.axis_size("unit")
    tok_count, feature_width = tokens.shape
    unit_width = gate_weight.shape[1]
    row_units = unit_count * unit_width
    per_exp = max(1, row_units // FF)
    part_width = feature_width // unit_count
    block_count = unit_width // BLK
    tile_count = active_blocks.shape[0]
    exp_index = lax.axis_index("exp")
    unit_index = lax.axis_index("unit")
    first_unit = (exp_index * unit_count + unit_index) * unit_width
    own_expert = first_unit // FF
    first_block = first_unit % FF // BLK
    local_expert = own_expert - exp_index * row_units // FF
    normed = normalize(tokens, norm_gain)
    slot_index = slot_numbers(route_ids.reshape(1, -1), EXPERTS).reshape(tok_count, 2)
    positions = jnp.arange(tok_count, dtype=jnp.int32)
    tile_of = (exp_index * tok_count + positions) // TILE
    route_slot = (route_ids * CAP + slot_index).reshape(-1)
    token_source = (
        jnp.full((EXPERTS * CAP,), tok_count, jnp.int32)
        .at[route_slot]
        .set(jnp.repeat(positions, 2))
    )
    row_experts = np.arange(exp_count)[:, None] * row_units // FF + np.arange(per_exp)[None, :]
    slot_source = token_source.reshape(EXPERTS, CAP)[row_experts]
    padded_tiles = jnp.concatenate([tile_of, jnp.zeros((1,), jnp.int32)])
    slot_tiles = padded_tiles[slot_source]
    active_mine = lax.dynamic_index_in_dim(active_blocks, own_expert, 1, keepdims=False)
    local_blocks = first_block + jnp.arange(block_count, dtype=jnp.int32)
    block_on = jnp.any(active_mine[:, :, None] == local_blocks[None, None, :], axis=1).astype(
        jnp.float32
    )
    row_part = lax.dynamic_slice_in_dim(normed, unit_index * part_width, part_width, 1)
    padded_rows = jnp.concatenate([row_part, jnp.zeros((1, part_width), jnp.bfloat16)], 0)
    whole_rows = lax.all_gather(
        lax.all_to_all(padded_rows[slot_source], "exp", split_axis=0, concat_axis=0, tiled=True),
        "unit",
        axis=3,
        tiled=True,
    )
    slot_count = whole_rows.shape[2]
    own_rows = lax.dynamic_index_in_dim(whole_rows, local_expert, 1, keepdims=False).reshape(
        -1, feature_width
    )
    own_tiles = lax.dynamic_index_in_dim(
        lax.all_to_all(slot_tiles, "exp", split_axis=0, concat_axis=0, tiled=True),
        local_expert,
        1,
        keepdims=False,
    ).reshape(-1)
    tile_hot = (own_tiles[:, None] == jnp.arange(tile_count, dtype=jnp.int32)[None, :]).astype(
        jnp.float32
    )
    row_mask = jnp.dot(tile_hot, block_on, precision=lax.Precision.HIGHEST)
    gate_acts = jnp.dot(own_rows, gate_weight, preferred_element_type=jnp.float32)
    up_acts = jnp.dot(own_rows, up_weight, preferred_element_type=jnp.float32)
    hidden = jax.nn.relu(gate_acts) * jax.nn.relu(up_acts)
    hidden = (hidden.reshape(-1, block_count, BLK) * row_mask[:, :, None]).reshape(-1, unit_width)
    hidden = hidden.astype(jnp.bfloat16)
    partial_value = jnp.dot(hidden, down_weight, preferred_element_type=jnp.float32)
    partial_value = partial_value.reshape(exp_count, slot_count, feature_width)
    result = jnp.zeros((exp_count, per_exp, slot_count, feature_width), jnp.float32)
    partial_all = lax.dynamic_update_index_in_dim(result, partial_value, local_expert, 1)

    def by_expert(returned):
        last_width = returned.shape[-1]
        if per_exp == 1:
            grouped = returned.reshape(EXPERTS, exp_count // EXPERTS, CAP, last_width)
            return jnp.sum(grouped, axis=1, dtype=jnp.float32)
        return returned.reshape(EXPERTS, CAP, last_width).astype(jnp.float32)

    summed = lax.psum_scatter(
        partial_all.astype(jnp.bfloat16), "unit", scatter_dimension=3, tiled=True
    ).astype(jnp.float32)
    returned = lax.all_to_all(
        summed.astype(jnp.bfloat16), "exp", split_axis=0, concat_axis=0, tiled=True
    ).astype(summed.dtype)
    per_expert = by_expert(returned)
    last_width = per_expert.shape[-1]
    picked = per_expert.reshape(EXPERTS * CAP, last_width)[route_slot].reshape(
        tok_count, 2, last_width
    )
    mixed = jnp.sum(route_weight[:, :, None] * picked, axis=1)
    return mixed.astype(jnp.bfloat16)


def place(sizes):
    exp_count, groups = sizes
    return lax.axis_index("exp"), lax.axis_index("unit") // 2, lax.axis_index("unit") % 2


def pick_rows(named, before, d):
    rows = named.shape[1]
    place_of = jnp.where(named[d : d + 1, :] > 0, before[d : d + 1, :], -1)
    return (place_of == lax.broadcasted_iota(jnp.int32, (CAP, rows), 0)).astype(F32)


def count_earlier(ids, experts):
    rows = ids.shape[1]
    earlier = (
        lax.broadcasted_iota(jnp.int32, (rows, rows), 0)
        < lax.broadcasted_iota(jnp.int32, (rows, rows), 1)
    ).astype(BF16)
    named = ((ids[0:1, :] == experts) | (ids[1:2, :] == experts)).astype(jnp.int32)
    before = jnp.dot(named.astype(BF16), earlier, preferred_element_type=F32)
    return named, before.astype(jnp.int32)


def group_experts(exp_count, groups, z, g, rows):
    distance = lax.broadcasted_iota(jnp.int32, (max(8, exp_count), rows), 0)
    return lax.rem(z + distance, exp_count) * groups + g


def fetch_rows(weight, line, buffer, sem):
    def start(index, carry):
        pltpu.make_async_copy(
            weight.at[
                pl.ds(line * BLOCK, BLOCK), pl.ds(pl.multiple_of(index * BLOCK, BLOCK), BLOCK)
            ],
            buffer.at[index],
            sem,
        ).start()
        return carry

    lax.fori_loop(0, buffer.shape[0], start, 0)


def fetch_columns(sizes, down, offset, keep, step, buffer, sem):
    exp_count, groups = sizes
    z, g, s = place(sizes)
    side = s if keep else 1 - s
    part = down.shape[1] // (2 * groups)
    column = (lax.rem(g + offset, groups) * 2 + side) * part + step * BLOCK

    def start(index, carry):
        pltpu.make_async_copy(
            down.at[
                pl.ds(pl.multiple_of(index * BLOCK, BLOCK), BLOCK),
                pl.ds(pl.multiple_of(column, BLOCK), BLOCK),
            ],
            buffer.at[index],
            sem,
        ).start()
        return carry

    lax.fori_loop(0, buffer.shape[0], start, 0)


def await_all(buffer, sem):
    pltpu.make_async_copy(buffer, buffer, sem).wait()


def stacked(buffer):
    return buffer[...].reshape(buffer.shape[0] * BLOCK, BLOCK)


def route_kernel(sizes, width, tokens_hbm, gain_hbm, ids_hbm, gate, own, buffer, *rest):
    exp_count, groups = sizes
    sends, (tokens, normed, gain, ids, sems, gate_sem) = rest[:-6], rest[-6:]
    rows, features = tokens.shape
    count = 4
    lines = [pl.ds(n * (rows // count), rows // count) for n in range(count)]
    pairs = [(gain_hbm, gain), (ids_hbm, ids)]
    pairs += [(tokens_hbm.at[part, :], tokens.at[part, :]) for part in lines]
    copies = [pltpu.make_async_copy(a, b, sems.at[n]) for n, (a, b) in enumerate(pairs)]
    for copy in copies:
        copy.start()
    fetch_rows(gate, 0, buffer, gate_sem)
    z, g, s = place(sizes)
    copies[0].wait()
    copies[1].wait()
    named, before = count_earlier(ids, group_experts(exp_count, groups, z, g, rows))
    picks = [pick_rows(named, before, d) for d in range(exp_count)]
    others = jnp.concatenate(picks[1:], axis=0).astype(BF16)
    step = 16
    for first in range(0, rows, step):
        if first % (rows // count) == 0:
            copies[2 + first // (rows // count)].wait()
        values = tokens[first : first + step, :].astype(F32)
        mean = jnp.sum(values * values, axis=1, keepdims=True) * (1.0 / features)
        inv_rms = lax.rsqrt(mean + EPSILON)
        normed[first : first + step, :] = (values * inv_rms * gain[...]).astype(BF16)
    start = pl.multiple_of(s * (features // 2), 128)
    found = jnp.dot(others, normed[:, pl.ds(start, width)], preferred_element_type=F32)
    for d, send in enumerate(sends):
        send[...] = found[d * CAP : (d + 1) * CAP, :].astype(BF16)
    own[...] = jnp.dot(
        picks[0].astype(BF16), normed[...], preferred_element_type=F32
    ).astype(BF16)
    await_all(buffer, gate_sem)


def distances(exp_count):
    middle = exp_count // 2
    return [middle] + [d for d in range(1, exp_count) if d != middle]


def arrivals(sizes):
    exp_count, groups = sizes
    order = distances(exp_count) + [0]
    early = [(o, d) for o in range(1, groups) for d in order]
    late = [(0, d) for d in order]
    return early, late


def table_kernel(
    sizes, ids_hbm, weights_hbm, after, gate, up, _, combine_high, combine_low, buffer, ids, weights,
    sems, sem
):
    exp_count, groups = sizes
    lines = gate.shape[0] // BLOCK
    last = READY - 1
    fetch_rows(gate if last < lines else up, last % lines, buffer, sem)
    pairs = ((ids_hbm, ids), (weights_hbm, weights))
    copies = [pltpu.make_async_copy(a, b, sems.at[n]) for n, (a, b) in enumerate(pairs)]
    for copy in copies:
        copy.start()
    for copy in copies:
        copy.wait()
    rows = ids.shape[1]
    z, g, s = place(sizes)
    zero = jnp.zeros((CAP, rows), F32)
    padded = combine_high.shape[2]
    batches = arrivals(sizes)
    experts = [
        lax.rem(z + d, exp_count) * groups + lax.rem(g - o + groups, groups)
        for batch in batches
        for o, d in batch
    ]
    line = lax.broadcasted_iota(jnp.int32, (max(8, len(experts)), rows), 0)
    listed = jnp.full(line.shape, -1, jnp.int32)
    for n, expert in enumerate(experts):
        listed = jnp.where(line == n, expert, listed)
    named, before = count_earlier(ids, listed)
    for order, batch in enumerate(batches):
        parts = []
        for n in range(len(batch)):
            entry = order * len(batch) + n
            here = pick_rows(named, before, entry) > 0
            first = jnp.where(here & (ids[0:1, :] == experts[entry]), weights[0:1, :], zero)
            second = jnp.where(here & (ids[1:2, :] == experts[entry]), weights[1:2, :], zero)
            parts.append(first + second)
        if padded > len(batch) * CAP:
            parts.append(jnp.zeros((padded - len(batch) * CAP, rows), F32))
        table = jnp.concatenate(parts, axis=0).T
        high = table.astype(BF16)
        combine_high[order] = high
        combine_low[order] = (table - high.astype(F32)).astype(BF16)
    await_all(buffer, sem)


def prepare_kernel(sizes, rows, active_hbm, gate, up, after, _, mask, *rest):
    exp_count, groups = sizes
    *buffers, active, small_sem, sems = rest
    z, g, s = place(sizes)
    small = pltpu.make_async_copy(active_hbm, active, small_sem)
    small.start()
    lines = gate.shape[0] // BLOCK
    for n, buffer in enumerate(buffers[1 : READY - 1], 1):
        fetch_rows(gate if n < lines else up, n % lines, buffer, sems.at[n])
    small.wait()
    unit_width = mask.shape[1]
    blocks = lax.broadcasted_iota(jnp.int32, mask.shape, 1) // BLK + s * (unit_width // BLK)
    source = lax.broadcasted_iota(jnp.int32, (mask.shape[0], 1), 0)
    own_expert = z * groups + g

    def add_entry(k, found):
        entry = jnp.full((mask.shape[0], 1), -1, jnp.int32)
        for d in range(exp_count):
            tile = lax.rem(z - d + exp_count, exp_count) * rows // TILE
            entry = jnp.where(source == d, active[tile, own_expert, k], entry)
        return jnp.where(blocks == entry, 1.0, found)

    mask[...] = lax.fori_loop(0, active.shape[2], add_entry, jnp.zeros(mask.shape, F32))
    for n, buffer in enumerate(buffers[1 : READY - 1], 1):
        await_all(buffer, sems.at[n])


def join_kernel(order, after, *refs):
    pieces = [refs[order.index(d + 1)][...].astype(F32) for d in range(len(order))]
    refs[-1][...] = jnp.concatenate(pieces, axis=0).astype(BF16)


def hidden_kernel(sizes, own, mine, other, *refs):
    exp_count, groups = sizes
    z, g, s = place(sizes)
    refs = list(refs)
    refs = refs[BUFFERS:]
    up, down, mask, _, hidden, gives = [refs.pop(0) for _ in range(6)]
    buffers = [refs.pop(0) for _ in range(BUFFERS)]
    total, rows, sems = refs
    half = own.shape[1] // 2
    features, unit_width = up.shape
    columns, lines = unit_width // BLOCK, features // BLOCK
    given = features // (2 * groups) // BLOCK
    count = len(buffers)

    def fetch(index):
        buffer, sem = buffers[index % count], sems.at[index % count]
        if index < 2 * lines:
            fetch_rows(up, index - lines, buffer, sem)
        elif index < 2 * lines + groups * given:
            order, step = divmod(index - 2 * lines, given)
            fetch_columns(sizes, down, order + 1, False, step, buffer, sem)
        elif index < 2 * lines + (groups + 1) * given:
            step = index - 2 * lines - groups * given
            fetch_columns(sizes, down, 1, True, step, buffer, sem)

    for index in range(READY, count):
        fetch(index)
    for source, side in ((mine, s), (other, 1 - s)):
        cols = pl.ds(pl.multiple_of(side * half, 128), half)
        joined = [own[:, cols].astype(F32), source[...].astype(F32)]
        rows[:, cols] = jnp.concatenate(joined, axis=0).astype(BF16)
    for index in range(0, 2 * lines, 2):
        pair = [buffers[(index + n) % count] for n in range(2)]
        for n in range(2):
            if index + n >= READY:
                await_all(pair[n], sems.at[(index + n) % count])
        line = index % lines
        left = [rows[:, (line + n) * BLOCK : (line + n + 1) * BLOCK] for n in range(2)]
        for column in range(columns):
            cols = slice(column * BLOCK, (column + 1) * BLOCK)
            value = jnp.dot(left[0], pair[0][column], preferred_element_type=F32)
            value = value + jnp.dot(left[1], pair[1][column], preferred_element_type=F32)
            if line > 0:
                value = total[:, cols] + value
            if line < lines - 2:
                total[:, cols] = value
                continue
            if index < lines:
                hidden[:, cols] = jnp.maximum(value, 0.0).astype(BF16)
                continue
            value = hidden[:, cols].astype(F32) * jnp.maximum(value, 0.0)
            parts = []
            for d in range(exp_count):
                parts.append(value[d * CAP : (d + 1) * CAP, :] * mask[d : d + 1, cols])
            hidden[:, cols] = jnp.concatenate(parts, axis=0).astype(BF16)
        for n in range(2):
            fetch(index + n + count)
    for index in range(2 * lines, 2 * lines + (groups + 1) * given):
        buffer = buffers[index % count]
        await_all(buffer, sems.at[index % count])
        step = index - 2 * lines
        if step < given:
            value = jnp.dot(hidden[...], stacked(buffer), preferred_element_type=F32)
            gives[:, step * BLOCK : (step + 1) * BLOCK] = value.astype(BF16)


def give_kernel(sizes, offset, hidden, *refs):
    exp_count, groups = sizes
    *weights, down, given, kept_weights, sem = refs
    fetch_columns(sizes, down, offset, True, 0, kept_weights, sem)
    for step, buffer in enumerate(weights):
        value = jnp.dot(hidden[...], stacked(buffer), preferred_element_type=F32)
        given[:, step * BLOCK : (step + 1) * BLOCK] = value.astype(BF16)
    await_all(kept_weights, sem)


def keep_kernel(sizes, offset, lacks, hidden, received, *refs):
    exp_count, groups = sizes
    refs = list(refs)
    extra = []
    if lacks:
        sems, scratch, down = refs.pop(), refs.pop(), refs.pop(0)
        extra = [scratch.at[n] for n in range(lacks)]
    held = received.shape[1] // BLOCK - lacks
    for n, buffer in enumerate(extra):
        fetch_columns(sizes, down, offset, True, held + n, buffer, sems.at[n])
    weights, outs = refs[:held] + extra, refs[held:]
    for step, buffer in enumerate(weights):
        if step >= held:
            await_all(buffer, sems.at[step - held])
        cols = slice(step * BLOCK, (step + 1) * BLOCK)
        value = jnp.dot(hidden[...], stacked(buffer), preferred_element_type=F32)
        value = value + received[:, cols].astype(F32)
        for d in range(exp_count):
            outs[d][:, cols] = value[d * CAP : (d + 1) * CAP, :].astype(BF16)


def combine_kernel(order, high, low, *refs):
    refs = list(refs)
    out = refs.pop()
    before = refs.pop(0) if order > 0 else None
    found = jnp.concatenate([r[...].astype(F32) for r in refs], axis=0).astype(BF16)
    count = found.shape[0]
    value = jnp.dot(high[order, :, :count], found, preferred_element_type=F32)
    value = value + jnp.dot(low[order, :, :count], found, preferred_element_type=F32)
    if before is not None:
        value = before[...] + value
    out[...] = value.astype(out.dtype)


def call(kernel, outs, ins, scratch=(), flops=0, moved=0, aliases=None):
    vmem = pl.BlockSpec(memory_space=pltpu.VMEM)
    arrays, specs = [], []
    for array, space in ins:
        if space in (pltpu.HBM, pltpu.VMEM):
            array = pltpu.with_memory_space_constraint(array, space)
        arrays.append(array)
        specs.append(vmem if space is None else pl.BlockSpec(memory_space=space))
    shapes = []
    for shape, kind, *space in outs:
        shapes.append(space[0](shape, kind) if space else jax.ShapeDtypeStruct(shape, kind))
    return pl.pallas_call(
        kernel,
        out_shape=shapes,
        in_specs=specs,
        out_specs=[vmem] * len(outs),
        scratch_shapes=list(scratch),
        input_output_aliases=aliases or {},
        compiler_params=pltpu.CompilerParams(vmem_limit_bytes=LIMIT << 20),
        cost_estimate=pl.CostEstimate(flops=flops, bytes_accessed=moved, transcendentals=0),
    )(*arrays)


def paired_experts(
    tokens, norm_gain, route_ids, route_weight, active_blocks, gate_weight, up_weight, down_weight
):
    exp_count, unit_count = lax.axis_size("exp"), lax.axis_size("unit")
    groups = unit_count // 2
    sizes = (exp_count, groups)
    tok_count, features = tokens.shape
    unit_width = gate_weight.shape[1]
    slots = exp_count * CAP
    half = features // 2
    width = half
    ids = route_ids.T
    weights = route_weight.T

    def shift(value, distance, group_shift=0):
        pairs = []
        for z in range(exp_count):
            for u in range(unit_count):
                target = (z + distance) % exp_count
                group = (u // 2 + group_shift) % groups
                pairs.append((z * unit_count + u, target * unit_count + group * 2 + u % 2))
        return lax.ppermute(value, ("exp", "unit"), pairs)

    def swap(value):
        return lax.ppermute(value, "unit", [(u, u ^ 1) for u in range(unit_count)])

    batch = exp_count - 1
    buffer = ((unit_width // BLOCK, BLOCK, BLOCK), BF16, pltpu.VMEM)
    piece_bytes = 2 * unit_width * BLOCK
    own, ready, *sends = call(
        functools.partial(route_kernel, sizes, width),
        [((CAP, features), BF16), buffer] + [((CAP, width), BF16)] * batch,
        [
            (tokens, pltpu.HBM),
            (norm_gain.reshape(1, -1), pltpu.HBM),
            (ids, pltpu.HBM),
            (gate_weight, pltpu.HBM),
        ],
        [
            pltpu.VMEM((tok_count, features), BF16),
            pltpu.VMEM((tok_count, features), BF16),
            pltpu.VMEM((1, features), F32),
            pltpu.VMEM(ids.shape, jnp.int32),
            pltpu.SemaphoreType.DMA((6,)),
            pltpu.SemaphoreType.DMA,
        ],
        flops=2 * tok_count * slots * width,
        moved=4 * tok_count * features + piece_bytes,
    )
    mask, *ready = call(
        functools.partial(prepare_kernel, sizes, tok_count),
        [((max(8, exp_count), unit_width), F32)] + [buffer] * BUFFERS,
        [
            (active_blocks, pltpu.HBM),
            (gate_weight, pltpu.HBM),
            (up_weight, pltpu.HBM),
            (own, pl.ANY),
            (ready, pltpu.VMEM),
        ],
        [
            pltpu.SMEM(active_blocks.shape, jnp.int32),
            pltpu.SemaphoreType.DMA,
            pltpu.SemaphoreType.DMA((READY,)),
        ],
        flops=2 * tok_count * slots * features,
        moved=(READY - 2) * piece_bytes,
        aliases={4: 1},
    )
    order = distances(exp_count)
    arrived = [shift(sends[d - 1], d) for d in order]
    mine = call(
        functools.partial(join_kernel, order),
        [((batch * CAP, width), BF16)],
        [(mask, pl.ANY)] + [(v, None) for v in arrived],
        moved=1 << 20,
    )[0]
    other = swap(mine)
    padded = -(-slots // 128) * 128
    combine_high, combine_low, ready[READY - 1] = call(
        functools.partial(table_kernel, sizes),
        [((2, tok_count, padded), BF16)] * 2 + [buffer],
        [
            (ids, pltpu.HBM),
            (weights, pltpu.HBM),
            (mine, pl.ANY),
            (gate_weight, pltpu.HBM),
            (up_weight, pltpu.HBM),
            (ready[READY - 1], pltpu.VMEM),
        ],
        [
            pltpu.VMEM(ids.shape, jnp.int32),
            pltpu.VMEM(weights.shape, F32),
            pltpu.SemaphoreType.DMA((2,)),
            pltpu.SemaphoreType.DMA,
        ],
        moved=1 << 22,
        aliases={5: 2},
    )
    part = features // unit_count
    hidden, first_given, *buffers = call(
        functools.partial(hidden_kernel, sizes),
        [((slots, unit_width), BF16), ((slots, part), BF16)] + [buffer] * BUFFERS,
        [(own, None), (mine, None), (other, None)]
        + [(v, pltpu.VMEM) for v in ready]
        + [(up_weight, pltpu.HBM), (down_weight, pltpu.HBM), (mask, None)]
        + [(combine_low, pl.ANY)],
        [
            pltpu.VMEM((slots, unit_width), F32),
            pltpu.VMEM((slots, features), BF16),
            pltpu.SemaphoreType.DMA((BUFFERS,)),
        ],
        flops=2 * 2 * slots * features * unit_width,
        moved=10 * piece_bytes,
        aliases={3 + n: 2 + n for n in range(BUFFERS)},
    )
    steps = part // BLOCK
    offsets = [(order + 1) % groups for order in range(groups)]
    first = 2 * features // BLOCK + groups * steps
    given = [first_given]
    kept_weights = [[buffers[(first + step) % BUFFERS] for step in range(steps)]]
    for order, offset in list(enumerate(offsets))[1:]:
        first = 2 * features // BLOCK + order * steps
        value, *kept = call(
            functools.partial(give_kernel, sizes, offset),
            [((slots, part), BF16), buffer],
            [(hidden, None)]
            + [(buffers[(first + step) % BUFFERS], pltpu.VMEM) for step in range(steps)]
            + [(down_weight, pltpu.HBM)],
            [pltpu.SemaphoreType.DMA],
            flops=2 * slots * unit_width * part,
            moved=piece_bytes,
        )
        given.append(value)
        kept_weights.append(kept)
    taken = [swap(value) for value in given]
    home = {}
    for order, offset in enumerate(offsets):
        lacks = steps - len(kept_weights[order])
        kept = call(
            functools.partial(keep_kernel, sizes, offset, lacks),
            [((CAP, part), BF16)] * exp_count,
            [(hidden, None), (taken[order], None)]
            + ([(down_weight, pltpu.HBM)] if lacks else [])
            + [(v, pltpu.VMEM) for v in kept_weights[order]],
            [
                pltpu.VMEM((lacks,) + buffer[0], BF16),
                pltpu.SemaphoreType.DMA((lacks,)),
            ]
            if lacks
            else [],
            flops=2 * slots * unit_width * part,
            moved=piece_bytes,
        )
        for d in distances(exp_count) + [0]:
            home[offset, d] = shift(kept[d], -d, offset) if d or offset else kept[d]
    mixed = None
    for order, batch in enumerate(arrivals(sizes)):
        last = order == 1
        mixed = call(
            functools.partial(combine_kernel, order),
            [((tok_count, part), BF16 if last else F32)],
            [(combine_high, None), (combine_low, None)]
            + ([(mixed, None)] if order else [])
            + [(home[key], None) for key in batch],
            flops=4 * tok_count * slots * part,
            moved=1 << 20,
        )[0]
    return mixed


def per_device(*operands):
    tokens, gate_weight = operands[0], operands[5]
    exp_count, unit_count = lax.axis_size("exp"), lax.axis_size("unit")
    unit_width = gate_weight.shape[1]
    paired = (
        2 * unit_width == FF
        and unit_count % 2 == 0
        and exp_count * unit_count // 2 == EXPERTS
        and TILE % tokens.shape[0] == 0
        and unit_width % BLOCK == 0
        and unit_count == 4
        and tokens.shape[1] % (unit_count * BLOCK) == 0
        and tokens.shape[1] <= READY * BLOCK <= 2 * tokens.shape[1]
    )
    return (paired_experts if paired else spread_experts)(*operands)


def solution(mesh):
    return jax.shard_map(
        per_device,
        mesh=mesh,
        in_specs=(
            P(("rep", "exp"), None),
            P(),
            P(("rep", "exp"), None),
            P(("rep", "exp"), None),
            P("rep", None, None),
            P(None, ("exp", "unit")),
            P(None, ("exp", "unit")),
            P(("exp", "unit"), None),
        ),
        out_specs=P(("rep", "exp"), "unit"),
        check_vma=False,
    )
```

```python
import functools

import jax
import jax.numpy as jnp
import numpy as np
from jax import lax
from jax.experimental import pallas as pl
from jax.experimental.pallas import tpu as pltpu
from jax.sharding import PartitionSpec as P

EXPERTS = 8
FF = 7168
BLK = 64
TILE = 256
CAP = 40

EPSILON = 1e-05

BLOCK = 512
READY = 12
BUFFERS = 13
LIMIT = 5

F32 = jnp.float32
BF16 = jnp.bfloat16


def normalize(tokens, norm_gain):
    values = tokens.astype(jnp.float32)
    inv_rms = lax.rsqrt(jnp.mean(values * values, axis=-1, keepdims=True) + EPSILON)
    return (values * inv_rms * norm_gain).astype(jnp.bfloat16)


def slot_numbers(entries, expert_count):
    onehot = (entries[..., None] == jnp.arange(expert_count, dtype=jnp.int32)).astype(jnp.int32)
    before = jnp.cumsum(onehot, axis=-2, dtype=jnp.int32) - onehot
    return jnp.sum(before * onehot, axis=-1)


def spread_experts(
    tokens, norm_gain, route_ids, route_weight, active_blocks, gate_weight, up_weight, down_weight
):
    exp_count = lax.axis_size("exp")
    unit_count = lax.axis_size("unit")
    tok_count, feature_width = tokens.shape
    unit_width = gate_weight.shape[1]
    row_units = unit_count * unit_width
    per_exp = max(1, row_units // FF)
    part_width = feature_width // unit_count
    block_count = unit_width // BLK
    tile_count = active_blocks.shape[0]
    exp_index = lax.axis_index("exp")
    unit_index = lax.axis_index("unit")
    first_unit = (exp_index * unit_count + unit_index) * unit_width
    own_expert = first_unit // FF
    first_block = first_unit % FF // BLK
    local_expert = own_expert - exp_index * row_units // FF
    normed = normalize(tokens, norm_gain)
    slot_index = slot_numbers(route_ids.reshape(1, -1), EXPERTS).reshape(tok_count, 2)
    positions = jnp.arange(tok_count, dtype=jnp.int32)
    tile_of = (exp_index * tok_count + positions) // TILE
    route_slot = (route_ids * CAP + slot_index).reshape(-1)
    token_source = (
        jnp.full((EXPERTS * CAP,), tok_count, jnp.int32)
        .at[route_slot]
        .set(jnp.repeat(positions, 2))
    )
    row_experts = np.arange(exp_count)[:, None] * row_units // FF + np.arange(per_exp)[None, :]
    slot_source = token_source.reshape(EXPERTS, CAP)[row_experts]
    padded_tiles = jnp.concatenate([tile_of, jnp.zeros((1,), jnp.int32)])
    slot_tiles = padded_tiles[slot_source]
    active_mine = lax.dynamic_index_in_dim(active_blocks, own_expert, 1, keepdims=False)
    local_blocks = first_block + jnp.arange(block_count, dtype=jnp.int32)
    block_on = jnp.any(active_mine[:, :, None] == local_blocks[None, None, :], axis=1).astype(
        jnp.float32
    )
    row_part = lax.dynamic_slice_in_dim(normed, unit_index * part_width, part_width, 1)
    padded_rows = jnp.concatenate([row_part, jnp.zeros((1, part_width), jnp.bfloat16)], 0)
    whole_rows = lax.all_gather(
        lax.all_to_all(padded_rows[slot_source], "exp", split_axis=0, concat_axis=0, tiled=True),
        "unit",
        axis=3,
        tiled=True,
    )
    slot_count = whole_rows.shape[2]
    own_rows = lax.dynamic_index_in_dim(whole_rows, local_expert, 1, keepdims=False).reshape(
        -1, feature_width
    )
    own_tiles = lax.dynamic_index_in_dim(
        lax.all_to_all(slot_tiles, "exp", split_axis=0, concat_axis=0, tiled=True),
        local_expert,
        1,
        keepdims=False,
    ).reshape(-1)
    tile_hot = (own_tiles[:, None] == jnp.arange(tile_count, dtype=jnp.int32)[None, :]).astype(
        jnp.float32
    )
    row_mask = jnp.dot(tile_hot, block_on, precision=lax.Precision.HIGHEST)
    gate_acts = jnp.dot(own_rows, gate_weight, preferred_element_type=jnp.float32)
    up_acts = jnp.dot(own_rows, up_weight, preferred_element_type=jnp.float32)
    hidden = jax.nn.relu(gate_acts) * jax.nn.relu(up_acts)
    hidden = (hidden.reshape(-1, block_count, BLK) * row_mask[:, :, None]).reshape(-1, unit_width)
    hidden = hidden.astype(jnp.bfloat16)
    partial_value = jnp.dot(hidden, down_weight, preferred_element_type=jnp.float32)
    partial_value = partial_value.reshape(exp_count, slot_count, feature_width)
    result = jnp.zeros((exp_count, per_exp, slot_count, feature_width), jnp.float32)
    partial_all = lax.dynamic_update_index_in_dim(result, partial_value, local_expert, 1)

    def by_expert(returned):
        last_width = returned.shape[-1]
        if per_exp == 1:
            grouped = returned.reshape(EXPERTS, exp_count // EXPERTS, CAP, last_width)
            return jnp.sum(grouped, axis=1, dtype=jnp.float32)
        return returned.reshape(EXPERTS, CAP, last_width).astype(jnp.float32)

    summed = lax.psum_scatter(
        partial_all.astype(jnp.bfloat16), "unit", scatter_dimension=3, tiled=True
    ).astype(jnp.float32)
    returned = lax.all_to_all(
        summed.astype(jnp.bfloat16), "exp", split_axis=0, concat_axis=0, tiled=True
    ).astype(summed.dtype)
    per_expert = by_expert(returned)
    last_width = per_expert.shape[-1]
    picked = per_expert.reshape(EXPERTS * CAP, last_width)[route_slot].reshape(
        tok_count, 2, last_width
    )
    mixed = jnp.sum(route_weight[:, :, None] * picked, axis=1)
    return mixed.astype(jnp.bfloat16)


def place(sizes):
    exp_count, groups = sizes
    return lax.axis_index("exp"), lax.axis_index("unit") // 2, lax.axis_index("unit") % 2


def pick_rows(named, before, d):
    rows = named.shape[1]
    place_of = jnp.where(named[d : d + 1, :] > 0, before[d : d + 1, :], -1)
    return (place_of == lax.broadcasted_iota(jnp.int32, (CAP, rows), 0)).astype(F32)


def count_earlier(ids, experts):
    rows = ids.shape[1]
    earlier = (
        lax.broadcasted_iota(jnp.int32, (rows, rows), 0)
        < lax.broadcasted_iota(jnp.int32, (rows, rows), 1)
    ).astype(BF16)
    named = ((ids[0:1, :] == experts) | (ids[1:2, :] == experts)).astype(jnp.int32)
    before = jnp.dot(named.astype(BF16), earlier, preferred_element_type=F32)
    return named, before.astype(jnp.int32)


def group_experts(exp_count, groups, z, g, rows):
    distance = lax.broadcasted_iota(jnp.int32, (max(8, exp_count), rows), 0)
    return lax.rem(z + distance, exp_count) * groups + g


def fetch_rows(weight, line, buffer, sem):
    def start(index, carry):
        pltpu.make_async_copy(
            weight.at[
                pl.ds(line * BLOCK, BLOCK), pl.ds(pl.multiple_of(index * BLOCK, BLOCK), BLOCK)
            ],
            buffer.at[index],
            sem,
        ).start()
        return carry

    lax.fori_loop(0, buffer.shape[0], start, 0)


def fetch_columns(sizes, down, offset, keep, step, buffer, sem):
    exp_count, groups = sizes
    z, g, s = place(sizes)
    side = s if keep else 1 - s
    part = down.shape[1] // (2 * groups)
    column = (lax.rem(g + offset, groups) * 2 + side) * part + step * BLOCK

    def start(index, carry):
        pltpu.make_async_copy(
            down.at[
                pl.ds(pl.multiple_of(index * BLOCK, BLOCK), BLOCK),
                pl.ds(pl.multiple_of(column, BLOCK), BLOCK),
            ],
            buffer.at[index],
            sem,
        ).start()
        return carry

    lax.fori_loop(0, buffer.shape[0], start, 0)


def await_all(buffer, sem):
    pltpu.make_async_copy(buffer, buffer, sem).wait()


def stacked(buffer):
    return buffer[...].reshape(buffer.shape[0] * BLOCK, BLOCK)


def route_kernel(sizes, width, tokens_hbm, gain_hbm, ids_hbm, gate, own, buffer, *rest):
    exp_count, groups = sizes
    sends, (tokens, normed, gain, ids, sems, gate_sem) = rest[:-6], rest[-6:]
    rows, features = tokens.shape
    count = 4
    lines = [pl.ds(n * (rows // count), rows // count) for n in range(count)]
    pairs = [(gain_hbm, gain), (ids_hbm, ids)]
    pairs += [(tokens_hbm.at[part, :], tokens.at[part, :]) for part in lines]
    copies = [pltpu.make_async_copy(a, b, sems.at[n]) for n, (a, b) in enumerate(pairs)]
    for copy in copies:
        copy.start()
    fetch_rows(gate, 0, buffer, gate_sem)
    z, g, s = place(sizes)
    copies[0].wait()
    copies[1].wait()
    named, before = count_earlier(ids, group_experts(exp_count, groups, z, g, rows))
    picks = [pick_rows(named, before, d) for d in range(exp_count)]
    others = jnp.concatenate(picks[1:], axis=0).astype(BF16)
    step = 16
    for first in range(0, rows, step):
        if first % (rows // count) == 0:
            copies[2 + first // (rows // count)].wait()
        values = tokens[first : first + step, :].astype(F32)
        mean = jnp.sum(values * values, axis=1, keepdims=True) * (1.0 / features)
        inv_rms = lax.rsqrt(mean + EPSILON)
        normed[first : first + step, :] = (values * inv_rms * gain[...]).astype(BF16)
    start = pl.multiple_of(s * (features // 2), 128)
    found = jnp.dot(others, normed[:, pl.ds(start, width)], preferred_element_type=F32)
    for d, send in enumerate(sends):
        send[...] = found[d * CAP : (d + 1) * CAP, :].astype(BF16)
    own[...] = jnp.dot(
        picks[0].astype(BF16), normed[...], preferred_element_type=F32
    ).astype(BF16)
    await_all(buffer, gate_sem)


def distances(exp_count):
    middle = exp_count // 2
    return [middle] + [d for d in range(1, exp_count) if d != middle]


def arrivals(sizes):
    exp_count, groups = sizes
    order = distances(exp_count) + [0]
    early = [(o, d) for o in range(1, groups) for d in order]
    late = [(0, d) for d in order]
    return early, late


def table_kernel(
    sizes, ids_hbm, weights_hbm, after, gate, up, _, combine_high, combine_low, buffer, ids, weights,
    sems, sem
):
    exp_count, groups = sizes
    lines = gate.shape[0] // BLOCK
    last = READY - 1
    fetch_rows(gate if last < lines else up, last % lines, buffer, sem)
    pairs = ((ids_hbm, ids), (weights_hbm, weights))
    copies = [pltpu.make_async_copy(a, b, sems.at[n]) for n, (a, b) in enumerate(pairs)]
    for copy in copies:
        copy.start()
    for copy in copies:
        copy.wait()
    rows = ids.shape[1]
    z, g, s = place(sizes)
    zero = jnp.zeros((CAP, rows), F32)
    padded = combine_high.shape[2]
    batches = arrivals(sizes)
    experts = [
        lax.rem(z + d, exp_count) * groups + lax.rem(g - o + groups, groups)
        for batch in batches
        for o, d in batch
    ]
    line = lax.broadcasted_iota(jnp.int32, (max(8, len(experts)), rows), 0)
    listed = jnp.full(line.shape, -1, jnp.int32)
    for n, expert in enumerate(experts):
        listed = jnp.where(line == n, expert, listed)
    named, before = count_earlier(ids, listed)
    for order, batch in enumerate(batches):
        parts = []
        for n in range(len(batch)):
            entry = order * len(batch) + n
            here = pick_rows(named, before, entry) > 0
            first = jnp.where(here & (ids[0:1, :] == experts[entry]), weights[0:1, :], zero)
            second = jnp.where(here & (ids[1:2, :] == experts[entry]), weights[1:2, :], zero)
            parts.append(first + second)
        if padded > len(batch) * CAP:
            parts.append(jnp.zeros((padded - len(batch) * CAP, rows), F32))
        table = jnp.concatenate(parts, axis=0).T
        high = table.astype(BF16)
        combine_high[order] = high
        combine_low[order] = (table - high.astype(F32)).astype(BF16)
    await_all(buffer, sem)


def prepare_kernel(sizes, rows, active_hbm, gate, up, after, _, mask, *rest):
    exp_count, groups = sizes
    *buffers, active, small_sem, sems = rest
    z, g, s = place(sizes)
    small = pltpu.make_async_copy(active_hbm, active, small_sem)
    small.start()
    lines = gate.shape[0] // BLOCK
    for n, buffer in enumerate(buffers[1 : READY - 1], 1):
        fetch_rows(gate if n < lines else up, n % lines, buffer, sems.at[n])
    small.wait()
    unit_width = mask.shape[1]
    blocks = lax.broadcasted_iota(jnp.int32, mask.shape, 1) // BLK + s * (unit_width // BLK)
    source = lax.broadcasted_iota(jnp.int32, (mask.shape[0], 1), 0)
    own_expert = z * groups + g

    def add_entry(k, found):
        entry = jnp.full((mask.shape[0], 1), -1, jnp.int32)
        for d in range(exp_count):
            tile = lax.rem(z - d + exp_count, exp_count) * rows // TILE
            entry = jnp.where(source == d, active[tile, own_expert, k], entry)
        return jnp.where(blocks == entry, 1.0, found)

    mask[...] = lax.fori_loop(0, active.shape[2], add_entry, jnp.zeros(mask.shape, F32))
    for n, buffer in enumerate(buffers[1 : READY - 1], 1):
        await_all(buffer, sems.at[n])


def join_kernel(order, after, *refs):
    pieces = [refs[order.index(d + 1)][...].astype(F32) for d in range(len(order))]
    refs[-1][...] = jnp.concatenate(pieces, axis=0).astype(BF16)


def hidden_kernel(sizes, own, mine, other, *refs):
    exp_count, groups = sizes
    z, g, s = place(sizes)
    refs = list(refs)
    refs = refs[BUFFERS:]
    up, down, mask, _, hidden, gives = [refs.pop(0) for _ in range(6)]
    buffers = [refs.pop(0) for _ in range(BUFFERS)]
    total, rows, sems = refs
    half = own.shape[1] // 2
    features, unit_width = up.shape
    columns, lines = unit_width // BLOCK, features // BLOCK
    given = features // (2 * groups) // BLOCK
    count = len(buffers)

    def fetch(index):
        buffer, sem = buffers[index % count], sems.at[index % count]
        if index < 2 * lines:
            fetch_rows(up, index - lines, buffer, sem)
        elif index < 2 * lines + groups * given:
            order, step = divmod(index - 2 * lines, given)
            fetch_columns(sizes, down, order + 1, False, step, buffer, sem)
        elif index < 2 * lines + (groups + 1) * given:
            step = index - 2 * lines - groups * given
            fetch_columns(sizes, down, 1, True, step, buffer, sem)

    for index in range(READY, count):
        fetch(index)
    for source, side in ((mine, s), (other, 1 - s)):
        cols = pl.ds(pl.multiple_of(side * half, 128), half)
        joined = [own[:, cols].astype(F32), source[...].astype(F32)]
        rows[:, cols] = jnp.concatenate(joined, axis=0).astype(BF16)
    for index in range(0, 2 * lines, 2):
        pair = [buffers[(index + n) % count] for n in range(2)]
        for n in range(2):
            if index + n >= READY:
                await_all(pair[n], sems.at[(index + n) % count])
        line = index % lines
        left = [rows[:, (line + n) * BLOCK : (line + n + 1) * BLOCK] for n in range(2)]
        for column in range(columns):
            cols = slice(column * BLOCK, (column + 1) * BLOCK)
            value = jnp.dot(left[0], pair[0][column], preferred_element_type=F32)
            value = value + jnp.dot(left[1], pair[1][column], preferred_element_type=F32)
            if line > 0:
                value = total[:, cols] + value
            if line < lines - 2:
                total[:, cols] = value
                continue
            if index < lines:
                hidden[:, cols] = jnp.maximum(value, 0.0).astype(BF16)
                continue
            value = hidden[:, cols].astype(F32) * jnp.maximum(value, 0.0)
            parts = []
            for d in range(exp_count):
                parts.append(value[d * CAP : (d + 1) * CAP, :] * mask[d : d + 1, cols])
            hidden[:, cols] = jnp.concatenate(parts, axis=0).astype(BF16)
        for n in range(2):
            fetch(index + n + count)
    for index in range(2 * lines, 2 * lines + (groups + 1) * given):
        buffer = buffers[index % count]
        await_all(buffer, sems.at[index % count])
        step = index - 2 * lines
        if step < given:
            value = jnp.dot(hidden[...], stacked(buffer), preferred_element_type=F32)
            gives[:, step * BLOCK : (step + 1) * BLOCK] = value.astype(BF16)


def give_kernel(sizes, offset, hidden, *refs):
    exp_count, groups = sizes
    *weights, down, given, kept_weights, sem = refs
    fetch_columns(sizes, down, offset, True, 0, kept_weights, sem)
    for step, buffer in enumerate(weights):
        value = jnp.dot(hidden[...], stacked(buffer), preferred_element_type=F32)
        given[:, step * BLOCK : (step + 1) * BLOCK] = value.astype(BF16)
    await_all(kept_weights, sem)


def keep_kernel(sizes, offset, lacks, hidden, received, *refs):
    exp_count, groups = sizes
    refs = list(refs)
    extra = []
    if lacks:
        sems, scratch, down = refs.pop(), refs.pop(), refs.pop(0)
        extra = [scratch.at[n] for n in range(lacks)]
    held = received.shape[1] // BLOCK - lacks
    for n, buffer in enumerate(extra):
        fetch_columns(sizes, down, offset, True, held + n, buffer, sems.at[n])
    weights, outs = refs[:held] + extra, refs[held:]
    for step, buffer in enumerate(weights):
        if step >= held:
            await_all(buffer, sems.at[step - held])
        cols = slice(step * BLOCK, (step + 1) * BLOCK)
        value = jnp.dot(hidden[...], stacked(buffer), preferred_element_type=F32)
        value = value + received[:, cols].astype(F32)
        for d in range(exp_count):
            outs[d][:, cols] = value[d * CAP : (d + 1) * CAP, :].astype(BF16)


def combine_kernel(order, high, low, *refs):
    refs = list(refs)
    out = refs.pop()
    before = refs.pop(0) if order > 0 else None
    found = jnp.concatenate([r[...].astype(F32) for r in refs], axis=0).astype(BF16)
    count = found.shape[0]
    value = jnp.dot(high[order, :, :count], found, preferred_element_type=F32)
    value = value + jnp.dot(low[order, :, :count], found, preferred_element_type=F32)
    if before is not None:
        value = before[...] + value
    out[...] = value.astype(out.dtype)


def call(kernel, outs, ins, scratch=(), flops=0, moved=0, aliases=None):
    vmem = pl.BlockSpec(memory_space=pltpu.VMEM)
    arrays, specs = [], []
    for array, space in ins:
        if space in (pltpu.HBM, pltpu.VMEM):
            array = pltpu.with_memory_space_constraint(array, space)
        arrays.append(array)
        specs.append(vmem if space is None else pl.BlockSpec(memory_space=space))
    shapes = []
    for shape, kind, *space in outs:
        shapes.append(space[0](shape, kind) if space else jax.ShapeDtypeStruct(shape, kind))
    return pl.pallas_call(
        kernel,
        out_shape=shapes,
        in_specs=specs,
        out_specs=[vmem] * len(outs),
        scratch_shapes=list(scratch),
        input_output_aliases=aliases or {},
        compiler_params=pltpu.CompilerParams(vmem_limit_bytes=LIMIT << 20),
        cost_estimate=pl.CostEstimate(flops=flops, bytes_accessed=moved, transcendentals=0),
    )(*arrays)


def paired_experts(
    tokens, norm_gain, route_ids, route_weight, active_blocks, gate_weight, up_weight, down_weight
):
    exp_count, unit_count = lax.axis_size("exp"), lax.axis_size("unit")
    groups = unit_count // 2
    sizes = (exp_count, groups)
    tok_count, features = tokens.shape
    unit_width = gate_weight.shape[1]
    slots = exp_count * CAP
    half = features // 2
    width = half
    ids = route_ids.T
    weights = route_weight.T

    def shift(value, distance, group_shift=0):
        pairs = []
        for z in range(exp_count):
            for u in range(unit_count):
                target = (z + distance) % exp_count
                group = (u // 2 + group_shift) % groups
                pairs.append((z * unit_count + u, target * unit_count + group * 2 + u % 2))
        return lax.ppermute(value, ("exp", "unit"), pairs)

    def swap(value):
        return lax.ppermute(value, "unit", [(u, u ^ 1) for u in range(unit_count)])

    batch = exp_count - 1
    buffer = ((unit_width // BLOCK, BLOCK, BLOCK), BF16, pltpu.VMEM)
    piece_bytes = 2 * unit_width * BLOCK
    own, ready, *sends = call(
        functools.partial(route_kernel, sizes, width),
        [((CAP, features), BF16), buffer] + [((CAP, width), BF16)] * batch,
        [
            (tokens, pltpu.HBM),
            (norm_gain.reshape(1, -1), pltpu.HBM),
            (ids, pltpu.HBM),
            (gate_weight, pltpu.HBM),
        ],
        [
            pltpu.VMEM((tok_count, features), BF16),
            pltpu.VMEM((tok_count, features), BF16),
            pltpu.VMEM((1, features), F32),
            pltpu.VMEM(ids.shape, jnp.int32),
            pltpu.SemaphoreType.DMA((6,)),
            pltpu.SemaphoreType.DMA,
        ],
        flops=2 * tok_count * slots * width,
        moved=4 * tok_count * features + piece_bytes,
    )
    mask, *ready = call(
        functools.partial(prepare_kernel, sizes, tok_count),
        [((max(8, exp_count), unit_width), F32)] + [buffer] * BUFFERS,
        [
            (active_blocks, pltpu.HBM),
            (gate_weight, pltpu.HBM),
            (up_weight, pltpu.HBM),
            (own, pl.ANY),
            (ready, pltpu.VMEM),
        ],
        [
            pltpu.SMEM(active_blocks.shape, jnp.int32),
            pltpu.SemaphoreType.DMA,
            pltpu.SemaphoreType.DMA((READY,)),
        ],
        flops=2 * tok_count * slots * features,
        moved=(READY - 2) * piece_bytes,
        aliases={4: 1},
    )
    order = list(range(1, exp_count))
    arrived = [shift(sends[d - 1], d) for d in order]
    mine = call(
        functools.partial(join_kernel, order),
        [((batch * CAP, width), BF16)],
        [(mask, pl.ANY)] + [(v, None) for v in arrived],
        moved=1 << 20,
    )[0]
    other = swap(mine)
    padded = -(-slots // 128) * 128
    combine_high, combine_low, ready[READY - 1] = call(
        functools.partial(table_kernel, sizes),
        [((2, tok_count, padded), BF16)] * 2 + [buffer],
        [
            (ids, pltpu.HBM),
            (weights, pltpu.HBM),
            (mine, pl.ANY),
            (gate_weight, pltpu.HBM),
            (up_weight, pltpu.HBM),
            (ready[READY - 1], pltpu.VMEM),
        ],
        [
            pltpu.VMEM(ids.shape, jnp.int32),
            pltpu.VMEM(weights.shape, F32),
            pltpu.SemaphoreType.DMA((2,)),
            pltpu.SemaphoreType.DMA,
        ],
        moved=1 << 22,
        aliases={5: 2},
    )
    part = features // unit_count
    hidden, first_given, *buffers = call(
        functools.partial(hidden_kernel, sizes),
        [((slots, unit_width), BF16), ((slots, part), BF16)] + [buffer] * BUFFERS,
        [(own, None), (mine, None), (other, None)]
        + [(v, pltpu.VMEM) for v in ready]
        + [(up_weight, pltpu.HBM), (down_weight, pltpu.HBM), (mask, None)]
        + [(combine_low, pl.ANY)],
        [
            pltpu.VMEM((slots, unit_width), F32),
            pltpu.VMEM((slots, features), BF16),
            pltpu.SemaphoreType.DMA((BUFFERS,)),
        ],
        flops=2 * 2 * slots * features * unit_width,
        moved=10 * piece_bytes,
        aliases={3 + n: 2 + n for n in range(BUFFERS)},
    )
    steps = part // BLOCK
    offsets = [(order + 1) % groups for order in range(groups)]
    first = 2 * features // BLOCK + groups * steps
    given = [first_given]
    kept_weights = [[buffers[(first + step) % BUFFERS] for step in range(steps)]]
    for order, offset in list(enumerate(offsets))[1:]:
        first = 2 * features // BLOCK + order * steps
        value, *kept = call(
            functools.partial(give_kernel, sizes, offset),
            [((slots, part), BF16), buffer],
            [(hidden, None)]
            + [(buffers[(first + step) % BUFFERS], pltpu.VMEM) for step in range(steps)]
            + [(down_weight, pltpu.HBM)],
            [pltpu.SemaphoreType.DMA],
            flops=2 * slots * unit_width * part,
            moved=piece_bytes,
        )
        given.append(value)
        kept_weights.append(kept)
    taken = [swap(value) for value in given]
    home = {}
    for order, offset in enumerate(offsets):
        lacks = steps - len(kept_weights[order])
        kept = call(
            functools.partial(keep_kernel, sizes, offset, lacks),
            [((CAP, part), BF16)] * exp_count,
            [(hidden, None), (taken[order], None)]
            + ([(down_weight, pltpu.HBM)] if lacks else [])
            + [(v, pltpu.VMEM) for v in kept_weights[order]],
            [
                pltpu.VMEM((lacks,) + buffer[0], BF16),
                pltpu.SemaphoreType.DMA((lacks,)),
            ]
            if lacks
            else [],
            flops=2 * slots * unit_width * part,
            moved=piece_bytes,
        )
        for d in distances(exp_count) + [0]:
            home[offset, d] = shift(kept[d], -d, offset) if d or offset else kept[d]
    mixed = None
    for order, batch in enumerate(arrivals(sizes)):
        last = order == 1
        mixed = call(
            functools.partial(combine_kernel, order),
            [((tok_count, part), BF16 if last else F32)],
            [(combine_high, None), (combine_low, None)]
            + ([(mixed, None)] if order else [])
            + [(home[key], None) for key in batch],
            flops=4 * tok_count * slots * part,
            moved=1 << 20,
        )[0]
    return mixed


def per_device(*operands):
    tokens, gate_weight = operands[0], operands[5]
    exp_count, unit_count = lax.axis_size("exp"), lax.axis_size("unit")
    unit_width = gate_weight.shape[1]
    paired = (
        2 * unit_width == FF
        and unit_count % 2 == 0
        and exp_count * unit_count // 2 == EXPERTS
        and TILE % tokens.shape[0] == 0
        and unit_width % BLOCK == 0
        and unit_count == 4
        and tokens.shape[1] % (unit_count * BLOCK) == 0
        and tokens.shape[1] <= READY * BLOCK <= 2 * tokens.shape[1]
    )
    return (paired_experts if paired else spread_experts)(*operands)


def solution(mesh):
    return jax.shard_map(
        per_device,
        mesh=mesh,
        in_specs=(
            P(("rep", "exp"), None),
            P(),
            P(("rep", "exp"), None),
            P(("rep", "exp"), None),
            P("rep", None, None),
            P(None, ("exp", "unit")),
            P(None, ("exp", "unit")),
            P(("exp", "unit"), None),
        ),
        out_specs=P(("rep", "exp"), "unit"),
        check_vma=False,
    )
```
